32 devices in a mesh: grp: 2 (over y), ka: 4 (over z), pb: 2 (over x), wa: 2 (over core).
Axes of the slice: x: 2, y: 2, z: 4, core: 2. Of those that a mesh axis runs over, the one named last changes fastest.
Arguments:
- green: bfloat16 [2, 8, 2, 8, 208], P('wa', ('grp', 'ka'), 'pb'), parts along dimension 1, may hold values from -14 to 14
- fields: float32 [2, 2, 8, 256], P('wa', 'pb', 'grp'), parts along dimension 2, may hold values from -5 to 5
- orbitals: float32 [2, 8, 8, 208], P('wa', 'ka', 'grp'), parts along dimension 2, may hold values from -6 to 6
- chol_half: bfloat16 [2, 8, 2, 104, 256], P('pb', 'ka'), may hold values from -0.21875 to 0.21875
- chol_full: bfloat16 [2, 8, 2, 676, 256], P('pb', 'ka'), may hold values from -0.0546875 to 0.0546875
- chol_count: int32 [2], replicated, may hold values from 128 to 256, as said below
- kq_map: int32 [2, 8], replicated, may hold values from 0 to 7, each once within a row
Outputs:
- propagated: float32 [2, 8, 8, 208], P('wa', 'ka', 'grp'), parts along dimension 2
- energy: float32 [2, 8], P('wa', ('grp', 'ka')), parts along dimension 1
The draws below stay inside these ranges and needn't reach their ends.
There are 2 independent parts, one for each index of `grp`. The reference program is written for one: setup_inputs(seed, part) draws one part's arguments, and reference() takes and returns one part's arrays. A program takes and returns all parts, laid end to end along the dimension named above; an argument that names none is the same for every part. Nothing has to cross between parts.
Inputs may be any that keep to these rules, and one draw needn't show every extreme that they name: `chol_count`: one momentum transfer keeps all 256 vectors.
All inputs are finite; a program needn't handle non-finite values.
Results may differ from the reference program's by a relative error of at most 0.0037.
Values may be sent and summed in bfloat16 or wider, within the bound.
No kernel may reach another device: no remote copies, remote signals or barrier semaphores. Data moves between devices by JAX's collectives and lax.ppermute only.
A program may use at most 64 MiB of HBM per device.

```python
import jax
import jax.numpy as jnp
from jax import lax

M = 26
NOCC = 4
NCHOL = 256
TAYLOR = 3
NK = 8
WH = 4
NQW = 2
N_WA = 2


def draw_green(key, part):
    key = jax.random.fold_in(key, 5)
    key_base, key_spread = jax.random.split(key, 2)
    shape = (N_WA, WH, NQW, NK, 2 * NOCC * M)
    rising = jnp.exp(jnp.log(3.0) * jnp.arange(NK, dtype=jnp.float32) / max(NK - 1, 1))
    spread = jnp.exp(jax.random.uniform(key_spread, shape[:4], minval=-1.15, maxval=1.15))
    base = jnp.clip(jax.random.normal(key_base, shape), -4.0, 4.0)
    values = 0.35 * base * rising[None, None, None, :, None] * spread[..., None]
    return values.astype(jnp.bfloat16)


def draw_chol_count(key, part):
    key = jax.random.fold_in(key, 7)
    key_order, key_value = jax.random.split(key, 2)
    order = jax.random.permutation(key_order, NQW)
    values = jax.random.randint(key_value, (NQW,), NCHOL // 2, NCHOL + 1)
    values = jnp.where(order == 0, NCHOL, values)
    return values.astype(jnp.int32)


def levels(key, extent, shards, low, largest):
    loudness, own = 1.0, jax.random.fold_in(key, 6)
    for axis_at, shards_of in shards:
        steps = jnp.exp(jax.random.uniform(jax.random.fold_in(own, axis_at), (shards_of,), jnp.float32, low / len(shards), largest / len(shards)))
        loudness = loudness * jnp.repeat(steps, extent[axis_at] // shards_of).reshape([-1 if axis == axis_at else 1 for axis in range(len(extent))])
    return loudness


def scatter_about(stream_key, extent, scale, limit, shards=(), kind=jnp.bfloat16):
    array = scale * jax.random.normal(stream_key, extent, jnp.float32)
    if shards:
        array = array * levels(stream_key, extent, shards, -0.22, 0.18)
    return jnp.clip(array, -limit, limit).astype(kind)


def setup_inputs(seed: int = 0, part: int = 0) -> dict:
    key_of = jax.random.split(jax.random.key(seed), 8)
    part_splits = jax.random.split(jax.random.fold_in(key_of[7], part), 8)
    green = draw_green(jax.random.fold_in(jax.random.fold_in(key_of[7], part), 71), part)
    fields = scatter_about(part_splits[1], (N_WA, NQW, WH, NCHOL), 1.0, 5.0, ((0, 2), (1, 2)), jnp.float32)
    orbitals = scatter_about(part_splits[2], (N_WA, NK, WH, 2 * NOCC * M), 1.0, 6.0, ((0, 2), (1, 4)), jnp.float32)
    chol_half = scatter_about(key_of[3], (NQW, NK, 2, NOCC * M, NCHOL), (NK * NOCC * M) ** -0.5, 0.21875, ((0, 2), (1, 4)))
    chol_full = scatter_about(key_of[4], (NQW, NK, 2, M * M, NCHOL), (NQW * NCHOL * M) ** -0.5, 0.0546875, ((0, 2), (1, 4)))
    chol_count = draw_chol_count(jax.random.fold_in(key_of[7], 71), part)
    kq_map = jax.vmap(lambda own: jax.random.permutation(own, NK))(jax.random.split(key_of[6], NQW)).reshape((NQW, NK)).astype(jnp.int32)
    return {"green": green, "fields": fields, "orbitals": orbitals, "chol_half": chol_half, "chol_full": chol_full, "chol_count": chol_count, "kq_map": kq_map}


BIAS_STEP = 0.5
PROP_STEP = 0.5


def complex_sum(pattern, left_re, left_im, right_re, right_im):
    real_part = jnp.einsum(pattern, left_re, right_re) - jnp.einsum(pattern, left_im, right_im)
    imag_part = jnp.einsum(pattern, left_re, right_im) + jnp.einsum(pattern, left_im, right_re)
    return real_part, imag_part


def reference(green, fields, orbitals, chol_half, chol_full, chol_count, kq_map):
    walkers = N_WA * WH
    pair_width = NOCC * M
    vec_mask = (jnp.arange(NCHOL, dtype=jnp.int32)[None, :] < chol_count[:, None]).astype(jnp.float32)
    greens = green.astype(jnp.float32).reshape(walkers, NQW, NK, 2, pair_width)
    hartree = jnp.zeros((walkers,), jnp.float32)
    exchange = jnp.zeros((walkers,), jnp.float32)
    operators = []
    for transfer in range(NQW):
        green_part = greens[:, transfer]
        chol_part = chol_half[transfer].astype(jnp.float32)
        bias_re, bias_im = complex_sum("wkx,kxn->wn", green_part[:, :, 0], green_part[:, :, 1], chol_part[:, 0], chol_part[:, 1])
        bias_re = bias_re * vec_mask[transfer]
        bias_im = bias_im * vec_mask[transfer]
        hartree = hartree + 0.5 * jnp.sum(bias_re * bias_re + bias_im * bias_im, axis=1)
        field_now = fields[:, transfer].reshape(walkers, NCHOL)
        shift_re = ((field_now - BIAS_STEP * bias_re) * vec_mask[transfer]).astype(jnp.bfloat16)
        shift_im = (-BIAS_STEP * bias_im * vec_mask[transfer]).astype(jnp.bfloat16)
        shift_re = lax.optimization_barrier(shift_re).astype(jnp.float32)
        shift_im = lax.optimization_barrier(shift_im).astype(jnp.float32)

        def exchange_step(running, kpoint):
            chol_row = lax.dynamic_index_in_dim(chol_part, kpoint, 0, keepdims=False).reshape(2, NOCC, M, NCHOL)
            green_row = lax.dynamic_index_in_dim(green_part, kpoint, 1, keepdims=False).reshape(walkers, 2, NOCC, M)
            cross_re, cross_im = complex_sum("ipn,wjp->wijn", chol_row[0], chol_row[1], green_row[:, 0], green_row[:, 1])
            weight = jnp.sum((cross_re * cross_re + cross_im * cross_im) * vec_mask[transfer], axis=(1, 2, 3))
            return running + weight, None

        summed, _ = lax.scan(exchange_step, jnp.zeros((walkers,), jnp.float32), jnp.arange(NK, dtype=jnp.int32))
        exchange = exchange + 0.5 * summed
        chol_whole = chol_full[transfer].astype(jnp.float32)
        prop_re, prop_im = complex_sum("wn,kyn->wky", shift_re, shift_im, chol_whole[:, 0], chol_whole[:, 1])
        prop_re = lax.optimization_barrier((PROP_STEP * prop_re).astype(jnp.bfloat16)).astype(jnp.float32)
        prop_im = lax.optimization_barrier((PROP_STEP * prop_im).astype(jnp.bfloat16)).astype(jnp.float32)
        operators.append((prop_re.reshape(walkers, NK, M, M), prop_im.reshape(walkers, NK, M, M)))
    energy = ((hartree - exchange) / (NQW * NCHOL)).reshape(N_WA, WH)
    initial = orbitals.reshape(N_WA, NK, WH, 2, NOCC, M).transpose(0, 2, 1, 3, 4, 5).reshape(walkers, NK, 2, NOCC, M)
    summed_terms = initial
    current = initial
    for degree in range(1, TAYLOR + 1):
        rounded = lax.optimization_barrier(current.astype(jnp.bfloat16)).astype(jnp.float32)
        applied = jnp.zeros_like(current)
        for transfer in range(NQW):
            shifted_rows = jnp.take(rounded, kq_map[transfer], axis=1)
            out_re, out_im = complex_sum("wkpq,wkiq->wkip", operators[transfer][0], operators[transfer][1], shifted_rows[:, :, 0], shifted_rows[:, :, 1])
            applied = applied + jnp.stack([out_re, out_im], axis=2)
        current = applied / degree
        summed_terms = summed_terms + current
    propagated = summed_terms.reshape(N_WA, WH, NK, 2 * pair_width).transpose(0, 2, 1, 3)
    return propagated, energy
```

```python
import functools

import jax
import jax.numpy as jnp
from jax import lax
from jax.experimental import pallas as pl
from jax.experimental.pallas import tpu as pltpu
from jax.sharding import PartitionSpec as P

M = 26
NOCC = 4
TAYLOR = 3
LANES = 128


BIAS_STEP = 0.5
PROP_STEP = 0.5

F32 = jnp.float32
BF16 = jnp.bfloat16


def complex_dot(pattern, left_re, left_im, right_re, right_im):
    real_part = jnp.einsum(
        pattern, left_re, right_re, preferred_element_type=jnp.float32
    ) - jnp.einsum(pattern, left_im, right_im, preferred_element_type=jnp.float32)
    imag_part = jnp.einsum(
        pattern, left_re, right_im, preferred_element_type=jnp.float32
    ) + jnp.einsum(pattern, left_im, right_re, preferred_element_type=jnp.float32)
    return (real_part, imag_part)


def make_picker(wanted):

    def picker(shard_rows):
        row_count = shard_rows.shape[0]
        select = (wanted[:, None] == jnp.arange(row_count, dtype=jnp.int32)[None, :]).astype(
            jnp.bfloat16
        )
        return jnp.dot(select, shard_rows, preferred_element_type=jnp.float32)

    return picker


def with_collectives(green, fields, orbitals, chol_half, chol_full, chol_count, kq_map):
    q_local = chol_half.shape[0]
    k_local = chol_half.shape[1]
    pair_width = chol_half.shape[3]
    chol_cols = chol_half.shape[4]
    ka_count = lax.axis_size("ka")
    pb_count = lax.axis_size("pb")
    ka_pos = lax.axis_index("ka")
    pb_pos = lax.axis_index("pb")
    local_green = lax.all_to_all(green, "ka", split_axis=3, concat_axis=1, tiled=True)
    walkers = local_green.shape[1]
    per_device = walkers // ka_count
    greens = local_green[0].reshape(walkers, q_local, k_local, 2, pair_width)
    counts = lax.dynamic_slice_in_dim(chol_count, pb_pos * q_local, q_local)
    vec_mask = (jnp.arange(chol_cols, dtype=jnp.int32)[None, :] < counts[:, None]).astype(
        jnp.float32
    )
    bias_re, bias_im = complex_dot(
        "wqkx,qkxn->qwn",
        greens[:, :, :, 0],
        greens[:, :, :, 1],
        chol_half[:, :, 0],
        chol_half[:, :, 1],
    )
    own_rows = (jnp.arange(walkers, dtype=jnp.int32) // per_device == ka_pos).astype(jnp.float32)
    bias_re, bias_im = lax.psum((bias_re, bias_im), "ka")
    bias_re = bias_re * vec_mask[:, None, :]
    bias_im = bias_im * vec_mask[:, None, :]
    hartree = 0.5 * jnp.sum(bias_re * bias_re + bias_im * bias_im, axis=(0, 2)) * own_rows
    field_now = jnp.transpose(fields, (1, 0, 2, 3)).reshape(q_local, walkers, chol_cols)
    shift_re = ((field_now - BIAS_STEP * bias_re) * vec_mask[:, None, :]).astype(jnp.bfloat16)
    shift_im = (-BIAS_STEP * bias_im * vec_mask[:, None, :]).astype(jnp.bfloat16)
    exchange = jnp.zeros((walkers,), jnp.float32)
    for transfer in range(q_local):
        for kpoint in range(k_local):
            chol_row = chol_half[transfer, kpoint].reshape(2, NOCC, M, chol_cols)
            green_row = greens[:, transfer, kpoint].reshape(walkers, 2, NOCC, M)
            cross_re, cross_im = complex_dot(
                "ipn,wjp->wijn", chol_row[0], chol_row[1], green_row[:, 0], green_row[:, 1]
            )
            exchange = exchange + 0.5 * jnp.sum(
                (cross_re * cross_re + cross_im * cross_im) * vec_mask[transfer], axis=(1, 2, 3)
            )
    prop_re, prop_im = complex_dot(
        "qwn,qkyn->qwky", shift_re, shift_im, chol_full[:, :, 0], chol_full[:, :, 1]
    )
    shape = (q_local, walkers, k_local, M, M)
    oper_re = (PROP_STEP * prop_re).astype(jnp.bfloat16).reshape(shape)
    oper_im = (PROP_STEP * prop_im).astype(jnp.bfloat16).reshape(shape)
    normalizer = q_local * pb_count * chol_cols
    total_energy = lax.psum(hartree - exchange, ("ka", "pb")) / normalizer
    energy = lax.dynamic_slice_in_dim(total_energy, ka_pos * per_device, per_device).reshape(
        1, per_device
    )
    initial = orbitals[0].reshape(k_local, walkers, 2, NOCC, M)
    row_width = 2 * pair_width
    my_rows = lax.dynamic_slice_in_dim(kq_map, pb_pos * q_local, q_local, 0)
    wanted = lax.dynamic_slice_in_dim(my_rows, ka_pos * k_local, k_local, 1).reshape(
        q_local * k_local
    )
    picker = make_picker(wanted)
    current = initial
    summed_terms = initial
    for degree in range(1, TAYLOR + 1):
        rounded = current.astype(jnp.bfloat16).reshape(k_local, walkers * row_width)
        fetched = picker(lax.all_gather(rounded, "ka", axis=0, tiled=True))
        shifted_rows = fetched.astype(jnp.bfloat16).reshape(q_local, k_local, walkers, 2, NOCC, M)
        out_re, out_im = complex_dot(
            "xwkpq,xkwiq->kwip",
            oper_re,
            oper_im,
            shifted_rows[:, :, :, 0],
            shifted_rows[:, :, :, 1],
        )
        applied = jnp.stack([out_re, out_im], axis=2)
        applied = lax.psum(applied, "pb")
        current = applied / degree
        summed_terms = summed_terms + current
    propagated = summed_terms.reshape(1, k_local, walkers, row_width)
    return (propagated, energy)


def ring(array, axis, shift):
    size = lax.axis_size(axis)
    return lax.ppermute(array, axis, [(at, (at + shift) % size) for at in range(size)])


def pair_ring(array, ka_shift, pb_shift):
    ka_count, pb_count = lax.axis_size("ka"), lax.axis_size("pb")
    pairs = []
    for ka_at in range(ka_count):
        for pb_at in range(pb_count):
            to_ka, to_pb = (ka_at + ka_shift) % ka_count, (pb_at + pb_shift) % pb_count
            pairs.append((ka_at * pb_count + pb_at, to_ka * pb_count + to_pb))
    return lax.ppermute(array, ("ka", "pb"), pairs)


def origin(axis, shift):
    size = lax.axis_size(axis)
    return lax.rem(lax.axis_index(axis) + (size - shift), size)


def column_mask(count_ref, rows, columns):
    kept = count_ref[lax.axis_index("pb")]
    return lax.broadcasted_iota(jnp.int32, (rows, columns), 1) < kept


def bias_kernel(ka_count, k_local, *refs):
    greens, (chol_ref, bias_ref, own_ref, table) = refs[:ka_count], refs[ka_count:]
    for shift, green_ref in enumerate(greens):
        table[origin("ka", shift)] = green_ref[...].astype(F32)
    first = lax.axis_index("ka") * k_local
    width = chol_ref.shape[2]
    total = jnp.zeros(bias_ref.shape, F32)
    for k in range(k_local):
        rows = jnp.concatenate(
            [table[w, pl.ds(first + k, 1), :] for w in range(ka_count)], axis=0
        )
        real, imag = rows[:, :width], rows[:, width:]
        both = jnp.concatenate([real, imag], axis=0)
        turned = jnp.concatenate([-imag, real], axis=0)
        own_ref[k] = both
        total += jnp.dot(both.astype(BF16), chol_ref[k, 0], preferred_element_type=F32)
        total += jnp.dot(turned.astype(BF16), chol_ref[k, 1], preferred_element_type=F32)
    bias_ref[...] = total


def exchange_kernel(k_local, count_ref, own_ref, chol_ref, out_ref):
    walkers, width, columns = own_ref.shape[1] // 2, own_ref.shape[2], chol_ref.shape[3]
    rows = 2 * walkers
    lane = lax.broadcasted_iota(jnp.int32, (rows, LANES), 1)
    total = jnp.zeros((rows, columns), F32)
    for k in range(k_local):
        both = jnp.concatenate([own_ref[k], jnp.zeros((rows, LANES - width), F32)], axis=1)
        turned = jnp.concatenate([-both[walkers:], both[:walkers]], axis=0)
        sides = []
        for side in (both, turned):
            rolled = {
                step: side if step == 0 else pltpu.roll(side, (step * M) % LANES, 1)
                for step in range(1 - NOCC, NOCC)
            }
            blocks = []
            for i in range(NOCC):
                inside = (lane >= i * M) & (lane < (i + 1) * M)
                for j in range(NOCC):
                    blocks.append(jnp.where(inside, rolled[i - j], 0.0))
            sides.append(jnp.concatenate(blocks, axis=0)[:, :width].astype(BF16))
        cross = jnp.dot(sides[0], chol_ref[k, 0], preferred_element_type=F32)
        cross += jnp.dot(sides[1], chol_ref[k, 1], preferred_element_type=F32)
        cross = cross * cross
        for block in range(NOCC * NOCC):
            total += cross[block * rows : (block + 1) * rows]
    total = jnp.where(column_mask(count_ref, rows, columns), total, 0.0)
    total = total[:walkers] + total[walkers:]
    summed = 0.5 * jnp.sum(total, axis=1, keepdims=True)
    out_ref[...] = jnp.broadcast_to(summed, out_ref.shape)


def operator_kernel(ka_count, k_local, count_ref, *refs):
    parts = refs[:ka_count]
    fields_ref, exchange_ref, chol_ref, out_ref, straight, crossed, turned_ref = refs[ka_count:]
    bias = parts[0][...]
    for part in parts[1:]:
        bias = bias + part[...]
    walkers, columns = fields_ref.shape
    pairs = M * M
    bias = jnp.where(column_mask(count_ref, 2 * walkers, columns), bias, 0.0)
    bias_re, bias_im = bias[:walkers], bias[walkers:]
    hartree = 0.5 * jnp.sum(bias_re * bias_re + bias_im * bias_im, axis=1, keepdims=True)
    own = lax.broadcasted_iota(jnp.int32, (walkers, 1), 0) == lax.axis_index("ka")
    energy = jnp.where(own, hartree, 0.0) - exchange_ref[:, :1]
    kept = column_mask(count_ref, walkers, columns)
    shift_re = jnp.where(kept, fields_ref[...] - BIAS_STEP * bias_re, 0.0)
    shift_im = jnp.where(kept, -BIAS_STEP * bias_im, 0.0)
    for k in range(k_local):
        before, after = k * walkers, (k_local - 1 - k) * walkers

        def placed(first, second):
            gap = jnp.zeros((before, columns), F32), jnp.zeros((after, columns), F32)
            rest = jnp.zeros((LANES - 2 * k_local * walkers, columns), F32)
            pieces = [gap[0], first, gap[1], gap[0], second, gap[1], rest]
            return jnp.concatenate([p for p in pieces if p.shape[0]], axis=0)

        sides = jnp.concatenate(
            [placed(shift_re, shift_im), placed(-shift_im, shift_re)], axis=0
        ).astype(BF16)
        product = lax.dot_general(
            chol_ref[k], sides, (((1,), (1,)), ((), ())), preferred_element_type=F32
        )
        if k == 0:
            straight[...] = product[:, :LANES]
            crossed[...] = product[:, LANES:]
        else:
            straight[...] += product[:, :LANES]
            crossed[...] += product[:, LANES:]
    turned_ref[:pairs] = PROP_STEP * (
        straight[pl.ds(0, pairs, stride=2), :] + crossed[pl.ds(1, pairs, stride=2), :]
    )
    rows = out_ref.shape[0]
    width = out_ref.shape[1]
    lane = lax.broadcasted_iota(jnp.int32, (rows, LANES), 1)
    for at in range(0, width, LANES):
        block = turned_ref[at : at + LANES].T[:rows]
        if at + LANES > pairs:
            share = jnp.concatenate([energy, jnp.zeros((rows - walkers, 1), F32)], axis=0)
            block = jnp.where(lane + at < pairs, block, 0.0)
            for piece in range(3):
                head = share.astype(BF16).astype(F32)
                block = jnp.where(lane + at == pairs + piece, head, block)
                share = share - head
        out_ref[:, at : at + LANES] = block.astype(BF16)


def start_kernel(ka_count, pb_count, walkers, map_ref, *refs):
    orbitals, (picks_ref, first_ref, table) = refs[:ka_count], refs[ka_count:]
    k_local, _, width = orbitals[0].shape
    kpoints = k_local * ka_count
    half = LANES // 2
    lane = lax.broadcasted_iota(jnp.int32, (1, LANES), 1)
    lane_q = lax.rem(lane, half) // (kpoints * walkers)
    lane_k = lax.rem(lane, kpoints * walkers) // walkers
    source = jnp.zeros((1, LANES), jnp.int32)
    for q in range(pb_count):
        for k in range(kpoints):
            source = jnp.where((lane_q == q) & (lane_k == k), map_ref[q, k], source)
    wanted = source * walkers + lax.rem(lane, walkers)
    row = lax.broadcasted_iota(jnp.int32, (LANES, LANES), 0)
    real = jnp.where(row == wanted, 1.0, 0.0)
    sign = jnp.where(lane < half, 1.0, -1.0)
    imag = jnp.where(row == wanted + half, sign, 0.0)
    picks = jnp.concatenate([real, imag], axis=1).astype(BF16)
    picks_ref[...] = picks
    pair = width // 2
    table[...] = jnp.zeros_like(table)
    for shift, rows_ref in enumerate(orbitals):
        count = k_local * walkers
        start = pl.multiple_of(origin("ka", shift) * count, count)
        rows = jnp.concatenate([rows_ref[k] for k in range(k_local)], axis=0)
        table[pl.ds(start, count), :pair] = rows[:, :pair]
        table[pl.ds(start + half, count), :pair] = rows[:, pair:]
    turned = table[...].T[:pair].astype(BF16)
    first_ref[...] = jnp.dot(turned, picks, preferred_element_type=F32)


def taylor_kernel(ka_count, pb_count, normalizer, *refs):
    blocks = refs[: ka_count * pb_count]
    picks_ref, first_ref, orbitals_ref, out_ref, energy_ref, table, turned, picked, term = refs[
        ka_count * pb_count :
    ]
    half = LANES // 2
    pairs = M * M
    rows = blocks[0].shape[0] // 2
    for at, block_ref in enumerate(blocks):
        ka_from, pb_from = origin("ka", at // pb_count), origin("pb", at % pb_count)
        start = pl.multiple_of((pb_from * ka_count + ka_from) * rows, rows)
        block = block_ref[...].astype(F32)
        table[pl.ds(start, rows), :] = block[:rows]
        table[pl.ds(start + half, rows), :] = block[rows:]
    for at in range(0, table.shape[1], LANES):
        turned[at : at + LANES] = table[:, at : at + LANES].T
    ka_pos = lax.axis_index("ka")
    last = pairs // LANES * LANES
    shares = table[:half, last : last + LANES]
    lane = lax.broadcasted_iota(jnp.int32, shares.shape, 1) + last
    row = lax.broadcasted_iota(jnp.int32, shares.shape, 0)
    shares = jnp.where(
        (lane >= pairs) & (lane < pairs + 3) & (lax.rem(row, rows) == ka_pos), shares, 0.0
    )
    shares = jnp.sum(jnp.sum(shares, axis=0, keepdims=True), axis=1, keepdims=True)
    energy_ref[...] = shares / normalizer
    sums = [jnp.zeros((M, LANES), F32) for _ in range(NOCC)]
    for degree in range(1, TAYLOR + 1):
        source = first_ref if degree == 1 else picked
        straight = [jnp.zeros((M, LANES), F32) for _ in range(NOCC)]
        crossed = [jnp.zeros((M, LANES), F32) for _ in range(NOCC)]
        for c in range(M):
            column = turned[pl.ds(c, M, stride=M), :]
            for i in range(NOCC):
                at = i * M + c
                straight[i] += column * source[at : at + 1, :LANES]
                crossed[i] += column * source[at : at + 1, LANES:]
        for i in range(NOCC):
            applied = straight[i] + pltpu.roll(crossed[i], half, 1)
            applied = applied + pltpu.roll(applied, LANES - half // pb_count, 1)
            current = applied / degree
            sums[i] = sums[i] + current
            term[i * M : (i + 1) * M] = current if degree < TAYLOR else sums[i]
        if degree < TAYLOR:
            picked[...] = jnp.dot(
                term[: NOCC * M].astype(BF16), picks_ref[...], preferred_element_type=F32
            )
    term[NOCC * M :] = jnp.zeros((LANES - NOCC * M, LANES), F32)
    table[:, :LANES] = term[...].T
    k_local, walkers, _ = out_ref.shape
    pair = NOCC * M
    start = pl.multiple_of(ka_pos * rows, rows)
    real = table[pl.ds(start, rows), :pair]
    imag = table[pl.ds(start + half, rows), :pair]
    both = jnp.concatenate([real, imag], axis=1)
    for k in range(k_local):
        out_ref[k] = orbitals_ref[k] + both[k * walkers : (k + 1) * walkers]


def call(kernel, out, scratch=(), scalars=0, operands=0):
    smem = [pl.BlockSpec(memory_space=pltpu.SMEM)] * scalars
    vmem = [pl.BlockSpec(memory_space=pltpu.VMEM)] * operands
    return pl.pallas_call(
        kernel,
        out_shape=out,
        in_specs=smem + vmem,
        out_specs=jax.tree.map(lambda _: pl.BlockSpec(memory_space=pltpu.VMEM), out),
        scratch_shapes=list(scratch),
        compiler_params=pltpu.CompilerParams(vmem_limit_bytes=24 * 2**20),
    )


def direct(green, fields, orbitals, chol_half, chol_full, chol_count, kq_map):
    k_local, pair_width, chol_cols = chol_half.shape[1], chol_half.shape[3], chol_half.shape[4]
    ka_count, pb_count = lax.axis_size("ka"), lax.axis_size("pb")
    walkers = ka_count
    kpoints = green.shape[3]
    shape = jax.ShapeDtypeStruct
    own_green = green.reshape(kpoints, 2 * pair_width)
    own_orbitals = orbitals.reshape(k_local, walkers, 2 * pair_width)
    greens = [own_green] + [ring(own_green, "ka", s) for s in range(1, ka_count)]
    windows = [own_orbitals] + [ring(own_orbitals, "ka", s) for s in range(1, ka_count)]
    half = chol_half.reshape(k_local, 2, pair_width, chol_cols)
    full = jnp.transpose(chol_full[0], (0, 2, 1, 3)).reshape(k_local, 2 * M * M, chol_cols)
    bias, own = call(
        functools.partial(bias_kernel, ka_count, k_local),
        (shape((2 * walkers, chol_cols), F32), shape((k_local, 2 * walkers, pair_width), F32)),
        [pltpu.VMEM((walkers, kpoints, 2 * pair_width), F32)],
        operands=ka_count + 1,
    )(*greens, half)
    parts = [bias] + [ring(bias, "ka", s) for s in range(1, ka_count)]
    exchange = call(
        functools.partial(exchange_kernel, k_local),
        shape((walkers, LANES), F32),
        scalars=1,
        operands=2,
    )(chol_count, own, half)
    rows = 2 * k_local * walkers
    width = -(-(M * M + 3) // LANES) * LANES
    block = call(
        functools.partial(operator_kernel, ka_count, k_local),
        shape((rows, width), BF16),
        [pltpu.VMEM((2 * M * M, LANES), F32)] * 2 + [pltpu.VMEM((width, LANES), F32)],
        scalars=1,
        operands=ka_count + 3,
    )(chol_count, *parts, fields.reshape(walkers, chol_cols), exchange, full)
    blocks = [
        pair_ring(block, a, b) if a or b else block
        for a in range(ka_count)
        for b in range(pb_count)
    ]
    picks, first = call(
        functools.partial(start_kernel, ka_count, pb_count, walkers),
        (shape((LANES, 2 * LANES), BF16), shape((pair_width, 2 * LANES), F32)),
        [pltpu.VMEM((LANES, LANES), F32)],
        scalars=1,
        operands=ka_count,
    )(kq_map, *windows)
    propagated, energy = call(
        functools.partial(taylor_kernel, ka_count, pb_count, float(pb_count * chol_cols)),
        (shape((k_local, walkers, 2 * pair_width), F32), shape((1, 1), F32)),
        [
            pltpu.VMEM((LANES, width), F32),
            pltpu.VMEM((width, LANES), F32),
            pltpu.VMEM((pair_width, 2 * LANES), F32),
            pltpu.VMEM((LANES, LANES), F32),
        ],
        operands=ka_count * pb_count + 3,
    )(*blocks, picks, first, own_orbitals)
    return (propagated[None], energy)


def on_device(green, fields, orbitals, chol_half, chol_full, chol_count, kq_map):
    ka_count, pb_count = lax.axis_size("ka"), lax.axis_size("pb")
    walkers = orbitals.shape[2]
    fits = 2 * pb_count * kq_map.shape[1] * walkers == LANES
    if fits and chol_half.shape[0] == 1 and walkers == ka_count:
        return direct(green, fields, orbitals, chol_half, chol_full, chol_count, kq_map)
    return with_collectives(green, fields, orbitals, chol_half, chol_full, chol_count, kq_map)


def solution(mesh):
    placed = (
        P("wa", ("grp", "ka"), "pb", None, None),
        P("wa", "pb", "grp", None),
        P("wa", "ka", "grp", None),
        P("pb", "ka", None, None, None),
        P("pb", "ka", None, None, None),
        P(),
        P(),
    )
    return jax.shard_map(
        on_device,
        mesh=mesh,
        in_specs=placed,
        out_specs=(P("wa", "ka", "grp", None), P("wa", ("grp", "ka"))),
        check_vma=False,
    )
```

```python
import functools

import jax
import jax.numpy as jnp
from jax import lax
from jax.experimental import pallas as pl
from jax.experimental.pallas import tpu as pltpu
from jax.sharding import PartitionSpec as P

M = 26
NOCC = 4
TAYLOR = 3
LANES = 128


BIAS_STEP = 0.5
PROP_STEP = 0.5

F32 = jnp.float32
BF16 = jnp.bfloat16


def complex_dot(pattern, left_re, left_im, right_re, right_im):
    real_part = jnp.einsum(
        pattern, left_re, right_re, preferred_element_type=jnp.float32
    ) - jnp.einsum(pattern, left_im, right_im, preferred_element_type=jnp.float32)
    imag_part = jnp.einsum(
        pattern, left_re, right_im, preferred_element_type=jnp.float32
    ) + jnp.einsum(pattern, left_im, right_re, preferred_element_type=jnp.float32)
    return (real_part, imag_part)


def make_picker(wanted):

    def picker(shard_rows):
        row_count = shard_rows.shape[0]
        select = (wanted[:, None] == jnp.arange(row_count, dtype=jnp.int32)[None, :]).astype(
            jnp.bfloat16
        )
        return jnp.dot(select, shard_rows, preferred_element_type=jnp.float32)

    return picker


def with_collectives(green, fields, orbitals, chol_half, chol_full, chol_count, kq_map):
    q_local = chol_half.shape[0]
    k_local = chol_half.shape[1]
    pair_width = chol_half.shape[3]
    chol_cols = chol_half.shape[4]
    ka_count = lax.axis_size("ka")
    pb_count = lax.axis_size("pb")
    ka_pos = lax.axis_index("ka")
    pb_pos = lax.axis_index("pb")
    local_green = lax.all_to_all(green, "ka", split_axis=3, concat_axis=1, tiled=True)
    walkers = local_green.shape[1]
    per_device = walkers // ka_count
    greens = local_green[0].reshape(walkers, q_local, k_local, 2, pair_width)
    counts = lax.dynamic_slice_in_dim(chol_count, pb_pos * q_local, q_local)
    vec_mask = (jnp.arange(chol_cols, dtype=jnp.int32)[None, :] < counts[:, None]).astype(
        jnp.float32
    )
    bias_re, bias_im = complex_dot(
        "wqkx,qkxn->qwn",
        greens[:, :, :, 0],
        greens[:, :, :, 1],
        chol_half[:, :, 0],
        chol_half[:, :, 1],
    )
    own_rows = (jnp.arange(walkers, dtype=jnp.int32) // per_device == ka_pos).astype(jnp.float32)
    bias_re, bias_im = lax.psum((bias_re, bias_im), "ka")
    bias_re = bias_re * vec_mask[:, None, :]
    bias_im = bias_im * vec_mask[:, None, :]
    hartree = 0.5 * jnp.sum(bias_re * bias_re + bias_im * bias_im, axis=(0, 2)) * own_rows
    field_now = jnp.transpose(fields, (1, 0, 2, 3)).reshape(q_local, walkers, chol_cols)
    shift_re = ((field_now - BIAS_STEP * bias_re) * vec_mask[:, None, :]).astype(jnp.bfloat16)
    shift_im = (-BIAS_STEP * bias_im * vec_mask[:, None, :]).astype(jnp.bfloat16)
    exchange = jnp.zeros((walkers,), jnp.float32)
    for transfer in range(q_local):
        for kpoint in range(k_local):
            chol_row = chol_half[transfer, kpoint].reshape(2, NOCC, M, chol_cols)
            green_row = greens[:, transfer, kpoint].reshape(walkers, 2, NOCC, M)
            cross_re, cross_im = complex_dot(
                "ipn,wjp->wijn", chol_row[0], chol_row[1], green_row[:, 0], green_row[:, 1]
            )
            exchange = exchange + 0.5 * jnp.sum(
                (cross_re * cross_re + cross_im * cross_im) * vec_mask[transfer], axis=(1, 2, 3)
            )
    prop_re, prop_im = complex_dot(
        "qwn,qkyn->qwky", shift_re, shift_im, chol_full[:, :, 0], chol_full[:, :, 1]
    )
    shape = (q_local, walkers, k_local, M, M)
    oper_re = (PROP_STEP * prop_re).astype(jnp.bfloat16).reshape(shape)
    oper_im = (PROP_STEP * prop_im).astype(jnp.bfloat16).reshape(shape)
    normalizer = q_local * pb_count * chol_cols
    total_energy = lax.psum(hartree - exchange, ("ka", "pb")) / normalizer
    energy = lax.dynamic_slice_in_dim(total_energy, ka_pos * per_device, per_device).reshape(
        1, per_device
    )
    initial = orbitals[0].reshape(k_local, walkers, 2, NOCC, M)
    row_width = 2 * pair_width
    my_rows = lax.dynamic_slice_in_dim(kq_map, pb_pos * q_local, q_local, 0)
    wanted = lax.dynamic_slice_in_dim(my_rows, ka_pos * k_local, k_local, 1).reshape(
        q_local * k_local
    )
    picker = make_picker(wanted)
    current = initial
    summed_terms = initial
    for degree in range(1, TAYLOR + 1):
        rounded = current.astype(jnp.bfloat16).reshape(k_local, walkers * row_width)
        fetched = picker(lax.all_gather(rounded, "ka", axis=0, tiled=True))
        shifted_rows = fetched.astype(jnp.bfloat16).reshape(q_local, k_local, walkers, 2, NOCC, M)
        out_re, out_im = complex_dot(
            "xwkpq,xkwiq->kwip",
            oper_re,
            oper_im,
            shifted_rows[:, :, :, 0],
            shifted_rows[:, :, :, 1],
        )
        applied = jnp.stack([out_re, out_im], axis=2)
        applied = lax.psum(applied, "pb")
        current = applied / degree
        summed_terms = summed_terms + current
    propagated = summed_terms.reshape(1, k_local, walkers, row_width)
    return (propagated, energy)


def column_mask(count_ref, rows, columns):
    kept = count_ref[lax.axis_index("pb")]
    return lax.broadcasted_iota(jnp.int32, (rows, columns), 1) < kept


def pack_kernel(green_ref, orbitals_ref, out_ref):
    peers, rows, _ = out_ref.shape
    kpoints, width = green_ref.shape
    k_local = kpoints // peers
    green = green_ref[...].astype(F32)
    window = jnp.concatenate([orbitals_ref[k] for k in range(k_local)], axis=0)
    gap = jnp.zeros((rows - window.shape[0] - k_local, width), F32)
    for peer in range(peers):
        block = jnp.concatenate([green[peer * k_local : (peer + 1) * k_local], gap, window], axis=0)
        out_ref[peer, :, :width] = block.astype(BF16)
        out_ref[peer, :, width:] = jnp.zeros((rows, out_ref.shape[2] - width), BF16)


def bias_kernel(k_local, packed_ref, chol_ref, bias_ref, own_ref):
    copies, rows, columns = bias_ref.shape
    width = chol_ref.shape[2]
    blocks = [packed_ref[w].astype(F32) for w in range(packed_ref.shape[0])]
    total = jnp.zeros((rows, columns), F32)
    for k in range(k_local):
        green = jnp.concatenate([block[k : k + 1] for block in blocks], axis=0)
        real, imag = green[:, :width], green[:, width : 2 * width]
        both = jnp.concatenate([real, imag], axis=0)
        turned = jnp.concatenate([-imag, real], axis=0)
        own_ref[k] = both
        total += jnp.dot(both.astype(BF16), chol_ref[k, 0], preferred_element_type=F32)
        total += jnp.dot(turned.astype(BF16), chol_ref[k, 1], preferred_element_type=F32)
    for copy in range(copies):
        bias_ref[copy] = total


def exchange_kernel(k_local, count_ref, own_ref, chol_ref, out_ref):
    walkers, width, columns = own_ref.shape[1] // 2, own_ref.shape[2], chol_ref.shape[3]
    rows = 2 * walkers
    lane = lax.broadcasted_iota(jnp.int32, (rows, LANES), 1)
    total = jnp.zeros((rows, columns), F32)
    for k in range(k_local):
        both = jnp.concatenate([own_ref[k], jnp.zeros((rows, LANES - width), F32)], axis=1)
        turned = jnp.concatenate([-both[walkers:], both[:walkers]], axis=0)
        sides = []
        for side in (both, turned):
            rolled = {
                step: side if step == 0 else pltpu.roll(side, (step * M) % LANES, 1)
                for step in range(1 - NOCC, NOCC)
            }
            blocks = []
            for i in range(NOCC):
                inside = (lane >= i * M) & (lane < (i + 1) * M)
                for j in range(NOCC):
                    blocks.append(jnp.where(inside, rolled[i - j], 0.0))
            sides.append(jnp.concatenate(blocks, axis=0)[:, :width].astype(BF16))
        cross = jnp.dot(sides[0], chol_ref[k, 0], preferred_element_type=F32)
        cross += jnp.dot(sides[1], chol_ref[k, 1], preferred_element_type=F32)
        cross = cross * cross
        for block in range(NOCC * NOCC):
            total += cross[block * rows : (block + 1) * rows]
    total = jnp.where(column_mask(count_ref, rows, columns), total, 0.0)
    total = total[:walkers] + total[walkers:]
    summed = 0.5 * jnp.sum(total, axis=1, keepdims=True)
    out_ref[...] = jnp.broadcast_to(summed, out_ref.shape)


def operator_kernel(k_local, count_ref, parts_ref, fields_ref, exchange_ref, chol_ref, out_ref, products, turned_ref):
    bias = parts_ref[0]
    for part in range(1, parts_ref.shape[0]):
        bias = bias + parts_ref[part]
    walkers, columns = fields_ref.shape
    pairs = M * M
    tiles = columns // LANES
    group = LANES // (2 * tiles)
    bias = jnp.where(column_mask(count_ref, 2 * walkers, columns), bias, 0.0)
    bias_re, bias_im = bias[:walkers], bias[walkers:]
    hartree = 0.5 * jnp.sum(bias_re * bias_re + bias_im * bias_im, axis=1, keepdims=True)
    own = lax.broadcasted_iota(jnp.int32, (walkers, 1), 0) == lax.axis_index("ka")
    energy = jnp.where(own, hartree, 0.0) - exchange_ref[:, :1]
    kept = column_mask(count_ref, walkers, columns)
    shift_re = jnp.where(kept, fields_ref[...] - BIAS_STEP * bias_re, 0.0)
    shift_im = jnp.where(kept, -BIAS_STEP * bias_im, 0.0)
    span = k_local * walkers
    for k in range(k_local):
        before, after = k * walkers, span - (k + 1) * walkers
        pieces = []
        for tile in range(tiles):
            at = slice(tile * LANES, (tile + 1) * LANES)
            for first, second in ((shift_re, shift_im), (-shift_im, shift_re)):
                for side in (first, second):
                    pieces += [(before, None), (walkers, side[:, at]), (after, None)]
                pieces.append((group - 2 * span, None))
        sides = jnp.concatenate(
            [jnp.zeros((n, LANES), F32) if p is None else p for n, p in pieces if n], axis=0
        ).astype(BF16)
        product = lax.dot_general(
            chol_ref[k], sides, (((1,), (1,)), ((), ())), preferred_element_type=F32
        )
        if k == 0:
            products[...] = product
        else:
            products[...] += product
    lane = lax.broadcasted_iota(jnp.int32, (pairs, LANES), 1)
    merged = products[pl.ds(0, pairs, stride=2 * tiles), :]
    for at in range(1, 2 * tiles):
        row = products[pl.ds(at, pairs, stride=2 * tiles), :]
        merged = jnp.where(lane >= at * group, row, merged)
    turned_ref[:pairs] = merged
    copies, rows, width = out_ref.shape
    lane = lax.broadcasted_iota(jnp.int32, (rows, LANES), 1)
    for at in range(0, width, LANES):
        block = turned_ref[at : at + LANES].T
        block = PROP_STEP * sum(block[n * group : n * group + rows] for n in range(2 * tiles))
        if at + LANES > pairs:
            share = jnp.concatenate([energy, jnp.zeros((rows - walkers, 1), F32)], axis=0)
            block = jnp.where(lane + at < pairs, block, 0.0)
            for piece in range(3):
                head = share.astype(BF16).astype(F32)
                block = jnp.where(lane + at == pairs + piece, head, block)
                share = share - head
        for copy in range(copies):
            out_ref[copy, :, at : at + LANES] = block.astype(BF16)


def start_kernel(pb_count, map_ref, packed_ref, picks_ref, first_ref, table):
    ka_count, packed_rows, _ = packed_ref.shape
    kpoints = map_ref.shape[1]
    pair = first_ref.shape[0]
    walkers = ka_count
    count = kpoints // ka_count * walkers
    half = LANES // 2
    lane = lax.broadcasted_iota(jnp.int32, (1, LANES), 1)
    lane_q = lax.rem(lane, half) // (kpoints * walkers)
    lane_k = lax.rem(lane, kpoints * walkers) // walkers
    source = jnp.zeros((1, LANES), jnp.int32)
    for q in range(pb_count):
        for k in range(kpoints):
            source = jnp.where((lane_q == q) & (lane_k == k), map_ref[q, k], source)
    wanted = source * walkers + lax.rem(lane, walkers)
    row = lax.broadcasted_iota(jnp.int32, (LANES, LANES), 0)
    real = jnp.where(row == wanted, 1.0, 0.0)
    sign = jnp.where(lane < half, 1.0, -1.0)
    imag = jnp.where(row == wanted + half, sign, 0.0)
    picks = jnp.concatenate([real, imag], axis=1).astype(BF16)
    picks_ref[...] = picks
    table[...] = jnp.zeros_like(table)
    for peer in range(ka_count):
        rows = packed_ref[peer].astype(F32)[packed_rows - count :]
        table[peer * count : (peer + 1) * count, :pair] = rows[:, :pair]
        table[peer * count + half : (peer + 1) * count + half, :pair] = rows[:, pair : 2 * pair]
    turned = table[...].T[:pair].astype(BF16)
    first_ref[...] = jnp.dot(turned, picks, preferred_element_type=F32)


def taylor_kernel(
    pb_count, normalizer, blocks_ref, picks_ref, first_ref, orbitals_ref, out_ref, energy_ref,
    table, turned, picked, term,
):
    half = LANES // 2
    pairs = M * M
    ka_count = blocks_ref.shape[0] // pb_count
    rows = blocks_ref.shape[1] // 2
    for at in range(ka_count * pb_count):
        ka_from, pb_from = at // pb_count, at % pb_count
        start = (pb_from * ka_count + ka_from) * rows
        block = blocks_ref[at].astype(F32)
        table[start : start + rows, :] = block[:rows]
        table[start + half : start + half + rows, :] = block[rows:]
    for at in range(0, table.shape[1], LANES):
        turned[at : at + LANES] = table[:, at : at + LANES].T
    ka_pos = lax.axis_index("ka")
    last = pairs // LANES * LANES
    shares = table[:half, last : last + LANES]
    lane = lax.broadcasted_iota(jnp.int32, shares.shape, 1) + last
    row = lax.broadcasted_iota(jnp.int32, shares.shape, 0)
    shares = jnp.where(
        (lane >= pairs) & (lane < pairs + 3) & (lax.rem(row, rows) == ka_pos), shares, 0.0
    )
    shares = jnp.sum(jnp.sum(shares, axis=0, keepdims=True), axis=1, keepdims=True)
    energy_ref[...] = shares / normalizer
    sums = [jnp.zeros((M, LANES), F32) for _ in range(NOCC)]
    for degree in range(1, TAYLOR + 1):
        source = first_ref if degree == 1 else picked
        straight = [jnp.zeros((M, LANES), F32) for _ in range(NOCC)]
        crossed = [jnp.zeros((M, LANES), F32) for _ in range(NOCC)]
        for c in range(M):
            column = turned[pl.ds(c, M, stride=M), :]
            for i in range(NOCC):
                at = i * M + c
                straight[i] += column * source[at : at + 1, :LANES]
                crossed[i] += column * source[at : at + 1, LANES:]
        for i in range(NOCC):
            applied = straight[i] + pltpu.roll(crossed[i], half, 1)
            applied = applied + pltpu.roll(applied, LANES - half // pb_count, 1)
            current = applied / degree
            sums[i] = sums[i] + current
            term[i * M : (i + 1) * M] = current if degree < TAYLOR else sums[i]
        if degree < TAYLOR:
            picked[...] = jnp.dot(
                term[: NOCC * M].astype(BF16), picks_ref[...], preferred_element_type=F32
            )
    term[NOCC * M :] = jnp.zeros((LANES - NOCC * M, LANES), F32)
    table[:, :LANES] = term[...].T
    k_local, walkers, _ = out_ref.shape
    pair = NOCC * M
    start = pl.multiple_of(ka_pos * rows, rows)
    real = table[pl.ds(start, rows), :pair]
    imag = table[pl.ds(start + half, rows), :pair]
    both = jnp.concatenate([real, imag], axis=1)
    for k in range(k_local):
        out_ref[k] = orbitals_ref[k] + both[k * walkers : (k + 1) * walkers]


def call(kernel, out, scratch=(), scalars=0, operands=0):
    smem = [pl.BlockSpec(memory_space=pltpu.SMEM)] * scalars
    vmem = [pl.BlockSpec(memory_space=pltpu.VMEM)] * operands
    return pl.pallas_call(
        kernel,
        out_shape=out,
        in_specs=smem + vmem,
        out_specs=jax.tree.map(lambda _: pl.BlockSpec(memory_space=pltpu.VMEM), out),
        scratch_shapes=list(scratch),
        compiler_params=pltpu.CompilerParams(vmem_limit_bytes=24 * 2**20),
    )


def direct(green, fields, orbitals, chol_half, chol_full, chol_count, kq_map):
    k_local, pair_width, chol_cols = chol_half.shape[1], chol_half.shape[3], chol_half.shape[4]
    ka_count, pb_count = lax.axis_size("ka"), lax.axis_size("pb")
    walkers = ka_count
    kpoints = green.shape[3]
    span = k_local * walkers
    shape = jax.ShapeDtypeStruct
    own_orbitals = orbitals.reshape(k_local, walkers, 2 * pair_width)
    half = chol_half.reshape(k_local, 2, pair_width, chol_cols)
    tiles = chol_cols // LANES
    full = jnp.transpose(
        chol_full.reshape(k_local, 2, M * M, tiles, LANES), (0, 2, 3, 1, 4)
    ).reshape(k_local, M * M * tiles * 2, LANES)
    packed = call(
        pack_kernel,
        shape((ka_count, 8 + span, 2 * LANES), BF16),
        operands=2,
    )(green.reshape(kpoints, 2 * pair_width), own_orbitals)
    packed = lax.all_to_all(packed, "ka", 0, 0, tiled=True)
    bias, own = call(
        functools.partial(bias_kernel, k_local),
        (
            shape((ka_count, 2 * walkers, chol_cols), F32),
            shape((k_local, 2 * walkers, pair_width), F32),
        ),
        operands=2,
    )(packed, half)
    parts = lax.all_to_all(bias, "ka", 0, 0, tiled=True)
    exchange = call(
        functools.partial(exchange_kernel, k_local),
        shape((walkers, LANES), F32),
        scalars=1,
        operands=2,
    )(chol_count, own, half)
    width = -(-(M * M + 3) // LANES) * LANES
    blocks = call(
        functools.partial(operator_kernel, k_local),
        shape((ka_count * pb_count, 2 * span, width), BF16),
        [pltpu.VMEM((2 * M * M * tiles, LANES), F32), pltpu.VMEM((width, LANES), F32)],
        scalars=1,
        operands=4,
    )(chol_count, parts, fields.reshape(walkers, chol_cols), exchange, full)
    blocks = lax.all_to_all(blocks, ("ka", "pb"), 0, 0, tiled=True)
    picks, first = call(
        functools.partial(start_kernel, pb_count),
        (shape((LANES, 2 * LANES), BF16), shape((pair_width, 2 * LANES), F32)),
        [pltpu.VMEM((LANES, LANES), F32)],
        scalars=1,
        operands=1,
    )(kq_map, packed)
    propagated, energy = call(
        functools.partial(taylor_kernel, pb_count, float(pb_count * chol_cols)),
        (shape((k_local, walkers, 2 * pair_width), F32), shape((1, 1), F32)),
        [
            pltpu.VMEM((LANES, width), F32),
            pltpu.VMEM((width, LANES), F32),
            pltpu.VMEM((pair_width, 2 * LANES), F32),
            pltpu.VMEM((LANES, LANES), F32),
        ],
        operands=4,
    )(blocks, picks, first, own_orbitals)
    return (propagated[None], energy)


def on_device(green, fields, orbitals, chol_half, chol_full, chol_count, kq_map):
    ka_count, pb_count = lax.axis_size("ka"), lax.axis_size("pb")
    walkers = orbitals.shape[2]
    fits = 2 * pb_count * kq_map.shape[1] * walkers == LANES
    fits = fits and chol_half.shape[1] * walkers == 8 and chol_half.shape[4] == 2 * LANES
    if fits and chol_half.shape[0] == 1 and walkers == ka_count:
        return direct(green, fields, orbitals, chol_half, chol_full, chol_count, kq_map)
    return with_collectives(green, fields, orbitals, chol_half, chol_full, chol_count, kq_map)


def solution(mesh):
    placed = (
        P("wa", ("grp", "ka"), "pb", None, None),
        P("wa", "pb", "grp", None),
        P("wa", "ka", "grp", None),
        P("pb", "ka", None, None, None),
        P("pb", "ka", None, None, None),
        P(),
        P(),
    )
    return jax.shard_map(
        on_device,
        mesh=mesh,
        in_specs=placed,
        out_specs=(P("wa", "ka", "grp", None), P("wa", ("grp", "ka"))),
        check_vma=False,
    )
```

```python
import functools

import jax
import jax.numpy as jnp
from jax import lax
from jax.experimental import pallas as pl
from jax.experimental.pallas import tpu as pltpu
from jax.sharding import PartitionSpec as P

M = 26
NOCC = 4
TAYLOR = 3
LANES = 128


BIAS_STEP = 0.5
PROP_STEP = 0.5

F32 = jnp.float32
BF16 = jnp.bfloat16


def complex_dot(pattern, left_re, left_im, right_re, right_im):
    real_part = jnp.einsum(
        pattern, left_re, right_re, preferred_element_type=jnp.float32
    ) - jnp.einsum(pattern, left_im, right_im, preferred_element_type=jnp.float32)
    imag_part = jnp.einsum(
        pattern, left_re, right_im, preferred_element_type=jnp.float32
    ) + jnp.einsum(pattern, left_im, right_re, preferred_element_type=jnp.float32)
    return (real_part, imag_part)


def make_picker(wanted):

    def picker(shard_rows):
        row_count = shard_rows.shape[0]
        select = (wanted[:, None] == jnp.arange(row_count, dtype=jnp.int32)[None, :]).astype(
            jnp.bfloat16
        )
        return jnp.dot(select, shard_rows, preferred_element_type=jnp.float32)

    return picker


def with_collectives(green, fields, orbitals, chol_half, chol_full, chol_count, kq_map):
    q_local = chol_half.shape[0]
    k_local = chol_half.shape[1]
    pair_width = chol_half.shape[3]
    chol_cols = chol_half.shape[4]
    ka_count = lax.axis_size("ka")
    pb_count = lax.axis_size("pb")
    ka_pos = lax.axis_index("ka")
    pb_pos = lax.axis_index("pb")
    local_green = lax.all_to_all(green, "ka", split_axis=3, concat_axis=1, tiled=True)
    walkers = local_green.shape[1]
    per_device = walkers // ka_count
    greens = local_green[0].reshape(walkers, q_local, k_local, 2, pair_width)
    counts = lax.dynamic_slice_in_dim(chol_count, pb_pos * q_local, q_local)
    vec_mask = (jnp.arange(chol_cols, dtype=jnp.int32)[None, :] < counts[:, None]).astype(
        jnp.float32
    )
    bias_re, bias_im = complex_dot(
        "wqkx,qkxn->qwn",
        greens[:, :, :, 0],
        greens[:, :, :, 1],
        chol_half[:, :, 0],
        chol_half[:, :, 1],
    )
    own_rows = (jnp.arange(walkers, dtype=jnp.int32) // per_device == ka_pos).astype(jnp.float32)
    bias_re, bias_im = lax.psum((bias_re, bias_im), "ka")
    bias_re = bias_re * vec_mask[:, None, :]
    bias_im = bias_im * vec_mask[:, None, :]
    hartree = 0.5 * jnp.sum(bias_re * bias_re + bias_im * bias_im, axis=(0, 2)) * own_rows
    field_now = jnp.transpose(fields, (1, 0, 2, 3)).reshape(q_local, walkers, chol_cols)
    shift_re = ((field_now - BIAS_STEP * bias_re) * vec_mask[:, None, :]).astype(jnp.bfloat16)
    shift_im = (-BIAS_STEP * bias_im * vec_mask[:, None, :]).astype(jnp.bfloat16)
    exchange = jnp.zeros((walkers,), jnp.float32)
    for transfer in range(q_local):
        for kpoint in range(k_local):
            chol_row = chol_half[transfer, kpoint].reshape(2, NOCC, M, chol_cols)
            green_row = greens[:, transfer, kpoint].reshape(walkers, 2, NOCC, M)
            cross_re, cross_im = complex_dot(
                "ipn,wjp->wijn", chol_row[0], chol_row[1], green_row[:, 0], green_row[:, 1]
            )
            exchange = exchange + 0.5 * jnp.sum(
                (cross_re * cross_re + cross_im * cross_im) * vec_mask[transfer], axis=(1, 2, 3)
            )
    prop_re, prop_im = complex_dot(
        "qwn,qkyn->qwky", shift_re, shift_im, chol_full[:, :, 0], chol_full[:, :, 1]
    )
    shape = (q_local, walkers, k_local, M, M)
    oper_re = (PROP_STEP * prop_re).astype(jnp.bfloat16).reshape(shape)
    oper_im = (PROP_STEP * prop_im).astype(jnp.bfloat16).reshape(shape)
    normalizer = q_local * pb_count * chol_cols
    total_energy = lax.psum(hartree - exchange, ("ka", "pb")) / normalizer
    energy = lax.dynamic_slice_in_dim(total_energy, ka_pos * per_device, per_device).reshape(
        1, per_device
    )
    initial = orbitals[0].reshape(k_local, walkers, 2, NOCC, M)
    row_width = 2 * pair_width
    my_rows = lax.dynamic_slice_in_dim(kq_map, pb_pos * q_local, q_local, 0)
    wanted = lax.dynamic_slice_in_dim(my_rows, ka_pos * k_local, k_local, 1).reshape(
        q_local * k_local
    )
    picker = make_picker(wanted)
    current = initial
    summed_terms = initial
    for degree in range(1, TAYLOR + 1):
        rounded = current.astype(jnp.bfloat16).reshape(k_local, walkers * row_width)
        fetched = picker(lax.all_gather(rounded, "ka", axis=0, tiled=True))
        shifted_rows = fetched.astype(jnp.bfloat16).reshape(q_local, k_local, walkers, 2, NOCC, M)
        out_re, out_im = complex_dot(
            "xwkpq,xkwiq->kwip",
            oper_re,
            oper_im,
            shifted_rows[:, :, :, 0],
            shifted_rows[:, :, :, 1],
        )
        applied = jnp.stack([out_re, out_im], axis=2)
        applied = lax.psum(applied, "pb")
        current = applied / degree
        summed_terms = summed_terms + current
    propagated = summed_terms.reshape(1, k_local, walkers, row_width)
    return (propagated, energy)


def ring(array, axis, shift):
    size = lax.axis_size(axis)
    return lax.ppermute(array, axis, [(at, (at + shift) % size) for at in range(size)])


def origin(axis, shift):
    size = lax.axis_size(axis)
    return lax.rem(lax.axis_index(axis) + (size - shift), size)


def prepare_kernel(pb_count, walkers, loads, map_ref, count_ref, *refs):
    sources, (mask_ref, picks_ref) = refs[:loads], refs[loads : loads + 2]
    targets, sems = refs[loads + 2 : 2 * loads + 2], refs[-1]
    copies = [
        pltpu.make_async_copy(source, target, sems.at[at])
        for at, (source, target) in enumerate(zip(sources, targets))
    ]
    for copy in copies:
        copy.start()
    kept = count_ref[lax.axis_index("pb")]
    column = lax.broadcasted_iota(jnp.int32, mask_ref.shape, 1)
    mask_ref[...] = jnp.where(column < kept, 1.0, 0.0)
    kpoints = map_ref.shape[1]
    half = LANES // 2
    lane = lax.broadcasted_iota(jnp.int32, (1, LANES), 1)
    lane_q = lax.rem(lane, half) // (kpoints * walkers)
    lane_k = lax.rem(lane, kpoints * walkers) // walkers
    source = jnp.zeros((1, LANES), jnp.int32)
    for q in range(pb_count):
        for k in range(kpoints):
            source = jnp.where((lane_q == q) & (lane_k == k), map_ref[q, k], source)
    wanted = source * walkers + lax.rem(lane, walkers)
    row = lax.broadcasted_iota(jnp.int32, (LANES, LANES), 0)
    real = jnp.where(row == wanted, 1.0, 0.0)
    sign = jnp.where(lane < half, 1.0, -1.0)
    imag = jnp.where(row == wanted + half, sign, 0.0)
    picks_ref[...] = jnp.concatenate([real, imag], axis=1).astype(BF16)
    for copy in copies:
        copy.wait()


def bias_kernel(ka_count, k_local, *refs):
    greens, (chol_ref, orbitals_ref, bias_ref, own_ref, table) = refs[:ka_count], refs[ka_count:]
    for shift, green_ref in enumerate(greens):
        table[origin("ka", shift)] = green_ref[...].astype(F32)
    first = lax.axis_index("ka") * k_local
    width = chol_ref.shape[2]
    rows = 2 * ka_count
    total = jnp.zeros((rows, bias_ref.shape[1]), F32)
    for k in range(k_local):
        green = jnp.concatenate(
            [table[w, pl.ds(first + k, 1), :] for w in range(ka_count)], axis=0
        )
        real, imag = green[:, :width], green[:, width:]
        both = jnp.concatenate([real, imag], axis=0)
        turned = jnp.concatenate([-imag, real], axis=0)
        own_ref[k] = both
        total += jnp.dot(both.astype(BF16), chol_ref[k, 0], preferred_element_type=F32)
        total += jnp.dot(turned.astype(BF16), chol_ref[k, 1], preferred_element_type=F32)
    bias_ref[:rows] = total
    window = jnp.concatenate([orbitals_ref[k] for k in range(k_local)], axis=0)
    count, width = window.shape
    bias_ref[rows : rows + count, :width] = window
    bias_ref[rows : rows + count, width:] = jnp.zeros((count, bias_ref.shape[1] - width), F32)


def exchange_kernel(k_local, own_ref, chol_ref, mask_ref, out_ref):
    walkers, width, columns = own_ref.shape[1] // 2, own_ref.shape[2], chol_ref.shape[3]
    rows = 2 * walkers
    lane = lax.broadcasted_iota(jnp.int32, (rows, LANES), 1)
    total = jnp.zeros((rows, columns), F32)
    for k in range(k_local):
        both = jnp.concatenate([own_ref[k], jnp.zeros((rows, LANES - width), F32)], axis=1)
        turned = jnp.concatenate([-both[walkers:], both[:walkers]], axis=0)
        sides = []
        for side in (both, turned):
            rolled = {
                step: side if step == 0 else pltpu.roll(side, (step * M) % LANES, 1)
                for step in range(1 - NOCC, NOCC)
            }
            blocks = []
            for i in range(NOCC):
                inside = (lane >= i * M) & (lane < (i + 1) * M)
                for j in range(NOCC):
                    blocks.append(jnp.where(inside, rolled[i - j], 0.0))
            sides.append(jnp.concatenate(blocks, axis=0)[:, :width].astype(BF16))
        cross = jnp.dot(sides[0], chol_ref[k, 0], preferred_element_type=F32)
        cross += jnp.dot(sides[1], chol_ref[k, 1], preferred_element_type=F32)
        cross = cross * cross
        for block in range(NOCC * NOCC):
            total += cross[block * rows : (block + 1) * rows]
    total = total * mask_ref[:rows]
    total = total[:walkers] + total[walkers:]
    summed = 0.5 * jnp.sum(total, axis=1, keepdims=True)
    out_ref[...] = jnp.broadcast_to(summed, out_ref.shape)


def operator_kernel(ka_count, k_local, *refs):
    parts = refs[:ka_count]
    fields_ref, mask_ref, exchange_ref, chol_ref, out_ref, products, turned_ref = refs[ka_count:]
    walkers, columns = fields_ref.shape
    bias = parts[0][: 2 * walkers]
    for part in parts[1:]:
        bias = bias + part[: 2 * walkers]
    pairs = M * M
    tiles = columns // LANES
    group = LANES // (2 * tiles)
    bias = bias * mask_ref[: 2 * walkers]
    bias_re, bias_im = bias[:walkers], bias[walkers:]
    hartree = 0.5 * jnp.sum(bias_re * bias_re + bias_im * bias_im, axis=1, keepdims=True)
    own = lax.broadcasted_iota(jnp.int32, (walkers, 1), 0) == lax.axis_index("ka")
    energy = jnp.where(own, hartree, 0.0) - exchange_ref[:, :1]
    kept = mask_ref[:walkers]
    shift_re = (fields_ref[...] - BIAS_STEP * bias_re) * kept
    shift_im = -BIAS_STEP * bias_im * kept
    span = k_local * walkers
    weights = []
    for k in range(k_local):
        before, after = k * walkers, span - (k + 1) * walkers
        pieces = []
        for tile in range(tiles):
            at = slice(tile * LANES, (tile + 1) * LANES)
            for first, second in ((shift_re, shift_im), (-shift_im, shift_re)):
                for side in (first, second):
                    pieces += [(before, None), (walkers, side[:, at]), (after, None)]
                pieces.append((group - 2 * span, None))
        weights.append(
            jnp.concatenate(
                [jnp.zeros((n, LANES), F32) if p is None else p for n, p in pieces if n], axis=0
            ).astype(BF16)
        )
    products[...] = lax.dot_general(
        jnp.concatenate([chol_ref[k] for k in range(k_local)], axis=1),
        jnp.concatenate(weights, axis=1),
        (((1,), (1,)), ((), ())),
        preferred_element_type=F32,
    )
    lane = lax.broadcasted_iota(jnp.int32, (pairs, LANES), 1)
    merged = products[pl.ds(0, pairs, stride=2 * tiles), :]
    for at in range(1, 2 * tiles):
        row = products[pl.ds(at, pairs, stride=2 * tiles), :]
        merged = jnp.where(lane >= at * group, row, merged)
    turned_ref[:pairs] = merged
    copies, rows, width = out_ref.shape
    lane = lax.broadcasted_iota(jnp.int32, (rows, LANES), 1)
    for at in range(0, width, LANES):
        block = turned_ref[at : at + LANES].T
        block = PROP_STEP * sum(block[n * group : n * group + rows] for n in range(2 * tiles))
        if at + LANES > pairs:
            share = jnp.concatenate([energy, jnp.zeros((rows - walkers, 1), F32)], axis=0)
            block = jnp.where(lane + at < pairs, block, 0.0)
            for piece in range(3):
                head = share.astype(BF16).astype(F32)
                block = jnp.where(lane + at == pairs + piece, head, block)
                share = share - head
        for copy in range(copies):
            out_ref[copy, :, at : at + LANES] = block.astype(BF16)


def taylor_kernel(ka_count, pb_count, normalizer, blocks_ref, *refs):
    windows = refs[:ka_count]
    picks_ref, orbitals_ref, out_ref, energy_ref, table, turned, picked, term = refs[ka_count:]
    half = LANES // 2
    pairs = M * M
    pair = NOCC * M
    rows = blocks_ref.shape[1] // 2
    for at in range(ka_count * pb_count):
        ka_from, pb_from = at // pb_count, at % pb_count
        start = (pb_from * ka_count + ka_from) * rows
        block = blocks_ref[at].astype(F32)
        table[start : start + rows, :] = block[:rows]
        table[start + half : start + half + rows, :] = block[rows:]
    for at in range(0, table.shape[1], LANES):
        turned[at : at + LANES] = table[:, at : at + LANES].T
    ka_pos = lax.axis_index("ka")
    last = pairs // LANES * LANES
    shares = table[:half, last : last + LANES]
    lane = lax.broadcasted_iota(jnp.int32, shares.shape, 1) + last
    row = lax.broadcasted_iota(jnp.int32, shares.shape, 0)
    shares = jnp.where(
        (lane >= pairs) & (lane < pairs + 3) & (lax.rem(row, rows) == ka_pos), shares, 0.0
    )
    shares = jnp.sum(jnp.sum(shares, axis=0, keepdims=True), axis=1, keepdims=True)
    energy_ref[...] = shares / normalizer
    term[...] = jnp.zeros_like(term)
    for shift, window_ref in enumerate(windows):
        start = pl.multiple_of(origin("ka", shift) * rows, rows)
        window = window_ref[window_ref.shape[0] - rows :]
        term[pl.ds(start, rows), :pair] = window[:, :pair]
        term[pl.ds(start + half, rows), :pair] = window[:, pair : 2 * pair]
    picked[...] = jnp.dot(
        term[...].T[:pair].astype(BF16), picks_ref[...], preferred_element_type=F32
    )
    sums = [jnp.zeros((M, LANES), F32) for _ in range(NOCC)]
    for degree in range(1, TAYLOR + 1):
        source = picked
        straight = [jnp.zeros((M, LANES), F32) for _ in range(NOCC)]
        crossed = [jnp.zeros((M, LANES), F32) for _ in range(NOCC)]
        for c in range(M):
            column = turned[pl.ds(c, M, stride=M), :]
            for i in range(NOCC):
                at = i * M + c
                straight[i] += column * source[at : at + 1, :LANES]
                crossed[i] += column * source[at : at + 1, LANES:]
        for i in range(NOCC):
            applied = straight[i] + pltpu.roll(crossed[i], half, 1)
            applied = applied + pltpu.roll(applied, LANES - half // pb_count, 1)
            current = applied / degree
            sums[i] = sums[i] + current
            term[i * M : (i + 1) * M] = current if degree < TAYLOR else sums[i]
        if degree < TAYLOR:
            picked[...] = jnp.dot(
                term[: NOCC * M].astype(BF16), picks_ref[...], preferred_element_type=F32
            )
    term[NOCC * M :] = jnp.zeros((LANES - NOCC * M, LANES), F32)
    table[:, :LANES] = term[...].T
    k_local, walkers, _ = out_ref.shape
    start = pl.multiple_of(ka_pos * rows, rows)
    real = table[pl.ds(start, rows), :pair]
    imag = table[pl.ds(start + half, rows), :pair]
    both = jnp.concatenate([real, imag], axis=1)
    for k in range(k_local):
        out_ref[k] = orbitals_ref[k] + both[k * walkers : (k + 1) * walkers]


def call(kernel, out, scratch=(), scalars=0, operands=0, arrays=0):
    spaces = [pltpu.SMEM] * scalars + [pl.ANY] * arrays + [pltpu.VMEM] * operands
    return pl.pallas_call(
        kernel,
        out_shape=out,
        in_specs=[pl.BlockSpec(memory_space=space) for space in spaces],
        out_specs=jax.tree.map(lambda _: pl.BlockSpec(memory_space=pltpu.VMEM), out),
        scratch_shapes=list(scratch),
        compiler_params=pltpu.CompilerParams(vmem_limit_bytes=24 * 2**20),
    )


def direct(green, fields, orbitals, chol_half, chol_full, chol_count, kq_map):
    k_local, pair_width, chol_cols = chol_half.shape[1], chol_half.shape[3], chol_half.shape[4]
    ka_count, pb_count = lax.axis_size("ka"), lax.axis_size("pb")
    walkers = ka_count
    kpoints = green.shape[3]
    span = k_local * walkers
    shape = jax.ShapeDtypeStruct
    tiles = chol_cols // LANES
    own_green = green.reshape(kpoints, 2 * pair_width)
    greens = [own_green] + [ring(own_green, "ka", s) for s in range(1, ka_count)]
    loaded = (
        chol_half.reshape(k_local, 2, pair_width, chol_cols),
        jnp.transpose(
            chol_full.reshape(k_local, 2, M * M, tiles, LANES), (0, 2, 3, 1, 4)
        ).reshape(k_local, M * M * tiles * 2, LANES),
        fields.reshape(walkers, chol_cols),
        orbitals.reshape(k_local, walkers, 2 * pair_width),
    )
    mask, picks, half, full, own_fields, own_orbitals = call(
        functools.partial(prepare_kernel, pb_count, walkers, len(loaded)),
        (
            shape((2 * walkers, chol_cols), F32),
            shape((LANES, 2 * LANES), BF16),
            *(shape(x.shape, x.dtype) for x in loaded),
        ),
        [pltpu.SemaphoreType.DMA((len(loaded),))],
        scalars=2,
        arrays=len(loaded),
    )(kq_map, chol_count, *loaded)
    bias, own = call(
        functools.partial(bias_kernel, ka_count, k_local),
        (
            shape((2 * walkers + span, chol_cols), F32),
            shape((k_local, 2 * walkers, pair_width), F32),
        ),
        [pltpu.VMEM((walkers, kpoints, 2 * pair_width), F32)],
        operands=ka_count + 2,
    )(*greens, half, own_orbitals)
    parts = [bias] + [ring(bias, "ka", s) for s in range(1, ka_count)]
    exchange = call(
        functools.partial(exchange_kernel, k_local),
        shape((walkers, LANES), F32),
        operands=3,
    )(own, half, mask)
    width = -(-(M * M + 3) // LANES) * LANES
    blocks = call(
        functools.partial(operator_kernel, ka_count, k_local),
        shape((ka_count * pb_count, 2 * span, width), BF16),
        [pltpu.VMEM((2 * M * M * tiles, LANES), F32), pltpu.VMEM((width, LANES), F32)],
        operands=ka_count + 4,
    )(*parts, own_fields, mask, exchange, full)
    blocks = lax.all_to_all(blocks, ("ka", "pb"), 0, 0, tiled=True)
    propagated, energy = call(
        functools.partial(taylor_kernel, ka_count, pb_count, float(pb_count * chol_cols)),
        (shape((k_local, walkers, 2 * pair_width), F32), shape((1, 1), F32)),
        [
            pltpu.VMEM((LANES, width), F32),
            pltpu.VMEM((width, LANES), F32),
            pltpu.VMEM((pair_width, 2 * LANES), F32),
            pltpu.VMEM((LANES, LANES), F32),
        ],
        operands=ka_count + 3,
    )(blocks, *parts, picks, own_orbitals)
    return (propagated[None], energy)


def on_device(green, fields, orbitals, chol_half, chol_full, chol_count, kq_map):
    ka_count, pb_count = lax.axis_size("ka"), lax.axis_size("pb")
    walkers = orbitals.shape[2]
    fits = 2 * pb_count * kq_map.shape[1] * walkers == LANES
    fits = fits and chol_half.shape[1] * walkers == 8 and chol_half.shape[4] == 2 * LANES
    if fits and chol_half.shape[0] == 1 and walkers == ka_count:
        return direct(green, fields, orbitals, chol_half, chol_full, chol_count, kq_map)
    return with_collectives(green, fields, orbitals, chol_half, chol_full, chol_count, kq_map)


def solution(mesh):
    placed = (
        P("wa", ("grp", "ka"), "pb", None, None),
        P("wa", "pb", "grp", None),
        P("wa", "ka", "grp", None),
        P("pb", "ka", None, None, None),
        P("pb", "ka", None, None, None),
        P(),
        P(),
    )
    return jax.shard_map(
        on_device,
        mesh=mesh,
        in_specs=placed,
        out_specs=(P("wa", "ka", "grp", None), P("wa", ("grp", "ka"))),
        check_vma=False,
    )
```

```python
import functools

import jax
import jax.numpy as jnp
from jax import lax
from jax.experimental import pallas as pl
from jax.experimental.pallas import tpu as pltpu
from jax.sharding import PartitionSpec as P

M = 26
NOCC = 4
TAYLOR = 3
LANES = 128


BIAS_STEP = 0.5
PROP_STEP = 0.5

F32 = jnp.float32
BF16 = jnp.bfloat16


def complex_dot(pattern, left_re, left_im, right_re, right_im):
    real_part = jnp.einsum(
        pattern, left_re, right_re, preferred_element_type=jnp.float32
    ) - jnp.einsum(pattern, left_im, right_im, preferred_element_type=jnp.float32)
    imag_part = jnp.einsum(
        pattern, left_re, right_im, preferred_element_type=jnp.float32
    ) + jnp.einsum(pattern, left_im, right_re, preferred_element_type=jnp.float32)
    return (real_part, imag_part)


def make_picker(wanted):

    def picker(shard_rows):
        row_count = shard_rows.shape[0]
        select = (wanted[:, None] == jnp.arange(row_count, dtype=jnp.int32)[None, :]).astype(
            jnp.bfloat16
        )
        return jnp.dot(select, shard_rows, preferred_element_type=jnp.float32)

    return picker


def with_collectives(green, fields, orbitals, chol_half, chol_full, chol_count, kq_map):
    q_local = chol_half.shape[0]
    k_local = chol_half.shape[1]
    pair_width = chol_half.shape[3]
    chol_cols = chol_half.shape[4]
    ka_count = lax.axis_size("ka")
    pb_count = lax.axis_size("pb")
    ka_pos = lax.axis_index("ka")
    pb_pos = lax.axis_index("pb")
    local_green = lax.all_to_all(green, "ka", split_axis=3, concat_axis=1, tiled=True)
    walkers = local_green.shape[1]
    per_device = walkers // ka_count
    greens = local_green[0].reshape(walkers, q_local, k_local, 2, pair_width)
    counts = lax.dynamic_slice_in_dim(chol_count, pb_pos * q_local, q_local)
    vec_mask = (jnp.arange(chol_cols, dtype=jnp.int32)[None, :] < counts[:, None]).astype(
        jnp.float32
    )
    bias_re, bias_im = complex_dot(
        "wqkx,qkxn->qwn",
        greens[:, :, :, 0],
        greens[:, :, :, 1],
        chol_half[:, :, 0],
        chol_half[:, :, 1],
    )
    own_rows = (jnp.arange(walkers, dtype=jnp.int32) // per_device == ka_pos).astype(jnp.float32)
    bias_re, bias_im = lax.psum((bias_re, bias_im), "ka")
    bias_re = bias_re * vec_mask[:, None, :]
    bias_im = bias_im * vec_mask[:, None, :]
    hartree = 0.5 * jnp.sum(bias_re * bias_re + bias_im * bias_im, axis=(0, 2)) * own_rows
    field_now = jnp.transpose(fields, (1, 0, 2, 3)).reshape(q_local, walkers, chol_cols)
    shift_re = ((field_now - BIAS_STEP * bias_re) * vec_mask[:, None, :]).astype(jnp.bfloat16)
    shift_im = (-BIAS_STEP * bias_im * vec_mask[:, None, :]).astype(jnp.bfloat16)
    exchange = jnp.zeros((walkers,), jnp.float32)
    for transfer in range(q_local):
        for kpoint in range(k_local):
            chol_row = chol_half[transfer, kpoint].reshape(2, NOCC, M, chol_cols)
            green_row = greens[:, transfer, kpoint].reshape(walkers, 2, NOCC, M)
            cross_re, cross_im = complex_dot(
                "ipn,wjp->wijn", chol_row[0], chol_row[1], green_row[:, 0], green_row[:, 1]
            )
            exchange = exchange + 0.5 * jnp.sum(
                (cross_re * cross_re + cross_im * cross_im) * vec_mask[transfer], axis=(1, 2, 3)
            )
    prop_re, prop_im = complex_dot(
        "qwn,qkyn->qwky", shift_re, shift_im, chol_full[:, :, 0], chol_full[:, :, 1]
    )
    shape = (q_local, walkers, k_local, M, M)
    oper_re = (PROP_STEP * prop_re).astype(jnp.bfloat16).reshape(shape)
    oper_im = (PROP_STEP * prop_im).astype(jnp.bfloat16).reshape(shape)
    normalizer = q_local * pb_count * chol_cols
    total_energy = lax.psum(hartree - exchange, ("ka", "pb")) / normalizer
    energy = lax.dynamic_slice_in_dim(total_energy, ka_pos * per_device, per_device).reshape(
        1, per_device
    )
    initial = orbitals[0].reshape(k_local, walkers, 2, NOCC, M)
    row_width = 2 * pair_width
    my_rows = lax.dynamic_slice_in_dim(kq_map, pb_pos * q_local, q_local, 0)
    wanted = lax.dynamic_slice_in_dim(my_rows, ka_pos * k_local, k_local, 1).reshape(
        q_local * k_local
    )
    picker = make_picker(wanted)
    current = initial
    summed_terms = initial
    for degree in range(1, TAYLOR + 1):
        rounded = current.astype(jnp.bfloat16).reshape(k_local, walkers * row_width)
        fetched = picker(lax.all_gather(rounded, "ka", axis=0, tiled=True))
        shifted_rows = fetched.astype(jnp.bfloat16).reshape(q_local, k_local, walkers, 2, NOCC, M)
        out_re, out_im = complex_dot(
            "xwkpq,xkwiq->kwip",
            oper_re,
            oper_im,
            shifted_rows[:, :, :, 0],
            shifted_rows[:, :, :, 1],
        )
        applied = jnp.stack([out_re, out_im], axis=2)
        applied = lax.psum(applied, "pb")
        current = applied / degree
        summed_terms = summed_terms + current
    propagated = summed_terms.reshape(1, k_local, walkers, row_width)
    return (propagated, energy)


def swap(array, axis, step):
    size = lax.axis_size(axis)
    return lax.ppermute(array, axis, [(at, at ^ step) for at in range(size)])


def origin(axis, step):
    return lax.axis_index(axis) ^ step


def prepare_kernel(pb_count, walkers, map_ref, count_ref, mask_ref, picks_ref):
    kept = count_ref[lax.axis_index("pb")]
    column = lax.broadcasted_iota(jnp.int32, mask_ref.shape, 1)
    mask_ref[...] = jnp.where(column < kept, 1.0, 0.0)
    kpoints = map_ref.shape[1]
    half = LANES // 2
    lane = lax.broadcasted_iota(jnp.int32, (1, LANES), 1)
    lane_q = lax.rem(lane, half) // (kpoints * walkers)
    lane_k = lax.rem(lane, kpoints * walkers) // walkers
    source = jnp.zeros((1, LANES), jnp.int32)
    for q in range(pb_count):
        for k in range(kpoints):
            source = jnp.where((lane_q == q) & (lane_k == k), map_ref[q, k], source)
    wanted = source * walkers + lax.rem(lane, walkers)
    row = lax.broadcasted_iota(jnp.int32, (LANES, LANES), 0)
    real = jnp.where(row == wanted, 1.0, 0.0)
    sign = jnp.where(lane < half, 1.0, -1.0)
    imag = jnp.where(row == wanted + half, sign, 0.0)
    picks_ref[...] = jnp.concatenate([real, imag], axis=1).astype(BF16)


def bias_kernel(ka_count, k_local, *refs):
    greens = refs[:ka_count]
    chol_ref, orbitals_ref, mask_ref, bias_ref, own_ref, table = refs[ka_count:]
    for step, green_ref in enumerate(greens):
        table[origin("ka", step)] = green_ref[...].astype(F32)
    first = lax.axis_index("ka") * k_local
    width = chol_ref.shape[2]
    rows = 2 * ka_count
    total = jnp.zeros((rows, bias_ref.shape[1]), F32)
    for k in range(k_local):
        green = jnp.concatenate(
            [table[w, pl.ds(first + k, 1), :] for w in range(ka_count)], axis=0
        )
        real, imag = green[:, :width], green[:, width:]
        both = jnp.concatenate([real, imag], axis=0)
        turned = jnp.concatenate([-imag, real], axis=0)
        own_ref[k] = both
        total += jnp.dot(both.astype(BF16), chol_ref[k, 0], preferred_element_type=F32)
        total += jnp.dot(turned.astype(BF16), chol_ref[k, 1], preferred_element_type=F32)
    bias_ref[:rows] = total * mask_ref[...]
    window = jnp.concatenate([orbitals_ref[k] for k in range(k_local)], axis=0)
    count, width = window.shape
    bias_ref[rows : rows + count, :width] = window
    bias_ref[rows : rows + count, width:] = jnp.zeros((count, bias_ref.shape[1] - width), F32)


def exchange_kernel(k_local, own_ref, chol_ref, mask_ref, out_ref):
    walkers, width, columns = own_ref.shape[1] // 2, own_ref.shape[2], chol_ref.shape[3]
    rows = 2 * walkers
    lane = lax.broadcasted_iota(jnp.int32, (rows, LANES), 1)
    total = jnp.zeros((rows, columns), F32)
    for k in range(k_local):
        both = jnp.concatenate([own_ref[k], jnp.zeros((rows, LANES - width), F32)], axis=1)
        turned = jnp.concatenate([-both[walkers:], both[:walkers]], axis=0)
        sides = []
        for side in (both, turned):
            rolled = {
                step: side if step == 0 else pltpu.roll(side, (step * M) % LANES, 1)
                for step in range(1 - NOCC, NOCC)
            }
            blocks = []
            for i in range(NOCC):
                inside = (lane >= i * M) & (lane < (i + 1) * M)
                for j in range(NOCC):
                    blocks.append(jnp.where(inside, rolled[i - j], 0.0))
            sides.append(jnp.concatenate(blocks, axis=0)[:, :width].astype(BF16))
        cross = jnp.dot(sides[0], chol_ref[k, 0], preferred_element_type=F32)
        cross += jnp.dot(sides[1], chol_ref[k, 1], preferred_element_type=F32)
        cross = cross * cross
        for block in range(NOCC * NOCC):
            total += cross[block * rows : (block + 1) * rows]
    total = total * mask_ref[:rows]
    total = total[:walkers] + total[walkers:]
    summed = 0.5 * jnp.sum(total, axis=1, keepdims=True)
    out_ref[...] = jnp.broadcast_to(summed, out_ref.shape)


def operator_kernel(ka_count, k_local, *refs):
    parts = refs[:ka_count]
    fields_ref, mask_ref, exchange_ref, chol_ref, out_ref, products, turned_ref = refs[ka_count:]
    walkers, columns = fields_ref.shape
    bias = parts[0][: 2 * walkers]
    for part in parts[1:]:
        bias = bias + part[: 2 * walkers]
    pairs = M * M
    tiles = columns // LANES
    group = LANES // (2 * tiles)
    bias_re, bias_im = bias[:walkers], bias[walkers:]
    hartree = 0.5 * jnp.sum(bias_re * bias_re + bias_im * bias_im, axis=1, keepdims=True)
    own = lax.broadcasted_iota(jnp.int32, (walkers, 1), 0) == lax.axis_index("ka")
    energy = jnp.where(own, hartree, 0.0) - exchange_ref[:, :1]
    kept = mask_ref[:walkers]
    shift_re = (fields_ref[...] - BIAS_STEP * bias_re) * kept
    shift_im = -BIAS_STEP * bias_im * kept
    span = k_local * walkers
    weights = []
    for k in range(k_local):
        before, after = k * walkers, span - (k + 1) * walkers
        pieces = []
        for tile in range(tiles):
            at = slice(tile * LANES, (tile + 1) * LANES)
            for first, second in ((shift_re, shift_im), (-shift_im, shift_re)):
                for side in (first, second):
                    pieces += [(before, None), (walkers, side[:, at]), (after, None)]
                pieces.append((group - 2 * span, None))
        weights.append(
            jnp.concatenate(
                [jnp.zeros((n, LANES), F32) if p is None else p for n, p in pieces if n], axis=0
            ).astype(BF16)
        )
    products[...] = lax.dot_general(
        jnp.concatenate([chol_ref[k] for k in range(k_local)], axis=1),
        jnp.concatenate(weights, axis=1),
        (((1,), (1,)), ((), ())),
        preferred_element_type=F32,
    )
    lane = lax.broadcasted_iota(jnp.int32, (pairs, LANES), 1)
    merged = products[pl.ds(0, pairs, stride=2 * tiles), :]
    for at in range(1, 2 * tiles):
        row = products[pl.ds(at, pairs, stride=2 * tiles), :]
        merged = jnp.where(lane >= at * group, row, merged)
    turned_ref[:pairs] = merged
    copies, rows, width = out_ref.shape
    lane = lax.broadcasted_iota(jnp.int32, (rows, LANES), 1)
    for at in range(0, width, LANES):
        block = turned_ref[at : at + LANES].T
        block = PROP_STEP * sum(block[n * group : n * group + rows] for n in range(2 * tiles))
        if at + LANES > pairs:
            share = jnp.concatenate([energy, jnp.zeros((rows - walkers, 1), F32)], axis=0)
            block = jnp.where(lane + at < pairs, block, 0.0)
            for piece in range(3):
                head = share.astype(BF16).astype(F32)
                block = jnp.where(lane + at == pairs + piece, head, block)
                share = share - head
        for copy in range(copies):
            out_ref[copy, :, at : at + LANES] = block.astype(BF16)


def taylor_kernel(ka_count, pb_count, normalizer, blocks_ref, *refs):
    windows = refs[:ka_count]
    picks_ref, orbitals_ref, out_ref, energy_ref, table, turned, picked, term = refs[ka_count:]
    half = LANES // 2
    pairs = M * M
    pair = NOCC * M
    rows = blocks_ref.shape[1] // 2
    for at in range(ka_count * pb_count):
        ka_from, pb_from = at // pb_count, at % pb_count
        start = (pb_from * ka_count + ka_from) * rows
        block = blocks_ref[at].astype(F32)
        table[start : start + rows, :] = block[:rows]
        table[start + half : start + half + rows, :] = block[rows:]
    for at in range(0, table.shape[1], LANES):
        turned[at : at + LANES] = table[:, at : at + LANES].T
    ka_pos = lax.axis_index("ka")
    last = pairs // LANES * LANES
    shares = table[:half, last : last + LANES]
    lane = lax.broadcasted_iota(jnp.int32, shares.shape, 1) + last
    row = lax.broadcasted_iota(jnp.int32, shares.shape, 0)
    shares = jnp.where(
        (lane >= pairs) & (lane < pairs + 3) & (lax.rem(row, rows) == ka_pos), shares, 0.0
    )
    shares = jnp.sum(jnp.sum(shares, axis=0, keepdims=True), axis=1, keepdims=True)
    energy_ref[...] = shares / normalizer
    term[...] = jnp.zeros_like(term)
    for step, window_ref in enumerate(windows):
        start = pl.multiple_of(origin("ka", step) * rows, rows)
        window = window_ref[window_ref.shape[0] - rows :]
        term[pl.ds(start, rows), :pair] = window[:, :pair]
        term[pl.ds(start + half, rows), :pair] = window[:, pair : 2 * pair]
    picked[...] = jnp.dot(
        term[...].T[:pair].astype(BF16), picks_ref[...], preferred_element_type=F32
    )
    sums = [jnp.zeros((M, LANES), F32) for _ in range(NOCC)]
    for degree in range(1, TAYLOR + 1):
        source = picked
        straight = [jnp.zeros((M, LANES), F32) for _ in range(NOCC)]
        crossed = [jnp.zeros((M, LANES), F32) for _ in range(NOCC)]
        for c in range(M):
            column = turned[pl.ds(c, M, stride=M), :]
            for i in range(NOCC):
                at = i * M + c
                straight[i] += column * source[at : at + 1, :LANES]
                crossed[i] += column * source[at : at + 1, LANES:]
        for i in range(NOCC):
            applied = straight[i] + pltpu.roll(crossed[i], half, 1)
            applied = applied + pltpu.roll(applied, LANES - half // pb_count, 1)
            current = applied / degree
            sums[i] = sums[i] + current
            term[i * M : (i + 1) * M] = current if degree < TAYLOR else sums[i]
        if degree < TAYLOR:
            picked[...] = jnp.dot(
                term[: NOCC * M].astype(BF16), picks_ref[...], preferred_element_type=F32
            )
    term[NOCC * M :] = jnp.zeros((LANES - NOCC * M, LANES), F32)
    table[:, :LANES] = term[...].T
    k_local, walkers, _ = out_ref.shape
    start = pl.multiple_of(ka_pos * rows, rows)
    real = table[pl.ds(start, rows), :pair]
    imag = table[pl.ds(start + half, rows), :pair]
    both = jnp.concatenate([real, imag], axis=1)
    for k in range(k_local):
        out_ref[k] = orbitals_ref[k] + both[k * walkers : (k + 1) * walkers]


def call(kernel, out, scratch=(), scalars=0, operands=0, flops=None):
    spaces = [pltpu.SMEM] * scalars + [pltpu.VMEM] * operands
    cost = None
    if flops is not None:
        cost = pl.CostEstimate(flops=flops, bytes_accessed=0, transcendentals=0)
    return pl.pallas_call(
        kernel,
        out_shape=out,
        in_specs=[pl.BlockSpec(memory_space=space) for space in spaces],
        out_specs=jax.tree.map(lambda _: pl.BlockSpec(memory_space=pltpu.VMEM), out),
        scratch_shapes=list(scratch),
        cost_estimate=cost,
        compiler_params=pltpu.CompilerParams(vmem_limit_bytes=24 * 2**20),
    )


def direct(green, fields, orbitals, chol_half, chol_full, chol_count, kq_map):
    k_local, pair_width, chol_cols = chol_half.shape[1], chol_half.shape[3], chol_half.shape[4]
    ka_count, pb_count = lax.axis_size("ka"), lax.axis_size("pb")
    walkers = ka_count
    kpoints = green.shape[3]
    span = k_local * walkers
    shape = jax.ShapeDtypeStruct
    tiles = chol_cols // LANES
    own_green = green.reshape(kpoints, 2 * pair_width)
    greens = [own_green] + [swap(own_green, "ka", s) for s in range(1, ka_count)]
    half = chol_half.reshape(k_local, 2, pair_width, chol_cols)
    full = jnp.transpose(
        chol_full.reshape(k_local, 2, M * M, tiles, LANES), (0, 2, 3, 1, 4)
    ).reshape(k_local, M * M * tiles * 2, LANES)
    own_fields = fields.reshape(walkers, chol_cols)
    own_orbitals = orbitals.reshape(k_local, walkers, 2 * pair_width)
    mask, picks = call(
        functools.partial(prepare_kernel, pb_count, walkers),
        (shape((2 * walkers, chol_cols), F32), shape((LANES, 2 * LANES), BF16)),
        scalars=2,
        flops=10**9,
    )(kq_map, chol_count)
    bias, own = call(
        functools.partial(bias_kernel, ka_count, k_local),
        (
            shape((2 * walkers + span, chol_cols), F32),
            shape((k_local, 2 * walkers, pair_width), F32),
        ),
        [pltpu.VMEM((walkers, kpoints, 2 * pair_width), F32)],
        operands=ka_count + 3,
    )(*greens, half, own_orbitals, mask)
    parts = [bias] + [swap(bias, "ka", s) for s in range(1, ka_count)]
    exchange = call(
        functools.partial(exchange_kernel, k_local),
        shape((walkers, LANES), F32),
        operands=3,
    )(own, half, mask)
    width = -(-(M * M + 3) // LANES) * LANES
    blocks = call(
        functools.partial(operator_kernel, ka_count, k_local),
        shape((ka_count * pb_count, 2 * span, width), BF16),
        [pltpu.VMEM((2 * M * M * tiles, LANES), F32), pltpu.VMEM((width, LANES), F32)],
        operands=ka_count + 4,
    )(*parts, own_fields, mask, exchange, full)
    blocks = lax.all_to_all(blocks, ("ka", "pb"), 0, 0, tiled=True)
    propagated, energy = call(
        functools.partial(taylor_kernel, ka_count, pb_count, float(pb_count * chol_cols)),
        (shape((k_local, walkers, 2 * pair_width), F32), shape((1, 1), F32)),
        [
            pltpu.VMEM((LANES, width), F32),
            pltpu.VMEM((width, LANES), F32),
            pltpu.VMEM((pair_width, 2 * LANES), F32),
            pltpu.VMEM((LANES, LANES), F32),
        ],
        operands=ka_count + 3,
    )(blocks, *parts, picks, own_orbitals)
    return (propagated[None], energy)


def on_device(green, fields, orbitals, chol_half, chol_full, chol_count, kq_map):
    ka_count, pb_count = lax.axis_size("ka"), lax.axis_size("pb")
    walkers = orbitals.shape[2]
    fits = 2 * pb_count * kq_map.shape[1] * walkers == LANES
    fits = fits and chol_half.shape[1] * walkers == 8 and chol_half.shape[4] == 2 * LANES
    fits = fits and ka_count & (ka_count - 1) == 0
    if fits and chol_half.shape[0] == 1 and walkers == ka_count:
        return direct(green, fields, orbitals, chol_half, chol_full, chol_count, kq_map)
    return with_collectives(green, fields, orbitals, chol_half, chol_full, chol_count, kq_map)


def solution(mesh):
    placed = (
        P("wa", ("grp", "ka"), "pb", None, None),
        P("wa", "pb", "grp", None),
        P("wa", "ka", "grp", None),
        P("pb", "ka", None, None, None),
        P("pb", "ka", None, None, None),
        P(),
        P(),
    )
    return jax.shard_map(
        on_device,
        mesh=mesh,
        in_specs=placed,
        out_specs=(P("wa", "ka", "grp", None), P("wa", ("grp", "ka"))),
        check_vma=False,
    )
```

```python
import functools

import jax
import jax.numpy as jnp
from jax import lax
from jax.experimental import pallas as pl
from jax.experimental.pallas import tpu as pltpu
from jax.sharding import PartitionSpec as P

M = 26
NOCC = 4
TAYLOR = 3
LANES = 128
ROWS = 32


BIAS_STEP = 0.5
PROP_STEP = 0.5

F32 = jnp.float32
BF16 = jnp.bfloat16


def complex_dot(pattern, left_re, left_im, right_re, right_im):
    real_part = jnp.einsum(
        pattern, left_re, right_re, preferred_element_type=jnp.float32
    ) - jnp.einsum(pattern, left_im, right_im, preferred_element_type=jnp.float32)
    imag_part = jnp.einsum(
        pattern, left_re, right_im, preferred_element_type=jnp.float32
    ) + jnp.einsum(pattern, left_im, right_re, preferred_element_type=jnp.float32)
    return (real_part, imag_part)


def make_picker(wanted):

    def picker(shard_rows):
        row_count = shard_rows.shape[0]
        select = (wanted[:, None] == jnp.arange(row_count, dtype=jnp.int32)[None, :]).astype(
            jnp.bfloat16
        )
        return jnp.dot(select, shard_rows, preferred_element_type=jnp.float32)

    return picker


def with_collectives(green, fields, orbitals, chol_half, chol_full, chol_count, kq_map):
    q_local = chol_half.shape[0]
    k_local = chol_half.shape[1]
    pair_width = chol_half.shape[3]
    chol_cols = chol_half.shape[4]
    ka_count = lax.axis_size("ka")
    pb_count = lax.axis_size("pb")
    ka_pos = lax.axis_index("ka")
    pb_pos = lax.axis_index("pb")
    local_green = lax.all_to_all(green, "ka", split_axis=3, concat_axis=1, tiled=True)
    walkers = local_green.shape[1]
    per_device = walkers // ka_count
    greens = local_green[0].reshape(walkers, q_local, k_local, 2, pair_width)
    counts = lax.dynamic_slice_in_dim(chol_count, pb_pos * q_local, q_local)
    vec_mask = (jnp.arange(chol_cols, dtype=jnp.int32)[None, :] < counts[:, None]).astype(
        jnp.float32
    )
    bias_re, bias_im = complex_dot(
        "wqkx,qkxn->qwn",
        greens[:, :, :, 0],
        greens[:, :, :, 1],
        chol_half[:, :, 0],
        chol_half[:, :, 1],
    )
    own_rows = (jnp.arange(walkers, dtype=jnp.int32) // per_device == ka_pos).astype(jnp.float32)
    bias_re, bias_im = lax.psum((bias_re, bias_im), "ka")
    bias_re = bias_re * vec_mask[:, None, :]
    bias_im = bias_im * vec_mask[:, None, :]
    hartree = 0.5 * jnp.sum(bias_re * bias_re + bias_im * bias_im, axis=(0, 2)) * own_rows
    field_now = jnp.transpose(fields, (1, 0, 2, 3)).reshape(q_local, walkers, chol_cols)
    shift_re = ((field_now - BIAS_STEP * bias_re) * vec_mask[:, None, :]).astype(jnp.bfloat16)
    shift_im = (-BIAS_STEP * bias_im * vec_mask[:, None, :]).astype(jnp.bfloat16)
    exchange = jnp.zeros((walkers,), jnp.float32)
    for transfer in range(q_local):
        for kpoint in range(k_local):
            chol_row = chol_half[transfer, kpoint].reshape(2, NOCC, M, chol_cols)
            green_row = greens[:, transfer, kpoint].reshape(walkers, 2, NOCC, M)
            cross_re, cross_im = complex_dot(
                "ipn,wjp->wijn", chol_row[0], chol_row[1], green_row[:, 0], green_row[:, 1]
            )
            exchange = exchange + 0.5 * jnp.sum(
                (cross_re * cross_re + cross_im * cross_im) * vec_mask[transfer], axis=(1, 2, 3)
            )
    prop_re, prop_im = complex_dot(
        "qwn,qkyn->qwky", shift_re, shift_im, chol_full[:, :, 0], chol_full[:, :, 1]
    )
    shape = (q_local, walkers, k_local, M, M)
    oper_re = (PROP_STEP * prop_re).astype(jnp.bfloat16).reshape(shape)
    oper_im = (PROP_STEP * prop_im).astype(jnp.bfloat16).reshape(shape)
    normalizer = q_local * pb_count * chol_cols
    total_energy = lax.psum(hartree - exchange, ("ka", "pb")) / normalizer
    energy = lax.dynamic_slice_in_dim(total_energy, ka_pos * per_device, per_device).reshape(
        1, per_device
    )
    initial = orbitals[0].reshape(k_local, walkers, 2, NOCC, M)
    row_width = 2 * pair_width
    my_rows = lax.dynamic_slice_in_dim(kq_map, pb_pos * q_local, q_local, 0)
    wanted = lax.dynamic_slice_in_dim(my_rows, ka_pos * k_local, k_local, 1).reshape(
        q_local * k_local
    )
    picker = make_picker(wanted)
    current = initial
    summed_terms = initial
    for degree in range(1, TAYLOR + 1):
        rounded = current.astype(jnp.bfloat16).reshape(k_local, walkers * row_width)
        fetched = picker(lax.all_gather(rounded, "ka", axis=0, tiled=True))
        shifted_rows = fetched.astype(jnp.bfloat16).reshape(q_local, k_local, walkers, 2, NOCC, M)
        out_re, out_im = complex_dot(
            "xwkpq,xkwiq->kwip",
            oper_re,
            oper_im,
            shifted_rows[:, :, :, 0],
            shifted_rows[:, :, :, 1],
        )
        applied = jnp.stack([out_re, out_im], axis=2)
        applied = lax.psum(applied, "pb")
        current = applied / degree
        summed_terms = summed_terms + current
    propagated = summed_terms.reshape(1, k_local, walkers, row_width)
    return (propagated, energy)


def swap(array, axis, step):
    size = lax.axis_size(axis)
    return lax.ppermute(array, axis, [(at, at ^ step) for at in range(size)])


def origin(axis, step):
    return lax.axis_index(axis) ^ step


def prepare_kernel(ka_count, pb_count, walkers, map_ref, count_ref, mask_ref, picks_ref):
    kept = count_ref[lax.axis_index("pb")]
    column = lax.broadcasted_iota(jnp.int32, mask_ref.shape, 1)
    mask_ref[...] = jnp.where(column < kept, 1.0, 0.0)
    kpoints = map_ref.shape[1]
    k_local = kpoints // ka_count
    span = k_local * walkers
    lane = lax.broadcasted_iota(jnp.int32, (1, LANES), 1)
    lane_q = lane // (LANES // pb_count)
    lane_ka = lax.rem(lane, LANES // pb_count) // (2 * span)
    lane_part = lax.rem(lane, 2 * span) // span
    lane_k = lane_ka * k_local + lax.rem(lane, span) // walkers
    wanted = jnp.zeros((1, LANES), jnp.int32)
    for q in range(pb_count):
        for k in range(kpoints):
            source = map_ref[q, k]
            source = source // k_local * (2 * span) + lax.rem(source, k_local) * walkers
            wanted = jnp.where((lane_q == q) & (lane_k == k), source, wanted)
    wanted = wanted + lax.rem(lane, walkers)
    row = lax.broadcasted_iota(jnp.int32, (LANES, LANES), 0)
    real = jnp.where(row == wanted, 1.0, 0.0)
    imag = jnp.where(row == wanted + span, jnp.where(lane_part == 0, 1.0, -1.0), 0.0)
    picks_ref[...] = jnp.concatenate([real, imag], axis=1).astype(BF16)


def bias_kernel(ka_count, k_local, *refs):
    greens = refs[:ka_count]
    chol_ref, orbitals_ref, mask_ref, bias_ref, own_ref, table = refs[ka_count:]
    for step, green_ref in enumerate(greens):
        table[origin("ka", step)] = green_ref[...].astype(F32)
    first = lax.axis_index("ka") * k_local
    width = chol_ref.shape[2]
    rows = 2 * ka_count
    total = jnp.zeros((rows, bias_ref.shape[1]), F32)
    for k in range(k_local):
        green = jnp.concatenate(
            [table[w, pl.ds(first + k, 1), :] for w in range(ka_count)], axis=0
        )
        real, imag = green[:, :width], green[:, width:]
        both = jnp.concatenate([real, imag], axis=0)
        turned = jnp.concatenate([-imag, real], axis=0)
        own_ref[k] = both
        total += jnp.dot(both.astype(BF16), chol_ref[k, 0], preferred_element_type=F32)
        total += jnp.dot(turned.astype(BF16), chol_ref[k, 1], preferred_element_type=F32)
    bias_ref[:rows] = total * mask_ref[...]
    window = jnp.concatenate([orbitals_ref[k] for k in range(k_local)], axis=0)
    count, width = window.shape
    bias_ref[rows : rows + count, :width] = window
    bias_ref[rows : rows + count, width:] = jnp.zeros((count, bias_ref.shape[1] - width), F32)


def exchange_kernel(k_local, own_ref, chol_ref, mask_ref, out_ref):
    walkers, width, columns = own_ref.shape[1] // 2, own_ref.shape[2], chol_ref.shape[3]
    rows = 2 * walkers
    lane = lax.broadcasted_iota(jnp.int32, (rows, LANES), 1)
    total = jnp.zeros((rows, columns), F32)
    for k in range(k_local):
        both = jnp.concatenate([own_ref[k], jnp.zeros((rows, LANES - width), F32)], axis=1)
        turned = jnp.concatenate([-both[walkers:], both[:walkers]], axis=0)
        sides = []
        for side in (both, turned):
            rolled = {
                step: side if step == 0 else pltpu.roll(side, (step * M) % LANES, 1)
                for step in range(1 - NOCC, NOCC)
            }
            blocks = []
            for i in range(NOCC):
                inside = (lane >= i * M) & (lane < (i + 1) * M)
                for j in range(NOCC):
                    blocks.append(jnp.where(inside, rolled[i - j], 0.0))
            sides.append(jnp.concatenate(blocks, axis=0)[:, :width].astype(BF16))
        cross = jnp.dot(sides[0], chol_ref[k, 0], preferred_element_type=F32)
        cross += jnp.dot(sides[1], chol_ref[k, 1], preferred_element_type=F32)
        cross = cross * cross
        for block in range(NOCC * NOCC):
            total += cross[block * rows : (block + 1) * rows]
    total = total * mask_ref[:rows]
    total = total[:walkers] + total[walkers:]
    summed = 0.5 * jnp.sum(total, axis=1, keepdims=True)
    out_ref[...] = jnp.broadcast_to(summed, out_ref.shape)


def operator_kernel(ka_count, k_local, *refs):
    parts = refs[:ka_count]
    fields_ref, mask_ref, exchange_ref, chol_ref, out_ref, products, turned_ref = refs[ka_count:]
    walkers, columns = fields_ref.shape
    bias = parts[0][: 2 * walkers]
    for part in parts[1:]:
        bias = bias + part[: 2 * walkers]
    pairs = M * M
    tiles = columns // LANES
    group = LANES // (2 * tiles)
    bias_re, bias_im = bias[:walkers], bias[walkers:]
    hartree = 0.5 * jnp.sum(bias_re * bias_re + bias_im * bias_im, axis=1, keepdims=True)
    own = lax.broadcasted_iota(jnp.int32, (walkers, 1), 0) == lax.axis_index("ka")
    energy = jnp.where(own, hartree, 0.0) - exchange_ref[:, :1]
    kept = mask_ref[:walkers]
    shift_re = (fields_ref[...] - BIAS_STEP * bias_re) * kept
    shift_im = -BIAS_STEP * bias_im * kept
    span = k_local * walkers
    weights = []
    for k in range(k_local):
        before, after = k * walkers, span - (k + 1) * walkers
        pieces = []
        for tile in range(tiles):
            at = slice(tile * LANES, (tile + 1) * LANES)
            for first, second in ((shift_re, shift_im), (-shift_im, shift_re)):
                for side in (first, second):
                    pieces += [(before, None), (walkers, side[:, at]), (after, None)]
                pieces.append((group - 2 * span, None))
        weights.append(
            jnp.concatenate(
                [jnp.zeros((n, LANES), F32) if p is None else p for n, p in pieces if n], axis=0
            ).astype(BF16)
        )
    products[...] = lax.dot_general(
        jnp.concatenate([chol_ref[k] for k in range(k_local)], axis=1),
        jnp.concatenate(weights, axis=1),
        (((1,), (1,)), ((), ())),
        preferred_element_type=F32,
    )
    lane = lax.broadcasted_iota(jnp.int32, (pairs, LANES), 1)
    merged = products[pl.ds(0, pairs, stride=2 * tiles), :]
    for at in range(1, 2 * tiles):
        row = products[pl.ds(at, pairs, stride=2 * tiles), :]
        merged = jnp.where(lane >= at * group, row, merged)
    turned_ref[:pairs] = merged
    copies, rows, width = out_ref.shape
    lane = lax.broadcasted_iota(jnp.int32, (rows, LANES), 1)
    for at in range(0, width, LANES):
        block = turned_ref[at : at + LANES].T
        block = PROP_STEP * sum(block[n * group : n * group + rows] for n in range(2 * tiles))
        if at + LANES > pairs:
            share = jnp.concatenate([energy, jnp.zeros((rows - walkers, 1), F32)], axis=0)
            block = jnp.where(lane + at < pairs, block, 0.0)
            for piece in range(3):
                head = share.astype(BF16).astype(F32)
                block = jnp.where(lane + at == pairs + piece, head, block)
                share = share - head
        for copy in range(copies):
            out_ref[copy, :, at : at + LANES] = block.astype(BF16)


def taylor_kernel(ka_count, pb_count, normalizer, blocks_ref, *refs):
    windows = refs[:ka_count]
    picks_ref, orbitals_ref, out_ref, energy_ref, turned, picked, term = refs[ka_count:]
    pairs = M * M
    pair = NOCC * M
    k_local, walkers, _ = out_ref.shape
    span = k_local * walkers
    ka_pos = lax.axis_index("ka")
    term[...] = jnp.zeros_like(term)
    for step, window_ref in enumerate(windows):
        start = pl.multiple_of(origin("ka", step) * (2 * span), 2 * span)
        window = window_ref[window_ref.shape[0] - span :]
        term[pl.ds(start, span), :pair] = window[:, :pair]
        term[pl.ds(start + span, span), :pair] = window[:, pair : 2 * pair]
    picked[...] = jnp.dot(term[...].T.astype(BF16), picks_ref[...], preferred_element_type=F32)
    count, rows, width = blocks_ref.shape
    for at in range(0, width, LANES):
        tile = jnp.concatenate([blocks_ref[n, :, at : at + LANES] for n in range(count)], axis=0)
        turned[at : at + LANES] = tile.T.astype(F32)
    shares = turned[pairs : pairs + 3]
    lane = lax.broadcasted_iota(jnp.int32, shares.shape, 1)
    shares = jnp.where(lax.rem(lane, 2 * span) == ka_pos, shares, 0.0)
    shares = jnp.sum(jnp.sum(shares, axis=0, keepdims=True), axis=1, keepdims=True)
    energy_ref[...] = shares / normalizer
    lane = lax.broadcasted_iota(jnp.int32, (M, LANES), 1)
    imaginary = lax.rem(lane, 2 * span) >= span
    sums = [jnp.zeros((M, LANES), F32) for _ in range(NOCC)]
    for degree in range(1, TAYLOR + 1):
        stride = M if degree == 1 else ROWS
        straight = [jnp.zeros((M, LANES), F32) for _ in range(NOCC)]
        crossed = [jnp.zeros((M, LANES), F32) for _ in range(NOCC)]
        for c in range(M):
            column = turned[pl.ds(c, M, stride=M), :]
            for i in range(NOCC):
                at = i * stride + c
                straight[i] += column * picked[at : at + 1, :LANES]
                crossed[i] += column * picked[at : at + 1, LANES:]
        for i in range(NOCC):
            other = jnp.where(
                imaginary, pltpu.roll(crossed[i], span, 1), pltpu.roll(crossed[i], LANES - span, 1)
            )
            applied = straight[i] + other
            applied = applied + pltpu.roll(applied, LANES // pb_count, 1)
            current = applied / degree
            sums[i] = sums[i] + current
            term[i * ROWS : i * ROWS + M] = current if degree < TAYLOR else sums[i]
        if degree < TAYLOR:
            picked[...] = jnp.dot(
                term[...].astype(BF16), picks_ref[...], preferred_element_type=F32
            )
    turned[:LANES] = term[...].T
    both = turned[pl.ds(pl.multiple_of(ka_pos * (2 * span), 2 * span), 2 * span), :]
    both = jnp.concatenate([both[:, i * ROWS : i * ROWS + M] for i in range(NOCC)], axis=1)
    both = jnp.concatenate([both[:span], both[span:]], axis=1)
    for k in range(k_local):
        out_ref[k] = orbitals_ref[k] + both[k * walkers : (k + 1) * walkers]


def call(kernel, out, scratch=(), scalars=0, operands=0, flops=None):
    spaces = [pltpu.SMEM] * scalars + [pltpu.VMEM] * operands
    cost = None
    if flops is not None:
        cost = pl.CostEstimate(flops=flops, bytes_accessed=0, transcendentals=0)
    return pl.pallas_call(
        kernel,
        out_shape=out,
        in_specs=[pl.BlockSpec(memory_space=space) for space in spaces],
        out_specs=jax.tree.map(lambda _: pl.BlockSpec(memory_space=pltpu.VMEM), out),
        scratch_shapes=list(scratch),
        cost_estimate=cost,
        compiler_params=pltpu.CompilerParams(vmem_limit_bytes=24 * 2**20),
    )


def direct(green, fields, orbitals, chol_half, chol_full, chol_count, kq_map):
    k_local, pair_width, chol_cols = chol_half.shape[1], chol_half.shape[3], chol_half.shape[4]
    ka_count, pb_count = lax.axis_size("ka"), lax.axis_size("pb")
    walkers = ka_count
    kpoints = green.shape[3]
    span = k_local * walkers
    shape = jax.ShapeDtypeStruct
    tiles = chol_cols // LANES
    own_green = green.reshape(kpoints, 2 * pair_width)
    greens = [own_green] + [swap(own_green, "ka", s) for s in range(1, ka_count)]
    half = chol_half.reshape(k_local, 2, pair_width, chol_cols)
    full = jnp.transpose(
        chol_full.reshape(k_local, 2, M * M, tiles, LANES), (0, 2, 3, 1, 4)
    ).reshape(k_local, M * M * tiles * 2, LANES)
    own_fields = fields.reshape(walkers, chol_cols)
    own_orbitals = orbitals.reshape(k_local, walkers, 2 * pair_width)
    mask, picks = call(
        functools.partial(prepare_kernel, ka_count, pb_count, walkers),
        (shape((2 * walkers, chol_cols), F32), shape((LANES, 2 * LANES), BF16)),
        scalars=2,
        flops=10**9,
    )(kq_map, chol_count)
    bias, own = call(
        functools.partial(bias_kernel, ka_count, k_local),
        (
            shape((2 * walkers + span, chol_cols), F32),
            shape((k_local, 2 * walkers, pair_width), F32),
        ),
        [pltpu.VMEM((walkers, kpoints, 2 * pair_width), F32)],
        operands=ka_count + 3,
    )(*greens, half, own_orbitals, mask)
    parts = [bias] + [swap(bias, "ka", s) for s in range(1, ka_count)]
    exchange = call(
        functools.partial(exchange_kernel, k_local),
        shape((walkers, LANES), F32),
        operands=3,
    )(own, half, mask)
    width = -(-(M * M + 3) // LANES) * LANES
    blocks = call(
        functools.partial(operator_kernel, ka_count, k_local),
        shape((ka_count * pb_count, 2 * span, width), BF16),
        [pltpu.VMEM((2 * M * M * tiles, LANES), F32), pltpu.VMEM((width, LANES), F32)],
        operands=ka_count + 4,
    )(*parts, own_fields, mask, exchange, full)
    blocks = lax.all_to_all(blocks, ("pb", "ka"), 0, 0, tiled=True)
    propagated, energy = call(
        functools.partial(taylor_kernel, ka_count, pb_count, float(pb_count * chol_cols)),
        (shape((k_local, walkers, 2 * pair_width), F32), shape((1, 1), F32)),
        [
            pltpu.VMEM((width, LANES), F32),
            pltpu.VMEM((NOCC * ROWS, 2 * LANES), F32),
            pltpu.VMEM((LANES, LANES), F32),
        ],
        operands=ka_count + 3,
    )(blocks, *parts, picks, own_orbitals)
    return (propagated[None], energy)


def on_device(green, fields, orbitals, chol_half, chol_full, chol_count, kq_map):
    ka_count, pb_count = lax.axis_size("ka"), lax.axis_size("pb")
    walkers = orbitals.shape[2]
    fits = 2 * pb_count * kq_map.shape[1] * walkers == LANES
    fits = fits and chol_half.shape[1] * walkers == 8 and chol_half.shape[4] == 2 * LANES
    fits = fits and ka_count & (ka_count - 1) == 0
    if fits and chol_half.shape[0] == 1 and walkers == ka_count:
        return direct(green, fields, orbitals, chol_half, chol_full, chol_count, kq_map)
    return with_collectives(green, fields, orbitals, chol_half, chol_full, chol_count, kq_map)


def solution(mesh):
    placed = (
        P("wa", ("grp", "ka"), "pb", None, None),
        P("wa", "pb", "grp", None),
        P("wa", "ka", "grp", None),
        P("pb", "ka", None, None, None),
        P("pb", "ka", None, None, None),
        P(),
        P(),
    )
    return jax.shard_map(
        on_device,
        mesh=mesh,
        in_specs=placed,
        out_specs=(P("wa", "ka", "grp", None), P("wa", ("grp", "ka"))),
        check_vma=False,
    )
```

```python
import functools

import jax
import jax.numpy as jnp
from jax import lax
from jax.experimental import pallas as pl
from jax.experimental.pallas import tpu as pltpu
from jax.sharding import PartitionSpec as P

M = 26
NOCC = 4
TAYLOR = 3
LANES = 128
ROWS = 32

GREEN_ROUNDS = (
    ((3, 0), (2, 1)),
    ((0, 3), (2, 0), (3, 1), (1, 2)),
    ((0, 1), (3, 2), (1, 3)),
    ((0, 2), (2, 3), (1, 0)),
)[::-1]
BIAS_ROUNDS = (
    ((0, 1), (3, 2), (2, 3)),
    ((3, 1), (2, 0), (1, 3)),
    ((1, 2), (3, 0), (0, 3)),
    ((1, 0), (0, 2), (2, 1)),
)[::-1]


BIAS_STEP = 0.5
PROP_STEP = 0.5

F32 = jnp.float32
BF16 = jnp.bfloat16


def complex_dot(pattern, left_re, left_im, right_re, right_im):
    real_part = jnp.einsum(
        pattern, left_re, right_re, preferred_element_type=jnp.float32
    ) - jnp.einsum(pattern, left_im, right_im, preferred_element_type=jnp.float32)
    imag_part = jnp.einsum(
        pattern, left_re, right_im, preferred_element_type=jnp.float32
    ) + jnp.einsum(pattern, left_im, right_re, preferred_element_type=jnp.float32)
    return (real_part, imag_part)


def make_picker(wanted):

    def picker(shard_rows):
        row_count = shard_rows.shape[0]
        select = (wanted[:, None] == jnp.arange(row_count, dtype=jnp.int32)[None, :]).astype(
            jnp.bfloat16
        )
        return jnp.dot(select, shard_rows, preferred_element_type=jnp.float32)

    return picker


def with_collectives(green, fields, orbitals, chol_half, chol_full, chol_count, kq_map):
    q_local = chol_half.shape[0]
    k_local = chol_half.shape[1]
    pair_width = chol_half.shape[3]
    chol_cols = chol_half.shape[4]
    ka_count = lax.axis_size("ka")
    pb_count = lax.axis_size("pb")
    ka_pos = lax.axis_index("ka")
    pb_pos = lax.axis_index("pb")
    local_green = lax.all_to_all(green, "ka", split_axis=3, concat_axis=1, tiled=True)
    walkers = local_green.shape[1]
    per_device = walkers // ka_count
    greens = local_green[0].reshape(walkers, q_local, k_local, 2, pair_width)
    counts = lax.dynamic_slice_in_dim(chol_count, pb_pos * q_local, q_local)
    vec_mask = (jnp.arange(chol_cols, dtype=jnp.int32)[None, :] < counts[:, None]).astype(
        jnp.float32
    )
    bias_re, bias_im = complex_dot(
        "wqkx,qkxn->qwn",
        greens[:, :, :, 0],
        greens[:, :, :, 1],
        chol_half[:, :, 0],
        chol_half[:, :, 1],
    )
    own_rows = (jnp.arange(walkers, dtype=jnp.int32) // per_device == ka_pos).astype(jnp.float32)
    bias_re, bias_im = lax.psum((bias_re, bias_im), "ka")
    bias_re = bias_re * vec_mask[:, None, :]
    bias_im = bias_im * vec_mask[:, None, :]
    hartree = 0.5 * jnp.sum(bias_re * bias_re + bias_im * bias_im, axis=(0, 2)) * own_rows
    field_now = jnp.transpose(fields, (1, 0, 2, 3)).reshape(q_local, walkers, chol_cols)
    shift_re = ((field_now - BIAS_STEP * bias_re) * vec_mask[:, None, :]).astype(jnp.bfloat16)
    shift_im = (-BIAS_STEP * bias_im * vec_mask[:, None, :]).astype(jnp.bfloat16)
    exchange = jnp.zeros((walkers,), jnp.float32)
    for transfer in range(q_local):
        for kpoint in range(k_local):
            chol_row = chol_half[transfer, kpoint].reshape(2, NOCC, M, chol_cols)
            green_row = greens[:, transfer, kpoint].reshape(walkers, 2, NOCC, M)
            cross_re, cross_im = complex_dot(
                "ipn,wjp->wijn", chol_row[0], chol_row[1], green_row[:, 0], green_row[:, 1]
            )
            exchange = exchange + 0.5 * jnp.sum(
                (cross_re * cross_re + cross_im * cross_im) * vec_mask[transfer], axis=(1, 2, 3)
            )
    prop_re, prop_im = complex_dot(
        "qwn,qkyn->qwky", shift_re, shift_im, chol_full[:, :, 0], chol_full[:, :, 1]
    )
    shape = (q_local, walkers, k_local, M, M)
    oper_re = (PROP_STEP * prop_re).astype(jnp.bfloat16).reshape(shape)
    oper_im = (PROP_STEP * prop_im).astype(jnp.bfloat16).reshape(shape)
    normalizer = q_local * pb_count * chol_cols
    total_energy = lax.psum(hartree - exchange, ("ka", "pb")) / normalizer
    energy = lax.dynamic_slice_in_dim(total_energy, ka_pos * per_device, per_device).reshape(
        1, per_device
    )
    initial = orbitals[0].reshape(k_local, walkers, 2, NOCC, M)
    row_width = 2 * pair_width
    my_rows = lax.dynamic_slice_in_dim(kq_map, pb_pos * q_local, q_local, 0)
    wanted = lax.dynamic_slice_in_dim(my_rows, ka_pos * k_local, k_local, 1).reshape(
        q_local * k_local
    )
    picker = make_picker(wanted)
    current = initial
    summed_terms = initial
    for degree in range(1, TAYLOR + 1):
        rounded = current.astype(jnp.bfloat16).reshape(k_local, walkers * row_width)
        fetched = picker(lax.all_gather(rounded, "ka", axis=0, tiled=True))
        shifted_rows = fetched.astype(jnp.bfloat16).reshape(q_local, k_local, walkers, 2, NOCC, M)
        out_re, out_im = complex_dot(
            "xwkpq,xkwiq->kwip",
            oper_re,
            oper_im,
            shifted_rows[:, :, :, 0],
            shifted_rows[:, :, :, 1],
        )
        applied = jnp.stack([out_re, out_im], axis=2)
        applied = lax.psum(applied, "pb")
        current = applied / degree
        summed_terms = summed_terms + current
    propagated = summed_terms.reshape(1, k_local, walkers, row_width)
    return (propagated, energy)


def exchange(array, axis, rounds):
    return [array] + [lax.ppermute(array, axis, pairs) for pairs in rounds]


def origins(axis, rounds):
    at, size = lax.axis_index(axis), lax.axis_size(axis)
    found = [at]
    for pairs in rounds:
        source = jnp.int32(size)
        for sender, receiver in pairs:
            source = jnp.where(at == receiver, sender, source)
        found.append(source)
    return found


def prepare_kernel(ka_count, pb_count, walkers, map_ref, count_ref, mask_ref, picks_ref):
    kept = count_ref[lax.axis_index("pb")]
    column = lax.broadcasted_iota(jnp.int32, mask_ref.shape, 1)
    mask_ref[...] = jnp.where(column < kept, 1.0, 0.0)
    kpoints = map_ref.shape[1]
    k_local = kpoints // ka_count
    span = k_local * walkers
    lane = lax.broadcasted_iota(jnp.int32, (1, LANES), 1)
    lane_q = lane // (LANES // pb_count)
    lane_ka = lax.rem(lane, LANES // pb_count) // (2 * span)
    lane_part = lax.rem(lane, 2 * span) // span
    lane_k = lane_ka * k_local + lax.rem(lane, span) // walkers
    wanted = jnp.zeros((1, LANES), jnp.int32)
    for q in range(pb_count):
        for k in range(kpoints):
            source = map_ref[q, k]
            source = source // k_local * (2 * span) + lax.rem(source, k_local) * walkers
            wanted = jnp.where((lane_q == q) & (lane_k == k), source, wanted)
    wanted = wanted + lax.rem(lane, walkers)
    row = lax.broadcasted_iota(jnp.int32, (LANES, LANES), 0)
    real = jnp.where(row == wanted, 1.0, 0.0)
    imag = jnp.where(row == wanted + span, jnp.where(lane_part == 0, 1.0, -1.0), 0.0)
    picks_ref[...] = jnp.concatenate([real, imag], axis=1).astype(BF16)


def bias_kernel(ka_count, k_local, *refs):
    *greens, chol_ref, orbitals_ref, mask_ref, bias_ref, own_ref, table = refs
    for source, green_ref in zip(origins("ka", GREEN_ROUNDS), greens):
        table[source] = green_ref[...].astype(F32)
    first = lax.axis_index("ka") * k_local
    width = chol_ref.shape[2]
    rows = 2 * ka_count
    total = jnp.zeros((rows, bias_ref.shape[1]), F32)
    for k in range(k_local):
        green = jnp.concatenate(
            [table[w, pl.ds(first + k, 1), :] for w in range(ka_count)], axis=0
        )
        real, imag = green[:, :width], green[:, width:]
        both = jnp.concatenate([real, imag], axis=0)
        turned = jnp.concatenate([-imag, real], axis=0)
        own_ref[k] = both
        total += jnp.dot(both.astype(BF16), chol_ref[k, 0], preferred_element_type=F32)
        total += jnp.dot(turned.astype(BF16), chol_ref[k, 1], preferred_element_type=F32)
    bias_ref[:rows] = total * mask_ref[...]
    window = jnp.concatenate([orbitals_ref[k] for k in range(k_local)], axis=0)
    count, width = window.shape
    bias_ref[rows : rows + count, :width] = window
    bias_ref[rows : rows + count, width:] = jnp.zeros((count, bias_ref.shape[1] - width), F32)


def exchange_kernel(k_local, own_ref, chol_ref, mask_ref, out_ref):
    walkers, width, columns = own_ref.shape[1] // 2, own_ref.shape[2], chol_ref.shape[3]
    rows = 2 * walkers
    lane = lax.broadcasted_iota(jnp.int32, (rows, LANES), 1)
    total = jnp.zeros((rows, columns), F32)
    for k in range(k_local):
        both = jnp.concatenate([own_ref[k], jnp.zeros((rows, LANES - width), F32)], axis=1)
        turned = jnp.concatenate([-both[walkers:], both[:walkers]], axis=0)
        sides = []
        for side in (both, turned):
            rolled = {
                step: side if step == 0 else pltpu.roll(side, (step * M) % LANES, 1)
                for step in range(1 - NOCC, NOCC)
            }
            blocks = []
            for i in range(NOCC):
                inside = (lane >= i * M) & (lane < (i + 1) * M)
                for j in range(NOCC):
                    blocks.append(jnp.where(inside, rolled[i - j], 0.0))
            sides.append(jnp.concatenate(blocks, axis=0)[:, :width].astype(BF16))
        cross = jnp.dot(sides[0], chol_ref[k, 0], preferred_element_type=F32)
        cross += jnp.dot(sides[1], chol_ref[k, 1], preferred_element_type=F32)
        cross = cross * cross
        for block in range(NOCC * NOCC):
            total += cross[block * rows : (block + 1) * rows]
    total = total * mask_ref[:rows]
    total = total[:walkers] + total[walkers:]
    summed = 0.5 * jnp.sum(total, axis=1, keepdims=True)
    out_ref[...] = jnp.broadcast_to(summed, out_ref.shape)


def operator_kernel(k_local, *refs):
    *parts, fields_ref, mask_ref, exchange_ref, chol_ref, out_ref, products, turned_ref = refs
    walkers, columns = fields_ref.shape
    bias = parts[0][: 2 * walkers]
    for part in parts[1:]:
        bias = bias + part[: 2 * walkers]
    pairs = M * M
    tiles = columns // LANES
    group = LANES // (2 * tiles)
    bias_re, bias_im = bias[:walkers], bias[walkers:]
    hartree = 0.5 * jnp.sum(bias_re * bias_re + bias_im * bias_im, axis=1, keepdims=True)
    own = lax.broadcasted_iota(jnp.int32, (walkers, 1), 0) == lax.axis_index("ka")
    energy = jnp.where(own, hartree, 0.0) - exchange_ref[:, :1]
    kept = mask_ref[:walkers]
    shift_re = (fields_ref[...] - BIAS_STEP * bias_re) * kept
    shift_im = -BIAS_STEP * bias_im * kept
    span = k_local * walkers
    weights = []
    for k in range(k_local):
        before, after = k * walkers, span - (k + 1) * walkers
        pieces = []
        for tile in range(tiles):
            at = slice(tile * LANES, (tile + 1) * LANES)
            for first, second in ((shift_re, shift_im), (-shift_im, shift_re)):
                for side in (first, second):
                    pieces += [(before, None), (walkers, side[:, at]), (after, None)]
                pieces.append((group - 2 * span, None))
        weights.append(
            jnp.concatenate(
                [jnp.zeros((n, LANES), F32) if p is None else p for n, p in pieces if n], axis=0
            ).astype(BF16)
        )
    products[...] = lax.dot_general(
        jnp.concatenate([chol_ref[k] for k in range(k_local)], axis=1),
        jnp.concatenate(weights, axis=1),
        (((1,), (1,)), ((), ())),
        preferred_element_type=F32,
    )
    lane = lax.broadcasted_iota(jnp.int32, (pairs, LANES), 1)
    merged = products[pl.ds(0, pairs, stride=2 * tiles), :]
    for at in range(1, 2 * tiles):
        row = products[pl.ds(at, pairs, stride=2 * tiles), :]
        merged = jnp.where(lane >= at * group, row, merged)
    turned_ref[:pairs] = merged
    copies, rows, width = out_ref.shape
    lane = lax.broadcasted_iota(jnp.int32, (rows, LANES), 1)
    for at in range(0, width, LANES):
        block = turned_ref[at : at + LANES].T
        block = PROP_STEP * sum(block[n * group : n * group + rows] for n in range(2 * tiles))
        if at + LANES > pairs:
            share = jnp.concatenate([energy, jnp.zeros((rows - walkers, 1), F32)], axis=0)
            block = jnp.where(lane + at < pairs, block, 0.0)
            for piece in range(3):
                head = share.astype(BF16).astype(F32)
                block = jnp.where(lane + at == pairs + piece, head, block)
                share = share - head
        for copy in range(copies):
            out_ref[copy, :, at : at + LANES] = block.astype(BF16)


def taylor_kernel(pb_count, normalizer, blocks_ref, *refs):
    *windows, picks_ref, orbitals_ref, out_ref, energy_ref, turned, picked, term = refs
    pairs = M * M
    pair = NOCC * M
    k_local, walkers, _ = out_ref.shape
    span = k_local * walkers
    ka_pos = lax.axis_index("ka")
    term[...] = jnp.zeros_like(term)
    for source, window_ref in zip(origins("ka", BIAS_ROUNDS), windows):
        start = pl.multiple_of(source * (2 * span), 2 * span)
        window = window_ref[window_ref.shape[0] - span :]
        term[pl.ds(start, span), :pair] = window[:, :pair]
        term[pl.ds(start + span, span), :pair] = window[:, pair : 2 * pair]
    picked[...] = jnp.dot(term[...].T.astype(BF16), picks_ref[...], preferred_element_type=F32)
    count, rows, width = blocks_ref.shape
    for at in range(0, width, LANES):
        tile = jnp.concatenate([blocks_ref[n, :, at : at + LANES] for n in range(count)], axis=0)
        turned[at : at + LANES] = tile.T.astype(F32)
    shares = turned[pairs : pairs + 3]
    lane = lax.broadcasted_iota(jnp.int32, shares.shape, 1)
    shares = jnp.where(lax.rem(lane, 2 * span) == ka_pos, shares, 0.0)
    shares = jnp.sum(jnp.sum(shares, axis=0, keepdims=True), axis=1, keepdims=True)
    energy_ref[...] = shares / normalizer
    lane = lax.broadcasted_iota(jnp.int32, (M, LANES), 1)
    imaginary = lax.rem(lane, 2 * span) >= span
    sums = [jnp.zeros((M, LANES), F32) for _ in range(NOCC)]
    for degree in range(1, TAYLOR + 1):
        stride = M if degree == 1 else ROWS
        straight = [jnp.zeros((M, LANES), F32) for _ in range(NOCC)]
        crossed = [jnp.zeros((M, LANES), F32) for _ in range(NOCC)]
        for c in range(M):
            column = turned[pl.ds(c, M, stride=M), :]
            for i in range(NOCC):
                at = i * stride + c
                straight[i] += column * picked[at : at + 1, :LANES]
                crossed[i] += column * picked[at : at + 1, LANES:]
        for i in range(NOCC):
            other = jnp.where(
                imaginary, pltpu.roll(crossed[i], span, 1), pltpu.roll(crossed[i], LANES - span, 1)
            )
            applied = straight[i] + other
            applied = applied + pltpu.roll(applied, LANES // pb_count, 1)
            current = applied / degree
            sums[i] = sums[i] + current
            term[i * ROWS : i * ROWS + M] = current if degree < TAYLOR else sums[i]
        if degree < TAYLOR:
            picked[...] = jnp.dot(
                term[...].astype(BF16), picks_ref[...], preferred_element_type=F32
            )
    turned[:LANES] = term[...].T
    both = turned[pl.ds(pl.multiple_of(ka_pos * (2 * span), 2 * span), 2 * span), :]
    both = jnp.concatenate([both[:, i * ROWS : i * ROWS + M] for i in range(NOCC)], axis=1)
    both = jnp.concatenate([both[:span], both[span:]], axis=1)
    for k in range(k_local):
        out_ref[k] = orbitals_ref[k] + both[k * walkers : (k + 1) * walkers]


def call(kernel, out, scratch=(), scalars=0, operands=0, flops=None):
    spaces = [pltpu.SMEM] * scalars + [pltpu.VMEM] * operands
    cost = None
    if flops is not None:
        cost = pl.CostEstimate(flops=flops, bytes_accessed=0, transcendentals=0)
    return pl.pallas_call(
        kernel,
        out_shape=out,
        in_specs=[pl.BlockSpec(memory_space=space) for space in spaces],
        out_specs=jax.tree.map(lambda _: pl.BlockSpec(memory_space=pltpu.VMEM), out),
        scratch_shapes=list(scratch),
        cost_estimate=cost,
        compiler_params=pltpu.CompilerParams(vmem_limit_bytes=24 * 2**20),
    )


def direct(green, fields, orbitals, chol_half, chol_full, chol_count, kq_map):
    k_local, pair_width, chol_cols = chol_half.shape[1], chol_half.shape[3], chol_half.shape[4]
    ka_count, pb_count = lax.axis_size("ka"), lax.axis_size("pb")
    walkers = ka_count
    kpoints = green.shape[3]
    span = k_local * walkers
    shape = jax.ShapeDtypeStruct
    tiles = chol_cols // LANES
    own_green = green.reshape(kpoints, 2 * pair_width)
    greens = exchange(own_green, "ka", GREEN_ROUNDS)
    half = chol_half.reshape(k_local, 2, pair_width, chol_cols)
    full = jnp.transpose(
        chol_full.reshape(k_local, 2, M * M, tiles, LANES), (0, 2, 3, 1, 4)
    ).reshape(k_local, M * M * tiles * 2, LANES)
    own_fields = fields.reshape(walkers, chol_cols)
    own_orbitals = orbitals.reshape(k_local, walkers, 2 * pair_width)
    mask, picks = call(
        functools.partial(prepare_kernel, ka_count, pb_count, walkers),
        (shape((2 * walkers, chol_cols), F32), shape((LANES, 2 * LANES), BF16)),
        scalars=2,
        flops=10**9,
    )(kq_map, chol_count)
    bias, own = call(
        functools.partial(bias_kernel, ka_count, k_local),
        (
            shape((2 * walkers + span, chol_cols), F32),
            shape((k_local, 2 * walkers, pair_width), F32),
        ),
        [pltpu.VMEM((walkers + 1, kpoints, 2 * pair_width), F32)],
        operands=len(greens) + 3,
    )(*greens, half, own_orbitals, mask)
    parts = exchange(bias, "ka", BIAS_ROUNDS)
    shares = call(
        functools.partial(exchange_kernel, k_local),
        shape((walkers, LANES), F32),
        operands=3,
    )(own, half, mask)
    width = -(-(M * M + 3) // LANES) * LANES
    blocks = call(
        functools.partial(operator_kernel, k_local),
        shape((ka_count * pb_count, 2 * span, width), BF16),
        [pltpu.VMEM((2 * M * M * tiles, LANES), F32), pltpu.VMEM((width, LANES), F32)],
        operands=len(parts) + 4,
    )(*parts, own_fields, mask, shares, full)
    blocks = lax.all_to_all(blocks, ("pb", "ka"), 0, 0, tiled=True)
    propagated, energy = call(
        functools.partial(taylor_kernel, pb_count, float(pb_count * chol_cols)),
        (shape((k_local, walkers, 2 * pair_width), F32), shape((1, 1), F32)),
        [
            pltpu.VMEM((width, LANES), F32),
            pltpu.VMEM((NOCC * ROWS, 2 * LANES), F32),
            pltpu.VMEM((LANES, LANES), F32),
        ],
        operands=len(parts) + 3,
    )(blocks, *parts, picks, own_orbitals)
    return (propagated[None], energy)


def on_device(green, fields, orbitals, chol_half, chol_full, chol_count, kq_map):
    ka_count, pb_count = lax.axis_size("ka"), lax.axis_size("pb")
    walkers = orbitals.shape[2]
    fits = 2 * pb_count * kq_map.shape[1] * walkers == LANES
    fits = fits and chol_half.shape[1] * walkers == 8 and chol_half.shape[4] == 2 * LANES
    fits = fits and ka_count == 4
    if fits and chol_half.shape[0] == 1 and walkers == ka_count:
        return direct(green, fields, orbitals, chol_half, chol_full, chol_count, kq_map)
    return with_collectives(green, fields, orbitals, chol_half, chol_full, chol_count, kq_map)


def solution(mesh):
    placed = (
        P("wa", ("grp", "ka"), "pb", None, None),
        P("wa", "pb", "grp", None),
        P("wa", "ka", "grp", None),
        P("pb", "ka", None, None, None),
        P("pb", "ka", None, None, None),
        P(),
        P(),
    )
    return jax.shard_map(
        on_device,
        mesh=mesh,
        in_specs=placed,
        out_specs=(P("wa", "ka", "grp", None), P("wa", ("grp", "ka"))),
        check_vma=False,
    )
```

```python
import functools

import jax
import jax.numpy as jnp
from jax import lax
from jax.experimental import pallas as pl
from jax.experimental.pallas import tpu as pltpu
from jax.sharding import PartitionSpec as P

M = 26
NOCC = 4
TAYLOR = 3
LANES = 128
ROWS = 32

GREEN_ROUNDS = (
    ((3, 0), (2, 1), (1, 3), (0, 2)),
    ((3, 1), (2, 0), (0, 3), (1, 2)),
    ((1, 0), (3, 2), (2, 3), (0, 1)),
)[::-1]
BIAS_ROUNDS = (
    ((0, 3), (3, 0), (1, 2), (2, 1)),
    ((1, 0), (0, 2), (2, 3), (3, 1)),
    ((3, 2), (0, 1), (2, 0), (1, 3)),
)[::-1]


BIAS_STEP = 0.5
PROP_STEP = 0.5

F32 = jnp.float32
BF16 = jnp.bfloat16


def complex_dot(pattern, left_re, left_im, right_re, right_im):
    real_part = jnp.einsum(
        pattern, left_re, right_re, preferred_element_type=jnp.float32
    ) - jnp.einsum(pattern, left_im, right_im, preferred_element_type=jnp.float32)
    imag_part = jnp.einsum(
        pattern, left_re, right_im, preferred_element_type=jnp.float32
    ) + jnp.einsum(pattern, left_im, right_re, preferred_element_type=jnp.float32)
    return (real_part, imag_part)


def make_picker(wanted):

    def picker(shard_rows):
        row_count = shard_rows.shape[0]
        select = (wanted[:, None] == jnp.arange(row_count, dtype=jnp.int32)[None, :]).astype(
            jnp.bfloat16
        )
        return jnp.dot(select, shard_rows, preferred_element_type=jnp.float32)

    return picker


def with_collectives(green, fields, orbitals, chol_half, chol_full, chol_count, kq_map):
    q_local = chol_half.shape[0]
    k_local = chol_half.shape[1]
    pair_width = chol_half.shape[3]
    chol_cols = chol_half.shape[4]
    ka_count = lax.axis_size("ka")
    pb_count = lax.axis_size("pb")
    ka_pos = lax.axis_index("ka")
    pb_pos = lax.axis_index("pb")
    local_green = lax.all_to_all(green, "ka", split_axis=3, concat_axis=1, tiled=True)
    walkers = local_green.shape[1]
    per_device = walkers // ka_count
    greens = local_green[0].reshape(walkers, q_local, k_local, 2, pair_width)
    counts = lax.dynamic_slice_in_dim(chol_count, pb_pos * q_local, q_local)
    vec_mask = (jnp.arange(chol_cols, dtype=jnp.int32)[None, :] < counts[:, None]).astype(
        jnp.float32
    )
    bias_re, bias_im = complex_dot(
        "wqkx,qkxn->qwn",
        greens[:, :, :, 0],
        greens[:, :, :, 1],
        chol_half[:, :, 0],
        chol_half[:, :, 1],
    )
    own_rows = (jnp.arange(walkers, dtype=jnp.int32) // per_device == ka_pos).astype(jnp.float32)
    bias_re, bias_im = lax.psum((bias_re, bias_im), "ka")
    bias_re = bias_re * vec_mask[:, None, :]
    bias_im = bias_im * vec_mask[:, None, :]
    hartree = 0.5 * jnp.sum(bias_re * bias_re + bias_im * bias_im, axis=(0, 2)) * own_rows
    field_now = jnp.transpose(fields, (1, 0, 2, 3)).reshape(q_local, walkers, chol_cols)
    shift_re = ((field_now - BIAS_STEP * bias_re) * vec_mask[:, None, :]).astype(jnp.bfloat16)
    shift_im = (-BIAS_STEP * bias_im * vec_mask[:, None, :]).astype(jnp.bfloat16)
    exchange = jnp.zeros((walkers,), jnp.float32)
    for transfer in range(q_local):
        for kpoint in range(k_local):
            chol_row = chol_half[transfer, kpoint].reshape(2, NOCC, M, chol_cols)
            green_row = greens[:, transfer, kpoint].reshape(walkers, 2, NOCC, M)
            cross_re, cross_im = complex_dot(
                "ipn,wjp->wijn", chol_row[0], chol_row[1], green_row[:, 0], green_row[:, 1]
            )
            exchange = exchange + 0.5 * jnp.sum(
                (cross_re * cross_re + cross_im * cross_im) * vec_mask[transfer], axis=(1, 2, 3)
            )
    prop_re, prop_im = complex_dot(
        "qwn,qkyn->qwky", shift_re, shift_im, chol_full[:, :, 0], chol_full[:, :, 1]
    )
    shape = (q_local, walkers, k_local, M, M)
    oper_re = (PROP_STEP * prop_re).astype(jnp.bfloat16).reshape(shape)
    oper_im = (PROP_STEP * prop_im).astype(jnp.bfloat16).reshape(shape)
    normalizer = q_local * pb_count * chol_cols
    total_energy = lax.psum(hartree - exchange, ("ka", "pb")) / normalizer
    energy = lax.dynamic_slice_in_dim(total_energy, ka_pos * per_device, per_device).reshape(
        1, per_device
    )
    initial = orbitals[0].reshape(k_local, walkers, 2, NOCC, M)
    row_width = 2 * pair_width
    my_rows = lax.dynamic_slice_in_dim(kq_map, pb_pos * q_local, q_local, 0)
    wanted = lax.dynamic_slice_in_dim(my_rows, ka_pos * k_local, k_local, 1).reshape(
        q_local * k_local
    )
    picker = make_picker(wanted)
    current = initial
    summed_terms = initial
    for degree in range(1, TAYLOR + 1):
        rounded = current.astype(jnp.bfloat16).reshape(k_local, walkers * row_width)
        fetched = picker(lax.all_gather(rounded, "ka", axis=0, tiled=True))
        shifted_rows = fetched.astype(jnp.bfloat16).reshape(q_local, k_local, walkers, 2, NOCC, M)
        out_re, out_im = complex_dot(
            "xwkpq,xkwiq->kwip",
            oper_re,
            oper_im,
            shifted_rows[:, :, :, 0],
            shifted_rows[:, :, :, 1],
        )
        applied = jnp.stack([out_re, out_im], axis=2)
        applied = lax.psum(applied, "pb")
        current = applied / degree
        summed_terms = summed_terms + current
    propagated = summed_terms.reshape(1, k_local, walkers, row_width)
    return (propagated, energy)


def exchange(array, axis, rounds):
    return [array] + [lax.ppermute(array, axis, pairs) for pairs in rounds]


def origins(axis, rounds):
    at = lax.axis_index(axis)
    found = [at]
    for pairs in rounds:
        source = jnp.int32(0)
        for sender, receiver in pairs:
            source = jnp.where(at == receiver, sender, source)
        found.append(source)
    return found


def prepare_kernel(ka_count, pb_count, walkers, map_ref, count_ref, mask_ref, picks_ref):
    kept = count_ref[lax.axis_index("pb")]
    column = lax.broadcasted_iota(jnp.int32, mask_ref.shape, 1)
    mask_ref[...] = jnp.where(column < kept, 1.0, 0.0)
    kpoints = map_ref.shape[1]
    k_local = kpoints // ka_count
    span = k_local * walkers
    lane = lax.broadcasted_iota(jnp.int32, (1, LANES), 1)
    lane_q = lane // (LANES // pb_count)
    lane_ka = lax.rem(lane, LANES // pb_count) // (2 * span)
    lane_part = lax.rem(lane, 2 * span) // span
    lane_k = lane_ka * k_local + lax.rem(lane, span) // walkers
    wanted = jnp.zeros((1, LANES), jnp.int32)
    for q in range(pb_count):
        for k in range(kpoints):
            source = map_ref[q, k]
            source = source // k_local * (2 * span) + lax.rem(source, k_local) * walkers
            wanted = jnp.where((lane_q == q) & (lane_k == k), source, wanted)
    wanted = wanted + lax.rem(lane, walkers)
    row = lax.broadcasted_iota(jnp.int32, (LANES, LANES), 0)
    real = jnp.where(row == wanted, 1.0, 0.0)
    imag = jnp.where(row == wanted + span, jnp.where(lane_part == 0, 1.0, -1.0), 0.0)
    picks_ref[...] = jnp.concatenate([real, imag], axis=1).astype(BF16)


def bias_kernel(ka_count, k_local, *refs):
    *greens, chol_ref, orbitals_ref, mask_ref, bias_ref, own_ref, table = refs
    for source, green_ref in zip(origins("ka", GREEN_ROUNDS), greens):
        table[source] = green_ref[...].astype(F32)
    first = lax.axis_index("ka") * k_local
    width = chol_ref.shape[2]
    rows = 2 * ka_count
    total = jnp.zeros((rows, bias_ref.shape[1]), F32)
    for k in range(k_local):
        green = jnp.concatenate(
            [table[w, pl.ds(first + k, 1), :] for w in range(ka_count)], axis=0
        )
        real, imag = green[:, :width], green[:, width:]
        both = jnp.concatenate([real, imag], axis=0)
        turned = jnp.concatenate([-imag, real], axis=0)
        own_ref[k] = both
        total += jnp.dot(both.astype(BF16), chol_ref[k, 0], preferred_element_type=F32)
        total += jnp.dot(turned.astype(BF16), chol_ref[k, 1], preferred_element_type=F32)
    bias_ref[:rows] = total * mask_ref[...]
    window = jnp.concatenate([orbitals_ref[k] for k in range(k_local)], axis=0)
    count, width = window.shape
    bias_ref[rows : rows + count, :width] = window
    bias_ref[rows : rows + count, width:] = jnp.zeros((count, bias_ref.shape[1] - width), F32)


def exchange_kernel(k_local, own_ref, chol_ref, mask_ref, out_ref):
    walkers, width, columns = own_ref.shape[1] // 2, own_ref.shape[2], chol_ref.shape[3]
    rows = 2 * walkers
    lane = lax.broadcasted_iota(jnp.int32, (rows, LANES), 1)
    total = jnp.zeros((rows, columns), F32)
    for k in range(k_local):
        both = jnp.concatenate([own_ref[k], jnp.zeros((rows, LANES - width), F32)], axis=1)
        turned = jnp.concatenate([-both[walkers:], both[:walkers]], axis=0)
        sides = []
        for side in (both, turned):
            rolled = {
                step: side if step == 0 else pltpu.roll(side, (step * M) % LANES, 1)
                for step in range(1 - NOCC, NOCC)
            }
            blocks = []
            for i in range(NOCC):
                inside = (lane >= i * M) & (lane < (i + 1) * M)
                for j in range(NOCC):
                    blocks.append(jnp.where(inside, rolled[i - j], 0.0))
            sides.append(jnp.concatenate(blocks, axis=0)[:, :width].astype(BF16))
        cross = jnp.dot(sides[0], chol_ref[k, 0], preferred_element_type=F32)
        cross += jnp.dot(sides[1], chol_ref[k, 1], preferred_element_type=F32)
        cross = cross * cross
        for block in range(NOCC * NOCC):
            total += cross[block * rows : (block + 1) * rows]
    total = total * mask_ref[:rows]
    total = total[:walkers] + total[walkers:]
    summed = 0.5 * jnp.sum(total, axis=1, keepdims=True)
    out_ref[...] = jnp.broadcast_to(summed, out_ref.shape)


def operator_kernel(k_local, *refs):
    *parts, fields_ref, mask_ref, exchange_ref, chol_ref, out_ref, products, turned_ref = refs
    walkers, columns = fields_ref.shape
    bias = parts[0][: 2 * walkers]
    for part in parts[1:]:
        bias = bias + part[: 2 * walkers]
    pairs = M * M
    tiles = columns // LANES
    group = LANES // (2 * tiles)
    bias_re, bias_im = bias[:walkers], bias[walkers:]
    hartree = 0.5 * jnp.sum(bias_re * bias_re + bias_im * bias_im, axis=1, keepdims=True)
    own = lax.broadcasted_iota(jnp.int32, (walkers, 1), 0) == lax.axis_index("ka")
    energy = jnp.where(own, hartree, 0.0) - exchange_ref[:, :1]
    kept = mask_ref[:walkers]
    shift_re = (fields_ref[...] - BIAS_STEP * bias_re) * kept
    shift_im = -BIAS_STEP * bias_im * kept
    span = k_local * walkers
    weights = []
    for k in range(k_local):
        before, after = k * walkers, span - (k + 1) * walkers
        pieces = []
        for tile in range(tiles):
            at = slice(tile * LANES, (tile + 1) * LANES)
            for first, second in ((shift_re, shift_im), (-shift_im, shift_re)):
                for side in (first, second):
                    pieces += [(before, None), (walkers, side[:, at]), (after, None)]
                pieces.append((group - 2 * span, None))
        weights.append(
            jnp.concatenate(
                [jnp.zeros((n, LANES), F32) if p is None else p for n, p in pieces if n], axis=0
            ).astype(BF16)
        )
    products[...] = lax.dot_general(
        jnp.concatenate([chol_ref[k] for k in range(k_local)], axis=1),
        jnp.concatenate(weights, axis=1),
        (((1,), (1,)), ((), ())),
        preferred_element_type=F32,
    )
    lane = lax.broadcasted_iota(jnp.int32, (pairs, LANES), 1)
    merged = products[pl.ds(0, pairs, stride=2 * tiles), :]
    for at in range(1, 2 * tiles):
        row = products[pl.ds(at, pairs, stride=2 * tiles), :]
        merged = jnp.where(lane >= at * group, row, merged)
    turned_ref[:pairs] = merged
    copies, rows, width = out_ref.shape
    lane = lax.broadcasted_iota(jnp.int32, (rows, LANES), 1)
    for at in range(0, width, LANES):
        block = turned_ref[at : at + LANES].T
        block = PROP_STEP * sum(block[n * group : n * group + rows] for n in range(2 * tiles))
        if at + LANES > pairs:
            share = jnp.concatenate([energy, jnp.zeros((rows - walkers, 1), F32)], axis=0)
            block = jnp.where(lane + at < pairs, block, 0.0)
            for piece in range(3):
                head = share.astype(BF16).astype(F32)
                block = jnp.where(lane + at == pairs + piece, head, block)
                share = share - head
        for copy in range(copies):
            out_ref[copy, :, at : at + LANES] = block.astype(BF16)


def taylor_kernel(pb_count, normalizer, blocks_ref, *refs):
    *windows, picks_ref, orbitals_ref, out_ref, energy_ref, turned, picked, term = refs
    pairs = M * M
    pair = NOCC * M
    k_local, walkers, _ = out_ref.shape
    span = k_local * walkers
    ka_pos = lax.axis_index("ka")
    term[...] = jnp.zeros_like(term)
    for source, window_ref in zip(origins("ka", BIAS_ROUNDS), windows):
        start = pl.multiple_of(source * (2 * span), 2 * span)
        window = window_ref[window_ref.shape[0] - span :]
        term[pl.ds(start, span), :pair] = window[:, :pair]
        term[pl.ds(start + span, span), :pair] = window[:, pair : 2 * pair]
    picked[...] = jnp.dot(term[...].T.astype(BF16), picks_ref[...], preferred_element_type=F32)
    count, rows, width = blocks_ref.shape
    for at in range(0, width, LANES):
        tile = jnp.concatenate([blocks_ref[n, :, at : at + LANES] for n in range(count)], axis=0)
        turned[at : at + LANES] = tile.T.astype(F32)
    shares = turned[pairs : pairs + 3]
    lane = lax.broadcasted_iota(jnp.int32, shares.shape, 1)
    shares = jnp.where(lax.rem(lane, 2 * span) == ka_pos, shares, 0.0)
    shares = jnp.sum(jnp.sum(shares, axis=0, keepdims=True), axis=1, keepdims=True)
    energy_ref[...] = shares / normalizer
    lane = lax.broadcasted_iota(jnp.int32, (M, LANES), 1)
    imaginary = lax.rem(lane, 2 * span) >= span
    sums = [jnp.zeros((M, LANES), F32) for _ in range(NOCC)]
    for degree in range(1, TAYLOR + 1):
        stride = M if degree == 1 else ROWS
        straight = [jnp.zeros((M, LANES), F32) for _ in range(NOCC)]
        crossed = [jnp.zeros((M, LANES), F32) for _ in range(NOCC)]
        for c in range(M):
            column = turned[pl.ds(c, M, stride=M), :]
            for i in range(NOCC):
                at = i * stride + c
                straight[i] += column * picked[at : at + 1, :LANES]
                crossed[i] += column * picked[at : at + 1, LANES:]
        for i in range(NOCC):
            other = jnp.where(
                imaginary, pltpu.roll(crossed[i], span, 1), pltpu.roll(crossed[i], LANES - span, 1)
            )
            applied = straight[i] + other
            applied = applied + pltpu.roll(applied, LANES // pb_count, 1)
            current = applied / degree
            sums[i] = sums[i] + current
            term[i * ROWS : i * ROWS + M] = current if degree < TAYLOR else sums[i]
        if degree < TAYLOR:
            picked[...] = jnp.dot(
                term[...].astype(BF16), picks_ref[...], preferred_element_type=F32
            )
    turned[:LANES] = term[...].T
    both = turned[pl.ds(pl.multiple_of(ka_pos * (2 * span), 2 * span), 2 * span), :]
    both = jnp.concatenate([both[:, i * ROWS : i * ROWS + M] for i in range(NOCC)], axis=1)
    both = jnp.concatenate([both[:span], both[span:]], axis=1)
    for k in range(k_local):
        out_ref[k] = orbitals_ref[k] + both[k * walkers : (k + 1) * walkers]


def call(kernel, out, scratch=(), scalars=0, operands=0, flops=None):
    spaces = [pltpu.SMEM] * scalars + [pltpu.VMEM] * operands
    cost = None
    if flops is not None:
        cost = pl.CostEstimate(flops=flops, bytes_accessed=0, transcendentals=0)
    return pl.pallas_call(
        kernel,
        out_shape=out,
        in_specs=[pl.BlockSpec(memory_space=space) for space in spaces],
        out_specs=jax.tree.map(lambda _: pl.BlockSpec(memory_space=pltpu.VMEM), out),
        scratch_shapes=list(scratch),
        cost_estimate=cost,
        compiler_params=pltpu.CompilerParams(vmem_limit_bytes=24 * 2**20),
    )


def direct(green, fields, orbitals, chol_half, chol_full, chol_count, kq_map):
    k_local, pair_width, chol_cols = chol_half.shape[1], chol_half.shape[3], chol_half.shape[4]
    ka_count, pb_count = lax.axis_size("ka"), lax.axis_size("pb")
    walkers = ka_count
    kpoints = green.shape[3]
    span = k_local * walkers
    shape = jax.ShapeDtypeStruct
    tiles = chol_cols // LANES
    own_green = green.reshape(kpoints, 2 * pair_width)
    greens = exchange(own_green, "ka", GREEN_ROUNDS)
    half = chol_half.reshape(k_local, 2, pair_width, chol_cols)
    full = jnp.transpose(
        chol_full.reshape(k_local, 2, M * M, tiles, LANES), (0, 2, 3, 1, 4)
    ).reshape(k_local, M * M * tiles * 2, LANES)
    own_fields = fields.reshape(walkers, chol_cols)
    own_orbitals = orbitals.reshape(k_local, walkers, 2 * pair_width)
    mask, picks = call(
        functools.partial(prepare_kernel, ka_count, pb_count, walkers),
        (shape((2 * walkers, chol_cols), F32), shape((LANES, 2 * LANES), BF16)),
        scalars=2,
        flops=10**9,
    )(kq_map, chol_count)
    bias, own = call(
        functools.partial(bias_kernel, ka_count, k_local),
        (
            shape((2 * walkers + span, chol_cols), F32),
            shape((k_local, 2 * walkers, pair_width), F32),
        ),
        [pltpu.VMEM((walkers, kpoints, 2 * pair_width), F32)],
        operands=len(greens) + 3,
    )(*greens, half, own_orbitals, mask)
    parts = exchange(bias, "ka", BIAS_ROUNDS)
    shares = call(
        functools.partial(exchange_kernel, k_local),
        shape((walkers, LANES), F32),
        operands=3,
    )(own, half, mask)
    width = -(-(M * M + 3) // LANES) * LANES
    blocks = call(
        functools.partial(operator_kernel, k_local),
        shape((ka_count * pb_count, 2 * span, width), BF16),
        [pltpu.VMEM((2 * M * M * tiles, LANES), F32), pltpu.VMEM((width, LANES), F32)],
        operands=len(parts) + 4,
    )(*parts, own_fields, mask, shares, full)
    blocks = lax.all_to_all(blocks, ("pb", "ka"), 0, 0, tiled=True)
    propagated, energy = call(
        functools.partial(taylor_kernel, pb_count, float(pb_count * chol_cols)),
        (shape((k_local, walkers, 2 * pair_width), F32), shape((1, 1), F32)),
        [
            pltpu.VMEM((width, LANES), F32),
            pltpu.VMEM((NOCC * ROWS, 2 * LANES), F32),
            pltpu.VMEM((LANES, LANES), F32),
        ],
        operands=len(parts) + 3,
    )(blocks, *parts, picks, own_orbitals)
    return (propagated[None], energy)


def on_device(green, fields, orbitals, chol_half, chol_full, chol_count, kq_map):
    ka_count, pb_count = lax.axis_size("ka"), lax.axis_size("pb")
    walkers = orbitals.shape[2]
    fits = 2 * pb_count * kq_map.shape[1] * walkers == LANES
    fits = fits and chol_half.shape[1] * walkers == 8 and chol_half.shape[4] == 2 * LANES
    fits = fits and ka_count == 4
    if fits and chol_half.shape[0] == 1 and walkers == ka_count:
        return direct(green, fields, orbitals, chol_half, chol_full, chol_count, kq_map)
    return with_collectives(green, fields, orbitals, chol_half, chol_full, chol_count, kq_map)


def solution(mesh):
    placed = (
        P("wa", ("grp", "ka"), "pb", None, None),
        P("wa", "pb", "grp", None),
        P("wa", "ka", "grp", None),
        P("pb", "ka", None, None, None),
        P("pb", "ka", None, None, None),
        P(),
        P(),
    )
    return jax.shard_map(
        on_device,
        mesh=mesh,
        in_specs=placed,
        out_specs=(P("wa", "ka", "grp", None), P("wa", ("grp", "ka"))),
        check_vma=False,
    )
```

```python
import functools

import jax
import jax.numpy as jnp
from jax import lax
from jax.experimental import pallas as pl
from jax.experimental.pallas import tpu as pltpu
from jax.sharding import PartitionSpec as P

M = 26
NOCC = 4
TAYLOR = 3
LANES = 128
ROWS = 32

GREEN_ROUNDS = (
    ((3, 0), (2, 1), (1, 3), (0, 2)),
    ((3, 1), (2, 0), (0, 3), (1, 2)),
    ((1, 0), (3, 2), (2, 3), (0, 1)),
)[::-1]
BIAS_ROUNDS = (
    ((0, 3), (3, 0), (1, 2), (2, 1)),
    ((1, 0), (0, 2), (2, 3), (3, 1)),
    ((3, 2), (0, 1), (2, 0), (1, 3)),
)[::-1]


BIAS_STEP = 0.5
PROP_STEP = 0.5

F32 = jnp.float32
BF16 = jnp.bfloat16


def complex_dot(pattern, left_re, left_im, right_re, right_im):
    real_part = jnp.einsum(
        pattern, left_re, right_re, preferred_element_type=jnp.float32
    ) - jnp.einsum(pattern, left_im, right_im, preferred_element_type=jnp.float32)
    imag_part = jnp.einsum(
        pattern, left_re, right_im, preferred_element_type=jnp.float32
    ) + jnp.einsum(pattern, left_im, right_re, preferred_element_type=jnp.float32)
    return (real_part, imag_part)


def make_picker(wanted):

    def picker(shard_rows):
        row_count = shard_rows.shape[0]
        select = (wanted[:, None] == jnp.arange(row_count, dtype=jnp.int32)[None, :]).astype(
            jnp.bfloat16
        )
        return jnp.dot(select, shard_rows, preferred_element_type=jnp.float32)

    return picker


def with_collectives(green, fields, orbitals, chol_half, chol_full, chol_count, kq_map):
    q_local = chol_half.shape[0]
    k_local = chol_half.shape[1]
    pair_width = chol_half.shape[3]
    chol_cols = chol_half.shape[4]
    ka_count = lax.axis_size("ka")
    pb_count = lax.axis_size("pb")
    ka_pos = lax.axis_index("ka")
    pb_pos = lax.axis_index("pb")
    local_green = lax.all_to_all(green, "ka", split_axis=3, concat_axis=1, tiled=True)
    walkers = local_green.shape[1]
    per_device = walkers // ka_count
    greens = local_green[0].reshape(walkers, q_local, k_local, 2, pair_width)
    counts = lax.dynamic_slice_in_dim(chol_count, pb_pos * q_local, q_local)
    vec_mask = (jnp.arange(chol_cols, dtype=jnp.int32)[None, :] < counts[:, None]).astype(
        jnp.float32
    )
    bias_re, bias_im = complex_dot(
        "wqkx,qkxn->qwn",
        greens[:, :, :, 0],
        greens[:, :, :, 1],
        chol_half[:, :, 0],
        chol_half[:, :, 1],
    )
    own_rows = (jnp.arange(walkers, dtype=jnp.int32) // per_device == ka_pos).astype(jnp.float32)
    bias_re, bias_im = lax.psum((bias_re, bias_im), "ka")
    bias_re = bias_re * vec_mask[:, None, :]
    bias_im = bias_im * vec_mask[:, None, :]
    hartree = 0.5 * jnp.sum(bias_re * bias_re + bias_im * bias_im, axis=(0, 2)) * own_rows
    field_now = jnp.transpose(fields, (1, 0, 2, 3)).reshape(q_local, walkers, chol_cols)
    shift_re = ((field_now - BIAS_STEP * bias_re) * vec_mask[:, None, :]).astype(jnp.bfloat16)
    shift_im = (-BIAS_STEP * bias_im * vec_mask[:, None, :]).astype(jnp.bfloat16)
    exchange = jnp.zeros((walkers,), jnp.float32)
    for transfer in range(q_local):
        for kpoint in range(k_local):
            chol_row = chol_half[transfer, kpoint].reshape(2, NOCC, M, chol_cols)
            green_row = greens[:, transfer, kpoint].reshape(walkers, 2, NOCC, M)
            cross_re, cross_im = complex_dot(
                "ipn,wjp->wijn", chol_row[0], chol_row[1], green_row[:, 0], green_row[:, 1]
            )
            exchange = exchange + 0.5 * jnp.sum(
                (cross_re * cross_re + cross_im * cross_im) * vec_mask[transfer], axis=(1, 2, 3)
            )
    prop_re, prop_im = complex_dot(
        "qwn,qkyn->qwky", shift_re, shift_im, chol_full[:, :, 0], chol_full[:, :, 1]
    )
    shape = (q_local, walkers, k_local, M, M)
    oper_re = (PROP_STEP * prop_re).astype(jnp.bfloat16).reshape(shape)
    oper_im = (PROP_STEP * prop_im).astype(jnp.bfloat16).reshape(shape)
    normalizer = q_local * pb_count * chol_cols
    total_energy = lax.psum(hartree - exchange, ("ka", "pb")) / normalizer
    energy = lax.dynamic_slice_in_dim(total_energy, ka_pos * per_device, per_device).reshape(
        1, per_device
    )
    initial = orbitals[0].reshape(k_local, walkers, 2, NOCC, M)
    row_width = 2 * pair_width
    my_rows = lax.dynamic_slice_in_dim(kq_map, pb_pos * q_local, q_local, 0)
    wanted = lax.dynamic_slice_in_dim(my_rows, ka_pos * k_local, k_local, 1).reshape(
        q_local * k_local
    )
    picker = make_picker(wanted)
    current = initial
    summed_terms = initial
    for degree in range(1, TAYLOR + 1):
        rounded = current.astype(jnp.bfloat16).reshape(k_local, walkers * row_width)
        fetched = picker(lax.all_gather(rounded, "ka", axis=0, tiled=True))
        shifted_rows = fetched.astype(jnp.bfloat16).reshape(q_local, k_local, walkers, 2, NOCC, M)
        out_re, out_im = complex_dot(
            "xwkpq,xkwiq->kwip",
            oper_re,
            oper_im,
            shifted_rows[:, :, :, 0],
            shifted_rows[:, :, :, 1],
        )
        applied = jnp.stack([out_re, out_im], axis=2)
        applied = lax.psum(applied, "pb")
        current = applied / degree
        summed_terms = summed_terms + current
    propagated = summed_terms.reshape(1, k_local, walkers, row_width)
    return (propagated, energy)


def exchange(array, axis, rounds):
    return [array] + [lax.ppermute(array, axis, pairs) for pairs in rounds]


def origins(axis, rounds):
    at = lax.axis_index(axis)
    found = [at]
    for pairs in rounds:
        source = jnp.int32(0)
        for sender, receiver in pairs:
            source = jnp.where(at == receiver, sender, source)
        found.append(source)
    return found


def prepare_kernel(ka_count, pb_count, walkers, map_ref, count_ref, mask_ref, picks_ref):
    kept = count_ref[lax.axis_index("pb")]
    column = lax.broadcasted_iota(jnp.int32, mask_ref.shape, 1)
    mask_ref[...] = jnp.where(column < kept, 1.0, 0.0)
    kpoints = map_ref.shape[1]
    k_local = kpoints // ka_count
    span = k_local * walkers
    lane = lax.broadcasted_iota(jnp.int32, (1, LANES), 1)
    lane_q = lane // (LANES // pb_count)
    lane_ka = lax.rem(lane, LANES // pb_count) // (2 * span)
    lane_part = lax.rem(lane, 2 * span) // span
    lane_k = lane_ka * k_local + lax.rem(lane, span) // walkers
    wanted = jnp.zeros((1, LANES), jnp.int32)
    for q in range(pb_count):
        for k in range(kpoints):
            source = map_ref[q, k]
            source = source // k_local * (2 * span) + lax.rem(source, k_local) * walkers
            wanted = jnp.where((lane_q == q) & (lane_k == k), source, wanted)
    wanted = wanted + lax.rem(lane, walkers)
    row = lax.broadcasted_iota(jnp.int32, (LANES, LANES), 0)
    real = jnp.where(row == wanted, 1.0, 0.0)
    imag = jnp.where(row == wanted + span, jnp.where(lane_part == 0, 1.0, -1.0), 0.0)
    picks_ref[...] = jnp.concatenate([real, imag], axis=1).astype(BF16)


def bias_kernel(ka_count, k_local, *refs):
    *greens, chol_ref, orbitals_ref, mask_ref, bias_ref, own_ref, table = refs
    for source, green_ref in zip(origins("ka", GREEN_ROUNDS), greens):
        table[source] = green_ref[...].astype(F32)
    first = lax.axis_index("ka") * k_local
    width = chol_ref.shape[2]
    rows = 2 * ka_count
    total = jnp.zeros((rows, bias_ref.shape[1]), F32)
    for k in range(k_local):
        green = jnp.concatenate(
            [table[w, pl.ds(first + k, 1), :] for w in range(ka_count)], axis=0
        )
        real, imag = green[:, :width], green[:, width:]
        both = jnp.concatenate([real, imag], axis=0)
        turned = jnp.concatenate([-imag, real], axis=0)
        own_ref[k] = both
        total += jnp.dot(both.astype(BF16), chol_ref[k, 0], preferred_element_type=F32)
        total += jnp.dot(turned.astype(BF16), chol_ref[k, 1], preferred_element_type=F32)
    bias_ref[:rows] = total * mask_ref[...]
    window = jnp.concatenate([orbitals_ref[k] for k in range(k_local)], axis=0)
    count, width = window.shape
    bias_ref[rows : rows + count, :width] = window
    bias_ref[rows : rows + count, width:] = jnp.zeros((count, bias_ref.shape[1] - width), F32)


def exchange_kernel(k_local, own_ref, chol_ref, mask_ref, out_ref):
    walkers, width, columns = own_ref.shape[1] // 2, own_ref.shape[2], chol_ref.shape[3]
    rows = 2 * walkers
    lane = lax.broadcasted_iota(jnp.int32, (rows, LANES), 1)
    total = jnp.zeros((rows, columns), F32)
    for k in range(k_local):
        both = jnp.concatenate([own_ref[k], jnp.zeros((rows, LANES - width), F32)], axis=1)
        turned = jnp.concatenate([-both[walkers:], both[:walkers]], axis=0)
        sides = []
        for side in (both, turned):
            rolled = {
                step: side if step == 0 else pltpu.roll(side, (step * M) % LANES, 1)
                for step in range(1 - NOCC, NOCC)
            }
            blocks = []
            for i in range(NOCC):
                inside = (lane >= i * M) & (lane < (i + 1) * M)
                for j in range(NOCC):
                    blocks.append(jnp.where(inside, rolled[i - j], 0.0))
            sides.append(jnp.concatenate(blocks, axis=0)[:, :width].astype(BF16))
        cross = jnp.dot(sides[0], chol_ref[k, 0], preferred_element_type=F32)
        cross += jnp.dot(sides[1], chol_ref[k, 1], preferred_element_type=F32)
        cross = cross * cross
        for block in range(NOCC * NOCC):
            total += cross[block * rows : (block + 1) * rows]
    total = total * mask_ref[:rows]
    total = total[:walkers] + total[walkers:]
    summed = 0.5 * jnp.sum(total, axis=1, keepdims=True)
    out_ref[...] = jnp.broadcast_to(summed, out_ref.shape)


def operator_kernel(k_local, *refs):
    *parts, fields_ref, mask_ref, exchange_ref, chol_ref, out_ref, products, turned_ref = refs
    walkers, columns = fields_ref.shape
    bias = parts[0][: 2 * walkers]
    for part in parts[1:]:
        bias = bias + part[: 2 * walkers]
    pairs = M * M
    tiles = columns // LANES
    group = LANES // (2 * tiles)
    bias_re, bias_im = bias[:walkers], bias[walkers:]
    hartree = 0.5 * jnp.sum(bias_re * bias_re + bias_im * bias_im, axis=1, keepdims=True)
    own = lax.broadcasted_iota(jnp.int32, (walkers, 1), 0) == lax.axis_index("ka")
    energy = jnp.where(own, hartree, 0.0) - exchange_ref[:, :1]
    kept = mask_ref[:walkers]
    shift_re = (fields_ref[...] - BIAS_STEP * bias_re) * kept
    shift_im = -BIAS_STEP * bias_im * kept
    span = k_local * walkers
    weights = []
    for k in range(k_local):
        before, after = k * walkers, span - (k + 1) * walkers
        pieces = []
        for tile in range(tiles):
            at = slice(tile * LANES, (tile + 1) * LANES)
            for first, second in ((shift_re, shift_im), (-shift_im, shift_re)):
                for side in (first, second):
                    pieces += [(before, None), (walkers, side[:, at]), (after, None)]
                pieces.append((group - 2 * span, None))
        weights.append(
            jnp.concatenate(
                [jnp.zeros((n, LANES), F32) if p is None else p for n, p in pieces if n], axis=0
            ).astype(BF16)
        )
    products[...] = lax.dot_general(
        jnp.concatenate([chol_ref[k] for k in range(k_local)], axis=1),
        jnp.concatenate(weights, axis=1),
        (((1,), (1,)), ((), ())),
        preferred_element_type=F32,
    )
    lane = lax.broadcasted_iota(jnp.int32, (pairs, LANES), 1)
    merged = products[pl.ds(0, pairs, stride=2 * tiles), :]
    for at in range(1, 2 * tiles):
        row = products[pl.ds(at, pairs, stride=2 * tiles), :]
        merged = jnp.where(lane >= at * group, row, merged)
    turned_ref[:pairs] = merged
    copies, rows, width = out_ref.shape
    lane = lax.broadcasted_iota(jnp.int32, (rows, LANES), 1)
    for at in range(0, width, LANES):
        block = turned_ref[at : at + LANES].T
        block = PROP_STEP * sum(block[n * group : n * group + rows] for n in range(2 * tiles))
        if at + LANES > pairs:
            share = jnp.concatenate([energy, jnp.zeros((rows - walkers, 1), F32)], axis=0)
            block = jnp.where(lane + at < pairs, block, 0.0)
            for piece in range(3):
                head = share.astype(BF16).astype(F32)
                block = jnp.where(lane + at == pairs + piece, head, block)
                share = share - head
        for copy in range(copies):
            out_ref[copy, :, at : at + LANES] = block.astype(BF16)


def taylor_kernel(pb_count, normalizer, blocks_ref, *refs):
    *windows, picks_ref, orbitals_ref, out_ref, energy_ref, turned, picked, term = refs
    pairs = M * M
    pair = NOCC * M
    k_local, walkers, _ = out_ref.shape
    span = k_local * walkers
    ka_pos = lax.axis_index("ka")
    term[...] = jnp.zeros_like(term)
    for source, window_ref in zip(origins("ka", BIAS_ROUNDS), windows):
        start = pl.multiple_of(source * (2 * span), 2 * span)
        window = window_ref[window_ref.shape[0] - span :]
        term[pl.ds(start, span), :pair] = window[:, :pair]
        term[pl.ds(start + span, span), :pair] = window[:, pair : 2 * pair]
    picked[...] = jnp.dot(term[...].T.astype(BF16), picks_ref[...], preferred_element_type=F32)
    count, rows, width = blocks_ref.shape
    for at in range(0, width, LANES):
        tile = jnp.concatenate([blocks_ref[n, :, at : at + LANES] for n in reversed(range(count))], axis=0)
        turned[at : at + LANES] = tile.T.astype(F32)
    shares = turned[pairs : pairs + 3]
    lane = lax.broadcasted_iota(jnp.int32, shares.shape, 1)
    shares = jnp.where(lax.rem(lane, 2 * span) == ka_pos, shares, 0.0)
    shares = jnp.sum(jnp.sum(shares, axis=0, keepdims=True), axis=1, keepdims=True)
    energy_ref[...] = shares / normalizer
    lane = lax.broadcasted_iota(jnp.int32, (M, LANES), 1)
    imaginary = lax.rem(lane, 2 * span) >= span
    sums = [jnp.zeros((M, LANES), F32) for _ in range(NOCC)]
    for degree in range(1, TAYLOR + 1):
        stride = M if degree == 1 else ROWS
        straight = [jnp.zeros((M, LANES), F32) for _ in range(NOCC)]
        crossed = [jnp.zeros((M, LANES), F32) for _ in range(NOCC)]
        for c in range(M):
            column = turned[pl.ds(c, M, stride=M), :]
            for i in range(NOCC):
                at = i * stride + c
                straight[i] += column * picked[at : at + 1, :LANES]
                crossed[i] += column * picked[at : at + 1, LANES:]
        for i in range(NOCC):
            other = jnp.where(
                imaginary, pltpu.roll(crossed[i], span, 1), pltpu.roll(crossed[i], LANES - span, 1)
            )
            applied = straight[i] + other
            applied = applied + pltpu.roll(applied, LANES // pb_count, 1)
            current = applied / degree
            sums[i] = sums[i] + current
            term[i * ROWS : i * ROWS + M] = current if degree < TAYLOR else sums[i]
        if degree < TAYLOR:
            picked[...] = jnp.dot(
                term[...].astype(BF16), picks_ref[...], preferred_element_type=F32
            )
    turned[:LANES] = term[...].T
    both = turned[pl.ds(pl.multiple_of(ka_pos * (2 * span), 2 * span), 2 * span), :]
    both = jnp.concatenate([both[:, i * ROWS : i * ROWS + M] for i in range(NOCC)], axis=1)
    both = jnp.concatenate([both[:span], both[span:]], axis=1)
    for k in range(k_local):
        out_ref[k] = orbitals_ref[k] + both[k * walkers : (k + 1) * walkers]


def call(kernel, out, scratch=(), scalars=0, operands=0, flops=None):
    spaces = [pltpu.SMEM] * scalars + [pltpu.VMEM] * operands
    cost = None
    if flops is not None:
        cost = pl.CostEstimate(flops=flops, bytes_accessed=0, transcendentals=0)
    return pl.pallas_call(
        kernel,
        out_shape=out,
        in_specs=[pl.BlockSpec(memory_space=space) for space in spaces],
        out_specs=jax.tree.map(lambda _: pl.BlockSpec(memory_space=pltpu.VMEM), out),
        scratch_shapes=list(scratch),
        cost_estimate=cost,
        compiler_params=pltpu.CompilerParams(vmem_limit_bytes=24 * 2**20),
    )


def direct(green, fields, orbitals, chol_half, chol_full, chol_count, kq_map):
    k_local, pair_width, chol_cols = chol_half.shape[1], chol_half.shape[3], chol_half.shape[4]
    ka_count, pb_count = lax.axis_size("ka"), lax.axis_size("pb")
    walkers = ka_count
    kpoints = green.shape[3]
    span = k_local * walkers
    shape = jax.ShapeDtypeStruct
    tiles = chol_cols // LANES
    own_green = green.reshape(kpoints, 2 * pair_width)
    greens = exchange(own_green, "ka", GREEN_ROUNDS)
    half = chol_half.reshape(k_local, 2, pair_width, chol_cols)
    full = jnp.transpose(
        chol_full.reshape(k_local, 2, M * M, tiles, LANES), (0, 2, 3, 1, 4)
    ).reshape(k_local, M * M * tiles * 2, LANES)
    own_fields = fields.reshape(walkers, chol_cols)
    own_orbitals = orbitals.reshape(k_local, walkers, 2 * pair_width)
    mask, picks = call(
        functools.partial(prepare_kernel, ka_count, pb_count, walkers),
        (shape((2 * walkers, chol_cols), F32), shape((LANES, 2 * LANES), BF16)),
        scalars=2,
        flops=10**9,
    )(kq_map, chol_count)
    bias, own = call(
        functools.partial(bias_kernel, ka_count, k_local),
        (
            shape((2 * walkers + span, chol_cols), F32),
            shape((k_local, 2 * walkers, pair_width), F32),
        ),
        [pltpu.VMEM((walkers, kpoints, 2 * pair_width), F32)],
        operands=len(greens) + 3,
    )(*greens, half, own_orbitals, mask)
    parts = exchange(bias, "ka", BIAS_ROUNDS)
    shares = call(
        functools.partial(exchange_kernel, k_local),
        shape((walkers, LANES), F32),
        operands=3,
    )(own, half, mask)
    width = -(-(M * M + 3) // LANES) * LANES
    blocks = call(
        functools.partial(operator_kernel, k_local),
        shape((ka_count * pb_count, 2 * span, width), BF16),
        [pltpu.VMEM((2 * M * M * tiles, LANES), F32), pltpu.VMEM((width, LANES), F32)],
        operands=len(parts) + 4,
    )(*parts, own_fields, mask, shares, full)
    group = list(range(ka_count * pb_count))[::-1]
    blocks = lax.all_to_all(
        blocks, ("pb", "ka"), 0, 0, axis_index_groups=[group], tiled=True
    )
    propagated, energy = call(
        functools.partial(taylor_kernel, pb_count, float(pb_count * chol_cols)),
        (shape((k_local, walkers, 2 * pair_width), F32), shape((1, 1), F32)),
        [
            pltpu.VMEM((width, LANES), F32),
            pltpu.VMEM((NOCC * ROWS, 2 * LANES), F32),
            pltpu.VMEM((LANES, LANES), F32),
        ],
        operands=len(parts) + 3,
    )(blocks, *parts, picks, own_orbitals)
    return (propagated[None], energy)


def on_device(green, fields, orbitals, chol_half, chol_full, chol_count, kq_map):
    ka_count, pb_count = lax.axis_size("ka"), lax.axis_size("pb")
    walkers = orbitals.shape[2]
    fits = 2 * pb_count * kq_map.shape[1] * walkers == LANES
    fits = fits and chol_half.shape[1] * walkers == 8 and chol_half.shape[4] == 2 * LANES
    fits = fits and ka_count == 4
    if fits and chol_half.shape[0] == 1 and walkers == ka_count:
        return direct(green, fields, orbitals, chol_half, chol_full, chol_count, kq_map)
    return with_collectives(green, fields, orbitals, chol_half, chol_full, chol_count, kq_map)


def solution(mesh):
    placed = (
        P("wa", ("grp", "ka"), "pb", None, None),
        P("wa", "pb", "grp", None),
        P("wa", "ka", "grp", None),
        P("pb", "ka", None, None, None),
        P("pb", "ka", None, None, None),
        P(),
        P(),
    )
    return jax.shard_map(
        on_device,
        mesh=mesh,
        in_specs=placed,
        out_specs=(P("wa", "ka", "grp", None), P("wa", ("grp", "ka"))),
        check_vma=False,
    )
```

```python
import functools

import jax
import jax.numpy as jnp
from jax import lax
from jax.experimental import pallas as pl
from jax.experimental.pallas import tpu as pltpu
from jax.sharding import PartitionSpec as P

M = 26
NOCC = 4
TAYLOR = 3
LANES = 128
ROWS = 32

GREEN_ROUNDS = (
    ((3, 0), (2, 1), (1, 3), (0, 2)),
    ((3, 1), (2, 0), (0, 3), (1, 2)),
    ((1, 0), (3, 2), (2, 3), (0, 1)),
)[::-1]
BIAS_ROUNDS = (
    ((0, 1), (1, 2), (2, 3), (3, 0)),
    ((0, 2), (1, 3), (2, 0), (3, 1)),
    ((0, 3), (1, 0), (2, 1), (3, 2)),
)[::-1]


BIAS_STEP = 0.5
PROP_STEP = 0.5

F32 = jnp.float32
BF16 = jnp.bfloat16


def complex_dot(pattern, left_re, left_im, right_re, right_im):
    real_part = jnp.einsum(
        pattern, left_re, right_re, preferred_element_type=jnp.float32
    ) - jnp.einsum(pattern, left_im, right_im, preferred_element_type=jnp.float32)
    imag_part = jnp.einsum(
        pattern, left_re, right_im, preferred_element_type=jnp.float32
    ) + jnp.einsum(pattern, left_im, right_re, preferred_element_type=jnp.float32)
    return (real_part, imag_part)


def make_picker(wanted):

    def picker(shard_rows):
        row_count = shard_rows.shape[0]
        select = (wanted[:, None] == jnp.arange(row_count, dtype=jnp.int32)[None, :]).astype(
            jnp.bfloat16
        )
        return jnp.dot(select, shard_rows, preferred_element_type=jnp.float32)

    return picker


def with_collectives(green, fields, orbitals, chol_half, chol_full, chol_count, kq_map):
    q_local = chol_half.shape[0]
    k_local = chol_half.shape[1]
    pair_width = chol_half.shape[3]
    chol_cols = chol_half.shape[4]
    ka_count = lax.axis_size("ka")
    pb_count = lax.axis_size("pb")
    ka_pos = lax.axis_index("ka")
    pb_pos = lax.axis_index("pb")
    local_green = lax.all_to_all(green, "ka", split_axis=3, concat_axis=1, tiled=True)
    walkers = local_green.shape[1]
    per_device = walkers // ka_count
    greens = local_green[0].reshape(walkers, q_local, k_local, 2, pair_width)
    counts = lax.dynamic_slice_in_dim(chol_count, pb_pos * q_local, q_local)
    vec_mask = (jnp.arange(chol_cols, dtype=jnp.int32)[None, :] < counts[:, None]).astype(
        jnp.float32
    )
    bias_re, bias_im = complex_dot(
        "wqkx,qkxn->qwn",
        greens[:, :, :, 0],
        greens[:, :, :, 1],
        chol_half[:, :, 0],
        chol_half[:, :, 1],
    )
    own_rows = (jnp.arange(walkers, dtype=jnp.int32) // per_device == ka_pos).astype(jnp.float32)
    bias_re, bias_im = lax.psum((bias_re, bias_im), "ka")
    bias_re = bias_re * vec_mask[:, None, :]
    bias_im = bias_im * vec_mask[:, None, :]
    hartree = 0.5 * jnp.sum(bias_re * bias_re + bias_im * bias_im, axis=(0, 2)) * own_rows
    field_now = jnp.transpose(fields, (1, 0, 2, 3)).reshape(q_local, walkers, chol_cols)
    shift_re = ((field_now - BIAS_STEP * bias_re) * vec_mask[:, None, :]).astype(jnp.bfloat16)
    shift_im = (-BIAS_STEP * bias_im * vec_mask[:, None, :]).astype(jnp.bfloat16)
    exchange = jnp.zeros((walkers,), jnp.float32)
    for transfer in range(q_local):
        for kpoint in range(k_local):
            chol_row = chol_half[transfer, kpoint].reshape(2, NOCC, M, chol_cols)
            green_row = greens[:, transfer, kpoint].reshape(walkers, 2, NOCC, M)
            cross_re, cross_im = complex_dot(
                "ipn,wjp->wijn", chol_row[0], chol_row[1], green_row[:, 0], green_row[:, 1]
            )
            exchange = exchange + 0.5 * jnp.sum(
                (cross_re * cross_re + cross_im * cross_im) * vec_mask[transfer], axis=(1, 2, 3)
            )
    prop_re, prop_im = complex_dot(
        "qwn,qkyn->qwky", shift_re, shift_im, chol_full[:, :, 0], chol_full[:, :, 1]
    )
    shape = (q_local, walkers, k_local, M, M)
    oper_re = (PROP_STEP * prop_re).astype(jnp.bfloat16).reshape(shape)
    oper_im = (PROP_STEP * prop_im).astype(jnp.bfloat16).reshape(shape)
    normalizer = q_local * pb_count * chol_cols
    total_energy = lax.psum(hartree - exchange, ("ka", "pb")) / normalizer
    energy = lax.dynamic_slice_in_dim(total_energy, ka_pos * per_device, per_device).reshape(
        1, per_device
    )
    initial = orbitals[0].reshape(k_local, walkers, 2, NOCC, M)
    row_width = 2 * pair_width
    my_rows = lax.dynamic_slice_in_dim(kq_map, pb_pos * q_local, q_local, 0)
    wanted = lax.dynamic_slice_in_dim(my_rows, ka_pos * k_local, k_local, 1).reshape(
        q_local * k_local
    )
    picker = make_picker(wanted)
    current = initial
    summed_terms = initial
    for degree in range(1, TAYLOR + 1):
        rounded = current.astype(jnp.bfloat16).reshape(k_local, walkers * row_width)
        fetched = picker(lax.all_gather(rounded, "ka", axis=0, tiled=True))
        shifted_rows = fetched.astype(jnp.bfloat16).reshape(q_local, k_local, walkers, 2, NOCC, M)
        out_re, out_im = complex_dot(
            "xwkpq,xkwiq->kwip",
            oper_re,
            oper_im,
            shifted_rows[:, :, :, 0],
            shifted_rows[:, :, :, 1],
        )
        applied = jnp.stack([out_re, out_im], axis=2)
        applied = lax.psum(applied, "pb")
        current = applied / degree
        summed_terms = summed_terms + current
    propagated = summed_terms.reshape(1, k_local, walkers, row_width)
    return (propagated, energy)


def exchange(array, axis, rounds):
    return [array] + [lax.ppermute(array, axis, pairs) for pairs in rounds]


def origins(axis, rounds):
    at = lax.axis_index(axis)
    found = [at]
    for pairs in rounds:
        source = jnp.int32(0)
        for sender, receiver in pairs:
            source = jnp.where(at == receiver, sender, source)
        found.append(source)
    return found


def prepare_kernel(ka_count, pb_count, walkers, map_ref, count_ref, mask_ref, picks_ref):
    kept = count_ref[lax.axis_index("pb")]
    column = lax.broadcasted_iota(jnp.int32, mask_ref.shape, 1)
    mask_ref[...] = jnp.where(column < kept, 1.0, 0.0)
    kpoints = map_ref.shape[1]
    k_local = kpoints // ka_count
    span = k_local * walkers
    lane = lax.broadcasted_iota(jnp.int32, (1, LANES), 1)
    lane_q = lane // (LANES // pb_count)
    lane_ka = lax.rem(lane, LANES // pb_count) // (2 * span)
    lane_part = lax.rem(lane, 2 * span) // span
    lane_k = lane_ka * k_local + lax.rem(lane, span) // walkers
    wanted = jnp.zeros((1, LANES), jnp.int32)
    for q in range(pb_count):
        for k in range(kpoints):
            source = map_ref[q, k]
            source = source // k_local * (2 * span) + lax.rem(source, k_local) * walkers
            wanted = jnp.where((lane_q == q) & (lane_k == k), source, wanted)
    wanted = wanted + lax.rem(lane, walkers)
    row = lax.broadcasted_iota(jnp.int32, (LANES, LANES), 0)
    real = jnp.where(row == wanted, 1.0, 0.0)
    imag = jnp.where(row == wanted + span, jnp.where(lane_part == 0, 1.0, -1.0), 0.0)
    picks_ref[...] = jnp.concatenate([real, imag], axis=1).astype(BF16)


def bias_kernel(ka_count, k_local, *refs):
    *greens, chol_ref, orbitals_ref, mask_ref, bias_ref, own_ref, table = refs
    for source, green_ref in zip(origins("ka", GREEN_ROUNDS), greens):
        table[source] = green_ref[...].astype(F32)
    first = lax.axis_index("ka") * k_local
    width = chol_ref.shape[2]
    rows = 2 * ka_count
    total = jnp.zeros((rows, bias_ref.shape[1]), F32)
    for k in range(k_local):
        green = jnp.concatenate(
            [table[w, pl.ds(first + k, 1), :] for w in range(ka_count)], axis=0
        )
        real, imag = green[:, :width], green[:, width:]
        both = jnp.concatenate([real, imag], axis=0)
        turned = jnp.concatenate([-imag, real], axis=0)
        own_ref[k] = both
        total += jnp.dot(both.astype(BF16), chol_ref[k, 0], preferred_element_type=F32)
        total += jnp.dot(turned.astype(BF16), chol_ref[k, 1], preferred_element_type=F32)
    bias_ref[:rows] = total * mask_ref[...]
    window = jnp.concatenate([orbitals_ref[k] for k in range(k_local)], axis=0)
    count, width = window.shape
    bias_ref[rows : rows + count, :width] = window
    bias_ref[rows : rows + count, width:] = jnp.zeros((count, bias_ref.shape[1] - width), F32)


def exchange_kernel(k_local, own_ref, chol_ref, mask_ref, out_ref):
    walkers, width, columns = own_ref.shape[1] // 2, own_ref.shape[2], chol_ref.shape[3]
    rows = 2 * walkers
    lane = lax.broadcasted_iota(jnp.int32, (rows, LANES), 1)
    total = jnp.zeros((rows, columns), F32)
    for k in range(k_local):
        both = jnp.concatenate([own_ref[k], jnp.zeros((rows, LANES - width), F32)], axis=1)
        turned = jnp.concatenate([-both[walkers:], both[:walkers]], axis=0)
        sides = []
        for side in (both, turned):
            rolled = {
                step: side if step == 0 else pltpu.roll(side, (step * M) % LANES, 1)
                for step in range(1 - NOCC, NOCC)
            }
            blocks = []
            for i in range(NOCC):
                inside = (lane >= i * M) & (lane < (i + 1) * M)
                for j in range(NOCC):
                    blocks.append(jnp.where(inside, rolled[i - j], 0.0))
            sides.append(jnp.concatenate(blocks, axis=0)[:, :width].astype(BF16))
        cross = jnp.dot(sides[0], chol_ref[k, 0], preferred_element_type=F32)
        cross += jnp.dot(sides[1], chol_ref[k, 1], preferred_element_type=F32)
        cross = cross * cross
        for block in range(NOCC * NOCC):
            total += cross[block * rows : (block + 1) * rows]
    total = total * mask_ref[:rows]
    total = total[:walkers] + total[walkers:]
    summed = 0.5 * jnp.sum(total, axis=1, keepdims=True)
    out_ref[...] = jnp.broadcast_to(summed, out_ref.shape)


def operator_kernel(k_local, *refs):
    *parts, fields_ref, mask_ref, exchange_ref, chol_ref, out_ref, products, turned_ref = refs
    walkers, columns = fields_ref.shape
    bias = parts[0][: 2 * walkers]
    for part in parts[1:]:
        bias = bias + part[: 2 * walkers]
    pairs = M * M
    tiles = columns // LANES
    group = LANES // (2 * tiles)
    bias_re, bias_im = bias[:walkers], bias[walkers:]
    hartree = 0.5 * jnp.sum(bias_re * bias_re + bias_im * bias_im, axis=1, keepdims=True)
    own = lax.broadcasted_iota(jnp.int32, (walkers, 1), 0) == lax.axis_index("ka")
    energy = jnp.where(own, hartree, 0.0) - exchange_ref[:, :1]
    kept = mask_ref[:walkers]
    shift_re = (fields_ref[...] - BIAS_STEP * bias_re) * kept
    shift_im = -BIAS_STEP * bias_im * kept
    span = k_local * walkers
    weights = []
    for k in range(k_local):
        before, after = k * walkers, span - (k + 1) * walkers
        pieces = []
        for tile in range(tiles):
            at = slice(tile * LANES, (tile + 1) * LANES)
            for first, second in ((shift_re, shift_im), (-shift_im, shift_re)):
                for side in (first, second):
                    pieces += [(before, None), (walkers, side[:, at]), (after, None)]
                pieces.append((group - 2 * span, None))
        weights.append(
            jnp.concatenate(
                [jnp.zeros((n, LANES), F32) if p is None else p for n, p in pieces if n], axis=0
            ).astype(BF16)
        )
    products[...] = lax.dot_general(
        jnp.concatenate([chol_ref[k] for k in range(k_local)], axis=1),
        jnp.concatenate(weights, axis=1),
        (((1,), (1,)), ((), ())),
        preferred_element_type=F32,
    )
    lane = lax.broadcasted_iota(jnp.int32, (pairs, LANES), 1)
    merged = products[pl.ds(0, pairs, stride=2 * tiles), :]
    for at in range(1, 2 * tiles):
        row = products[pl.ds(at, pairs, stride=2 * tiles), :]
        merged = jnp.where(lane >= at * group, row, merged)
    turned_ref[:pairs] = merged
    copies, rows, width = out_ref.shape
    lane = lax.broadcasted_iota(jnp.int32, (rows, LANES), 1)
    for at in range(0, width, LANES):
        block = turned_ref[at : at + LANES].T
        block = PROP_STEP * sum(block[n * group : n * group + rows] for n in range(2 * tiles))
        if at + LANES > pairs:
            share = jnp.concatenate([energy, jnp.zeros((rows - walkers, 1), F32)], axis=0)
            block = jnp.where(lane + at < pairs, block, 0.0)
            for piece in range(3):
                head = share.astype(BF16).astype(F32)
                block = jnp.where(lane + at == pairs + piece, head, block)
                share = share - head
        for copy in range(copies):
            out_ref[copy, :, at : at + LANES] = block.astype(BF16)


def taylor_kernel(pb_count, normalizer, blocks_ref, *refs):
    *windows, picks_ref, orbitals_ref, out_ref, energy_ref, turned, picked, term = refs
    pairs = M * M
    pair = NOCC * M
    k_local, walkers, _ = out_ref.shape
    span = k_local * walkers
    ka_pos = lax.axis_index("ka")
    term[...] = jnp.zeros_like(term)
    for source, window_ref in zip(origins("ka", BIAS_ROUNDS), windows):
        start = pl.multiple_of(source * (2 * span), 2 * span)
        window = window_ref[window_ref.shape[0] - span :]
        term[pl.ds(start, span), :pair] = window[:, :pair]
        term[pl.ds(start + span, span), :pair] = window[:, pair : 2 * pair]
    picked[...] = jnp.dot(term[...].T.astype(BF16), picks_ref[...], preferred_element_type=F32)
    count, rows, width = blocks_ref.shape
    for at in range(0, width, LANES):
        tile = jnp.concatenate([blocks_ref[n, :, at : at + LANES] for n in reversed(range(count))], axis=0)
        turned[at : at + LANES] = tile.T.astype(F32)
    shares = turned[pairs : pairs + 3]
    lane = lax.broadcasted_iota(jnp.int32, shares.shape, 1)
    shares = jnp.where(lax.rem(lane, 2 * span) == ka_pos, shares, 0.0)
    shares = jnp.sum(jnp.sum(shares, axis=0, keepdims=True), axis=1, keepdims=True)
    energy_ref[...] = shares / normalizer
    lane = lax.broadcasted_iota(jnp.int32, (M, LANES), 1)
    imaginary = lax.rem(lane, 2 * span) >= span
    sums = [jnp.zeros((M, LANES), F32) for _ in range(NOCC)]
    for degree in range(1, TAYLOR + 1):
        stride = M if degree == 1 else ROWS
        straight = [jnp.zeros((M, LANES), F32) for _ in range(NOCC)]
        crossed = [jnp.zeros((M, LANES), F32) for _ in range(NOCC)]
        for c in range(M):
            column = turned[pl.ds(c, M, stride=M), :]
            for i in range(NOCC):
                at = i * stride + c
                straight[i] += column * picked[at : at + 1, :LANES]
                crossed[i] += column * picked[at : at + 1, LANES:]
        for i in range(NOCC):
            other = jnp.where(
                imaginary, pltpu.roll(crossed[i], span, 1), pltpu.roll(crossed[i], LANES - span, 1)
            )
            applied = straight[i] + other
            applied = applied + pltpu.roll(applied, LANES // pb_count, 1)
            current = applied / degree
            sums[i] = sums[i] + current
            term[i * ROWS : i * ROWS + M] = current if degree < TAYLOR else sums[i]
        if degree < TAYLOR:
            picked[...] = jnp.dot(
                term[...].astype(BF16), picks_ref[...], preferred_element_type=F32
            )
    turned[:LANES] = term[...].T
    both = turned[pl.ds(pl.multiple_of(ka_pos * (2 * span), 2 * span), 2 * span), :]
    both = jnp.concatenate([both[:, i * ROWS : i * ROWS + M] for i in range(NOCC)], axis=1)
    both = jnp.concatenate([both[:span], both[span:]], axis=1)
    for k in range(k_local):
        out_ref[k] = orbitals_ref[k] + both[k * walkers : (k + 1) * walkers]


def call(kernel, out, scratch=(), scalars=0, operands=0, flops=None):
    spaces = [pltpu.SMEM] * scalars + [pltpu.VMEM] * operands
    cost = None
    if flops is not None:
        cost = pl.CostEstimate(flops=flops, bytes_accessed=0, transcendentals=0)
    return pl.pallas_call(
        kernel,
        out_shape=out,
        in_specs=[pl.BlockSpec(memory_space=space) for space in spaces],
        out_specs=jax.tree.map(lambda _: pl.BlockSpec(memory_space=pltpu.VMEM), out),
        scratch_shapes=list(scratch),
        cost_estimate=cost,
        compiler_params=pltpu.CompilerParams(vmem_limit_bytes=24 * 2**20),
    )


def direct(green, fields, orbitals, chol_half, chol_full, chol_count, kq_map):
    k_local, pair_width, chol_cols = chol_half.shape[1], chol_half.shape[3], chol_half.shape[4]
    ka_count, pb_count = lax.axis_size("ka"), lax.axis_size("pb")
    walkers = ka_count
    kpoints = green.shape[3]
    span = k_local * walkers
    shape = jax.ShapeDtypeStruct
    tiles = chol_cols // LANES
    own_green = green.reshape(kpoints, 2 * pair_width)
    greens = exchange(own_green, "ka", GREEN_ROUNDS)
    half = chol_half.reshape(k_local, 2, pair_width, chol_cols)
    full = jnp.transpose(
        chol_full.reshape(k_local, 2, M * M, tiles, LANES), (0, 2, 3, 1, 4)
    ).reshape(k_local, M * M * tiles * 2, LANES)
    own_fields = fields.reshape(walkers, chol_cols)
    own_orbitals = orbitals.reshape(k_local, walkers, 2 * pair_width)
    mask, picks = call(
        functools.partial(prepare_kernel, ka_count, pb_count, walkers),
        (shape((2 * walkers, chol_cols), F32), shape((LANES, 2 * LANES), BF16)),
        scalars=2,
        flops=10**9,
    )(kq_map, chol_count)
    bias, own = call(
        functools.partial(bias_kernel, ka_count, k_local),
        (
            shape((2 * walkers + span, chol_cols), F32),
            shape((k_local, 2 * walkers, pair_width), F32),
        ),
        [pltpu.VMEM((walkers, kpoints, 2 * pair_width), F32)],
        operands=len(greens) + 3,
    )(*greens, half, own_orbitals, mask)
    parts = exchange(bias, "ka", BIAS_ROUNDS)
    shares = call(
        functools.partial(exchange_kernel, k_local),
        shape((walkers, LANES), F32),
        operands=3,
    )(own, half, mask)
    width = -(-(M * M + 3) // LANES) * LANES
    blocks = call(
        functools.partial(operator_kernel, k_local),
        shape((ka_count * pb_count, 2 * span, width), BF16),
        [pltpu.VMEM((2 * M * M * tiles, LANES), F32), pltpu.VMEM((width, LANES), F32)],
        operands=len(parts) + 4,
    )(*parts, own_fields, mask, shares, full)
    group = list(range(ka_count * pb_count))[::-1]
    blocks = lax.all_to_all(
        blocks, ("pb", "ka"), 0, 0, axis_index_groups=[group], tiled=True
    )
    propagated, energy = call(
        functools.partial(taylor_kernel, pb_count, float(pb_count * chol_cols)),
        (shape((k_local, walkers, 2 * pair_width), F32), shape((1, 1), F32)),
        [
            pltpu.VMEM((width, LANES), F32),
            pltpu.VMEM((NOCC * ROWS, 2 * LANES), F32),
            pltpu.VMEM((LANES, LANES), F32),
        ],
        operands=len(parts) + 3,
    )(blocks, *parts, picks, own_orbitals)
    return (propagated[None], energy)


def on_device(green, fields, orbitals, chol_half, chol_full, chol_count, kq_map):
    ka_count, pb_count = lax.axis_size("ka"), lax.axis_size("pb")
    walkers = orbitals.shape[2]
    fits = 2 * pb_count * kq_map.shape[1] * walkers == LANES
    fits = fits and chol_half.shape[1] * walkers == 8 and chol_half.shape[4] == 2 * LANES
    fits = fits and ka_count == 4
    if fits and chol_half.shape[0] == 1 and walkers == ka_count:
        return direct(green, fields, orbitals, chol_half, chol_full, chol_count, kq_map)
    return with_collectives(green, fields, orbitals, chol_half, chol_full, chol_count, kq_map)


def solution(mesh):
    placed = (
        P("wa", ("grp", "ka"), "pb", None, None),
        P("wa", "pb", "grp", None),
        P("wa", "ka", "grp", None),
        P("pb", "ka", None, None, None),
        P("pb", "ka", None, None, None),
        P(),
        P(),
    )
    return jax.shard_map(
        on_device,
        mesh=mesh,
        in_specs=placed,
        out_specs=(P("wa", "ka", "grp", None), P("wa", ("grp", "ka"))),
        check_vma=False,
    )
```

```python
import functools

import jax
import jax.numpy as jnp
from jax import lax
from jax.experimental import pallas as pl
from jax.experimental.pallas import tpu as pltpu
from jax.sharding import PartitionSpec as P

M = 26
NOCC = 4
TAYLOR = 3
LANES = 128
ROWS = 32

GREEN_ROUNDS = (
    ((3, 0), (2, 1), (1, 3), (0, 2)),
    ((3, 1), (2, 0), (0, 3), (1, 2)),
    ((1, 0), (3, 2), (2, 3), (0, 1)),
)[::-1]
BIAS_ROUNDS = (
    ((0, 1), (1, 3), (2, 0), (3, 2)),
    ((0, 3), (3, 0), (1, 2), (2, 1)),
    ((0, 2), (1, 0), (2, 3), (3, 1)),
)[::-1]


BIAS_STEP = 0.5
PROP_STEP = 0.5

F32 = jnp.float32
BF16 = jnp.bfloat16


def complex_dot(pattern, left_re, left_im, right_re, right_im):
    real_part = jnp.einsum(
        pattern, left_re, right_re, preferred_element_type=jnp.float32
    ) - jnp.einsum(pattern, left_im, right_im, preferred_element_type=jnp.float32)
    imag_part = jnp.einsum(
        pattern, left_re, right_im, preferred_element_type=jnp.float32
    ) + jnp.einsum(pattern, left_im, right_re, preferred_element_type=jnp.float32)
    return (real_part, imag_part)


def make_picker(wanted):

    def picker(shard_rows):
        row_count = shard_rows.shape[0]
        select = (wanted[:, None] == jnp.arange(row_count, dtype=jnp.int32)[None, :]).astype(
            jnp.bfloat16
        )
        return jnp.dot(select, shard_rows, preferred_element_type=jnp.float32)

    return picker


def with_collectives(green, fields, orbitals, chol_half, chol_full, chol_count, kq_map):
    q_local = chol_half.shape[0]
    k_local = chol_half.shape[1]
    pair_width = chol_half.shape[3]
    chol_cols = chol_half.shape[4]
    ka_count = lax.axis_size("ka")
    pb_count = lax.axis_size("pb")
    ka_pos = lax.axis_index("ka")
    pb_pos = lax.axis_index("pb")
    local_green = lax.all_to_all(green, "ka", split_axis=3, concat_axis=1, tiled=True)
    walkers = local_green.shape[1]
    per_device = walkers // ka_count
    greens = local_green[0].reshape(walkers, q_local, k_local, 2, pair_width)
    counts = lax.dynamic_slice_in_dim(chol_count, pb_pos * q_local, q_local)
    vec_mask = (jnp.arange(chol_cols, dtype=jnp.int32)[None, :] < counts[:, None]).astype(
        jnp.float32
    )
    bias_re, bias_im = complex_dot(
        "wqkx,qkxn->qwn",
        greens[:, :, :, 0],
        greens[:, :, :, 1],
        chol_half[:, :, 0],
        chol_half[:, :, 1],
    )
    own_rows = (jnp.arange(walkers, dtype=jnp.int32) // per_device == ka_pos).astype(jnp.float32)
    bias_re, bias_im = lax.psum((bias_re, bias_im), "ka")
    bias_re = bias_re * vec_mask[:, None, :]
    bias_im = bias_im * vec_mask[:, None, :]
    hartree = 0.5 * jnp.sum(bias_re * bias_re + bias_im * bias_im, axis=(0, 2)) * own_rows
    field_now = jnp.transpose(fields, (1, 0, 2, 3)).reshape(q_local, walkers, chol_cols)
    shift_re = ((field_now - BIAS_STEP * bias_re) * vec_mask[:, None, :]).astype(jnp.bfloat16)
    shift_im = (-BIAS_STEP * bias_im * vec_mask[:, None, :]).astype(jnp.bfloat16)
    exchange = jnp.zeros((walkers,), jnp.float32)
    for transfer in range(q_local):
        for kpoint in range(k_local):
            chol_row = chol_half[transfer, kpoint].reshape(2, NOCC, M, chol_cols)
            green_row = greens[:, transfer, kpoint].reshape(walkers, 2, NOCC, M)
            cross_re, cross_im = complex_dot(
                "ipn,wjp->wijn", chol_row[0], chol_row[1], green_row[:, 0], green_row[:, 1]
            )
            exchange = exchange + 0.5 * jnp.sum(
                (cross_re * cross_re + cross_im * cross_im) * vec_mask[transfer], axis=(1, 2, 3)
            )
    prop_re, prop_im = complex_dot(
        "qwn,qkyn->qwky", shift_re, shift_im, chol_full[:, :, 0], chol_full[:, :, 1]
    )
    shape = (q_local, walkers, k_local, M, M)
    oper_re = (PROP_STEP * prop_re).astype(jnp.bfloat16).reshape(shape)
    oper_im = (PROP_STEP * prop_im).astype(jnp.bfloat16).reshape(shape)
    normalizer = q_local * pb_count * chol_cols
    total_energy = lax.psum(hartree - exchange, ("ka", "pb")) / normalizer
    energy = lax.dynamic_slice_in_dim(total_energy, ka_pos * per_device, per_device).reshape(
        1, per_device
    )
    initial = orbitals[0].reshape(k_local, walkers, 2, NOCC, M)
    row_width = 2 * pair_width
    my_rows = lax.dynamic_slice_in_dim(kq_map, pb_pos * q_local, q_local, 0)
    wanted = lax.dynamic_slice_in_dim(my_rows, ka_pos * k_local, k_local, 1).reshape(
        q_local * k_local
    )
    picker = make_picker(wanted)
    current = initial
    summed_terms = initial
    for degree in range(1, TAYLOR + 1):
        rounded = current.astype(jnp.bfloat16).reshape(k_local, walkers * row_width)
        fetched = picker(lax.all_gather(rounded, "ka", axis=0, tiled=True))
        shifted_rows = fetched.astype(jnp.bfloat16).reshape(q_local, k_local, walkers, 2, NOCC, M)
        out_re, out_im = complex_dot(
            "xwkpq,xkwiq->kwip",
            oper_re,
            oper_im,
            shifted_rows[:, :, :, 0],
            shifted_rows[:, :, :, 1],
        )
        applied = jnp.stack([out_re, out_im], axis=2)
        applied = lax.psum(applied, "pb")
        current = applied / degree
        summed_terms = summed_terms + current
    propagated = summed_terms.reshape(1, k_local, walkers, row_width)
    return (propagated, energy)


def exchange(array, axis, rounds):
    return [array] + [lax.ppermute(array, axis, pairs) for pairs in rounds]


def origins(axis, rounds):
    at = lax.axis_index(axis)
    found = [at]
    for pairs in rounds:
        source = jnp.int32(0)
        for sender, receiver in pairs:
            source = jnp.where(at == receiver, sender, source)
        found.append(source)
    return found


def operator_group(ka_count, pb_count):
    first = (pb_count - 1) * ka_count + ka_count // 2
    rest = [at for at in range(pb_count * ka_count) if at != first]
    return [first] + rest[::-1]


def prepare_kernel(ka_count, pb_count, walkers, map_ref, count_ref, mask_ref, picks_ref):
    kept = count_ref[lax.axis_index("pb")]
    column = lax.broadcasted_iota(jnp.int32, mask_ref.shape, 1)
    mask_ref[...] = jnp.where(column < kept, 1.0, 0.0)
    kpoints = map_ref.shape[1]
    k_local = kpoints // ka_count
    span = k_local * walkers
    lane = lax.broadcasted_iota(jnp.int32, (1, LANES), 1)
    lane_q = lane // (LANES // pb_count)
    lane_ka = lax.rem(lane, LANES // pb_count) // (2 * span)
    lane_part = lax.rem(lane, 2 * span) // span
    lane_k = lane_ka * k_local + lax.rem(lane, span) // walkers
    wanted = jnp.zeros((1, LANES), jnp.int32)
    for q in range(pb_count):
        for k in range(kpoints):
            source = map_ref[q, k]
            source = source // k_local * (2 * span) + lax.rem(source, k_local) * walkers
            wanted = jnp.where((lane_q == q) & (lane_k == k), source, wanted)
    wanted = wanted + lax.rem(lane, walkers)
    row = lax.broadcasted_iota(jnp.int32, (LANES, LANES), 0)
    real = jnp.where(row == wanted, 1.0, 0.0)
    imag = jnp.where(row == wanted + span, jnp.where(lane_part == 0, 1.0, -1.0), 0.0)
    picks_ref[...] = jnp.concatenate([real, imag], axis=1).astype(BF16)


def bias_kernel(ka_count, k_local, *refs):
    *greens, chol_ref, orbitals_ref, mask_ref, bias_ref, own_ref, table = refs
    for source, green_ref in zip(origins("ka", GREEN_ROUNDS), greens):
        table[source] = green_ref[...].astype(F32)
    first = lax.axis_index("ka") * k_local
    width = chol_ref.shape[2]
    rows = 2 * ka_count
    total = jnp.zeros((rows, bias_ref.shape[1]), F32)
    for k in range(k_local):
        green = jnp.concatenate(
            [table[w, pl.ds(first + k, 1), :] for w in range(ka_count)], axis=0
        )
        real, imag = green[:, :width], green[:, width:]
        both = jnp.concatenate([real, imag], axis=0)
        turned = jnp.concatenate([-imag, real], axis=0)
        own_ref[k] = both
        total += jnp.dot(both.astype(BF16), chol_ref[k, 0], preferred_element_type=F32)
        total += jnp.dot(turned.astype(BF16), chol_ref[k, 1], preferred_element_type=F32)
    bias_ref[:rows] = total * mask_ref[...]
    window = jnp.concatenate([orbitals_ref[k] for k in range(k_local)], axis=0)
    count, width = window.shape
    bias_ref[rows : rows + count, :width] = window
    bias_ref[rows : rows + count, width:] = jnp.zeros((count, bias_ref.shape[1] - width), F32)


def exchange_kernel(k_local, own_ref, chol_ref, mask_ref, out_ref):
    walkers, width, columns = own_ref.shape[1] // 2, own_ref.shape[2], chol_ref.shape[3]
    rows = 2 * walkers
    lane = lax.broadcasted_iota(jnp.int32, (rows, LANES), 1)
    total = jnp.zeros((rows, columns), F32)
    for k in range(k_local):
        both = jnp.concatenate([own_ref[k], jnp.zeros((rows, LANES - width), F32)], axis=1)
        turned = jnp.concatenate([-both[walkers:], both[:walkers]], axis=0)
        sides = []
        for side in (both, turned):
            rolled = {
                step: side if step == 0 else pltpu.roll(side, (step * M) % LANES, 1)
                for step in range(1 - NOCC, NOCC)
            }
            blocks = []
            for i in range(NOCC):
                inside = (lane >= i * M) & (lane < (i + 1) * M)
                for j in range(NOCC):
                    blocks.append(jnp.where(inside, rolled[i - j], 0.0))
            sides.append(jnp.concatenate(blocks, axis=0)[:, :width].astype(BF16))
        cross = jnp.dot(sides[0], chol_ref[k, 0], preferred_element_type=F32)
        cross += jnp.dot(sides[1], chol_ref[k, 1], preferred_element_type=F32)
        cross = cross * cross
        for block in range(NOCC * NOCC):
            total += cross[block * rows : (block + 1) * rows]
    total = total * mask_ref[:rows]
    total = total[:walkers] + total[walkers:]
    summed = 0.5 * jnp.sum(total, axis=1, keepdims=True)
    out_ref[...] = jnp.broadcast_to(summed, out_ref.shape)


def operator_kernel(k_local, *refs):
    *parts, fields_ref, mask_ref, exchange_ref, chol_ref, out_ref, products, turned_ref = refs
    walkers, columns = fields_ref.shape
    bias = parts[0][: 2 * walkers]
    for part in parts[1:]:
        bias = bias + part[: 2 * walkers]
    pairs = M * M
    tiles = columns // LANES
    group = LANES // (2 * tiles)
    bias_re, bias_im = bias[:walkers], bias[walkers:]
    hartree = 0.5 * jnp.sum(bias_re * bias_re + bias_im * bias_im, axis=1, keepdims=True)
    own = lax.broadcasted_iota(jnp.int32, (walkers, 1), 0) == lax.axis_index("ka")
    energy = jnp.where(own, hartree, 0.0) - exchange_ref[:, :1]
    kept = mask_ref[:walkers]
    shift_re = (fields_ref[...] - BIAS_STEP * bias_re) * kept
    shift_im = -BIAS_STEP * bias_im * kept
    span = k_local * walkers
    weights = []
    for k in range(k_local):
        before, after = k * walkers, span - (k + 1) * walkers
        pieces = []
        for tile in range(tiles):
            at = slice(tile * LANES, (tile + 1) * LANES)
            for first, second in ((shift_re, shift_im), (-shift_im, shift_re)):
                for side in (first, second):
                    pieces += [(before, None), (walkers, side[:, at]), (after, None)]
                pieces.append((group - 2 * span, None))
        weights.append(
            jnp.concatenate(
                [jnp.zeros((n, LANES), F32) if p is None else p for n, p in pieces if n], axis=0
            ).astype(BF16)
        )
    products[...] = lax.dot_general(
        jnp.concatenate([chol_ref[k] for k in range(k_local)], axis=1),
        jnp.concatenate(weights, axis=1),
        (((1,), (1,)), ((), ())),
        preferred_element_type=F32,
    )
    lane = lax.broadcasted_iota(jnp.int32, (pairs, LANES), 1)
    merged = products[pl.ds(0, pairs, stride=2 * tiles), :]
    for at in range(1, 2 * tiles):
        row = products[pl.ds(at, pairs, stride=2 * tiles), :]
        merged = jnp.where(lane >= at * group, row, merged)
    turned_ref[:pairs] = merged
    copies, rows, width = out_ref.shape
    lane = lax.broadcasted_iota(jnp.int32, (rows, LANES), 1)
    for at in range(0, width, LANES):
        block = turned_ref[at : at + LANES].T
        block = PROP_STEP * sum(block[n * group : n * group + rows] for n in range(2 * tiles))
        if at + LANES > pairs:
            share = jnp.concatenate([energy, jnp.zeros((rows - walkers, 1), F32)], axis=0)
            block = jnp.where(lane + at < pairs, block, 0.0)
            for piece in range(3):
                head = share.astype(BF16).astype(F32)
                block = jnp.where(lane + at == pairs + piece, head, block)
                share = share - head
        for copy in range(copies):
            out_ref[copy, :, at : at + LANES] = block.astype(BF16)


def taylor_kernel(pb_count, normalizer, blocks_ref, *refs):
    *windows, picks_ref, orbitals_ref, out_ref, energy_ref, turned, picked, term = refs
    pairs = M * M
    pair = NOCC * M
    k_local, walkers, _ = out_ref.shape
    span = k_local * walkers
    ka_pos = lax.axis_index("ka")
    term[...] = jnp.zeros_like(term)
    for source, window_ref in zip(origins("ka", BIAS_ROUNDS), windows):
        start = pl.multiple_of(source * (2 * span), 2 * span)
        window = window_ref[window_ref.shape[0] - span :]
        term[pl.ds(start, span), :pair] = window[:, :pair]
        term[pl.ds(start + span, span), :pair] = window[:, pair : 2 * pair]
    picked[...] = jnp.dot(term[...].T.astype(BF16), picks_ref[...], preferred_element_type=F32)
    count, _, width = blocks_ref.shape
    group = operator_group(count // pb_count, pb_count)
    places = [group.index(n) for n in range(count)]
    for at in range(0, width, LANES):
        tile = jnp.concatenate([blocks_ref[n, :, at : at + LANES] for n in places], axis=0)
        turned[at : at + LANES] = tile.T.astype(F32)
    shares = turned[pairs : pairs + 3]
    lane = lax.broadcasted_iota(jnp.int32, shares.shape, 1)
    shares = jnp.where(lax.rem(lane, 2 * span) == ka_pos, shares, 0.0)
    shares = jnp.sum(jnp.sum(shares, axis=0, keepdims=True), axis=1, keepdims=True)
    energy_ref[...] = shares / normalizer
    lane = lax.broadcasted_iota(jnp.int32, (M, LANES), 1)
    imaginary = lax.rem(lane, 2 * span) >= span
    sums = [jnp.zeros((M, LANES), F32) for _ in range(NOCC)]
    for degree in range(1, TAYLOR + 1):
        stride = M if degree == 1 else ROWS
        straight = [jnp.zeros((M, LANES), F32) for _ in range(NOCC)]
        crossed = [jnp.zeros((M, LANES), F32) for _ in range(NOCC)]
        for c in range(M):
            column = turned[pl.ds(c, M, stride=M), :]
            for i in range(NOCC):
                at = i * stride + c
                straight[i] += column * picked[at : at + 1, :LANES]
                crossed[i] += column * picked[at : at + 1, LANES:]
        for i in range(NOCC):
            other = jnp.where(
                imaginary, pltpu.roll(crossed[i], span, 1), pltpu.roll(crossed[i], LANES - span, 1)
            )
            applied = straight[i] + other
            applied = applied + pltpu.roll(applied, LANES // pb_count, 1)
            current = applied / degree
            sums[i] = sums[i] + current
            term[i * ROWS : i * ROWS + M] = current if degree < TAYLOR else sums[i]
        if degree < TAYLOR:
            picked[...] = jnp.dot(
                term[...].astype(BF16), picks_ref[...], preferred_element_type=F32
            )
    turned[:LANES] = term[...].T
    both = turned[pl.ds(pl.multiple_of(ka_pos * (2 * span), 2 * span), 2 * span), :]
    both = jnp.concatenate([both[:, i * ROWS : i * ROWS + M] for i in range(NOCC)], axis=1)
    both = jnp.concatenate([both[:span], both[span:]], axis=1)
    for k in range(k_local):
        out_ref[k] = orbitals_ref[k] + both[k * walkers : (k + 1) * walkers]


def call(kernel, out, scratch=(), scalars=0, operands=0, flops=None):
    spaces = [pltpu.SMEM] * scalars + [pltpu.VMEM] * operands
    cost = None
    if flops is not None:
        cost = pl.CostEstimate(flops=flops, bytes_accessed=0, transcendentals=0)
    return pl.pallas_call(
        kernel,
        out_shape=out,
        in_specs=[pl.BlockSpec(memory_space=space) for space in spaces],
        out_specs=jax.tree.map(lambda _: pl.BlockSpec(memory_space=pltpu.VMEM), out),
        scratch_shapes=list(scratch),
        cost_estimate=cost,
        compiler_params=pltpu.CompilerParams(vmem_limit_bytes=24 * 2**20),
    )


def direct(green, fields, orbitals, chol_half, chol_full, chol_count, kq_map):
    k_local, pair_width, chol_cols = chol_half.shape[1], chol_half.shape[3], chol_half.shape[4]
    ka_count, pb_count = lax.axis_size("ka"), lax.axis_size("pb")
    walkers = ka_count
    kpoints = green.shape[3]
    span = k_local * walkers
    shape = jax.ShapeDtypeStruct
    tiles = chol_cols // LANES
    own_green = green.reshape(kpoints, 2 * pair_width)
    greens = exchange(own_green, "ka", GREEN_ROUNDS)
    half = chol_half.reshape(k_local, 2, pair_width, chol_cols)
    full = jnp.transpose(
        chol_full.reshape(k_local, 2, M * M, tiles, LANES), (0, 2, 3, 1, 4)
    ).reshape(k_local, M * M * tiles * 2, LANES)
    own_fields = fields.reshape(walkers, chol_cols)
    own_orbitals = orbitals.reshape(k_local, walkers, 2 * pair_width)
    mask, picks = call(
        functools.partial(prepare_kernel, ka_count, pb_count, walkers),
        (shape((2 * walkers, chol_cols), F32), shape((LANES, 2 * LANES), BF16)),
        scalars=2,
        flops=10**9,
    )(kq_map, chol_count)
    bias, own = call(
        functools.partial(bias_kernel, ka_count, k_local),
        (
            shape((2 * walkers + span, chol_cols), F32),
            shape((k_local, 2 * walkers, pair_width), F32),
        ),
        [pltpu.VMEM((walkers, kpoints, 2 * pair_width), F32)],
        operands=len(greens) + 3,
    )(*greens, half, own_orbitals, mask)
    parts = exchange(bias, "ka", BIAS_ROUNDS)
    shares = call(
        functools.partial(exchange_kernel, k_local),
        shape((walkers, LANES), F32),
        operands=3,
    )(own, half, mask)
    width = -(-(M * M + 3) // LANES) * LANES
    blocks = call(
        functools.partial(operator_kernel, k_local),
        shape((ka_count * pb_count, 2 * span, width), BF16),
        [pltpu.VMEM((2 * M * M * tiles, LANES), F32), pltpu.VMEM((width, LANES), F32)],
        operands=len(parts) + 4,
    )(*parts, own_fields, mask, shares, full)
    group = operator_group(ka_count, pb_count)
    blocks = lax.all_to_all(
        blocks, ("pb", "ka"), 0, 0, axis_index_groups=[group], tiled=True
    )
    propagated, energy = call(
        functools.partial(taylor_kernel, pb_count, float(pb_count * chol_cols)),
        (shape((k_local, walkers, 2 * pair_width), F32), shape((1, 1), F32)),
        [
            pltpu.VMEM((width, LANES), F32),
            pltpu.VMEM((NOCC * ROWS, 2 * LANES), F32),
            pltpu.VMEM((LANES, LANES), F32),
        ],
        operands=len(parts) + 3,
    )(blocks, *parts, picks, own_orbitals)
    return (propagated[None], energy)


def on_device(green, fields, orbitals, chol_half, chol_full, chol_count, kq_map):
    ka_count, pb_count = lax.axis_size("ka"), lax.axis_size("pb")
    walkers = orbitals.shape[2]
    fits = 2 * pb_count * kq_map.shape[1] * walkers == LANES
    fits = fits and chol_half.shape[1] * walkers == 8 and chol_half.shape[4] == 2 * LANES
    fits = fits and ka_count == 4
    if fits and chol_half.shape[0] == 1 and walkers == ka_count:
        return direct(green, fields, orbitals, chol_half, chol_full, chol_count, kq_map)
    return with_collectives(green, fields, orbitals, chol_half, chol_full, chol_count, kq_map)


def solution(mesh):
    placed = (
        P("wa", ("grp", "ka"), "pb", None, None),
        P("wa", "pb", "grp", None),
        P("wa", "ka", "grp", None),
        P("pb", "ka", None, None, None),
        P("pb", "ka", None, None, None),
        P(),
        P(),
    )
    return jax.shard_map(
        on_device,
        mesh=mesh,
        in_specs=placed,
        out_specs=(P("wa", "ka", "grp", None), P("wa", ("grp", "ka"))),
        check_vma=False,
    )
```

```python
import functools

import jax
import jax.numpy as jnp
from jax import lax
from jax.experimental import pallas as pl
from jax.experimental.pallas import tpu as pltpu
from jax.sharding import PartitionSpec as P

M = 26
NOCC = 4
TAYLOR = 3
LANES = 128
ROWS = 32

GREEN_ROUNDS = (
    ((3, 0), (2, 1), (1, 3), (0, 2)),
    ((3, 1), (2, 0), (0, 3), (1, 2)),
    ((1, 0), (3, 2), (2, 3), (0, 1)),
)[::-1]
BIAS_ROUNDS = (
    ((0, 1), (1, 3), (2, 0), (3, 2)),
    ((0, 3), (3, 0), (1, 2), (2, 1)),
    ((0, 2), (1, 0), (2, 3), (3, 1)),
)[::-1]


BIAS_STEP = 0.5
PROP_STEP = 0.5

F32 = jnp.float32
BF16 = jnp.bfloat16


def complex_dot(pattern, left_re, left_im, right_re, right_im):
    real_part = jnp.einsum(
        pattern, left_re, right_re, preferred_element_type=jnp.float32
    ) - jnp.einsum(pattern, left_im, right_im, preferred_element_type=jnp.float32)
    imag_part = jnp.einsum(
        pattern, left_re, right_im, preferred_element_type=jnp.float32
    ) + jnp.einsum(pattern, left_im, right_re, preferred_element_type=jnp.float32)
    return (real_part, imag_part)


def make_picker(wanted):

    def picker(shard_rows):
        row_count = shard_rows.shape[0]
        select = (wanted[:, None] == jnp.arange(row_count, dtype=jnp.int32)[None, :]).astype(
            jnp.bfloat16
        )
        return jnp.dot(select, shard_rows, preferred_element_type=jnp.float32)

    return picker


def with_collectives(green, fields, orbitals, chol_half, chol_full, chol_count, kq_map):
    q_local = chol_half.shape[0]
    k_local = chol_half.shape[1]
    pair_width = chol_half.shape[3]
    chol_cols = chol_half.shape[4]
    ka_count = lax.axis_size("ka")
    pb_count = lax.axis_size("pb")
    ka_pos = lax.axis_index("ka")
    pb_pos = lax.axis_index("pb")
    local_green = lax.all_to_all(green, "ka", split_axis=3, concat_axis=1, tiled=True)
    walkers = local_green.shape[1]
    per_device = walkers // ka_count
    greens = local_green[0].reshape(walkers, q_local, k_local, 2, pair_width)
    counts = lax.dynamic_slice_in_dim(chol_count, pb_pos * q_local, q_local)
    vec_mask = (jnp.arange(chol_cols, dtype=jnp.int32)[None, :] < counts[:, None]).astype(
        jnp.float32
    )
    bias_re, bias_im = complex_dot(
        "wqkx,qkxn->qwn",
        greens[:, :, :, 0],
        greens[:, :, :, 1],
        chol_half[:, :, 0],
        chol_half[:, :, 1],
    )
    own_rows = (jnp.arange(walkers, dtype=jnp.int32) // per_device == ka_pos).astype(jnp.float32)
    bias_re, bias_im = lax.psum((bias_re, bias_im), "ka")
    bias_re = bias_re * vec_mask[:, None, :]
    bias_im = bias_im * vec_mask[:, None, :]
    hartree = 0.5 * jnp.sum(bias_re * bias_re + bias_im * bias_im, axis=(0, 2)) * own_rows
    field_now = jnp.transpose(fields, (1, 0, 2, 3)).reshape(q_local, walkers, chol_cols)
    shift_re = ((field_now - BIAS_STEP * bias_re) * vec_mask[:, None, :]).astype(jnp.bfloat16)
    shift_im = (-BIAS_STEP * bias_im * vec_mask[:, None, :]).astype(jnp.bfloat16)
    exchange = jnp.zeros((walkers,), jnp.float32)
    for transfer in range(q_local):
        for kpoint in range(k_local):
            chol_row = chol_half[transfer, kpoint].reshape(2, NOCC, M, chol_cols)
            green_row = greens[:, transfer, kpoint].reshape(walkers, 2, NOCC, M)
            cross_re, cross_im = complex_dot(
                "ipn,wjp->wijn", chol_row[0], chol_row[1], green_row[:, 0], green_row[:, 1]
            )
            exchange = exchange + 0.5 * jnp.sum(
                (cross_re * cross_re + cross_im * cross_im) * vec_mask[transfer], axis=(1, 2, 3)
            )
    prop_re, prop_im = complex_dot(
        "qwn,qkyn->qwky", shift_re, shift_im, chol_full[:, :, 0], chol_full[:, :, 1]
    )
    shape = (q_local, walkers, k_local, M, M)
    oper_re = (PROP_STEP * prop_re).astype(jnp.bfloat16).reshape(shape)
    oper_im = (PROP_STEP * prop_im).astype(jnp.bfloat16).reshape(shape)
    normalizer = q_local * pb_count * chol_cols
    total_energy = lax.psum(hartree - exchange, ("ka", "pb")) / normalizer
    energy = lax.dynamic_slice_in_dim(total_energy, ka_pos * per_device, per_device).reshape(
        1, per_device
    )
    initial = orbitals[0].reshape(k_local, walkers, 2, NOCC, M)
    row_width = 2 * pair_width
    my_rows = lax.dynamic_slice_in_dim(kq_map, pb_pos * q_local, q_local, 0)
    wanted = lax.dynamic_slice_in_dim(my_rows, ka_pos * k_local, k_local, 1).reshape(
        q_local * k_local
    )
    picker = make_picker(wanted)
    current = initial
    summed_terms = initial
    for degree in range(1, TAYLOR + 1):
        rounded = current.astype(jnp.bfloat16).reshape(k_local, walkers * row_width)
        fetched = picker(lax.all_gather(rounded, "ka", axis=0, tiled=True))
        shifted_rows = fetched.astype(jnp.bfloat16).reshape(q_local, k_local, walkers, 2, NOCC, M)
        out_re, out_im = complex_dot(
            "xwkpq,xkwiq->kwip",
            oper_re,
            oper_im,
            shifted_rows[:, :, :, 0],
            shifted_rows[:, :, :, 1],
        )
        applied = jnp.stack([out_re, out_im], axis=2)
        applied = lax.psum(applied, "pb")
        current = applied / degree
        summed_terms = summed_terms + current
    propagated = summed_terms.reshape(1, k_local, walkers, row_width)
    return (propagated, energy)


def exchange(array, axis, rounds):
    return [array] + [lax.ppermute(array, axis, pairs) for pairs in rounds]


def origins(axis, rounds):
    at = lax.axis_index(axis)
    found = [at]
    for pairs in rounds:
        source = jnp.int32(0)
        for sender, receiver in pairs:
            source = jnp.where(at == receiver, sender, source)
        found.append(source)
    return found


def operator_group(ka_count, pb_count):
    first = (pb_count - 1) * ka_count + ka_count // 2
    rest = [at for at in range(pb_count * ka_count) if at != first]
    return [first] + rest[::-1]


def prepare_kernel(ka_count, pb_count, walkers, map_ref, count_ref, mask_ref, picks_ref):
    kept = count_ref[lax.axis_index("pb")]
    column = lax.broadcasted_iota(jnp.int32, mask_ref.shape, 1)
    mask_ref[...] = jnp.where(column < kept, 1.0, 0.0)
    kpoints = map_ref.shape[1]
    k_local = kpoints // ka_count
    span = k_local * walkers
    lane = lax.broadcasted_iota(jnp.int32, (1, LANES), 1)
    lane_q = lane // (LANES // pb_count)
    lane_ka = lax.rem(lane, LANES // pb_count) // (2 * span)
    lane_part = lax.rem(lane, 2 * span) // span
    lane_k = lane_ka * k_local + lax.rem(lane, span) // walkers
    wanted = jnp.zeros((1, LANES), jnp.int32)
    for q in range(pb_count):
        for k in range(kpoints):
            source = map_ref[q, k]
            source = source // k_local * (2 * span) + lax.rem(source, k_local) * walkers
            wanted = jnp.where((lane_q == q) & (lane_k == k), source, wanted)
    wanted = wanted + lax.rem(lane, walkers)
    row = lax.broadcasted_iota(jnp.int32, (LANES, LANES), 0)
    real = jnp.where(row == wanted, 1.0, 0.0)
    imag = jnp.where(row == wanted + span, jnp.where(lane_part == 0, 1.0, -1.0), 0.0)
    picks_ref[...] = jnp.concatenate([real, imag], axis=1).astype(BF16)


def bias_kernel(ka_count, k_local, *refs):
    *greens, chol_ref, orbitals_ref, mask_ref, bias_ref, own_ref, table = refs
    for source, green_ref in zip(origins("ka", GREEN_ROUNDS), greens):
        table[source] = green_ref[...].astype(F32)
    first = lax.axis_index("ka") * k_local
    width = chol_ref.shape[2]
    rows = 2 * ka_count
    total = jnp.zeros((rows, bias_ref.shape[1]), F32)
    for k in range(k_local):
        green = jnp.concatenate(
            [table[w, pl.ds(first + k, 1), :] for w in range(ka_count)], axis=0
        )
        real, imag = green[:, :width], green[:, width:]
        both = jnp.concatenate([real, imag], axis=0)
        turned = jnp.concatenate([-imag, real], axis=0)
        own_ref[k] = both
        total += jnp.dot(both.astype(BF16), chol_ref[k, 0], preferred_element_type=F32)
        total += jnp.dot(turned.astype(BF16), chol_ref[k, 1], preferred_element_type=F32)
    bias_ref[:rows] = total * mask_ref[...]
    window = jnp.concatenate([orbitals_ref[k] for k in range(k_local)], axis=0)
    count, width = window.shape
    bias_ref[rows : rows + count, :width] = window
    bias_ref[rows : rows + count, width:] = jnp.zeros((count, bias_ref.shape[1] - width), F32)


def exchange_kernel(k_local, own_ref, chol_ref, mask_ref, out_ref):
    walkers, width, columns = own_ref.shape[1] // 2, own_ref.shape[2], chol_ref.shape[3]
    rows = 2 * walkers
    lane = lax.broadcasted_iota(jnp.int32, (rows, LANES), 1)
    total = jnp.zeros((rows, columns), F32)
    for k in range(k_local):
        both = jnp.concatenate([own_ref[k], jnp.zeros((rows, LANES - width), F32)], axis=1)
        turned = jnp.concatenate([-both[walkers:], both[:walkers]], axis=0)
        sides = []
        for side in (both, turned):
            rolled = {
                step: side if step == 0 else pltpu.roll(side, (step * M) % LANES, 1)
                for step in range(1 - NOCC, NOCC)
            }
            blocks = []
            for i in range(NOCC):
                inside = (lane >= i * M) & (lane < (i + 1) * M)
                for j in range(NOCC):
                    blocks.append(jnp.where(inside, rolled[i - j], 0.0))
            sides.append(jnp.concatenate(blocks, axis=0)[:, :width].astype(BF16))
        cross = jnp.dot(sides[0], chol_ref[k, 0], preferred_element_type=F32)
        cross += jnp.dot(sides[1], chol_ref[k, 1], preferred_element_type=F32)
        cross = cross * cross
        for block in range(NOCC * NOCC):
            total += cross[block * rows : (block + 1) * rows]
    total = total * mask_ref[:rows]
    total = total[:walkers] + total[walkers:]
    summed = 0.5 * jnp.sum(total, axis=1, keepdims=True)
    out_ref[...] = jnp.broadcast_to(summed, out_ref.shape)


def operator_kernel(k_local, *refs):
    *parts, fields_ref, mask_ref, exchange_ref, chol_ref, out_ref, products, turned_ref = refs
    walkers, columns = fields_ref.shape
    bias = parts[0][: 2 * walkers]
    for part in parts[1:]:
        bias = bias + part[: 2 * walkers]
    pairs = M * M
    tiles = columns // LANES
    group = LANES // (2 * tiles)
    bias_re, bias_im = bias[:walkers], bias[walkers:]
    hartree = 0.5 * jnp.sum(bias_re * bias_re + bias_im * bias_im, axis=1, keepdims=True)
    own = lax.broadcasted_iota(jnp.int32, (walkers, 1), 0) == lax.axis_index("ka")
    energy = jnp.where(own, hartree, 0.0) - exchange_ref[:, :1]
    kept = mask_ref[:walkers]
    shift_re = (fields_ref[...] - BIAS_STEP * bias_re) * kept
    shift_im = -BIAS_STEP * bias_im * kept
    span = k_local * walkers
    weights = []
    for k in range(k_local):
        before, after = k * walkers, span - (k + 1) * walkers
        pieces = []
        for tile in range(tiles):
            at = slice(tile * LANES, (tile + 1) * LANES)
            for first, second in ((shift_re, shift_im), (-shift_im, shift_re)):
                for side in (first, second):
                    pieces += [(before, None), (walkers, side[:, at]), (after, None)]
                pieces.append((group - 2 * span, None))
        weights.append(
            jnp.concatenate(
                [jnp.zeros((n, LANES), F32) if p is None else p for n, p in pieces if n], axis=0
            ).astype(BF16)
        )
    products[...] = lax.dot_general(
        jnp.concatenate([chol_ref[k] for k in range(k_local)], axis=1),
        jnp.concatenate(weights, axis=1),
        (((1,), (1,)), ((), ())),
        preferred_element_type=F32,
    )
    lane = lax.broadcasted_iota(jnp.int32, (pairs, LANES), 1)
    merged = products[pl.ds(0, pairs, stride=2 * tiles), :]
    for at in range(1, 2 * tiles):
        row = products[pl.ds(at, pairs, stride=2 * tiles), :]
        merged = jnp.where(lane >= at * group, row, merged)
    turned_ref[:pairs] = merged
    copies, rows, width = out_ref.shape
    lane = lax.broadcasted_iota(jnp.int32, (rows, LANES), 1)
    for at in range(0, width, LANES):
        block = turned_ref[at : at + LANES].T
        block = PROP_STEP * sum(block[n * group : n * group + rows] for n in range(2 * tiles))
        if at + LANES > pairs:
            share = jnp.concatenate([energy, jnp.zeros((rows - walkers, 1), F32)], axis=0)
            block = jnp.where(lane + at < pairs, block, 0.0)
            for piece in range(3):
                head = share.astype(BF16).astype(F32)
                block = jnp.where(lane + at == pairs + piece, head, block)
                share = share - head
        for copy in range(copies):
            out_ref[copy, :, at : at + LANES] = block.astype(BF16)


def taylor_kernel(pb_count, normalizer, blocks_ref, *refs):
    *windows, picks_ref, orbitals_ref, out_ref, energy_ref, turned, straight, crossed, term = refs
    pairs = M * M
    pair = NOCC * M
    k_local, walkers, _ = out_ref.shape
    span = k_local * walkers
    ka_pos = lax.axis_index("ka")
    picks = picks_ref[...]

    def pick(rows):
        both = jnp.dot(rows.astype(BF16), picks, preferred_element_type=F32)
        return both[:, :LANES], both[:, LANES:]

    term[...] = jnp.zeros_like(term)
    for source, window_ref in zip(origins("ka", BIAS_ROUNDS), windows):
        start = pl.multiple_of(source * (2 * span), 2 * span)
        window = window_ref[window_ref.shape[0] - span :]
        term[pl.ds(start, span), :pair] = window[:, :pair]
        term[pl.ds(start + span, span), :pair] = window[:, pair : 2 * pair]
    real, imag = pick(term[:LANES].T)
    straight[:LANES] = real
    crossed[:LANES] = imag
    count, _, width = blocks_ref.shape
    group = operator_group(count // pb_count, pb_count)
    places = [group.index(n) for n in range(count)]
    for at in range(0, width, LANES):
        tile = jnp.concatenate([blocks_ref[n, :, at : at + LANES] for n in places], axis=0)
        turned[at : at + LANES] = tile.T.astype(F32)
    shares = turned[pairs : pairs + 3]
    lane = lax.broadcasted_iota(jnp.int32, shares.shape, 1)
    shares = jnp.where(lax.rem(lane, 2 * span) == ka_pos, shares, 0.0)
    shares = jnp.sum(jnp.sum(shares, axis=0, keepdims=True), axis=1, keepdims=True)
    energy_ref[...] = shares / normalizer
    tall = 2 * NOCC
    lane = lax.broadcasted_iota(jnp.int32, (tall, LANES), 1)
    imaginary = lax.rem(lane, 2 * span) >= span
    upper = lax.broadcasted_iota(jnp.int32, (tall, LANES), 0) < NOCC
    columns = [
        jnp.concatenate(
            [straight[pl.ds(c, NOCC, stride=M), :], crossed[pl.ds(c, NOCC, stride=M), :]], axis=0
        )
        for c in range(M)
    ]
    for degree in range(1, TAYLOR + 1):
        for p in range(M):
            halves = [None, None]
            for c in range(M):
                row = turned[p * M + c : p * M + c + 1, :]
                product = jnp.broadcast_to(row, (tall, LANES)) * columns[c]
                half = halves[c % 2]
                halves[c % 2] = product if half is None else half + product
            applied = halves[0] + halves[1]
            other = jnp.where(
                imaginary, pltpu.roll(applied, span, 1), pltpu.roll(applied, LANES - span, 1)
            )
            applied = jnp.where(upper, applied, other)
            applied = applied + pltpu.roll(applied, NOCC, 0)
            applied = applied + pltpu.roll(applied, LANES // pb_count, 1)
            current = applied / degree
            at = slice(p * tall, (p + 1) * tall)
            if degree == 1:
                straight[at] = current
            else:
                straight[at] += current
            if degree < TAYLOR:
                term[at] = current
        if degree < TAYLOR:
            real, imag = pick(term[...])
            columns = [
                jnp.where(upper, real[c * tall : (c + 1) * tall], imag[c * tall : (c + 1) * tall])
                for c in range(M)
            ]
    for i in range(NOCC):
        term[i * ROWS : i * ROWS + M] = straight[pl.ds(i, M, stride=tall), :]
    turned[:LANES] = term[:LANES].T
    both = turned[pl.ds(pl.multiple_of(ka_pos * (2 * span), 2 * span), 2 * span), :]
    both = jnp.concatenate([both[:, i * ROWS : i * ROWS + M] for i in range(NOCC)], axis=1)
    both = jnp.concatenate([both[:span], both[span:]], axis=1)
    for k in range(k_local):
        out_ref[k] = orbitals_ref[k] + both[k * walkers : (k + 1) * walkers]


def call(kernel, out, scratch=(), scalars=0, operands=0, flops=None):
    spaces = [pltpu.SMEM] * scalars + [pltpu.VMEM] * operands
    cost = None
    if flops is not None:
        cost = pl.CostEstimate(flops=flops, bytes_accessed=0, transcendentals=0)
    return pl.pallas_call(
        kernel,
        out_shape=out,
        in_specs=[pl.BlockSpec(memory_space=space) for space in spaces],
        out_specs=jax.tree.map(lambda _: pl.BlockSpec(memory_space=pltpu.VMEM), out),
        scratch_shapes=list(scratch),
        cost_estimate=cost,
        compiler_params=pltpu.CompilerParams(vmem_limit_bytes=24 * 2**20),
    )


def direct(green, fields, orbitals, chol_half, chol_full, chol_count, kq_map):
    k_local, pair_width, chol_cols = chol_half.shape[1], chol_half.shape[3], chol_half.shape[4]
    ka_count, pb_count = lax.axis_size("ka"), lax.axis_size("pb")
    walkers = ka_count
    kpoints = green.shape[3]
    span = k_local * walkers
    shape = jax.ShapeDtypeStruct
    tiles = chol_cols // LANES
    own_green = green.reshape(kpoints, 2 * pair_width)
    greens = exchange(own_green, "ka", GREEN_ROUNDS)
    half = chol_half.reshape(k_local, 2, pair_width, chol_cols)
    full = jnp.transpose(
        chol_full.reshape(k_local, 2, M * M, tiles, LANES), (0, 2, 3, 1, 4)
    ).reshape(k_local, M * M * tiles * 2, LANES)
    own_fields = fields.reshape(walkers, chol_cols)
    own_orbitals = orbitals.reshape(k_local, walkers, 2 * pair_width)
    mask, picks = call(
        functools.partial(prepare_kernel, ka_count, pb_count, walkers),
        (shape((2 * walkers, chol_cols), F32), shape((LANES, 2 * LANES), BF16)),
        scalars=2,
        flops=10**9,
    )(kq_map, chol_count)
    bias, own = call(
        functools.partial(bias_kernel, ka_count, k_local),
        (
            shape((2 * walkers + span, chol_cols), F32),
            shape((k_local, 2 * walkers, pair_width), F32),
        ),
        [pltpu.VMEM((walkers, kpoints, 2 * pair_width), F32)],
        operands=len(greens) + 3,
    )(*greens, half, own_orbitals, mask)
    parts = exchange(bias, "ka", BIAS_ROUNDS)
    shares = call(
        functools.partial(exchange_kernel, k_local),
        shape((walkers, LANES), F32),
        operands=3,
    )(own, half, mask)
    width = -(-(M * M + 3) // LANES) * LANES
    blocks = call(
        functools.partial(operator_kernel, k_local),
        shape((ka_count * pb_count, 2 * span, width), BF16),
        [pltpu.VMEM((2 * M * M * tiles, LANES), F32), pltpu.VMEM((width, LANES), F32)],
        operands=len(parts) + 4,
    )(*parts, own_fields, mask, shares, full)
    group = operator_group(ka_count, pb_count)
    blocks = lax.all_to_all(
        blocks, ("pb", "ka"), 0, 0, axis_index_groups=[group], tiled=True
    )
    propagated, energy = call(
        functools.partial(taylor_kernel, pb_count, float(pb_count * chol_cols)),
        (shape((k_local, walkers, 2 * pair_width), F32), shape((1, 1), F32)),
        [
            pltpu.VMEM((width, LANES), F32),
            *[pltpu.VMEM((2 * NOCC * M, LANES), F32)] * 3,
        ],
        operands=len(parts) + 3,
    )(blocks, *parts, picks, own_orbitals)
    return (propagated[None], energy)


def on_device(green, fields, orbitals, chol_half, chol_full, chol_count, kq_map):
    ka_count, pb_count = lax.axis_size("ka"), lax.axis_size("pb")
    walkers = orbitals.shape[2]
    fits = 2 * pb_count * kq_map.shape[1] * walkers == LANES
    fits = fits and chol_half.shape[1] * walkers == 8 and chol_half.shape[4] == 2 * LANES
    fits = fits and ka_count == 4
    if fits and chol_half.shape[0] == 1 and walkers == ka_count:
        return direct(green, fields, orbitals, chol_half, chol_full, chol_count, kq_map)
    return with_collectives(green, fields, orbitals, chol_half, chol_full, chol_count, kq_map)


def solution(mesh):
    placed = (
        P("wa", ("grp", "ka"), "pb", None, None),
        P("wa", "pb", "grp", None),
        P("wa", "ka", "grp", None),
        P("pb", "ka", None, None, None),
        P("pb", "ka", None, None, None),
        P(),
        P(),
    )
    return jax.shard_map(
        on_device,
        mesh=mesh,
        in_specs=placed,
        out_specs=(P("wa", "ka", "grp", None), P("wa", ("grp", "ka"))),
        check_vma=False,
    )
```

```python
import functools

import jax
import jax.numpy as jnp
from jax import lax
from jax.experimental import pallas as pl
from jax.experimental.pallas import tpu as pltpu
from jax.sharding import PartitionSpec as P

M = 26
NOCC = 4
TAYLOR = 3
LANES = 128
ROWS = 32

GREEN_ROUNDS = (
    ((3, 0), (2, 1), (1, 3), (0, 2)),
    ((3, 1), (2, 0), (0, 3), (1, 2)),
    ((1, 0), (3, 2), (2, 3), (0, 1)),
)[::-1]
BIAS_ROUNDS = (
    ((0, 1), (1, 3), (2, 0), (3, 2)),
    ((0, 3), (3, 0), (1, 2), (2, 1)),
    ((0, 2), (1, 0), (2, 3), (3, 1)),
)[::-1]


BIAS_STEP = 0.5
PROP_STEP = 0.5

F32 = jnp.float32
BF16 = jnp.bfloat16


def complex_dot(pattern, left_re, left_im, right_re, right_im):
    real_part = jnp.einsum(
        pattern, left_re, right_re, preferred_element_type=jnp.float32
    ) - jnp.einsum(pattern, left_im, right_im, preferred_element_type=jnp.float32)
    imag_part = jnp.einsum(
        pattern, left_re, right_im, preferred_element_type=jnp.float32
    ) + jnp.einsum(pattern, left_im, right_re, preferred_element_type=jnp.float32)
    return (real_part, imag_part)


def make_picker(wanted):

    def picker(shard_rows):
        row_count = shard_rows.shape[0]
        select = (wanted[:, None] == jnp.arange(row_count, dtype=jnp.int32)[None, :]).astype(
            jnp.bfloat16
        )
        return jnp.dot(select, shard_rows, preferred_element_type=jnp.float32)

    return picker


def with_collectives(green, fields, orbitals, chol_half, chol_full, chol_count, kq_map):
    q_local = chol_half.shape[0]
    k_local = chol_half.shape[1]
    pair_width = chol_half.shape[3]
    chol_cols = chol_half.shape[4]
    ka_count = lax.axis_size("ka")
    pb_count = lax.axis_size("pb")
    ka_pos = lax.axis_index("ka")
    pb_pos = lax.axis_index("pb")
    local_green = lax.all_to_all(green, "ka", split_axis=3, concat_axis=1, tiled=True)
    walkers = local_green.shape[1]
    per_device = walkers // ka_count
    greens = local_green[0].reshape(walkers, q_local, k_local, 2, pair_width)
    counts = lax.dynamic_slice_in_dim(chol_count, pb_pos * q_local, q_local)
    vec_mask = (jnp.arange(chol_cols, dtype=jnp.int32)[None, :] < counts[:, None]).astype(
        jnp.float32
    )
    bias_re, bias_im = complex_dot(
        "wqkx,qkxn->qwn",
        greens[:, :, :, 0],
        greens[:, :, :, 1],
        chol_half[:, :, 0],
        chol_half[:, :, 1],
    )
    own_rows = (jnp.arange(walkers, dtype=jnp.int32) // per_device == ka_pos).astype(jnp.float32)
    bias_re, bias_im = lax.psum((bias_re, bias_im), "ka")
    bias_re = bias_re * vec_mask[:, None, :]
    bias_im = bias_im * vec_mask[:, None, :]
    hartree = 0.5 * jnp.sum(bias_re * bias_re + bias_im * bias_im, axis=(0, 2)) * own_rows
    field_now = jnp.transpose(fields, (1, 0, 2, 3)).reshape(q_local, walkers, chol_cols)
    shift_re = ((field_now - BIAS_STEP * bias_re) * vec_mask[:, None, :]).astype(jnp.bfloat16)
    shift_im = (-BIAS_STEP * bias_im * vec_mask[:, None, :]).astype(jnp.bfloat16)
    exchange = jnp.zeros((walkers,), jnp.float32)
    for transfer in range(q_local):
        for kpoint in range(k_local):
            chol_row = chol_half[transfer, kpoint].reshape(2, NOCC, M, chol_cols)
            green_row = greens[:, transfer, kpoint].reshape(walkers, 2, NOCC, M)
            cross_re, cross_im = complex_dot(
                "ipn,wjp->wijn", chol_row[0], chol_row[1], green_row[:, 0], green_row[:, 1]
            )
            exchange = exchange + 0.5 * jnp.sum(
                (cross_re * cross_re + cross_im * cross_im) * vec_mask[transfer], axis=(1, 2, 3)
            )
    prop_re, prop_im = complex_dot(
        "qwn,qkyn->qwky", shift_re, shift_im, chol_full[:, :, 0], chol_full[:, :, 1]
    )
    shape = (q_local, walkers, k_local, M, M)
    oper_re = (PROP_STEP * prop_re).astype(jnp.bfloat16).reshape(shape)
    oper_im = (PROP_STEP * prop_im).astype(jnp.bfloat16).reshape(shape)
    normalizer = q_local * pb_count * chol_cols
    total_energy = lax.psum(hartree - exchange, ("ka", "pb")) / normalizer
    energy = lax.dynamic_slice_in_dim(total_energy, ka_pos * per_device, per_device).reshape(
        1, per_device
    )
    initial = orbitals[0].reshape(k_local, walkers, 2, NOCC, M)
    row_width = 2 * pair_width
    my_rows = lax.dynamic_slice_in_dim(kq_map, pb_pos * q_local, q_local, 0)
    wanted = lax.dynamic_slice_in_dim(my_rows, ka_pos * k_local, k_local, 1).reshape(
        q_local * k_local
    )
    picker = make_picker(wanted)
    current = initial
    summed_terms = initial
    for degree in range(1, TAYLOR + 1):
        rounded = current.astype(jnp.bfloat16).reshape(k_local, walkers * row_width)
        fetched = picker(lax.all_gather(rounded, "ka", axis=0, tiled=True))
        shifted_rows = fetched.astype(jnp.bfloat16).reshape(q_local, k_local, walkers, 2, NOCC, M)
        out_re, out_im = complex_dot(
            "xwkpq,xkwiq->kwip",
            oper_re,
            oper_im,
            shifted_rows[:, :, :, 0],
            shifted_rows[:, :, :, 1],
        )
        applied = jnp.stack([out_re, out_im], axis=2)
        applied = lax.psum(applied, "pb")
        current = applied / degree
        summed_terms = summed_terms + current
    propagated = summed_terms.reshape(1, k_local, walkers, row_width)
    return (propagated, energy)


def exchange(array, axis, rounds):
    return [array] + [lax.ppermute(array, axis, pairs) for pairs in rounds]


def origins(axis, rounds):
    at = lax.axis_index(axis)
    found = [at]
    for pairs in rounds:
        source = jnp.int32(0)
        for sender, receiver in pairs:
            source = jnp.where(at == receiver, sender, source)
        found.append(source)
    return found


def operator_group(ka_count, pb_count):
    first = (pb_count - 1) * ka_count + ka_count // 2
    rest = [at for at in range(pb_count * ka_count) if at != first]
    return [first] + rest


def prepare_kernel(ka_count, pb_count, walkers, map_ref, count_ref, mask_ref, picks_ref):
    kept = count_ref[lax.axis_index("pb")]
    column = lax.broadcasted_iota(jnp.int32, mask_ref.shape, 1)
    mask_ref[...] = jnp.where(column < kept, 1.0, 0.0)
    kpoints = map_ref.shape[1]
    k_local = kpoints // ka_count
    span = k_local * walkers
    lane = lax.broadcasted_iota(jnp.int32, (1, LANES), 1)
    lane_q = lane // (LANES // pb_count)
    lane_ka = lax.rem(lane, LANES // pb_count) // (2 * span)
    lane_part = lax.rem(lane, 2 * span) // span
    lane_k = lane_ka * k_local + lax.rem(lane, span) // walkers
    wanted = jnp.zeros((1, LANES), jnp.int32)
    for q in range(pb_count):
        for k in range(kpoints):
            source = map_ref[q, k]
            source = source // k_local * (2 * span) + lax.rem(source, k_local) * walkers
            wanted = jnp.where((lane_q == q) & (lane_k == k), source, wanted)
    wanted = wanted + lax.rem(lane, walkers)
    row = lax.broadcasted_iota(jnp.int32, (LANES, LANES), 0)
    real = jnp.where(row == wanted, 1.0, 0.0)
    imag = jnp.where(row == wanted + span, jnp.where(lane_part == 0, 1.0, -1.0), 0.0)
    picks_ref[...] = jnp.concatenate([real, imag], axis=1).astype(BF16)


def bias_kernel(ka_count, k_local, *refs):
    *greens, chol_ref, orbitals_ref, mask_ref, bias_ref, own_ref, table = refs
    for source, green_ref in zip(origins("ka", GREEN_ROUNDS), greens):
        table[source] = green_ref[...].astype(F32)
    first = lax.axis_index("ka") * k_local
    width = chol_ref.shape[2]
    rows = 2 * ka_count
    total = jnp.zeros((rows, bias_ref.shape[1]), F32)
    for k in range(k_local):
        green = jnp.concatenate(
            [table[w, pl.ds(first + k, 1), :] for w in range(ka_count)], axis=0
        )
        real, imag = green[:, :width], green[:, width:]
        both = jnp.concatenate([real, imag], axis=0)
        turned = jnp.concatenate([-imag, real], axis=0)
        own_ref[k] = both
        total += jnp.dot(both.astype(BF16), chol_ref[k, 0], preferred_element_type=F32)
        total += jnp.dot(turned.astype(BF16), chol_ref[k, 1], preferred_element_type=F32)
    bias_ref[:rows] = total * mask_ref[...]
    window = jnp.concatenate([orbitals_ref[k] for k in range(k_local)], axis=0)
    count, width = window.shape
    bias_ref[rows : rows + count, :width] = window
    bias_ref[rows : rows + count, width:] = jnp.zeros((count, bias_ref.shape[1] - width), F32)


def exchange_kernel(k_local, own_ref, chol_ref, mask_ref, out_ref):
    walkers, width, columns = own_ref.shape[1] // 2, own_ref.shape[2], chol_ref.shape[3]
    rows = 2 * walkers
    lane = lax.broadcasted_iota(jnp.int32, (rows, LANES), 1)
    total = jnp.zeros((rows, columns), F32)
    for k in range(k_local):
        both = jnp.concatenate([own_ref[k], jnp.zeros((rows, LANES - width), F32)], axis=1)
        turned = jnp.concatenate([-both[walkers:], both[:walkers]], axis=0)
        sides = []
        for side in (both, turned):
            rolled = {
                step: side if step == 0 else pltpu.roll(side, (step * M) % LANES, 1)
                for step in range(1 - NOCC, NOCC)
            }
            blocks = []
            for i in range(NOCC):
                inside = (lane >= i * M) & (lane < (i + 1) * M)
                for j in range(NOCC):
                    blocks.append(jnp.where(inside, rolled[i - j], 0.0))
            sides.append(jnp.concatenate(blocks, axis=0)[:, :width].astype(BF16))
        cross = jnp.dot(sides[0], chol_ref[k, 0], preferred_element_type=F32)
        cross += jnp.dot(sides[1], chol_ref[k, 1], preferred_element_type=F32)
        cross = cross * cross
        for block in range(NOCC * NOCC):
            total += cross[block * rows : (block + 1) * rows]
    total = total * mask_ref[:rows]
    total = total[:walkers] + total[walkers:]
    summed = 0.5 * jnp.sum(total, axis=1, keepdims=True)
    out_ref[...] = jnp.broadcast_to(summed, out_ref.shape)


def operator_kernel(k_local, *refs):
    *parts, fields_ref, mask_ref, exchange_ref, chol_ref, out_ref, products, turned_ref = refs
    walkers, columns = fields_ref.shape
    bias = parts[0][: 2 * walkers]
    for part in parts[1:]:
        bias = bias + part[: 2 * walkers]
    pairs = M * M
    tiles = columns // LANES
    group = LANES // (2 * tiles)
    bias_re, bias_im = bias[:walkers], bias[walkers:]
    hartree = 0.5 * jnp.sum(bias_re * bias_re + bias_im * bias_im, axis=1, keepdims=True)
    own = lax.broadcasted_iota(jnp.int32, (walkers, 1), 0) == lax.axis_index("ka")
    energy = jnp.where(own, hartree, 0.0) - exchange_ref[:, :1]
    kept = mask_ref[:walkers]
    shift_re = (fields_ref[...] - BIAS_STEP * bias_re) * kept
    shift_im = -BIAS_STEP * bias_im * kept
    span = k_local * walkers
    weights = []
    for k in range(k_local):
        before, after = k * walkers, span - (k + 1) * walkers
        pieces = []
        for tile in range(tiles):
            at = slice(tile * LANES, (tile + 1) * LANES)
            for first, second in ((shift_re, shift_im), (-shift_im, shift_re)):
                for side in (first, second):
                    pieces += [(before, None), (walkers, side[:, at]), (after, None)]
                pieces.append((group - 2 * span, None))
        weights.append(
            jnp.concatenate(
                [jnp.zeros((n, LANES), F32) if p is None else p for n, p in pieces if n], axis=0
            ).astype(BF16)
        )
    products[...] = lax.dot_general(
        jnp.concatenate([chol_ref[k] for k in range(k_local)], axis=1),
        jnp.concatenate(weights, axis=1),
        (((1,), (1,)), ((), ())),
        preferred_element_type=F32,
    )
    lane = lax.broadcasted_iota(jnp.int32, (pairs, LANES), 1)
    merged = products[pl.ds(0, pairs, stride=2 * tiles), :]
    for at in range(1, 2 * tiles):
        row = products[pl.ds(at, pairs, stride=2 * tiles), :]
        merged = jnp.where(lane >= at * group, row, merged)
    turned_ref[:pairs] = merged
    copies, rows, width = out_ref.shape
    lane = lax.broadcasted_iota(jnp.int32, (rows, LANES), 1)
    for at in range(0, width, LANES):
        block = turned_ref[at : at + LANES].T
        block = PROP_STEP * sum(block[n * group : n * group + rows] for n in range(2 * tiles))
        if at + LANES > pairs:
            share = jnp.concatenate([energy, jnp.zeros((rows - walkers, 1), F32)], axis=0)
            block = jnp.where(lane + at < pairs, block, 0.0)
            for piece in range(3):
                head = share.astype(BF16).astype(F32)
                block = jnp.where(lane + at == pairs + piece, head, block)
                share = share - head
        for copy in range(copies):
            out_ref[copy, :, at : at + LANES] = block.astype(BF16)


def taylor_kernel(pb_count, normalizer, blocks_ref, *refs):
    *windows, picks_ref, orbitals_ref, out_ref, energy_ref, turned, picked, term = refs
    pairs = M * M
    pair = NOCC * M
    k_local, walkers, _ = out_ref.shape
    span = k_local * walkers
    ka_pos = lax.axis_index("ka")
    term[...] = jnp.zeros_like(term)
    for source, window_ref in zip(origins("ka", BIAS_ROUNDS), windows):
        start = pl.multiple_of(source * (2 * span), 2 * span)
        window = window_ref[window_ref.shape[0] - span :]
        term[pl.ds(start, span), :pair] = window[:, :pair]
        term[pl.ds(start + span, span), :pair] = window[:, pair : 2 * pair]
    picked[...] = jnp.dot(term[...].T.astype(BF16), picks_ref[...], preferred_element_type=F32)
    count, _, width = blocks_ref.shape
    group = operator_group(count // pb_count, pb_count)
    places = [group.index(n) for n in range(count)]
    for at in range(0, width, LANES):
        tile = jnp.concatenate([blocks_ref[n, :, at : at + LANES] for n in places], axis=0)
        turned[at : at + LANES] = tile.T.astype(F32)
    shares = turned[pairs : pairs + 3]
    lane = lax.broadcasted_iota(jnp.int32, shares.shape, 1)
    shares = jnp.where(lax.rem(lane, 2 * span) == ka_pos, shares, 0.0)
    shares = jnp.sum(jnp.sum(shares, axis=0, keepdims=True), axis=1, keepdims=True)
    energy_ref[...] = shares / normalizer
    lane = lax.broadcasted_iota(jnp.int32, (M, LANES), 1)
    imaginary = lax.rem(lane, 2 * span) >= span
    sums = [jnp.zeros((M, LANES), F32) for _ in range(NOCC)]
    for degree in range(1, TAYLOR + 1):
        stride = M if degree == 1 else ROWS
        straight = [jnp.zeros((M, LANES), F32) for _ in range(NOCC)]
        crossed = [jnp.zeros((M, LANES), F32) for _ in range(NOCC)]
        for c in range(M):
            column = turned[pl.ds(c, M, stride=M), :]
            for i in range(NOCC):
                at = i * stride + c
                straight[i] += column * picked[at : at + 1, :LANES]
                crossed[i] += column * picked[at : at + 1, LANES:]
        for i in range(NOCC):
            other = jnp.where(
                imaginary, pltpu.roll(crossed[i], span, 1), pltpu.roll(crossed[i], LANES - span, 1)
            )
            applied = straight[i] + other
            applied = applied + pltpu.roll(applied, LANES // pb_count, 1)
            current = applied / degree
            sums[i] = sums[i] + current
            term[i * ROWS : i * ROWS + M] = current if degree < TAYLOR else sums[i]
        if degree < TAYLOR:
            picked[...] = jnp.dot(
                term[...].astype(BF16), picks_ref[...], preferred_element_type=F32
            )
    turned[:LANES] = term[...].T
    both = turned[pl.ds(pl.multiple_of(ka_pos * (2 * span), 2 * span), 2 * span), :]
    both = jnp.concatenate([both[:, i * ROWS : i * ROWS + M] for i in range(NOCC)], axis=1)
    both = jnp.concatenate([both[:span], both[span:]], axis=1)
    for k in range(k_local):
        out_ref[k] = orbitals_ref[k] + both[k * walkers : (k + 1) * walkers]


def call(kernel, out, scratch=(), scalars=0, operands=0, flops=None):
    spaces = [pltpu.SMEM] * scalars + [pltpu.VMEM] * operands
    cost = None
    if flops is not None:
        cost = pl.CostEstimate(flops=flops, bytes_accessed=0, transcendentals=0)
    return pl.pallas_call(
        kernel,
        out_shape=out,
        in_specs=[pl.BlockSpec(memory_space=space) for space in spaces],
        out_specs=jax.tree.map(lambda _: pl.BlockSpec(memory_space=pltpu.VMEM), out),
        scratch_shapes=list(scratch),
        cost_estimate=cost,
        compiler_params=pltpu.CompilerParams(vmem_limit_bytes=24 * 2**20),
    )


def direct(green, fields, orbitals, chol_half, chol_full, chol_count, kq_map):
    k_local, pair_width, chol_cols = chol_half.shape[1], chol_half.shape[3], chol_half.shape[4]
    ka_count, pb_count = lax.axis_size("ka"), lax.axis_size("pb")
    walkers = ka_count
    kpoints = green.shape[3]
    span = k_local * walkers
    shape = jax.ShapeDtypeStruct
    tiles = chol_cols // LANES
    own_green = green.reshape(kpoints, 2 * pair_width)
    greens = exchange(own_green, "ka", GREEN_ROUNDS)
    half = chol_half.reshape(k_local, 2, pair_width, chol_cols)
    full = jnp.transpose(
        chol_full.reshape(k_local, 2, M * M, tiles, LANES), (0, 2, 3, 1, 4)
    ).reshape(k_local, M * M * tiles * 2, LANES)
    own_fields = fields.reshape(walkers, chol_cols)
    own_orbitals = orbitals.reshape(k_local, walkers, 2 * pair_width)
    mask, picks = call(
        functools.partial(prepare_kernel, ka_count, pb_count, walkers),
        (shape((2 * walkers, chol_cols), F32), shape((LANES, 2 * LANES), BF16)),
        scalars=2,
        flops=10**9,
    )(kq_map, chol_count)
    bias, own = call(
        functools.partial(bias_kernel, ka_count, k_local),
        (
            shape((2 * walkers + span, chol_cols), F32),
            shape((k_local, 2 * walkers, pair_width), F32),
        ),
        [pltpu.VMEM((walkers, kpoints, 2 * pair_width), F32)],
        operands=len(greens) + 3,
    )(*greens, half, own_orbitals, mask)
    parts = exchange(bias, "ka", BIAS_ROUNDS)
    shares = call(
        functools.partial(exchange_kernel, k_local),
        shape((walkers, LANES), F32),
        operands=3,
    )(own, half, mask)
    width = -(-(M * M + 3) // LANES) * LANES
    blocks = call(
        functools.partial(operator_kernel, k_local),
        shape((ka_count * pb_count, 2 * span, width), BF16),
        [pltpu.VMEM((2 * M * M * tiles, LANES), F32), pltpu.VMEM((width, LANES), F32)],
        operands=len(parts) + 4,
    )(*parts, own_fields, mask, shares, full)
    group = operator_group(ka_count, pb_count)
    blocks = lax.all_to_all(
        blocks, ("pb", "ka"), 0, 0, axis_index_groups=[group], tiled=True
    )
    propagated, energy = call(
        functools.partial(taylor_kernel, pb_count, float(pb_count * chol_cols)),
        (shape((k_local, walkers, 2 * pair_width), F32), shape((1, 1), F32)),
        [
            pltpu.VMEM((width, LANES), F32),
            pltpu.VMEM((NOCC * ROWS, 2 * LANES), F32),
            pltpu.VMEM((LANES, LANES), F32),
        ],
        operands=len(parts) + 3,
    )(blocks, *parts, picks, own_orbitals)
    return (propagated[None], energy)


def on_device(green, fields, orbitals, chol_half, chol_full, chol_count, kq_map):
    ka_count, pb_count = lax.axis_size("ka"), lax.axis_size("pb")
    walkers = orbitals.shape[2]
    fits = 2 * pb_count * kq_map.shape[1] * walkers == LANES
    fits = fits and chol_half.shape[1] * walkers == 8 and chol_half.shape[4] == 2 * LANES
    fits = fits and ka_count == 4
    if fits and chol_half.shape[0] == 1 and walkers == ka_count:
        return direct(green, fields, orbitals, chol_half, chol_full, chol_count, kq_map)
    return with_collectives(green, fields, orbitals, chol_half, chol_full, chol_count, kq_map)


def solution(mesh):
    placed = (
        P("wa", ("grp", "ka"), "pb", None, None),
        P("wa", "pb", "grp", None),
        P("wa", "ka", "grp", None),
        P("pb", "ka", None, None, None),
        P("pb", "ka", None, None, None),
        P(),
        P(),
    )
    return jax.shard_map(
        on_device,
        mesh=mesh,
        in_specs=placed,
        out_specs=(P("wa", "ka", "grp", None), P("wa", ("grp", "ka"))),
        check_vma=False,
    )
```

```python
import functools

import jax
import jax.numpy as jnp
from jax import lax
from jax.experimental import pallas as pl
from jax.experimental.pallas import tpu as pltpu
from jax.sharding import PartitionSpec as P

M = 26
NOCC = 4
TAYLOR = 3
LANES = 128
ROWS = 32

GREEN_ROUNDS = (
    ((3, 0), (2, 1), (1, 3), (0, 2)),
    ((3, 1), (2, 0), (0, 3), (1, 2)),
    ((1, 0), (3, 2), (2, 3), (0, 1)),
)[::-1]
BIAS_ROUNDS = (
    ((0, 1), (1, 3), (2, 0), (3, 2)),
    ((0, 3), (3, 0), (1, 2), (2, 1)),
    ((0, 2), (1, 0), (2, 3), (3, 1)),
)[::-1]


BIAS_STEP = 0.5
PROP_STEP = 0.5

F32 = jnp.float32
BF16 = jnp.bfloat16


def complex_dot(pattern, left_re, left_im, right_re, right_im):
    real_part = jnp.einsum(
        pattern, left_re, right_re, preferred_element_type=jnp.float32
    ) - jnp.einsum(pattern, left_im, right_im, preferred_element_type=jnp.float32)
    imag_part = jnp.einsum(
        pattern, left_re, right_im, preferred_element_type=jnp.float32
    ) + jnp.einsum(pattern, left_im, right_re, preferred_element_type=jnp.float32)
    return (real_part, imag_part)


def make_picker(wanted):

    def picker(shard_rows):
        row_count = shard_rows.shape[0]
        select = (wanted[:, None] == jnp.arange(row_count, dtype=jnp.int32)[None, :]).astype(
            jnp.bfloat16
        )
        return jnp.dot(select, shard_rows, preferred_element_type=jnp.float32)

    return picker


def with_collectives(green, fields, orbitals, chol_half, chol_full, chol_count, kq_map):
    q_local = chol_half.shape[0]
    k_local = chol_half.shape[1]
    pair_width = chol_half.shape[3]
    chol_cols = chol_half.shape[4]
    ka_count = lax.axis_size("ka")
    pb_count = lax.axis_size("pb")
    ka_pos = lax.axis_index("ka")
    pb_pos = lax.axis_index("pb")
    local_green = lax.all_to_all(green, "ka", split_axis=3, concat_axis=1, tiled=True)
    walkers = local_green.shape[1]
    per_device = walkers // ka_count
    greens = local_green[0].reshape(walkers, q_local, k_local, 2, pair_width)
    counts = lax.dynamic_slice_in_dim(chol_count, pb_pos * q_local, q_local)
    vec_mask = (jnp.arange(chol_cols, dtype=jnp.int32)[None, :] < counts[:, None]).astype(
        jnp.float32
    )
    bias_re, bias_im = complex_dot(
        "wqkx,qkxn->qwn",
        greens[:, :, :, 0],
        greens[:, :, :, 1],
        chol_half[:, :, 0],
        chol_half[:, :, 1],
    )
    own_rows = (jnp.arange(walkers, dtype=jnp.int32) // per_device == ka_pos).astype(jnp.float32)
    bias_re, bias_im = lax.psum((bias_re, bias_im), "ka")
    bias_re = bias_re * vec_mask[:, None, :]
    bias_im = bias_im * vec_mask[:, None, :]
    hartree = 0.5 * jnp.sum(bias_re * bias_re + bias_im * bias_im, axis=(0, 2)) * own_rows
    field_now = jnp.transpose(fields, (1, 0, 2, 3)).reshape(q_local, walkers, chol_cols)
    shift_re = ((field_now - BIAS_STEP * bias_re) * vec_mask[:, None, :]).astype(jnp.bfloat16)
    shift_im = (-BIAS_STEP * bias_im * vec_mask[:, None, :]).astype(jnp.bfloat16)
    exchange = jnp.zeros((walkers,), jnp.float32)
    for transfer in range(q_local):
        for kpoint in range(k_local):
            chol_row = chol_half[transfer, kpoint].reshape(2, NOCC, M, chol_cols)
            green_row = greens[:, transfer, kpoint].reshape(walkers, 2, NOCC, M)
            cross_re, cross_im = complex_dot(
                "ipn,wjp->wijn", chol_row[0], chol_row[1], green_row[:, 0], green_row[:, 1]
            )
            exchange = exchange + 0.5 * jnp.sum(
                (cross_re * cross_re + cross_im * cross_im) * vec_mask[transfer], axis=(1, 2, 3)
            )
    prop_re, prop_im = complex_dot(
        "qwn,qkyn->qwky", shift_re, shift_im, chol_full[:, :, 0], chol_full[:, :, 1]
    )
    shape = (q_local, walkers, k_local, M, M)
    oper_re = (PROP_STEP * prop_re).astype(jnp.bfloat16).reshape(shape)
    oper_im = (PROP_STEP * prop_im).astype(jnp.bfloat16).reshape(shape)
    normalizer = q_local * pb_count * chol_cols
    total_energy = lax.psum(hartree - exchange, ("ka", "pb")) / normalizer
    energy = lax.dynamic_slice_in_dim(total_energy, ka_pos * per_device, per_device).reshape(
        1, per_device
    )
    initial = orbitals[0].reshape(k_local, walkers, 2, NOCC, M)
    row_width = 2 * pair_width
    my_rows = lax.dynamic_slice_in_dim(kq_map, pb_pos * q_local, q_local, 0)
    wanted = lax.dynamic_slice_in_dim(my_rows, ka_pos * k_local, k_local, 1).reshape(
        q_local * k_local
    )
    picker = make_picker(wanted)
    current = initial
    summed_terms = initial
    for degree in range(1, TAYLOR + 1):
        rounded = current.astype(jnp.bfloat16).reshape(k_local, walkers * row_width)
        fetched = picker(lax.all_gather(rounded, "ka", axis=0, tiled=True))
        shifted_rows = fetched.astype(jnp.bfloat16).reshape(q_local, k_local, walkers, 2, NOCC, M)
        out_re, out_im = complex_dot(
            "xwkpq,xkwiq->kwip",
            oper_re,
            oper_im,
            shifted_rows[:, :, :, 0],
            shifted_rows[:, :, :, 1],
        )
        applied = jnp.stack([out_re, out_im], axis=2)
        applied = lax.psum(applied, "pb")
        current = applied / degree
        summed_terms = summed_terms + current
    propagated = summed_terms.reshape(1, k_local, walkers, row_width)
    return (propagated, energy)


def exchange(array, axis, rounds):
    return [array] + [lax.ppermute(array, axis, pairs) for pairs in rounds]


def origins(axis, rounds):
    at = lax.axis_index(axis)
    found = [at]
    for pairs in rounds:
        source = jnp.int32(0)
        for sender, receiver in pairs:
            source = jnp.where(at == receiver, sender, source)
        found.append(source)
    return found


def operator_group(ka_count, pb_count):
    first = (pb_count - 1) * ka_count + ka_count // 2
    rest = [at for at in range(pb_count * ka_count) if at != first]
    return [first] + sorted(rest, key=lambda at: -(at // ka_count + at % ka_count))


def prepare_kernel(ka_count, pb_count, walkers, map_ref, count_ref, mask_ref, picks_ref):
    kept = count_ref[lax.axis_index("pb")]
    column = lax.broadcasted_iota(jnp.int32, mask_ref.shape, 1)
    mask_ref[...] = jnp.where(column < kept, 1.0, 0.0)
    kpoints = map_ref.shape[1]
    k_local = kpoints // ka_count
    span = k_local * walkers
    lane = lax.broadcasted_iota(jnp.int32, (1, LANES), 1)
    lane_q = lane // (LANES // pb_count)
    lane_ka = lax.rem(lane, LANES // pb_count) // (2 * span)
    lane_part = lax.rem(lane, 2 * span) // span
    lane_k = lane_ka * k_local + lax.rem(lane, span) // walkers
    wanted = jnp.zeros((1, LANES), jnp.int32)
    for q in range(pb_count):
        for k in range(kpoints):
            source = map_ref[q, k]
            source = source // k_local * (2 * span) + lax.rem(source, k_local) * walkers
            wanted = jnp.where((lane_q == q) & (lane_k == k), source, wanted)
    wanted = wanted + lax.rem(lane, walkers)
    row = lax.broadcasted_iota(jnp.int32, (LANES, LANES), 0)
    real = jnp.where(row == wanted, 1.0, 0.0)
    imag = jnp.where(row == wanted + span, jnp.where(lane_part == 0, 1.0, -1.0), 0.0)
    picks_ref[...] = jnp.concatenate([real, imag], axis=1).astype(BF16)


def bias_kernel(ka_count, k_local, *refs):
    *greens, chol_ref, orbitals_ref, mask_ref, bias_ref, own_ref, table = refs
    for source, green_ref in zip(origins("ka", GREEN_ROUNDS), greens):
        table[source] = green_ref[...].astype(F32)
    first = lax.axis_index("ka") * k_local
    width = chol_ref.shape[2]
    rows = 2 * ka_count
    total = jnp.zeros((rows, bias_ref.shape[1]), F32)
    for k in range(k_local):
        green = jnp.concatenate(
            [table[w, pl.ds(first + k, 1), :] for w in range(ka_count)], axis=0
        )
        real, imag = green[:, :width], green[:, width:]
        both = jnp.concatenate([real, imag], axis=0)
        turned = jnp.concatenate([-imag, real], axis=0)
        own_ref[k] = both
        total += jnp.dot(both.astype(BF16), chol_ref[k, 0], preferred_element_type=F32)
        total += jnp.dot(turned.astype(BF16), chol_ref[k, 1], preferred_element_type=F32)
    bias_ref[:rows] = total * mask_ref[...]
    window = jnp.concatenate([orbitals_ref[k] for k in range(k_local)], axis=0)
    count, width = window.shape
    bias_ref[rows : rows + count, :width] = window
    bias_ref[rows : rows + count, width:] = jnp.zeros((count, bias_ref.shape[1] - width), F32)


def exchange_kernel(k_local, own_ref, chol_ref, mask_ref, out_ref):
    walkers, width, columns = own_ref.shape[1] // 2, own_ref.shape[2], chol_ref.shape[3]
    rows = 2 * walkers
    lane = lax.broadcasted_iota(jnp.int32, (rows, LANES), 1)
    total = jnp.zeros((rows, columns), F32)
    for k in range(k_local):
        both = jnp.concatenate([own_ref[k], jnp.zeros((rows, LANES - width), F32)], axis=1)
        turned = jnp.concatenate([-both[walkers:], both[:walkers]], axis=0)
        sides = []
        for side in (both, turned):
            rolled = {
                step: side if step == 0 else pltpu.roll(side, (step * M) % LANES, 1)
                for step in range(1 - NOCC, NOCC)
            }
            blocks = []
            for i in range(NOCC):
                inside = (lane >= i * M) & (lane < (i + 1) * M)
                for j in range(NOCC):
                    blocks.append(jnp.where(inside, rolled[i - j], 0.0))
            sides.append(jnp.concatenate(blocks, axis=0)[:, :width].astype(BF16))
        cross = jnp.dot(sides[0], chol_ref[k, 0], preferred_element_type=F32)
        cross += jnp.dot(sides[1], chol_ref[k, 1], preferred_element_type=F32)
        cross = cross * cross
        for block in range(NOCC * NOCC):
            total += cross[block * rows : (block + 1) * rows]
    total = total * mask_ref[:rows]
    total = total[:walkers] + total[walkers:]
    summed = 0.5 * jnp.sum(total, axis=1, keepdims=True)
    out_ref[...] = jnp.broadcast_to(summed, out_ref.shape)


def operator_kernel(k_local, *refs):
    *parts, fields_ref, mask_ref, exchange_ref, chol_ref, out_ref, products, turned_ref = refs
    walkers, columns = fields_ref.shape
    bias = parts[0][: 2 * walkers]
    for part in parts[1:]:
        bias = bias + part[: 2 * walkers]
    pairs = M * M
    tiles = columns // LANES
    group = LANES // (2 * tiles)
    bias_re, bias_im = bias[:walkers], bias[walkers:]
    hartree = 0.5 * jnp.sum(bias_re * bias_re + bias_im * bias_im, axis=1, keepdims=True)
    own = lax.broadcasted_iota(jnp.int32, (walkers, 1), 0) == lax.axis_index("ka")
    energy = jnp.where(own, hartree, 0.0) - exchange_ref[:, :1]
    kept = mask_ref[:walkers]
    shift_re = (fields_ref[...] - BIAS_STEP * bias_re) * kept
    shift_im = -BIAS_STEP * bias_im * kept
    span = k_local * walkers
    weights = []
    for k in range(k_local):
        before, after = k * walkers, span - (k + 1) * walkers
        pieces = []
        for tile in range(tiles):
            at = slice(tile * LANES, (tile + 1) * LANES)
            for first, second in ((shift_re, shift_im), (-shift_im, shift_re)):
                for side in (first, second):
                    pieces += [(before, None), (walkers, side[:, at]), (after, None)]
                pieces.append((group - 2 * span, None))
        weights.append(
            jnp.concatenate(
                [jnp.zeros((n, LANES), F32) if p is None else p for n, p in pieces if n], axis=0
            ).astype(BF16)
        )
    products[...] = lax.dot_general(
        jnp.concatenate([chol_ref[k] for k in range(k_local)], axis=1),
        jnp.concatenate(weights, axis=1),
        (((1,), (1,)), ((), ())),
        preferred_element_type=F32,
    )
    lane = lax.broadcasted_iota(jnp.int32, (pairs, LANES), 1)
    merged = products[pl.ds(0, pairs, stride=2 * tiles), :]
    for at in range(1, 2 * tiles):
        row = products[pl.ds(at, pairs, stride=2 * tiles), :]
        merged = jnp.where(lane >= at * group, row, merged)
    turned_ref[:pairs] = merged
    copies, rows, width = out_ref.shape
    lane = lax.broadcasted_iota(jnp.int32, (rows, LANES), 1)
    for at in range(0, width, LANES):
        block = turned_ref[at : at + LANES].T
        block = PROP_STEP * sum(block[n * group : n * group + rows] for n in range(2 * tiles))
        if at + LANES > pairs:
            share = jnp.concatenate([energy, jnp.zeros((rows - walkers, 1), F32)], axis=0)
            block = jnp.where(lane + at < pairs, block, 0.0)
            for piece in range(3):
                head = share.astype(BF16).astype(F32)
                block = jnp.where(lane + at == pairs + piece, head, block)
                share = share - head
        for copy in range(copies):
            out_ref[copy, :, at : at + LANES] = block.astype(BF16)


def taylor_kernel(pb_count, normalizer, blocks_ref, *refs):
    *windows, picks_ref, orbitals_ref, out_ref, energy_ref, turned, picked, term = refs
    pairs = M * M
    pair = NOCC * M
    k_local, walkers, _ = out_ref.shape
    span = k_local * walkers
    ka_pos = lax.axis_index("ka")
    term[...] = jnp.zeros_like(term)
    for source, window_ref in zip(origins("ka", BIAS_ROUNDS), windows):
        start = pl.multiple_of(source * (2 * span), 2 * span)
        window = window_ref[window_ref.shape[0] - span :]
        term[pl.ds(start, span), :pair] = window[:, :pair]
        term[pl.ds(start + span, span), :pair] = window[:, pair : 2 * pair]
    picked[...] = jnp.dot(term[...].T.astype(BF16), picks_ref[...], preferred_element_type=F32)
    count, _, width = blocks_ref.shape
    group = operator_group(count // pb_count, pb_count)
    places = [group.index(n) for n in range(count)]
    for at in range(0, width, LANES):
        tile = jnp.concatenate([blocks_ref[n, :, at : at + LANES] for n in places], axis=0)
        turned[at : at + LANES] = tile.T.astype(F32)
    shares = turned[pairs : pairs + 3]
    lane = lax.broadcasted_iota(jnp.int32, shares.shape, 1)
    shares = jnp.where(lax.rem(lane, 2 * span) == ka_pos, shares, 0.0)
    shares = jnp.sum(jnp.sum(shares, axis=0, keepdims=True), axis=1, keepdims=True)
    energy_ref[...] = shares / normalizer
    lane = lax.broadcasted_iota(jnp.int32, (M, LANES), 1)
    imaginary = lax.rem(lane, 2 * span) >= span
    sums = [jnp.zeros((M, LANES), F32) for _ in range(NOCC)]
    for degree in range(1, TAYLOR + 1):
        stride = M if degree == 1 else ROWS
        straight = [jnp.zeros((M, LANES), F32) for _ in range(NOCC)]
        crossed = [jnp.zeros((M, LANES), F32) for _ in range(NOCC)]
        for c in range(M):
            column = turned[pl.ds(c, M, stride=M), :]
            for i in range(NOCC):
                at = i * stride + c
                straight[i] += column * picked[at : at + 1, :LANES]
                crossed[i] += column * picked[at : at + 1, LANES:]
        for i in range(NOCC):
            other = jnp.where(
                imaginary, pltpu.roll(crossed[i], span, 1), pltpu.roll(crossed[i], LANES - span, 1)
            )
            applied = straight[i] + other
            applied = applied + pltpu.roll(applied, LANES // pb_count, 1)
            current = applied / degree
            sums[i] = sums[i] + current
            term[i * ROWS : i * ROWS + M] = current if degree < TAYLOR else sums[i]
        if degree < TAYLOR:
            picked[...] = jnp.dot(
                term[...].astype(BF16), picks_ref[...], preferred_element_type=F32
            )
    turned[:LANES] = term[...].T
    both = turned[pl.ds(pl.multiple_of(ka_pos * (2 * span), 2 * span), 2 * span), :]
    both = jnp.concatenate([both[:, i * ROWS : i * ROWS + M] for i in range(NOCC)], axis=1)
    both = jnp.concatenate([both[:span], both[span:]], axis=1)
    for k in range(k_local):
        out_ref[k] = orbitals_ref[k] + both[k * walkers : (k + 1) * walkers]


def call(kernel, out, scratch=(), scalars=0, operands=0, flops=None):
    spaces = [pltpu.SMEM] * scalars + [pltpu.VMEM] * operands
    cost = None
    if flops is not None:
        cost = pl.CostEstimate(flops=flops, bytes_accessed=0, transcendentals=0)
    return pl.pallas_call(
        kernel,
        out_shape=out,
        in_specs=[pl.BlockSpec(memory_space=space) for space in spaces],
        out_specs=jax.tree.map(lambda _: pl.BlockSpec(memory_space=pltpu.VMEM), out),
        scratch_shapes=list(scratch),
        cost_estimate=cost,
        compiler_params=pltpu.CompilerParams(vmem_limit_bytes=24 * 2**20),
    )


def direct(green, fields, orbitals, chol_half, chol_full, chol_count, kq_map):
    k_local, pair_width, chol_cols = chol_half.shape[1], chol_half.shape[3], chol_half.shape[4]
    ka_count, pb_count = lax.axis_size("ka"), lax.axis_size("pb")
    walkers = ka_count
    kpoints = green.shape[3]
    span = k_local * walkers
    shape = jax.ShapeDtypeStruct
    tiles = chol_cols // LANES
    own_green = green.reshape(kpoints, 2 * pair_width)
    greens = exchange(own_green, "ka", GREEN_ROUNDS)
    half = chol_half.reshape(k_local, 2, pair_width, chol_cols)
    full = jnp.transpose(
        chol_full.reshape(k_local, 2, M * M, tiles, LANES), (0, 2, 3, 1, 4)
    ).reshape(k_local, M * M * tiles * 2, LANES)
    own_fields = fields.reshape(walkers, chol_cols)
    own_orbitals = orbitals.reshape(k_local, walkers, 2 * pair_width)
    mask, picks = call(
        functools.partial(prepare_kernel, ka_count, pb_count, walkers),
        (shape((2 * walkers, chol_cols), F32), shape((LANES, 2 * LANES), BF16)),
        scalars=2,
        flops=10**9,
    )(kq_map, chol_count)
    bias, own = call(
        functools.partial(bias_kernel, ka_count, k_local),
        (
            shape((2 * walkers + span, chol_cols), F32),
            shape((k_local, 2 * walkers, pair_width), F32),
        ),
        [pltpu.VMEM((walkers, kpoints, 2 * pair_width), F32)],
        operands=len(greens) + 3,
    )(*greens, half, own_orbitals, mask)
    parts = exchange(bias, "ka", BIAS_ROUNDS)
    shares = call(
        functools.partial(exchange_kernel, k_local),
        shape((walkers, LANES), F32),
        operands=3,
    )(own, half, mask)
    width = -(-(M * M + 3) // LANES) * LANES
    blocks = call(
        functools.partial(operator_kernel, k_local),
        shape((ka_count * pb_count, 2 * span, width), BF16),
        [pltpu.VMEM((2 * M * M * tiles, LANES), F32), pltpu.VMEM((width, LANES), F32)],
        operands=len(parts) + 4,
    )(*parts, own_fields, mask, shares, full)
    group = operator_group(ka_count, pb_count)
    blocks = lax.all_to_all(
        blocks, ("pb", "ka"), 0, 0, axis_index_groups=[group], tiled=True
    )
    propagated, energy = call(
        functools.partial(taylor_kernel, pb_count, float(pb_count * chol_cols)),
        (shape((k_local, walkers, 2 * pair_width), F32), shape((1, 1), F32)),
        [
            pltpu.VMEM((width, LANES), F32),
            pltpu.VMEM((NOCC * ROWS, 2 * LANES), F32),
            pltpu.VMEM((LANES, LANES), F32),
        ],
        operands=len(parts) + 3,
    )(blocks, *parts, picks, own_orbitals)
    return (propagated[None], energy)


def on_device(green, fields, orbitals, chol_half, chol_full, chol_count, kq_map):
    ka_count, pb_count = lax.axis_size("ka"), lax.axis_size("pb")
    walkers = orbitals.shape[2]
    fits = 2 * pb_count * kq_map.shape[1] * walkers == LANES
    fits = fits and chol_half.shape[1] * walkers == 8 and chol_half.shape[4] == 2 * LANES
    fits = fits and ka_count == 4
    if fits and chol_half.shape[0] == 1 and walkers == ka_count:
        return direct(green, fields, orbitals, chol_half, chol_full, chol_count, kq_map)
    return with_collectives(green, fields, orbitals, chol_half, chol_full, chol_count, kq_map)


def solution(mesh):
    placed = (
        P("wa", ("grp", "ka"), "pb", None, None),
        P("wa", "pb", "grp", None),
        P("wa", "ka", "grp", None),
        P("pb", "ka", None, None, None),
        P("pb", "ka", None, None, None),
        P(),
        P(),
    )
    return jax.shard_map(
        on_device,
        mesh=mesh,
        in_specs=placed,
        out_specs=(P("wa", "ka", "grp", None), P("wa", ("grp", "ka"))),
        check_vma=False,
    )
```

```python
import functools

import jax
import jax.numpy as jnp
from jax import lax
from jax.experimental import pallas as pl
from jax.experimental.pallas import tpu as pltpu
from jax.sharding import PartitionSpec as P

M = 26
NOCC = 4
TAYLOR = 3
LANES = 128
ROWS = 32

GREEN_ROUNDS = (
    ((3, 0), (2, 1), (1, 3), (0, 2)),
    ((3, 1), (2, 0), (0, 3), (1, 2)),
    ((1, 0), (3, 2), (2, 3), (0, 1)),
)[::-1]
BIAS_ROUNDS = (
    ((0, 1), (1, 3), (2, 0), (3, 2)),
    ((0, 3), (3, 0), (1, 2), (2, 1)),
    ((0, 2), (1, 0), (2, 3), (3, 1)),
)[::-1]


BIAS_STEP = 0.5
PROP_STEP = 0.5

F32 = jnp.float32
BF16 = jnp.bfloat16


def complex_dot(pattern, left_re, left_im, right_re, right_im):
    real_part = jnp.einsum(
        pattern, left_re, right_re, preferred_element_type=jnp.float32
    ) - jnp.einsum(pattern, left_im, right_im, preferred_element_type=jnp.float32)
    imag_part = jnp.einsum(
        pattern, left_re, right_im, preferred_element_type=jnp.float32
    ) + jnp.einsum(pattern, left_im, right_re, preferred_element_type=jnp.float32)
    return (real_part, imag_part)


def make_picker(wanted):

    def picker(shard_rows):
        row_count = shard_rows.shape[0]
        select = (wanted[:, None] == jnp.arange(row_count, dtype=jnp.int32)[None, :]).astype(
            jnp.bfloat16
        )
        return jnp.dot(select, shard_rows, preferred_element_type=jnp.float32)

    return picker


def with_collectives(green, fields, orbitals, chol_half, chol_full, chol_count, kq_map):
    q_local = chol_half.shape[0]
    k_local = chol_half.shape[1]
    pair_width = chol_half.shape[3]
    chol_cols = chol_half.shape[4]
    ka_count = lax.axis_size("ka")
    pb_count = lax.axis_size("pb")
    ka_pos = lax.axis_index("ka")
    pb_pos = lax.axis_index("pb")
    local_green = lax.all_to_all(green, "ka", split_axis=3, concat_axis=1, tiled=True)
    walkers = local_green.shape[1]
    per_device = walkers // ka_count
    greens = local_green[0].reshape(walkers, q_local, k_local, 2, pair_width)
    counts = lax.dynamic_slice_in_dim(chol_count, pb_pos * q_local, q_local)
    vec_mask = (jnp.arange(chol_cols, dtype=jnp.int32)[None, :] < counts[:, None]).astype(
        jnp.float32
    )
    bias_re, bias_im = complex_dot(
        "wqkx,qkxn->qwn",
        greens[:, :, :, 0],
        greens[:, :, :, 1],
        chol_half[:, :, 0],
        chol_half[:, :, 1],
    )
    own_rows = (jnp.arange(walkers, dtype=jnp.int32) // per_device == ka_pos).astype(jnp.float32)
    bias_re, bias_im = lax.psum((bias_re, bias_im), "ka")
    bias_re = bias_re * vec_mask[:, None, :]
    bias_im = bias_im * vec_mask[:, None, :]
    hartree = 0.5 * jnp.sum(bias_re * bias_re + bias_im * bias_im, axis=(0, 2)) * own_rows
    field_now = jnp.transpose(fields, (1, 0, 2, 3)).reshape(q_local, walkers, chol_cols)
    shift_re = ((field_now - BIAS_STEP * bias_re) * vec_mask[:, None, :]).astype(jnp.bfloat16)
    shift_im = (-BIAS_STEP * bias_im * vec_mask[:, None, :]).astype(jnp.bfloat16)
    exchange = jnp.zeros((walkers,), jnp.float32)
    for transfer in range(q_local):
        for kpoint in range(k_local):
            chol_row = chol_half[transfer, kpoint].reshape(2, NOCC, M, chol_cols)
            green_row = greens[:, transfer, kpoint].reshape(walkers, 2, NOCC, M)
            cross_re, cross_im = complex_dot(
                "ipn,wjp->wijn", chol_row[0], chol_row[1], green_row[:, 0], green_row[:, 1]
            )
            exchange = exchange + 0.5 * jnp.sum(
                (cross_re * cross_re + cross_im * cross_im) * vec_mask[transfer], axis=(1, 2, 3)
            )
    prop_re, prop_im = complex_dot(
        "qwn,qkyn->qwky", shift_re, shift_im, chol_full[:, :, 0], chol_full[:, :, 1]
    )
    shape = (q_local, walkers, k_local, M, M)
    oper_re = (PROP_STEP * prop_re).astype(jnp.bfloat16).reshape(shape)
    oper_im = (PROP_STEP * prop_im).astype(jnp.bfloat16).reshape(shape)
    normalizer = q_local * pb_count * chol_cols
    total_energy = lax.psum(hartree - exchange, ("ka", "pb")) / normalizer
    energy = lax.dynamic_slice_in_dim(total_energy, ka_pos * per_device, per_device).reshape(
        1, per_device
    )
    initial = orbitals[0].reshape(k_local, walkers, 2, NOCC, M)
    row_width = 2 * pair_width
    my_rows = lax.dynamic_slice_in_dim(kq_map, pb_pos * q_local, q_local, 0)
    wanted = lax.dynamic_slice_in_dim(my_rows, ka_pos * k_local, k_local, 1).reshape(
        q_local * k_local
    )
    picker = make_picker(wanted)
    current = initial
    summed_terms = initial
    for degree in range(1, TAYLOR + 1):
        rounded = current.astype(jnp.bfloat16).reshape(k_local, walkers * row_width)
        fetched = picker(lax.all_gather(rounded, "ka", axis=0, tiled=True))
        shifted_rows = fetched.astype(jnp.bfloat16).reshape(q_local, k_local, walkers, 2, NOCC, M)
        out_re, out_im = complex_dot(
            "xwkpq,xkwiq->kwip",
            oper_re,
            oper_im,
            shifted_rows[:, :, :, 0],
            shifted_rows[:, :, :, 1],
        )
        applied = jnp.stack([out_re, out_im], axis=2)
        applied = lax.psum(applied, "pb")
        current = applied / degree
        summed_terms = summed_terms + current
    propagated = summed_terms.reshape(1, k_local, walkers, row_width)
    return (propagated, energy)


def exchange(array, axis, rounds):
    return [array] + [lax.ppermute(array, axis, pairs) for pairs in rounds]


def origins(axis, rounds):
    at = lax.axis_index(axis)
    found = [at]
    for pairs in rounds:
        source = jnp.int32(0)
        for sender, receiver in pairs:
            source = jnp.where(at == receiver, sender, source)
        found.append(source)
    return found


def operator_group(ka_count, pb_count):
    size = pb_count * ka_count
    first = (pb_count - 1) * ka_count + ka_count // 2
    return [(first - at) % size for at in range(size)]


def prepare_kernel(ka_count, pb_count, walkers, map_ref, count_ref, mask_ref, picks_ref):
    kept = count_ref[lax.axis_index("pb")]
    column = lax.broadcasted_iota(jnp.int32, mask_ref.shape, 1)
    mask_ref[...] = jnp.where(column < kept, 1.0, 0.0)
    kpoints = map_ref.shape[1]
    k_local = kpoints // ka_count
    span = k_local * walkers
    lane = lax.broadcasted_iota(jnp.int32, (1, LANES), 1)
    lane_q = lane // (LANES // pb_count)
    lane_ka = lax.rem(lane, LANES // pb_count) // (2 * span)
    lane_part = lax.rem(lane, 2 * span) // span
    lane_k = lane_ka * k_local + lax.rem(lane, span) // walkers
    wanted = jnp.zeros((1, LANES), jnp.int32)
    for q in range(pb_count):
        for k in range(kpoints):
            source = map_ref[q, k]
            source = source // k_local * (2 * span) + lax.rem(source, k_local) * walkers
            wanted = jnp.where((lane_q == q) & (lane_k == k), source, wanted)
    wanted = wanted + lax.rem(lane, walkers)
    row = lax.broadcasted_iota(jnp.int32, (LANES, LANES), 0)
    real = jnp.where(row == wanted, 1.0, 0.0)
    imag = jnp.where(row == wanted + span, jnp.where(lane_part == 0, 1.0, -1.0), 0.0)
    picks_ref[...] = jnp.concatenate([real, imag], axis=1).astype(BF16)


def bias_kernel(ka_count, k_local, *refs):
    *greens, chol_ref, orbitals_ref, mask_ref, bias_ref, own_ref, table = refs
    for source, green_ref in zip(origins("ka", GREEN_ROUNDS), greens):
        table[source] = green_ref[...].astype(F32)
    first = lax.axis_index("ka") * k_local
    width = chol_ref.shape[2]
    rows = 2 * ka_count
    total = jnp.zeros((rows, bias_ref.shape[1]), F32)
    for k in range(k_local):
        green = jnp.concatenate(
            [table[w, pl.ds(first + k, 1), :] for w in range(ka_count)], axis=0
        )
        real, imag = green[:, :width], green[:, width:]
        both = jnp.concatenate([real, imag], axis=0)
        turned = jnp.concatenate([-imag, real], axis=0)
        own_ref[k] = both
        total += jnp.dot(both.astype(BF16), chol_ref[k, 0], preferred_element_type=F32)
        total += jnp.dot(turned.astype(BF16), chol_ref[k, 1], preferred_element_type=F32)
    bias_ref[:rows] = total * mask_ref[...]
    window = jnp.concatenate([orbitals_ref[k] for k in range(k_local)], axis=0)
    count, width = window.shape
    bias_ref[rows : rows + count, :width] = window
    bias_ref[rows : rows + count, width:] = jnp.zeros((count, bias_ref.shape[1] - width), F32)


def exchange_kernel(k_local, own_ref, chol_ref, mask_ref, out_ref):
    walkers, width, columns = own_ref.shape[1] // 2, own_ref.shape[2], chol_ref.shape[3]
    rows = 2 * walkers
    lane = lax.broadcasted_iota(jnp.int32, (rows, LANES), 1)
    total = jnp.zeros((rows, columns), F32)
    for k in range(k_local):
        both = jnp.concatenate([own_ref[k], jnp.zeros((rows, LANES - width), F32)], axis=1)
        turned = jnp.concatenate([-both[walkers:], both[:walkers]], axis=0)
        sides = []
        for side in (both, turned):
            rolled = {
                step: side if step == 0 else pltpu.roll(side, (step * M) % LANES, 1)
                for step in range(1 - NOCC, NOCC)
            }
            blocks = []
            for i in range(NOCC):
                inside = (lane >= i * M) & (lane < (i + 1) * M)
                for j in range(NOCC):
                    blocks.append(jnp.where(inside, rolled[i - j], 0.0))
            sides.append(jnp.concatenate(blocks, axis=0)[:, :width].astype(BF16))
        cross = jnp.dot(sides[0], chol_ref[k, 0], preferred_element_type=F32)
        cross += jnp.dot(sides[1], chol_ref[k, 1], preferred_element_type=F32)
        cross = cross * cross
        for block in range(NOCC * NOCC):
            total += cross[block * rows : (block + 1) * rows]
    total = total * mask_ref[:rows]
    total = total[:walkers] + total[walkers:]
    summed = 0.5 * jnp.sum(total, axis=1, keepdims=True)
    out_ref[...] = jnp.broadcast_to(summed, out_ref.shape)


def operator_kernel(k_local, *refs):
    *parts, fields_ref, mask_ref, exchange_ref, chol_ref, out_ref, products, turned_ref = refs
    walkers, columns = fields_ref.shape
    bias = parts[0][: 2 * walkers]
    for part in parts[1:]:
        bias = bias + part[: 2 * walkers]
    pairs = M * M
    tiles = columns // LANES
    group = LANES // (2 * tiles)
    bias_re, bias_im = bias[:walkers], bias[walkers:]
    hartree = 0.5 * jnp.sum(bias_re * bias_re + bias_im * bias_im, axis=1, keepdims=True)
    own = lax.broadcasted_iota(jnp.int32, (walkers, 1), 0) == lax.axis_index("ka")
    energy = jnp.where(own, hartree, 0.0) - exchange_ref[:, :1]
    kept = mask_ref[:walkers]
    shift_re = (fields_ref[...] - BIAS_STEP * bias_re) * kept
    shift_im = -BIAS_STEP * bias_im * kept
    span = k_local * walkers
    weights = []
    for k in range(k_local):
        before, after = k * walkers, span - (k + 1) * walkers
        pieces = []
        for tile in range(tiles):
            at = slice(tile * LANES, (tile + 1) * LANES)
            for first, second in ((shift_re, shift_im), (-shift_im, shift_re)):
                for side in (first, second):
                    pieces += [(before, None), (walkers, side[:, at]), (after, None)]
                pieces.append((group - 2 * span, None))
        weights.append(
            jnp.concatenate(
                [jnp.zeros((n, LANES), F32) if p is None else p for n, p in pieces if n], axis=0
            ).astype(BF16)
        )
    products[...] = lax.dot_general(
        jnp.concatenate([chol_ref[k] for k in range(k_local)], axis=1),
        jnp.concatenate(weights, axis=1),
        (((1,), (1,)), ((), ())),
        preferred_element_type=F32,
    )
    lane = lax.broadcasted_iota(jnp.int32, (pairs, LANES), 1)
    merged = products[pl.ds(0, pairs, stride=2 * tiles), :]
    for at in range(1, 2 * tiles):
        row = products[pl.ds(at, pairs, stride=2 * tiles), :]
        merged = jnp.where(lane >= at * group, row, merged)
    turned_ref[:pairs] = merged
    copies, rows, width = out_ref.shape
    lane = lax.broadcasted_iota(jnp.int32, (rows, LANES), 1)
    for at in range(0, width, LANES):
        block = turned_ref[at : at + LANES].T
        block = PROP_STEP * sum(block[n * group : n * group + rows] for n in range(2 * tiles))
        if at + LANES > pairs:
            share = jnp.concatenate([energy, jnp.zeros((rows - walkers, 1), F32)], axis=0)
            block = jnp.where(lane + at < pairs, block, 0.0)
            for piece in range(3):
                head = share.astype(BF16).astype(F32)
                block = jnp.where(lane + at == pairs + piece, head, block)
                share = share - head
        for copy in range(copies):
            out_ref[copy, :, at : at + LANES] = block.astype(BF16)


def taylor_kernel(pb_count, normalizer, blocks_ref, *refs):
    *windows, picks_ref, orbitals_ref, out_ref, energy_ref, turned, picked, term = refs
    pairs = M * M
    pair = NOCC * M
    k_local, walkers, _ = out_ref.shape
    span = k_local * walkers
    ka_pos = lax.axis_index("ka")
    term[...] = jnp.zeros_like(term)
    for source, window_ref in zip(origins("ka", BIAS_ROUNDS), windows):
        start = pl.multiple_of(source * (2 * span), 2 * span)
        window = window_ref[window_ref.shape[0] - span :]
        term[pl.ds(start, span), :pair] = window[:, :pair]
        term[pl.ds(start + span, span), :pair] = window[:, pair : 2 * pair]
    picked[...] = jnp.dot(term[...].T.astype(BF16), picks_ref[...], preferred_element_type=F32)
    count, _, width = blocks_ref.shape
    group = operator_group(count // pb_count, pb_count)
    places = [group.index(n) for n in range(count)]
    for at in range(0, width, LANES):
        tile = jnp.concatenate([blocks_ref[n, :, at : at + LANES] for n in places], axis=0)
        turned[at : at + LANES] = tile.T.astype(F32)
    shares = turned[pairs : pairs + 3]
    lane = lax.broadcasted_iota(jnp.int32, shares.shape, 1)
    shares = jnp.where(lax.rem(lane, 2 * span) == ka_pos, shares, 0.0)
    shares = jnp.sum(jnp.sum(shares, axis=0, keepdims=True), axis=1, keepdims=True)
    energy_ref[...] = shares / normalizer
    lane = lax.broadcasted_iota(jnp.int32, (M, LANES), 1)
    imaginary = lax.rem(lane, 2 * span) >= span
    sums = [jnp.zeros((M, LANES), F32) for _ in range(NOCC)]
    for degree in range(1, TAYLOR + 1):
        stride = M if degree == 1 else ROWS
        straight = [jnp.zeros((M, LANES), F32) for _ in range(NOCC)]
        crossed = [jnp.zeros((M, LANES), F32) for _ in range(NOCC)]
        for c in range(M):
            column = turned[pl.ds(c, M, stride=M), :]
            for i in range(NOCC):
                at = i * stride + c
                straight[i] += column * picked[at : at + 1, :LANES]
                crossed[i] += column * picked[at : at + 1, LANES:]
        for i in range(NOCC):
            other = jnp.where(
                imaginary, pltpu.roll(crossed[i], span, 1), pltpu.roll(crossed[i], LANES - span, 1)
            )
            applied = straight[i] + other
            applied = applied + pltpu.roll(applied, LANES // pb_count, 1)
            current = applied / degree
            sums[i] = sums[i] + current
            term[i * ROWS : i * ROWS + M] = current if degree < TAYLOR else sums[i]
        if degree < TAYLOR:
            picked[...] = jnp.dot(
                term[...].astype(BF16), picks_ref[...], preferred_element_type=F32
            )
    turned[:LANES] = term[...].T
    both = turned[pl.ds(pl.multiple_of(ka_pos * (2 * span), 2 * span), 2 * span), :]
    both = jnp.concatenate([both[:, i * ROWS : i * ROWS + M] for i in range(NOCC)], axis=1)
    both = jnp.concatenate([both[:span], both[span:]], axis=1)
    for k in range(k_local):
        out_ref[k] = orbitals_ref[k] + both[k * walkers : (k + 1) * walkers]


def call(kernel, out, scratch=(), scalars=0, operands=0, flops=None):
    spaces = [pltpu.SMEM] * scalars + [pltpu.VMEM] * operands
    cost = None
    if flops is not None:
        cost = pl.CostEstimate(flops=flops, bytes_accessed=0, transcendentals=0)
    return pl.pallas_call(
        kernel,
        out_shape=out,
        in_specs=[pl.BlockSpec(memory_space=space) for space in spaces],
        out_specs=jax.tree.map(lambda _: pl.BlockSpec(memory_space=pltpu.VMEM), out),
        scratch_shapes=list(scratch),
        cost_estimate=cost,
        compiler_params=pltpu.CompilerParams(vmem_limit_bytes=24 * 2**20),
    )


def direct(green, fields, orbitals, chol_half, chol_full, chol_count, kq_map):
    k_local, pair_width, chol_cols = chol_half.shape[1], chol_half.shape[3], chol_half.shape[4]
    ka_count, pb_count = lax.axis_size("ka"), lax.axis_size("pb")
    walkers = ka_count
    kpoints = green.shape[3]
    span = k_local * walkers
    shape = jax.ShapeDtypeStruct
    tiles = chol_cols // LANES
    own_green = green.reshape(kpoints, 2 * pair_width)
    greens = exchange(own_green, "ka", GREEN_ROUNDS)
    half = chol_half.reshape(k_local, 2, pair_width, chol_cols)
    full = jnp.transpose(
        chol_full.reshape(k_local, 2, M * M, tiles, LANES), (0, 2, 3, 1, 4)
    ).reshape(k_local, M * M * tiles * 2, LANES)
    own_fields = fields.reshape(walkers, chol_cols)
    own_orbitals = orbitals.reshape(k_local, walkers, 2 * pair_width)
    mask, picks = call(
        functools.partial(prepare_kernel, ka_count, pb_count, walkers),
        (shape((2 * walkers, chol_cols), F32), shape((LANES, 2 * LANES), BF16)),
        scalars=2,
        flops=10**9,
    )(kq_map, chol_count)
    bias, own = call(
        functools.partial(bias_kernel, ka_count, k_local),
        (
            shape((2 * walkers + span, chol_cols), F32),
            shape((k_local, 2 * walkers, pair_width), F32),
        ),
        [pltpu.VMEM((walkers, kpoints, 2 * pair_width), F32)],
        operands=len(greens) + 3,
    )(*greens, half, own_orbitals, mask)
    parts = exchange(bias, "ka", BIAS_ROUNDS)
    shares = call(
        functools.partial(exchange_kernel, k_local),
        shape((walkers, LANES), F32),
        operands=3,
    )(own, half, mask)
    width = -(-(M * M + 3) // LANES) * LANES
    blocks = call(
        functools.partial(operator_kernel, k_local),
        shape((ka_count * pb_count, 2 * span, width), BF16),
        [pltpu.VMEM((2 * M * M * tiles, LANES), F32), pltpu.VMEM((width, LANES), F32)],
        operands=len(parts) + 4,
    )(*parts, own_fields, mask, shares, full)
    group = operator_group(ka_count, pb_count)
    blocks = lax.all_to_all(
        blocks, ("pb", "ka"), 0, 0, axis_index_groups=[group], tiled=True
    )
    propagated, energy = call(
        functools.partial(taylor_kernel, pb_count, float(pb_count * chol_cols)),
        (shape((k_local, walkers, 2 * pair_width), F32), shape((1, 1), F32)),
        [
            pltpu.VMEM((width, LANES), F32),
            pltpu.VMEM((NOCC * ROWS, 2 * LANES), F32),
            pltpu.VMEM((LANES, LANES), F32),
        ],
        operands=len(parts) + 3,
    )(blocks, *parts, picks, own_orbitals)
    return (propagated[None], energy)


def on_device(green, fields, orbitals, chol_half, chol_full, chol_count, kq_map):
    ka_count, pb_count = lax.axis_size("ka"), lax.axis_size("pb")
    walkers = orbitals.shape[2]
    fits = 2 * pb_count * kq_map.shape[1] * walkers == LANES
    fits = fits and chol_half.shape[1] * walkers == 8 and chol_half.shape[4] == 2 * LANES
    fits = fits and ka_count == 4
    if fits and chol_half.shape[0] == 1 and walkers == ka_count:
        return direct(green, fields, orbitals, chol_half, chol_full, chol_count, kq_map)
    return with_collectives(green, fields, orbitals, chol_half, chol_full, chol_count, kq_map)


def solution(mesh):
    placed = (
        P("wa", ("grp", "ka"), "pb", None, None),
        P("wa", "pb", "grp", None),
        P("wa", "ka", "grp", None),
        P("pb", "ka", None, None, None),
        P("pb", "ka", None, None, None),
        P(),
        P(),
    )
    return jax.shard_map(
        on_device,
        mesh=mesh,
        in_specs=placed,
        out_specs=(P("wa", "ka", "grp", None), P("wa", ("grp", "ka"))),
        check_vma=False,
    )
```

```python
import functools

import jax
import jax.numpy as jnp
from jax import lax
from jax.experimental import pallas as pl
from jax.experimental.pallas import tpu as pltpu
from jax.sharding import PartitionSpec as P

M = 26
NOCC = 4
TAYLOR = 3
LANES = 128
ROWS = 32

GREEN_ROUNDS = (
    ((3, 0), (2, 1), (1, 3), (0, 2)),
    ((3, 1), (2, 0), (0, 3), (1, 2)),
    ((1, 0), (3, 2), (2, 3), (0, 1)),
)[::-1]
BIAS_ROUNDS = (
    ((0, 1), (1, 3), (2, 0), (3, 2)),
    ((0, 3), (3, 0), (1, 2), (2, 1)),
    ((0, 2), (1, 0), (2, 3), (3, 1)),
)[::-1]


BIAS_STEP = 0.5
PROP_STEP = 0.5

F32 = jnp.float32
BF16 = jnp.bfloat16


def complex_dot(pattern, left_re, left_im, right_re, right_im):
    real_part = jnp.einsum(
        pattern, left_re, right_re, preferred_element_type=jnp.float32
    ) - jnp.einsum(pattern, left_im, right_im, preferred_element_type=jnp.float32)
    imag_part = jnp.einsum(
        pattern, left_re, right_im, preferred_element_type=jnp.float32
    ) + jnp.einsum(pattern, left_im, right_re, preferred_element_type=jnp.float32)
    return (real_part, imag_part)


def make_picker(wanted):

    def picker(shard_rows):
        row_count = shard_rows.shape[0]
        select = (wanted[:, None] == jnp.arange(row_count, dtype=jnp.int32)[None, :]).astype(
            jnp.bfloat16
        )
        return jnp.dot(select, shard_rows, preferred_element_type=jnp.float32)

    return picker


def with_collectives(green, fields, orbitals, chol_half, chol_full, chol_count, kq_map):
    q_local = chol_half.shape[0]
    k_local = chol_half.shape[1]
    pair_width = chol_half.shape[3]
    chol_cols = chol_half.shape[4]
    ka_count = lax.axis_size("ka")
    pb_count = lax.axis_size("pb")
    ka_pos = lax.axis_index("ka")
    pb_pos = lax.axis_index("pb")
    local_green = lax.all_to_all(green, "ka", split_axis=3, concat_axis=1, tiled=True)
    walkers = local_green.shape[1]
    per_device = walkers // ka_count
    greens = local_green[0].reshape(walkers, q_local, k_local, 2, pair_width)
    counts = lax.dynamic_slice_in_dim(chol_count, pb_pos * q_local, q_local)
    vec_mask = (jnp.arange(chol_cols, dtype=jnp.int32)[None, :] < counts[:, None]).astype(
        jnp.float32
    )
    bias_re, bias_im = complex_dot(
        "wqkx,qkxn->qwn",
        greens[:, :, :, 0],
        greens[:, :, :, 1],
        chol_half[:, :, 0],
        chol_half[:, :, 1],
    )
    own_rows = (jnp.arange(walkers, dtype=jnp.int32) // per_device == ka_pos).astype(jnp.float32)
    bias_re, bias_im = lax.psum((bias_re, bias_im), "ka")
    bias_re = bias_re * vec_mask[:, None, :]
    bias_im = bias_im * vec_mask[:, None, :]
    hartree = 0.5 * jnp.sum(bias_re * bias_re + bias_im * bias_im, axis=(0, 2)) * own_rows
    field_now = jnp.transpose(fields, (1, 0, 2, 3)).reshape(q_local, walkers, chol_cols)
    shift_re = ((field_now - BIAS_STEP * bias_re) * vec_mask[:, None, :]).astype(jnp.bfloat16)
    shift_im = (-BIAS_STEP * bias_im * vec_mask[:, None, :]).astype(jnp.bfloat16)
    exchange = jnp.zeros((walkers,), jnp.float32)
    for transfer in range(q_local):
        for kpoint in range(k_local):
            chol_row = chol_half[transfer, kpoint].reshape(2, NOCC, M, chol_cols)
            green_row = greens[:, transfer, kpoint].reshape(walkers, 2, NOCC, M)
            cross_re, cross_im = complex_dot(
                "ipn,wjp->wijn", chol_row[0], chol_row[1], green_row[:, 0], green_row[:, 1]
            )
            exchange = exchange + 0.5 * jnp.sum(
                (cross_re * cross_re + cross_im * cross_im) * vec_mask[transfer], axis=(1, 2, 3)
            )
    prop_re, prop_im = complex_dot(
        "qwn,qkyn->qwky", shift_re, shift_im, chol_full[:, :, 0], chol_full[:, :, 1]
    )
    shape = (q_local, walkers, k_local, M, M)
    oper_re = (PROP_STEP * prop_re).astype(jnp.bfloat16).reshape(shape)
    oper_im = (PROP_STEP * prop_im).astype(jnp.bfloat16).reshape(shape)
    normalizer = q_local * pb_count * chol_cols
    total_energy = lax.psum(hartree - exchange, ("ka", "pb")) / normalizer
    energy = lax.dynamic_slice_in_dim(total_energy, ka_pos * per_device, per_device).reshape(
        1, per_device
    )
    initial = orbitals[0].reshape(k_local, walkers, 2, NOCC, M)
    row_width = 2 * pair_width
    my_rows = lax.dynamic_slice_in_dim(kq_map, pb_pos * q_local, q_local, 0)
    wanted = lax.dynamic_slice_in_dim(my_rows, ka_pos * k_local, k_local, 1).reshape(
        q_local * k_local
    )
    picker = make_picker(wanted)
    current = initial
    summed_terms = initial
    for degree in range(1, TAYLOR + 1):
        rounded = current.astype(jnp.bfloat16).reshape(k_local, walkers * row_width)
        fetched = picker(lax.all_gather(rounded, "ka", axis=0, tiled=True))
        shifted_rows = fetched.astype(jnp.bfloat16).reshape(q_local, k_local, walkers, 2, NOCC, M)
        out_re, out_im = complex_dot(
            "xwkpq,xkwiq->kwip",
            oper_re,
            oper_im,
            shifted_rows[:, :, :, 0],
            shifted_rows[:, :, :, 1],
        )
        applied = jnp.stack([out_re, out_im], axis=2)
        applied = lax.psum(applied, "pb")
        current = applied / degree
        summed_terms = summed_terms + current
    propagated = summed_terms.reshape(1, k_local, walkers, row_width)
    return (propagated, energy)


def exchange(array, axis, rounds):
    return [array] + [lax.ppermute(array, axis, pairs) for pairs in rounds]


def origins(axis, rounds):
    at = lax.axis_index(axis)
    found = [at]
    for pairs in rounds:
        source = jnp.int32(0)
        for sender, receiver in pairs:
            source = jnp.where(at == receiver, sender, source)
        found.append(source)
    return found


def operator_group(ka_count, pb_count):
    first = (pb_count - 1) * ka_count + ka_count // 2
    rest = [at for at in range(pb_count * ka_count) if at != first]
    return [first] + rest[::-1]


def prepare_kernel(ka_count, pb_count, walkers, map_ref, count_ref, mask_ref, picks_ref, own_ref):
    kept = count_ref[lax.axis_index("pb")]
    column = lax.broadcasted_iota(jnp.int32, mask_ref.shape, 1)
    mask_ref[...] = jnp.where(column < kept, 1.0, 0.0)
    kpoints = map_ref.shape[1]
    k_local = kpoints // ka_count
    span = k_local * walkers

    def place(k):
        return k // k_local * (2 * span) + lax.rem(k, k_local) * walkers

    lane = lax.broadcasted_iota(jnp.int32, (1, LANES), 1)
    lane_q = lane // (LANES // pb_count)
    lane_ka = lax.rem(lane, LANES // pb_count) // (2 * span)
    lane_part = lax.rem(lane, 2 * span) // span
    lane_k = lane_ka * k_local + lax.rem(lane, span) // walkers
    wanted = jnp.zeros((1, LANES), jnp.int32)
    for q in range(pb_count):
        for k in range(kpoints):
            wanted = jnp.where((lane_q == q) & (lane_k == k), place(map_ref[q, k]), wanted)
    wanted = wanted + lax.rem(lane, walkers)
    group = 2 * span
    own_q = lax.rem(lane, pb_count * group) // group
    own_k = lax.rem(lane, span) // walkers
    own = jnp.zeros((1, LANES), jnp.int32)
    first = lax.axis_index("ka") * k_local
    for q in range(pb_count):
        for k in range(k_local):
            own = jnp.where((own_q == q) & (own_k == k), place(map_ref[q, first + k]), own)
    own_ref[...] = jnp.broadcast_to(own + lax.rem(lane, walkers), own_ref.shape)
    row = lax.broadcasted_iota(jnp.int32, (LANES, LANES), 0)
    real = jnp.where(row == wanted, 1.0, 0.0)
    imag = jnp.where(row == wanted + span, jnp.where(lane_part == 0, 1.0, -1.0), 0.0)
    picks_ref[...] = jnp.concatenate([real, imag], axis=1).astype(BF16)


def bias_kernel(ka_count, k_local, *refs):
    *greens, chol_ref, orbitals_ref, mask_ref, bias_ref, own_ref, table = refs
    for source, green_ref in zip(origins("ka", GREEN_ROUNDS), greens):
        table[source] = green_ref[...].astype(F32)
    first = lax.axis_index("ka") * k_local
    width = chol_ref.shape[2]
    rows = 2 * ka_count
    total = jnp.zeros((rows, bias_ref.shape[1]), F32)
    for k in range(k_local):
        green = jnp.concatenate(
            [table[w, pl.ds(first + k, 1), :] for w in range(ka_count)], axis=0
        )
        real, imag = green[:, :width], green[:, width:]
        both = jnp.concatenate([real, imag], axis=0)
        turned = jnp.concatenate([-imag, real], axis=0)
        own_ref[k] = both
        total += jnp.dot(both.astype(BF16), chol_ref[k, 0], preferred_element_type=F32)
        total += jnp.dot(turned.astype(BF16), chol_ref[k, 1], preferred_element_type=F32)
    bias_ref[:rows] = total * mask_ref[...]
    window = jnp.concatenate([orbitals_ref[k] for k in range(k_local)], axis=0)
    count, width = window.shape
    bias_ref[rows : rows + count, :width] = window
    bias_ref[rows : rows + count, width:] = jnp.zeros((count, bias_ref.shape[1] - width), F32)


def exchange_kernel(
    k_local, pb_count, own_ref, chol_ref, mask_ref, lanes_ref, out_ref, fold_ref, picks_ref
):
    walkers, width, columns = own_ref.shape[1] // 2, own_ref.shape[2], chol_ref.shape[3]
    rows = 2 * walkers
    lane = lax.broadcasted_iota(jnp.int32, (rows, LANES), 1)
    total = jnp.zeros((rows, columns), F32)
    for k in range(k_local):
        both = jnp.concatenate([own_ref[k], jnp.zeros((rows, LANES - width), F32)], axis=1)
        turned = jnp.concatenate([-both[walkers:], both[:walkers]], axis=0)
        sides = []
        for side in (both, turned):
            rolled = {
                step: side if step == 0 else pltpu.roll(side, (step * M) % LANES, 1)
                for step in range(1 - NOCC, NOCC)
            }
            blocks = []
            for i in range(NOCC):
                inside = (lane >= i * M) & (lane < (i + 1) * M)
                for j in range(NOCC):
                    blocks.append(jnp.where(inside, rolled[i - j], 0.0))
            sides.append(jnp.concatenate(blocks, axis=0)[:, :width].astype(BF16))
        cross = jnp.dot(sides[0], chol_ref[k, 0], preferred_element_type=F32)
        cross += jnp.dot(sides[1], chol_ref[k, 1], preferred_element_type=F32)
        cross = cross * cross
        for block in range(NOCC * NOCC):
            total += cross[block * rows : (block + 1) * rows]
    total = total * mask_ref[:rows]
    total = total[:walkers] + total[walkers:]
    summed = 0.5 * jnp.sum(total, axis=1, keepdims=True)
    out_ref[...] = jnp.broadcast_to(summed, out_ref.shape)
    span = k_local * walkers
    group = 2 * span
    lane = lax.broadcasted_iota(jnp.int32, (1, LANES), 1)
    source = lax.rem(lane, pb_count * group) // group * (LANES // pb_count) + lax.rem(lane, group)
    source = source + lax.axis_index("ka") * group
    row = lax.broadcasted_iota(jnp.int32, (LANES, LANES), 0)
    fold_ref[...] = jnp.where(row == source, 1.0, 0.0).astype(BF16)
    wanted = lanes_ref[:1]
    sign = jnp.where(lax.rem(lane, group) < span, 1.0, -1.0)
    for i in range(NOCC):
        inside = lane // (LANES // NOCC) == i
        real = jnp.where(inside & (row == wanted), 1.0, 0.0)
        imag = jnp.where(inside & (row == wanted + span), sign, 0.0)
        both = jnp.concatenate([real, imag], axis=1)
        picks_ref[i * LANES : (i + 1) * LANES] = both.astype(BF16)


def operator_kernel(k_local, *refs):
    *parts, fields_ref, mask_ref, exchange_ref, chol_ref, picks_ref = refs[:-5]
    out_ref, first_ref, products, turned_ref, term = refs[-5:]
    walkers, columns = fields_ref.shape
    bias = parts[0][: 2 * walkers]
    for part in parts[1:]:
        bias = bias + part[: 2 * walkers]
    pairs = M * M
    tiles = columns // LANES
    group = LANES // (2 * tiles)
    bias_re, bias_im = bias[:walkers], bias[walkers:]
    hartree = 0.5 * jnp.sum(bias_re * bias_re + bias_im * bias_im, axis=1, keepdims=True)
    own = lax.broadcasted_iota(jnp.int32, (walkers, 1), 0) == lax.axis_index("ka")
    energy = jnp.where(own, hartree, 0.0) - exchange_ref[:, :1]
    kept = mask_ref[:walkers]
    shift_re = (fields_ref[...] - BIAS_STEP * bias_re) * kept
    shift_im = -BIAS_STEP * bias_im * kept
    span = k_local * walkers
    pair = NOCC * M
    term[...] = jnp.zeros_like(term)
    for source, part in zip(origins("ka", BIAS_ROUNDS), parts):
        start = pl.multiple_of(source * (2 * span), 2 * span)
        window = part[2 * walkers :]
        term[pl.ds(start, span), :pair] = window[:, :pair]
        term[pl.ds(start + span, span), :pair] = window[:, pair : 2 * pair]
    first_ref[...] = jnp.dot(
        term[...].T.astype(BF16), picks_ref[...], preferred_element_type=F32
    )
    weights = []
    for k in range(k_local):
        before, after = k * walkers, span - (k + 1) * walkers
        pieces = []
        for tile in range(tiles):
            at = slice(tile * LANES, (tile + 1) * LANES)
            for first, second in ((shift_re, shift_im), (-shift_im, shift_re)):
                for side in (first, second):
                    pieces += [(before, None), (walkers, side[:, at]), (after, None)]
                pieces.append((group - 2 * span, None))
        weights.append(
            jnp.concatenate(
                [jnp.zeros((n, LANES), F32) if p is None else p for n, p in pieces if n], axis=0
            ).astype(BF16)
        )
    products[...] = lax.dot_general(
        jnp.concatenate([chol_ref[k] for k in range(k_local)], axis=1),
        jnp.concatenate(weights, axis=1),
        (((1,), (1,)), ((), ())),
        preferred_element_type=F32,
    )
    lane = lax.broadcasted_iota(jnp.int32, (pairs, LANES), 1)
    merged = products[pl.ds(0, pairs, stride=2 * tiles), :]
    for at in range(1, 2 * tiles):
        row = products[pl.ds(at, pairs, stride=2 * tiles), :]
        merged = jnp.where(lane >= at * group, row, merged)
    turned_ref[:pairs] = merged
    copies, rows, width = out_ref.shape
    lane = lax.broadcasted_iota(jnp.int32, (rows, LANES), 1)
    for at in range(0, width, LANES):
        block = turned_ref[at : at + LANES].T
        block = PROP_STEP * sum(block[n * group : n * group + rows] for n in range(2 * tiles))
        if at + LANES > pairs:
            share = jnp.concatenate([energy, jnp.zeros((rows - walkers, 1), F32)], axis=0)
            block = jnp.where(lane + at < pairs, block, 0.0)
            for piece in range(3):
                head = share.astype(BF16).astype(F32)
                block = jnp.where(lane + at == pairs + piece, head, block)
                share = share - head
        for copy in range(copies):
            out_ref[copy, :, at : at + LANES] = block.astype(BF16)


def taylor_kernel(
    pb_count, normalizer, blocks_ref, first_ref, picks_ref, fold_ref, own_picks_ref, orbitals_ref,
    out_ref, energy_ref, turned, folded, picked, term, kept,
):
    pairs = M * M
    k_local, walkers, _ = out_ref.shape
    span = k_local * walkers
    ka_pos = lax.axis_index("ka")
    count, _, width = blocks_ref.shape
    group = operator_group(count // pb_count, pb_count)
    places = [group.index(n) for n in range(count)]
    for at in range(0, width, LANES):
        tile = jnp.concatenate([blocks_ref[n, :, at : at + LANES] for n in places], axis=0).T
        turned[at : at + LANES] = tile.astype(F32)
        folded[at : at + LANES] = jnp.dot(tile, fold_ref[...], preferred_element_type=F32)
    shares = turned[pairs : pairs + 3]
    lane = lax.broadcasted_iota(jnp.int32, shares.shape, 1)
    shares = jnp.where(lax.rem(lane, 2 * span) == ka_pos, shares, 0.0)
    shares = jnp.sum(jnp.sum(shares, axis=0, keepdims=True), axis=1, keepdims=True)
    energy_ref[...] = shares / normalizer
    lane = lax.broadcasted_iota(jnp.int32, (M, LANES), 1)
    imaginary = lax.rem(lane, 2 * span) >= span

    def joined(straight, crossed):
        up, down = pltpu.roll(crossed, span, 1), pltpu.roll(crossed, LANES - span, 1)
        return straight + jnp.where(imaginary, up, down)

    sums = [None] * NOCC
    for degree in range(1, TAYLOR):
        source, stride = (first_ref, M) if degree == 1 else (picked, ROWS)
        straight = [jnp.zeros((M, LANES), F32) for _ in range(NOCC)]
        crossed = [jnp.zeros((M, LANES), F32) for _ in range(NOCC)]
        for c in range(M):
            column = turned[pl.ds(c, M, stride=M), :]
            for i in range(NOCC):
                at = i * stride + c
                straight[i] += column * source[at : at + 1, :LANES]
                crossed[i] += column * source[at : at + 1, LANES:]
        for i in range(NOCC):
            applied = joined(straight[i], crossed[i])
            applied = applied + pltpu.roll(applied, LANES // pb_count, 1)
            current = applied * (1.0 / degree)
            sums[i] = current if degree == 1 else sums[i] + current
            at = i * ROWS
            term[at : at + M] = current
            if degree == 1:
                term[at + M : at + ROWS] = jnp.zeros((ROWS - M, LANES), F32)
        if degree < TAYLOR - 1:
            picked[...] = jnp.dot(
                term[...].astype(BF16), picks_ref[...], preferred_element_type=F32
            )
    wide = jnp.concatenate([term[i * ROWS : (i + 1) * ROWS] for i in range(NOCC)], axis=1)
    picked[:ROWS] = jnp.dot(wide.astype(BF16), own_picks_ref[...], preferred_element_type=F32)
    for i in range(NOCC):
        kept[i * ROWS : i * ROWS + M] = sums[i]
        kept[i * ROWS + M : (i + 1) * ROWS] = jnp.zeros((ROWS - M, LANES), F32)
    turned[:LANES] = kept[...].T
    sums = turned[pl.ds(pl.multiple_of(ka_pos * (2 * span), 2 * span), 2 * span), :]
    straight = [jnp.zeros((M, LANES), F32) for _ in range(2)]
    crossed = [jnp.zeros((M, LANES), F32) for _ in range(2)]
    for c in range(M):
        column = folded[pl.ds(c, M, stride=M), :]
        straight[c % 2] += column * picked[c : c + 1, :LANES]
        crossed[c % 2] += column * picked[c : c + 1, LANES:]
    applied = joined(straight[0] + straight[1], crossed[0] + crossed[1])
    applied = (applied + pltpu.roll(applied, LANES - 2 * span, 1)) * (1.0 / TAYLOR)
    kept[:M] = applied
    kept[M:ROWS] = jnp.zeros((ROWS - M, LANES), F32)
    last = kept[:ROWS].T
    last = jnp.concatenate(
        [last[i * ROWS : i * ROWS + 2 * span] for i in range(NOCC)], axis=1
    )
    both = sums + last
    both = jnp.concatenate([both[:, i * ROWS : i * ROWS + M] for i in range(NOCC)], axis=1)
    both = jnp.concatenate([both[:span], both[span:]], axis=1)
    for k in range(k_local):
        out_ref[k] = orbitals_ref[k] + both[k * walkers : (k + 1) * walkers]


def call(kernel, out, scratch=(), scalars=0, operands=0, flops=None):
    spaces = [pltpu.SMEM] * scalars + [pltpu.VMEM] * operands
    cost = None
    if flops is not None:
        cost = pl.CostEstimate(flops=flops, bytes_accessed=0, transcendentals=0)
    return pl.pallas_call(
        kernel,
        out_shape=out,
        in_specs=[pl.BlockSpec(memory_space=space) for space in spaces],
        out_specs=jax.tree.map(lambda _: pl.BlockSpec(memory_space=pltpu.VMEM), out),
        scratch_shapes=list(scratch),
        cost_estimate=cost,
        compiler_params=pltpu.CompilerParams(vmem_limit_bytes=24 * 2**20),
    )


def direct(green, fields, orbitals, chol_half, chol_full, chol_count, kq_map):
    k_local, pair_width, chol_cols = chol_half.shape[1], chol_half.shape[3], chol_half.shape[4]
    ka_count, pb_count = lax.axis_size("ka"), lax.axis_size("pb")
    walkers = ka_count
    kpoints = green.shape[3]
    span = k_local * walkers
    shape = jax.ShapeDtypeStruct
    tiles = chol_cols // LANES
    own_green = green.reshape(kpoints, 2 * pair_width)
    greens = exchange(own_green, "ka", GREEN_ROUNDS)
    half = chol_half.reshape(k_local, 2, pair_width, chol_cols)
    full = jnp.transpose(
        chol_full.reshape(k_local, 2, M * M, tiles, LANES), (0, 2, 3, 1, 4)
    ).reshape(k_local, M * M * tiles * 2, LANES)
    own_fields = fields.reshape(walkers, chol_cols)
    own_orbitals = orbitals.reshape(k_local, walkers, 2 * pair_width)
    mask, picks, own_lanes = call(
        functools.partial(prepare_kernel, ka_count, pb_count, walkers),
        (
            shape((2 * walkers, chol_cols), F32),
            shape((LANES, 2 * LANES), BF16),
            shape((2 * walkers, LANES), jnp.int32),
        ),
        scalars=2,
        flops=10**9,
    )(kq_map, chol_count)
    bias, own = call(
        functools.partial(bias_kernel, ka_count, k_local),
        (
            shape((2 * walkers + span, chol_cols), F32),
            shape((k_local, 2 * walkers, pair_width), F32),
        ),
        [pltpu.VMEM((walkers, kpoints, 2 * pair_width), F32)],
        operands=len(greens) + 3,
    )(*greens, half, own_orbitals, mask)
    parts = exchange(bias, "ka", BIAS_ROUNDS)
    shares, fold, own_picks = call(
        functools.partial(exchange_kernel, k_local, pb_count),
        (
            shape((walkers, LANES), F32),
            shape((LANES, LANES), BF16),
            shape((NOCC * LANES, 2 * LANES), BF16),
        ),
        operands=4,
    )(own, half, mask, own_lanes)
    width = -(-(M * M + 3) // LANES) * LANES
    blocks, first = call(
        functools.partial(operator_kernel, k_local),
        (
            shape((ka_count * pb_count, 2 * span, width), BF16),
            shape((LANES, 2 * LANES), F32),
        ),
        [
            pltpu.VMEM((2 * M * M * tiles, LANES), F32),
            pltpu.VMEM((width, LANES), F32),
            pltpu.VMEM((LANES, LANES), F32),
        ],
        operands=len(parts) + 5,
    )(*parts, own_fields, mask, shares, full, picks)
    group = operator_group(ka_count, pb_count)
    blocks = lax.all_to_all(
        blocks, ("pb", "ka"), 0, 0, axis_index_groups=[group], tiled=True
    )
    propagated, energy = call(
        functools.partial(taylor_kernel, pb_count, float(pb_count * chol_cols)),
        (shape((k_local, walkers, 2 * pair_width), F32), shape((1, 1), F32)),
        [
            pltpu.VMEM((width, LANES), F32),
            pltpu.VMEM((width, LANES), F32),
            pltpu.VMEM((NOCC * ROWS, 2 * LANES), F32),
            pltpu.VMEM((NOCC * ROWS, LANES), F32),
            pltpu.VMEM((NOCC * ROWS, LANES), F32),
        ],
        operands=6,
    )(blocks, first, picks, fold, own_picks, own_orbitals)
    return (propagated[None], energy)


def on_device(green, fields, orbitals, chol_half, chol_full, chol_count, kq_map):
    ka_count, pb_count = lax.axis_size("ka"), lax.axis_size("pb")
    walkers = orbitals.shape[2]
    fits = 2 * pb_count * kq_map.shape[1] * walkers == LANES
    fits = fits and chol_half.shape[1] * walkers == 8 and chol_half.shape[4] == 2 * LANES
    fits = fits and ka_count == 4 and pb_count == 2
    if fits and chol_half.shape[0] == 1 and walkers == ka_count:
        return direct(green, fields, orbitals, chol_half, chol_full, chol_count, kq_map)
    return with_collectives(green, fields, orbitals, chol_half, chol_full, chol_count, kq_map)


def solution(mesh):
    placed = (
        P("wa", ("grp", "ka"), "pb", None, None),
        P("wa", "pb", "grp", None),
        P("wa", "ka", "grp", None),
        P("pb", "ka", None, None, None),
        P("pb", "ka", None, None, None),
        P(),
        P(),
    )
    return jax.shard_map(
        on_device,
        mesh=mesh,
        in_specs=placed,
        out_specs=(P("wa", "ka", "grp", None), P("wa", ("grp", "ka"))),
        check_vma=False,
    )
```

```python
import functools

import jax
import jax.numpy as jnp
from jax import lax
from jax.experimental import pallas as pl
from jax.experimental.pallas import tpu as pltpu
from jax.sharding import PartitionSpec as P

M = 26
NOCC = 4
TAYLOR = 3
LANES = 128
ROWS = 32

GREEN_ROUNDS = (
    ((3, 0), (2, 1), (1, 3), (0, 2)),
    ((3, 1), (2, 0), (0, 3), (1, 2)),
    ((1, 0), (3, 2), (2, 3), (0, 1)),
)[::-1]
BIAS_ROUNDS = (
    ((0, 1), (1, 3), (2, 0), (3, 2)),
    ((0, 3), (3, 0), (1, 2), (2, 1)),
    ((0, 2), (1, 0), (2, 3), (3, 1)),
)[::-1]


BIAS_STEP = 0.5
PROP_STEP = 0.5

F32 = jnp.float32
BF16 = jnp.bfloat16


def complex_dot(pattern, left_re, left_im, right_re, right_im):
    real_part = jnp.einsum(
        pattern, left_re, right_re, preferred_element_type=jnp.float32
    ) - jnp.einsum(pattern, left_im, right_im, preferred_element_type=jnp.float32)
    imag_part = jnp.einsum(
        pattern, left_re, right_im, preferred_element_type=jnp.float32
    ) + jnp.einsum(pattern, left_im, right_re, preferred_element_type=jnp.float32)
    return (real_part, imag_part)


def make_picker(wanted):

    def picker(shard_rows):
        row_count = shard_rows.shape[0]
        select = (wanted[:, None] == jnp.arange(row_count, dtype=jnp.int32)[None, :]).astype(
            jnp.bfloat16
        )
        return jnp.dot(select, shard_rows, preferred_element_type=jnp.float32)

    return picker


def with_collectives(green, fields, orbitals, chol_half, chol_full, chol_count, kq_map):
    q_local = chol_half.shape[0]
    k_local = chol_half.shape[1]
    pair_width = chol_half.shape[3]
    chol_cols = chol_half.shape[4]
    ka_count = lax.axis_size("ka")
    pb_count = lax.axis_size("pb")
    ka_pos = lax.axis_index("ka")
    pb_pos = lax.axis_index("pb")
    local_green = lax.all_to_all(green, "ka", split_axis=3, concat_axis=1, tiled=True)
    walkers = local_green.shape[1]
    per_device = walkers // ka_count
    greens = local_green[0].reshape(walkers, q_local, k_local, 2, pair_width)
    counts = lax.dynamic_slice_in_dim(chol_count, pb_pos * q_local, q_local)
    vec_mask = (jnp.arange(chol_cols, dtype=jnp.int32)[None, :] < counts[:, None]).astype(
        jnp.float32
    )
    bias_re, bias_im = complex_dot(
        "wqkx,qkxn->qwn",
        greens[:, :, :, 0],
        greens[:, :, :, 1],
        chol_half[:, :, 0],
        chol_half[:, :, 1],
    )
    own_rows = (jnp.arange(walkers, dtype=jnp.int32) // per_device == ka_pos).astype(jnp.float32)
    bias_re, bias_im = lax.psum((bias_re, bias_im), "ka")
    bias_re = bias_re * vec_mask[:, None, :]
    bias_im = bias_im * vec_mask[:, None, :]
    hartree = 0.5 * jnp.sum(bias_re * bias_re + bias_im * bias_im, axis=(0, 2)) * own_rows
    field_now = jnp.transpose(fields, (1, 0, 2, 3)).reshape(q_local, walkers, chol_cols)
    shift_re = ((field_now - BIAS_STEP * bias_re) * vec_mask[:, None, :]).astype(jnp.bfloat16)
    shift_im = (-BIAS_STEP * bias_im * vec_mask[:, None, :]).astype(jnp.bfloat16)
    exchange = jnp.zeros((walkers,), jnp.float32)
    for transfer in range(q_local):
        for kpoint in range(k_local):
            chol_row = chol_half[transfer, kpoint].reshape(2, NOCC, M, chol_cols)
            green_row = greens[:, transfer, kpoint].reshape(walkers, 2, NOCC, M)
            cross_re, cross_im = complex_dot(
                "ipn,wjp->wijn", chol_row[0], chol_row[1], green_row[:, 0], green_row[:, 1]
            )
            exchange = exchange + 0.5 * jnp.sum(
                (cross_re * cross_re + cross_im * cross_im) * vec_mask[transfer], axis=(1, 2, 3)
            )
    prop_re, prop_im = complex_dot(
        "qwn,qkyn->qwky", shift_re, shift_im, chol_full[:, :, 0], chol_full[:, :, 1]
    )
    shape = (q_local, walkers, k_local, M, M)
    oper_re = (PROP_STEP * prop_re).astype(jnp.bfloat16).reshape(shape)
    oper_im = (PROP_STEP * prop_im).astype(jnp.bfloat16).reshape(shape)
    normalizer = q_local * pb_count * chol_cols
    total_energy = lax.psum(hartree - exchange, ("ka", "pb")) / normalizer
    energy = lax.dynamic_slice_in_dim(total_energy, ka_pos * per_device, per_device).reshape(
        1, per_device
    )
    initial = orbitals[0].reshape(k_local, walkers, 2, NOCC, M)
    row_width = 2 * pair_width
    my_rows = lax.dynamic_slice_in_dim(kq_map, pb_pos * q_local, q_local, 0)
    wanted = lax.dynamic_slice_in_dim(my_rows, ka_pos * k_local, k_local, 1).reshape(
        q_local * k_local
    )
    picker = make_picker(wanted)
    current = initial
    summed_terms = initial
    for degree in range(1, TAYLOR + 1):
        rounded = current.astype(jnp.bfloat16).reshape(k_local, walkers * row_width)
        fetched = picker(lax.all_gather(rounded, "ka", axis=0, tiled=True))
        shifted_rows = fetched.astype(jnp.bfloat16).reshape(q_local, k_local, walkers, 2, NOCC, M)
        out_re, out_im = complex_dot(
            "xwkpq,xkwiq->kwip",
            oper_re,
            oper_im,
            shifted_rows[:, :, :, 0],
            shifted_rows[:, :, :, 1],
        )
        applied = jnp.stack([out_re, out_im], axis=2)
        applied = lax.psum(applied, "pb")
        current = applied / degree
        summed_terms = summed_terms + current
    propagated = summed_terms.reshape(1, k_local, walkers, row_width)
    return (propagated, energy)


def exchange(array, axis, rounds):
    return [array] + [lax.ppermute(array, axis, pairs) for pairs in rounds]


def origins(axis, rounds):
    at = lax.axis_index(axis)
    found = [at]
    for pairs in rounds:
        source = jnp.int32(0)
        for sender, receiver in pairs:
            source = jnp.where(at == receiver, sender, source)
        found.append(source)
    return found


def operator_group(ka_count, pb_count):
    first = (pb_count - 1) * ka_count + ka_count // 2
    rest = [at for at in range(pb_count * ka_count) if at != first]
    return [first] + rest[::-1]


def prepare_kernel(ka_count, pb_count, walkers, map_ref, count_ref, mask_ref, picks_ref):
    kept = count_ref[lax.axis_index("pb")]
    column = lax.broadcasted_iota(jnp.int32, mask_ref.shape, 1)
    mask_ref[...] = jnp.where(column < kept, 1.0, 0.0)
    kpoints = map_ref.shape[1]
    k_local = kpoints // ka_count
    span = k_local * walkers
    lane = lax.broadcasted_iota(jnp.int32, (1, LANES), 1)
    lane_q = lane // (LANES // pb_count)
    lane_ka = lax.rem(lane, LANES // pb_count) // (2 * span)
    lane_part = lax.rem(lane, 2 * span) // span
    lane_k = lane_ka * k_local + lax.rem(lane, span) // walkers
    wanted = jnp.zeros((1, LANES), jnp.int32)
    for q in range(pb_count):
        for k in range(kpoints):
            source = map_ref[q, k]
            source = source // k_local * (2 * span) + lax.rem(source, k_local) * walkers
            wanted = jnp.where((lane_q == q) & (lane_k == k), source, wanted)
    wanted = wanted + lax.rem(lane, walkers)
    row = lax.broadcasted_iota(jnp.int32, (LANES, LANES), 0)
    real = jnp.where(row == wanted, 1.0, 0.0)
    imag = jnp.where(row == wanted + span, jnp.where(lane_part == 0, 1.0, -1.0), 0.0)
    picks_ref[...] = jnp.concatenate([real, imag], axis=1).astype(BF16)


def bias_kernel(ka_count, k_local, *refs):
    *greens, chol_ref, orbitals_ref, mask_ref, bias_ref, own_ref, table = refs
    for source, green_ref in zip(origins("ka", GREEN_ROUNDS), greens):
        table[source] = green_ref[...].astype(F32)
    first = lax.axis_index("ka") * k_local
    width = chol_ref.shape[2]
    rows = 2 * ka_count
    total = jnp.zeros((rows, bias_ref.shape[1]), F32)
    for k in range(k_local):
        green = jnp.concatenate(
            [table[w, pl.ds(first + k, 1), :] for w in range(ka_count)], axis=0
        )
        real, imag = green[:, :width], green[:, width:]
        both = jnp.concatenate([real, imag], axis=0)
        turned = jnp.concatenate([-imag, real], axis=0)
        own_ref[k] = both
        total += jnp.dot(both.astype(BF16), chol_ref[k, 0], preferred_element_type=F32)
        total += jnp.dot(turned.astype(BF16), chol_ref[k, 1], preferred_element_type=F32)
    bias_ref[:rows] = total * mask_ref[...]
    window = jnp.concatenate([orbitals_ref[k] for k in range(k_local)], axis=0)
    count, width = window.shape
    bias_ref[rows : rows + count, :width] = window
    bias_ref[rows : rows + count, width:] = jnp.zeros((count, bias_ref.shape[1] - width), F32)


def exchange_kernel(k_local, own_ref, chol_ref, mask_ref, out_ref):
    walkers, width, columns = own_ref.shape[1] // 2, own_ref.shape[2], chol_ref.shape[3]
    rows = 2 * walkers
    lane = lax.broadcasted_iota(jnp.int32, (rows, LANES), 1)
    total = jnp.zeros((rows, columns), F32)
    for k in range(k_local):
        both = jnp.concatenate([own_ref[k], jnp.zeros((rows, LANES - width), F32)], axis=1)
        turned = jnp.concatenate([-both[walkers:], both[:walkers]], axis=0)
        sides = []
        for side in (both, turned):
            rolled = {
                step: side if step == 0 else pltpu.roll(side, (step * M) % LANES, 1)
                for step in range(1 - NOCC, NOCC)
            }
            blocks = []
            for i in range(NOCC):
                inside = (lane >= i * M) & (lane < (i + 1) * M)
                for j in range(NOCC):
                    blocks.append(jnp.where(inside, rolled[i - j], 0.0))
            sides.append(jnp.concatenate(blocks, axis=0)[:, :width].astype(BF16))
        cross = jnp.dot(sides[0], chol_ref[k, 0], preferred_element_type=F32)
        cross += jnp.dot(sides[1], chol_ref[k, 1], preferred_element_type=F32)
        cross = cross * cross
        for block in range(NOCC * NOCC):
            total += cross[block * rows : (block + 1) * rows]
    total = total * mask_ref[:rows]
    total = total[:walkers] + total[walkers:]
    summed = 0.5 * jnp.sum(total, axis=1, keepdims=True)
    out_ref[...] = jnp.broadcast_to(summed, out_ref.shape)


def operator_kernel(k_local, *refs):
    *parts, fields_ref, mask_ref, exchange_ref, chol_ref, out_ref, products, turned_ref = refs
    walkers, columns = fields_ref.shape
    bias = parts[0][: 2 * walkers]
    for part in parts[1:]:
        bias = bias + part[: 2 * walkers]
    pairs = M * M
    tiles = columns // LANES
    group = LANES // (2 * tiles)
    bias_re, bias_im = bias[:walkers], bias[walkers:]
    hartree = 0.5 * jnp.sum(bias_re * bias_re + bias_im * bias_im, axis=1, keepdims=True)
    own = lax.broadcasted_iota(jnp.int32, (walkers, 1), 0) == lax.axis_index("ka")
    energy = jnp.where(own, hartree, 0.0) - exchange_ref[:, :1]
    kept = mask_ref[:walkers]
    shift_re = (fields_ref[...] - BIAS_STEP * bias_re) * kept
    shift_im = -BIAS_STEP * bias_im * kept
    span = k_local * walkers
    weights = []
    for k in range(k_local):
        before, after = k * walkers, span - (k + 1) * walkers
        pieces = []
        for tile in range(tiles):
            at = slice(tile * LANES, (tile + 1) * LANES)
            for first, second in ((shift_re, shift_im), (-shift_im, shift_re)):
                for side in (first, second):
                    pieces += [(before, None), (walkers, side[:, at]), (after, None)]
                pieces.append((group - 2 * span, None))
        weights.append(
            jnp.concatenate(
                [jnp.zeros((n, LANES), F32) if p is None else p for n, p in pieces if n], axis=0
            ).astype(BF16)
        )
    products[...] = lax.dot_general(
        jnp.concatenate([chol_ref[k] for k in range(k_local)], axis=1),
        jnp.concatenate(weights, axis=1),
        (((1,), (1,)), ((), ())),
        preferred_element_type=F32,
    )
    lane = lax.broadcasted_iota(jnp.int32, (pairs, LANES), 1)
    merged = products[pl.ds(0, pairs, stride=2 * tiles), :]
    for at in range(1, 2 * tiles):
        row = products[pl.ds(at, pairs, stride=2 * tiles), :]
        merged = jnp.where(lane >= at * group, row, merged)
    turned_ref[:pairs] = merged
    copies, rows, width = out_ref.shape
    lane = lax.broadcasted_iota(jnp.int32, (rows, LANES), 1)
    for at in range(0, width, LANES):
        block = turned_ref[at : at + LANES].T
        block = PROP_STEP * sum(block[n * group : n * group + rows] for n in range(2 * tiles))
        if at + LANES > pairs:
            share = jnp.concatenate([energy, jnp.zeros((rows - walkers, 1), F32)], axis=0)
            block = jnp.where(lane + at < pairs, block, 0.0)
            for piece in range(3):
                head = share.astype(BF16).astype(F32)
                block = jnp.where(lane + at == pairs + piece, head, block)
                share = share - head
        for copy in range(copies):
            out_ref[copy, :, at : at + LANES] = block.astype(BF16)


def taylor_kernel(pb_count, normalizer, blocks_ref, *refs):
    *windows, picks_ref, orbitals_ref = refs[:-8]
    out_ref, energy_ref, turned, picked, term, result, total, sems = refs[-8:]
    pairs = M * M
    pair = NOCC * M
    k_local, walkers, _ = out_ref.shape
    span = k_local * walkers
    ka_pos = lax.axis_index("ka")
    term[...] = jnp.zeros_like(term)
    for source, window_ref in zip(origins("ka", BIAS_ROUNDS), windows):
        start = pl.multiple_of(source * (2 * span), 2 * span)
        window = window_ref[window_ref.shape[0] - span :]
        term[pl.ds(start, span), :pair] = window[:, :pair]
        term[pl.ds(start + span, span), :pair] = window[:, pair : 2 * pair]
    picked[...] = jnp.dot(term[...].T.astype(BF16), picks_ref[...], preferred_element_type=F32)
    count, _, width = blocks_ref.shape
    group = operator_group(count // pb_count, pb_count)
    places = [group.index(n) for n in range(count)]
    for at in range(0, width, LANES):
        tile = jnp.concatenate([blocks_ref[n, :, at : at + LANES] for n in places], axis=0)
        turned[at : at + LANES] = tile.T.astype(F32)
    shares = turned[pairs : pairs + 3]
    lane = lax.broadcasted_iota(jnp.int32, shares.shape, 1)
    shares = jnp.where(lax.rem(lane, 2 * span) == ka_pos, shares, 0.0)
    shares = jnp.sum(jnp.sum(shares, axis=0, keepdims=True), axis=1, keepdims=True)
    total[...] = shares / normalizer
    energy_copy = pltpu.make_async_copy(total, energy_ref, sems.at[0])
    energy_copy.start()
    lane = lax.broadcasted_iota(jnp.int32, (M, LANES), 1)
    imaginary = lax.rem(lane, 2 * span) >= span
    sums = [jnp.zeros((M, LANES), F32) for _ in range(NOCC)]
    for degree in range(1, TAYLOR + 1):
        stride = M if degree == 1 else ROWS
        straight = [jnp.zeros((M, LANES), F32) for _ in range(NOCC)]
        crossed = [jnp.zeros((M, LANES), F32) for _ in range(NOCC)]
        for c in range(M):
            column = turned[pl.ds(c, M, stride=M), :]
            for i in range(NOCC):
                at = i * stride + c
                straight[i] += column * picked[at : at + 1, :LANES]
                crossed[i] += column * picked[at : at + 1, LANES:]
        for i in range(NOCC):
            other = jnp.where(
                imaginary, pltpu.roll(crossed[i], span, 1), pltpu.roll(crossed[i], LANES - span, 1)
            )
            applied = straight[i] + other
            applied = applied + pltpu.roll(applied, LANES // pb_count, 1)
            current = applied * (1.0 / degree)
            sums[i] = sums[i] + current
            term[i * ROWS : i * ROWS + M] = current if degree < TAYLOR else sums[i]
        if degree < TAYLOR:
            picked[...] = jnp.dot(
                term[...].astype(BF16), picks_ref[...], preferred_element_type=F32
            )
    turned[:LANES] = term[...].T
    both = turned[pl.ds(pl.multiple_of(ka_pos * (2 * span), 2 * span), 2 * span), :]
    both = jnp.concatenate([both[:, i * ROWS : i * ROWS + M] for i in range(NOCC)], axis=1)
    both = jnp.concatenate([both[:span], both[span:]], axis=1)
    for k in range(k_local):
        result[k] = orbitals_ref[k] + both[k * walkers : (k + 1) * walkers]
    result_copy = pltpu.make_async_copy(result, out_ref, sems.at[1])
    result_copy.start()
    energy_copy.wait()
    result_copy.wait()


def call(kernel, out, scratch=(), scalars=0, operands=0, flops=None, space=pltpu.VMEM):
    spaces = [pltpu.SMEM] * scalars + [pltpu.VMEM] * operands
    cost = None
    if flops is not None:
        cost = pl.CostEstimate(flops=flops, bytes_accessed=0, transcendentals=0)
    return pl.pallas_call(
        kernel,
        out_shape=out,
        in_specs=[pl.BlockSpec(memory_space=space) for space in spaces],
        out_specs=jax.tree.map(lambda _: pl.BlockSpec(memory_space=space), out),
        scratch_shapes=list(scratch),
        cost_estimate=cost,
        compiler_params=pltpu.CompilerParams(vmem_limit_bytes=24 * 2**20),
    )


def direct(green, fields, orbitals, chol_half, chol_full, chol_count, kq_map):
    k_local, pair_width, chol_cols = chol_half.shape[1], chol_half.shape[3], chol_half.shape[4]
    ka_count, pb_count = lax.axis_size("ka"), lax.axis_size("pb")
    walkers = ka_count
    kpoints = green.shape[3]
    span = k_local * walkers
    shape = jax.ShapeDtypeStruct
    tiles = chol_cols // LANES
    own_green = green.reshape(kpoints, 2 * pair_width)
    greens = exchange(own_green, "ka", GREEN_ROUNDS)
    half = chol_half.reshape(k_local, 2, pair_width, chol_cols)
    full = jnp.transpose(
        chol_full.reshape(k_local, 2, M * M, tiles, LANES), (0, 2, 3, 1, 4)
    ).reshape(k_local, M * M * tiles * 2, LANES)
    own_fields = fields.reshape(walkers, chol_cols)
    own_orbitals = orbitals.reshape(k_local, walkers, 2 * pair_width)
    mask, picks = call(
        functools.partial(prepare_kernel, ka_count, pb_count, walkers),
        (shape((2 * walkers, chol_cols), F32), shape((LANES, 2 * LANES), BF16)),
        scalars=2,
        flops=10**9,
    )(kq_map, chol_count)
    bias, own = call(
        functools.partial(bias_kernel, ka_count, k_local),
        (
            shape((2 * walkers + span, chol_cols), F32),
            shape((k_local, 2 * walkers, pair_width), F32),
        ),
        [pltpu.VMEM((walkers, kpoints, 2 * pair_width), F32)],
        operands=len(greens) + 3,
    )(*greens, half, own_orbitals, mask)
    parts = exchange(bias, "ka", BIAS_ROUNDS)
    shares = call(
        functools.partial(exchange_kernel, k_local),
        shape((walkers, LANES), F32),
        operands=3,
    )(own, half, mask)
    width = -(-(M * M + 3) // LANES) * LANES
    blocks = call(
        functools.partial(operator_kernel, k_local),
        shape((ka_count * pb_count, 2 * span, width), BF16),
        [pltpu.VMEM((2 * M * M * tiles, LANES), F32), pltpu.VMEM((width, LANES), F32)],
        operands=len(parts) + 4,
    )(*parts, own_fields, mask, shares, full)
    group = operator_group(ka_count, pb_count)
    blocks = lax.all_to_all(
        blocks, ("pb", "ka"), 0, 0, axis_index_groups=[group], tiled=True
    )
    propagated, energy = call(
        functools.partial(taylor_kernel, pb_count, float(pb_count * chol_cols)),
        (shape((k_local, walkers, 2 * pair_width), F32), shape((1, 1), F32)),
        [
            pltpu.VMEM((width, LANES), F32),
            pltpu.VMEM((NOCC * ROWS, 2 * LANES), F32),
            pltpu.VMEM((LANES, LANES), F32),
            pltpu.VMEM((k_local, walkers, 2 * pair_width), F32),
            pltpu.VMEM((1, 1), F32),
            pltpu.SemaphoreType.DMA((2,)),
        ],
        operands=len(parts) + 3,
        space=pl.ANY,
    )(blocks, *parts, picks, own_orbitals)
    return (propagated[None], energy)


def on_device(green, fields, orbitals, chol_half, chol_full, chol_count, kq_map):
    ka_count, pb_count = lax.axis_size("ka"), lax.axis_size("pb")
    walkers = orbitals.shape[2]
    fits = 2 * pb_count * kq_map.shape[1] * walkers == LANES
    fits = fits and chol_half.shape[1] * walkers == 8 and chol_half.shape[4] == 2 * LANES
    fits = fits and ka_count == 4
    if fits and chol_half.shape[0] == 1 and walkers == ka_count:
        return direct(green, fields, orbitals, chol_half, chol_full, chol_count, kq_map)
    return with_collectives(green, fields, orbitals, chol_half, chol_full, chol_count, kq_map)


def solution(mesh):
    placed = (
        P("wa", ("grp", "ka"), "pb", None, None),
        P("wa", "pb", "grp", None),
        P("wa", "ka", "grp", None),
        P("pb", "ka", None, None, None),
        P("pb", "ka", None, None, None),
        P(),
        P(),
    )
    return jax.shard_map(
        on_device,
        mesh=mesh,
        in_specs=placed,
        out_specs=(P("wa", "ka", "grp", None), P("wa", ("grp", "ka"))),
        check_vma=False,
    )
```

```python
import functools

import jax
import jax.numpy as jnp
from jax import lax
from jax.experimental import pallas as pl
from jax.experimental.pallas import tpu as pltpu
from jax.sharding import PartitionSpec as P

M = 26
NOCC = 4
TAYLOR = 3
LANES = 128
ROWS = 32

GREEN_ROUNDS = (
    ((3, 0), (2, 1), (1, 3), (0, 2)),
    ((3, 1), (2, 0), (0, 3), (1, 2)),
    ((1, 0), (3, 2), (2, 3), (0, 1)),
)[::-1]
BIAS_ROUNDS = (
    ((0, 1), (1, 3), (2, 0), (3, 2)),
    ((0, 3), (3, 0), (1, 2), (2, 1)),
    ((0, 2), (1, 0), (2, 3), (3, 1)),
)[::-1]


BIAS_STEP = 0.5
PROP_STEP = 0.5

F32 = jnp.float32
BF16 = jnp.bfloat16


def complex_dot(pattern, left_re, left_im, right_re, right_im):
    real_part = jnp.einsum(
        pattern, left_re, right_re, preferred_element_type=jnp.float32
    ) - jnp.einsum(pattern, left_im, right_im, preferred_element_type=jnp.float32)
    imag_part = jnp.einsum(
        pattern, left_re, right_im, preferred_element_type=jnp.float32
    ) + jnp.einsum(pattern, left_im, right_re, preferred_element_type=jnp.float32)
    return (real_part, imag_part)


def make_picker(wanted):

    def picker(shard_rows):
        row_count = shard_rows.shape[0]
        select = (wanted[:, None] == jnp.arange(row_count, dtype=jnp.int32)[None, :]).astype(
            jnp.bfloat16
        )
        return jnp.dot(select, shard_rows, preferred_element_type=jnp.float32)

    return picker


def with_collectives(green, fields, orbitals, chol_half, chol_full, chol_count, kq_map):
    q_local = chol_half.shape[0]
    k_local = chol_half.shape[1]
    pair_width = chol_half.shape[3]
    chol_cols = chol_half.shape[4]
    ka_count = lax.axis_size("ka")
    pb_count = lax.axis_size("pb")
    ka_pos = lax.axis_index("ka")
    pb_pos = lax.axis_index("pb")
    local_green = lax.all_to_all(green, "ka", split_axis=3, concat_axis=1, tiled=True)
    walkers = local_green.shape[1]
    per_device = walkers // ka_count
    greens = local_green[0].reshape(walkers, q_local, k_local, 2, pair_width)
    counts = lax.dynamic_slice_in_dim(chol_count, pb_pos * q_local, q_local)
    vec_mask = (jnp.arange(chol_cols, dtype=jnp.int32)[None, :] < counts[:, None]).astype(
        jnp.float32
    )
    bias_re, bias_im = complex_dot(
        "wqkx,qkxn->qwn",
        greens[:, :, :, 0],
        greens[:, :, :, 1],
        chol_half[:, :, 0],
        chol_half[:, :, 1],
    )
    own_rows = (jnp.arange(walkers, dtype=jnp.int32) // per_device == ka_pos).astype(jnp.float32)
    bias_re, bias_im = lax.psum((bias_re, bias_im), "ka")
    bias_re = bias_re * vec_mask[:, None, :]
    bias_im = bias_im * vec_mask[:, None, :]
    hartree = 0.5 * jnp.sum(bias_re * bias_re + bias_im * bias_im, axis=(0, 2)) * own_rows
    field_now = jnp.transpose(fields, (1, 0, 2, 3)).reshape(q_local, walkers, chol_cols)
    shift_re = ((field_now - BIAS_STEP * bias_re) * vec_mask[:, None, :]).astype(jnp.bfloat16)
    shift_im = (-BIAS_STEP * bias_im * vec_mask[:, None, :]).astype(jnp.bfloat16)
    exchange = jnp.zeros((walkers,), jnp.float32)
    for transfer in range(q_local):
        for kpoint in range(k_local):
            chol_row = chol_half[transfer, kpoint].reshape(2, NOCC, M, chol_cols)
            green_row = greens[:, transfer, kpoint].reshape(walkers, 2, NOCC, M)
            cross_re, cross_im = complex_dot(
                "ipn,wjp->wijn", chol_row[0], chol_row[1], green_row[:, 0], green_row[:, 1]
            )
            exchange = exchange + 0.5 * jnp.sum(
                (cross_re * cross_re + cross_im * cross_im) * vec_mask[transfer], axis=(1, 2, 3)
            )
    prop_re, prop_im = complex_dot(
        "qwn,qkyn->qwky", shift_re, shift_im, chol_full[:, :, 0], chol_full[:, :, 1]
    )
    shape = (q_local, walkers, k_local, M, M)
    oper_re = (PROP_STEP * prop_re).astype(jnp.bfloat16).reshape(shape)
    oper_im = (PROP_STEP * prop_im).astype(jnp.bfloat16).reshape(shape)
    normalizer = q_local * pb_count * chol_cols
    total_energy = lax.psum(hartree - exchange, ("ka", "pb")) / normalizer
    energy = lax.dynamic_slice_in_dim(total_energy, ka_pos * per_device, per_device).reshape(
        1, per_device
    )
    initial = orbitals[0].reshape(k_local, walkers, 2, NOCC, M)
    row_width = 2 * pair_width
    my_rows = lax.dynamic_slice_in_dim(kq_map, pb_pos * q_local, q_local, 0)
    wanted = lax.dynamic_slice_in_dim(my_rows, ka_pos * k_local, k_local, 1).reshape(
        q_local * k_local
    )
    picker = make_picker(wanted)
    current = initial
    summed_terms = initial
    for degree in range(1, TAYLOR + 1):
        rounded = current.astype(jnp.bfloat16).reshape(k_local, walkers * row_width)
        fetched = picker(lax.all_gather(rounded, "ka", axis=0, tiled=True))
        shifted_rows = fetched.astype(jnp.bfloat16).reshape(q_local, k_local, walkers, 2, NOCC, M)
        out_re, out_im = complex_dot(
            "xwkpq,xkwiq->kwip",
            oper_re,
            oper_im,
            shifted_rows[:, :, :, 0],
            shifted_rows[:, :, :, 1],
        )
        applied = jnp.stack([out_re, out_im], axis=2)
        applied = lax.psum(applied, "pb")
        current = applied / degree
        summed_terms = summed_terms + current
    propagated = summed_terms.reshape(1, k_local, walkers, row_width)
    return (propagated, energy)


def exchange(array, axis, rounds):
    return [array] + [lax.ppermute(array, axis, pairs) for pairs in rounds]


def origins(axis, rounds):
    at = lax.axis_index(axis)
    found = [at]
    for pairs in rounds:
        source = jnp.int32(0)
        for sender, receiver in pairs:
            source = jnp.where(at == receiver, sender, source)
        found.append(source)
    return found


def operator_group(ka_count, pb_count):
    size = pb_count * ka_count
    cycle = [pb * ka_count + ka for ka in range(ka_count) for pb in range(pb_count)][::-1]
    first = cycle.index((pb_count - 1) * ka_count + ka_count // 2)
    return [cycle[(first + at) % size] for at in range(size)]


def prepare_kernel(ka_count, pb_count, walkers, map_ref, count_ref, mask_ref, picks_ref):
    kept = count_ref[lax.axis_index("pb")]
    column = lax.broadcasted_iota(jnp.int32, mask_ref.shape, 1)
    mask_ref[...] = jnp.where(column < kept, 1.0, 0.0)
    kpoints = map_ref.shape[1]
    k_local = kpoints // ka_count
    span = k_local * walkers
    lane = lax.broadcasted_iota(jnp.int32, (1, LANES), 1)
    lane_q = lane // (LANES // pb_count)
    lane_ka = lax.rem(lane, LANES // pb_count) // (2 * span)
    lane_part = lax.rem(lane, 2 * span) // span
    lane_k = lane_ka * k_local + lax.rem(lane, span) // walkers
    wanted = jnp.zeros((1, LANES), jnp.int32)
    for q in range(pb_count):
        for k in range(kpoints):
            source = map_ref[q, k]
            source = source // k_local * (2 * span) + lax.rem(source, k_local) * walkers
            wanted = jnp.where((lane_q == q) & (lane_k == k), source, wanted)
    wanted = wanted + lax.rem(lane, walkers)
    row = lax.broadcasted_iota(jnp.int32, (LANES, LANES), 0)
    real = jnp.where(row == wanted, 1.0, 0.0)
    imag = jnp.where(row == wanted + span, jnp.where(lane_part == 0, 1.0, -1.0), 0.0)
    picks_ref[...] = jnp.concatenate([real, imag], axis=1).astype(BF16)


def bias_kernel(ka_count, k_local, *refs):
    *greens, chol_ref, orbitals_ref, mask_ref, bias_ref, own_ref, table = refs
    for source, green_ref in zip(origins("ka", GREEN_ROUNDS), greens):
        table[source] = green_ref[...].astype(F32)
    first = lax.axis_index("ka") * k_local
    width = chol_ref.shape[2]
    rows = 2 * ka_count
    total = jnp.zeros((rows, bias_ref.shape[1]), F32)
    for k in range(k_local):
        green = jnp.concatenate(
            [table[w, pl.ds(first + k, 1), :] for w in range(ka_count)], axis=0
        )
        real, imag = green[:, :width], green[:, width:]
        both = jnp.concatenate([real, imag], axis=0)
        turned = jnp.concatenate([-imag, real], axis=0)
        own_ref[k] = both
        total += jnp.dot(both.astype(BF16), chol_ref[k, 0], preferred_element_type=F32)
        total += jnp.dot(turned.astype(BF16), chol_ref[k, 1], preferred_element_type=F32)
    bias_ref[:rows] = total * mask_ref[...]
    window = jnp.concatenate([orbitals_ref[k] for k in range(k_local)], axis=0)
    count, width = window.shape
    bias_ref[rows : rows + count, :width] = window
    bias_ref[rows : rows + count, width:] = jnp.zeros((count, bias_ref.shape[1] - width), F32)


def exchange_kernel(k_local, own_ref, chol_ref, mask_ref, out_ref):
    walkers, width, columns = own_ref.shape[1] // 2, own_ref.shape[2], chol_ref.shape[3]
    rows = 2 * walkers
    lane = lax.broadcasted_iota(jnp.int32, (rows, LANES), 1)
    total = jnp.zeros((rows, columns), F32)
    for k in range(k_local):
        both = jnp.concatenate([own_ref[k], jnp.zeros((rows, LANES - width), F32)], axis=1)
        turned = jnp.concatenate([-both[walkers:], both[:walkers]], axis=0)
        sides = []
        for side in (both, turned):
            rolled = {
                step: side if step == 0 else pltpu.roll(side, (step * M) % LANES, 1)
                for step in range(1 - NOCC, NOCC)
            }
            blocks = []
            for i in range(NOCC):
                inside = (lane >= i * M) & (lane < (i + 1) * M)
                for j in range(NOCC):
                    blocks.append(jnp.where(inside, rolled[i - j], 0.0))
            sides.append(jnp.concatenate(blocks, axis=0)[:, :width].astype(BF16))
        cross = jnp.dot(sides[0], chol_ref[k, 0], preferred_element_type=F32)
        cross += jnp.dot(sides[1], chol_ref[k, 1], preferred_element_type=F32)
        cross = cross * cross
        for block in range(NOCC * NOCC):
            total += cross[block * rows : (block + 1) * rows]
    total = total * mask_ref[:rows]
    total = total[:walkers] + total[walkers:]
    summed = 0.5 * jnp.sum(total, axis=1, keepdims=True)
    out_ref[...] = jnp.broadcast_to(summed, out_ref.shape)


def operator_kernel(k_local, *refs):
    *parts, fields_ref, mask_ref, exchange_ref, chol_ref, out_ref, products, turned_ref = refs
    walkers, columns = fields_ref.shape
    bias = parts[0][: 2 * walkers]
    for part in parts[1:]:
        bias = bias + part[: 2 * walkers]
    pairs = M * M
    tiles = columns // LANES
    group = LANES // (2 * tiles)
    bias_re, bias_im = bias[:walkers], bias[walkers:]
    hartree = 0.5 * jnp.sum(bias_re * bias_re + bias_im * bias_im, axis=1, keepdims=True)
    own = lax.broadcasted_iota(jnp.int32, (walkers, 1), 0) == lax.axis_index("ka")
    energy = jnp.where(own, hartree, 0.0) - exchange_ref[:, :1]
    kept = mask_ref[:walkers]
    shift_re = (fields_ref[...] - BIAS_STEP * bias_re) * kept
    shift_im = -BIAS_STEP * bias_im * kept
    span = k_local * walkers
    weights = []
    for k in range(k_local):
        before, after = k * walkers, span - (k + 1) * walkers
        pieces = []
        for tile in range(tiles):
            at = slice(tile * LANES, (tile + 1) * LANES)
            for first, second in ((shift_re, shift_im), (-shift_im, shift_re)):
                for side in (first, second):
                    pieces += [(before, None), (walkers, side[:, at]), (after, None)]
                pieces.append((group - 2 * span, None))
        weights.append(
            jnp.concatenate(
                [jnp.zeros((n, LANES), F32) if p is None else p for n, p in pieces if n], axis=0
            ).astype(BF16)
        )
    products[...] = lax.dot_general(
        jnp.concatenate([chol_ref[k] for k in range(k_local)], axis=1),
        jnp.concatenate(weights, axis=1),
        (((1,), (1,)), ((), ())),
        preferred_element_type=F32,
    )
    lane = lax.broadcasted_iota(jnp.int32, (pairs, LANES), 1)
    merged = products[pl.ds(0, pairs, stride=2 * tiles), :]
    for at in range(1, 2 * tiles):
        row = products[pl.ds(at, pairs, stride=2 * tiles), :]
        merged = jnp.where(lane >= at * group, row, merged)
    turned_ref[:pairs] = merged
    copies, rows, width = out_ref.shape
    lane = lax.broadcasted_iota(jnp.int32, (rows, LANES), 1)
    for at in range(0, width, LANES):
        block = turned_ref[at : at + LANES].T
        block = PROP_STEP * sum(block[n * group : n * group + rows] for n in range(2 * tiles))
        if at + LANES > pairs:
            share = jnp.concatenate([energy, jnp.zeros((rows - walkers, 1), F32)], axis=0)
            block = jnp.where(lane + at < pairs, block, 0.0)
            for piece in range(3):
                head = share.astype(BF16).astype(F32)
                block = jnp.where(lane + at == pairs + piece, head, block)
                share = share - head
        for copy in range(copies):
            out_ref[copy, :, at : at + LANES] = block.astype(BF16)


def taylor_kernel(pb_count, normalizer, blocks_ref, *refs):
    *windows, picks_ref, orbitals_ref, out_ref, energy_ref, turned, picked, term = refs
    pairs = M * M
    pair = NOCC * M
    k_local, walkers, _ = out_ref.shape
    span = k_local * walkers
    ka_pos = lax.axis_index("ka")
    term[...] = jnp.zeros_like(term)
    for source, window_ref in zip(origins("ka", BIAS_ROUNDS), windows):
        start = pl.multiple_of(source * (2 * span), 2 * span)
        window = window_ref[window_ref.shape[0] - span :]
        term[pl.ds(start, span), :pair] = window[:, :pair]
        term[pl.ds(start + span, span), :pair] = window[:, pair : 2 * pair]
    picked[...] = jnp.dot(term[...].T.astype(BF16), picks_ref[...], preferred_element_type=F32)
    count, _, width = blocks_ref.shape
    group = operator_group(count // pb_count, pb_count)
    places = [group.index(n) for n in range(count)]
    for at in range(0, width, LANES):
        tile = jnp.concatenate([blocks_ref[n, :, at : at + LANES] for n in places], axis=0)
        turned[at : at + LANES] = tile.T.astype(F32)
    shares = turned[pairs : pairs + 3]
    lane = lax.broadcasted_iota(jnp.int32, shares.shape, 1)
    shares = jnp.where(lax.rem(lane, 2 * span) == ka_pos, shares, 0.0)
    shares = jnp.sum(jnp.sum(shares, axis=0, keepdims=True), axis=1, keepdims=True)
    energy_ref[...] = shares / normalizer
    lane = lax.broadcasted_iota(jnp.int32, (M, LANES), 1)
    imaginary = lax.rem(lane, 2 * span) >= span
    sums = [jnp.zeros((M, LANES), F32) for _ in range(NOCC)]
    for degree in range(1, TAYLOR + 1):
        stride = M if degree == 1 else ROWS
        straight = [jnp.zeros((M, LANES), F32) for _ in range(NOCC)]
        crossed = [jnp.zeros((M, LANES), F32) for _ in range(NOCC)]
        for c in range(M):
            column = turned[pl.ds(c, M, stride=M), :]
            for i in range(NOCC):
                at = i * stride + c
                straight[i] += column * picked[at : at + 1, :LANES]
                crossed[i] += column * picked[at : at + 1, LANES:]
        for i in range(NOCC):
            other = jnp.where(
                imaginary, pltpu.roll(crossed[i], span, 1), pltpu.roll(crossed[i], LANES - span, 1)
            )
            applied = straight[i] + other
            applied = applied + pltpu.roll(applied, LANES // pb_count, 1)
            current = applied / degree
            sums[i] = sums[i] + current
            term[i * ROWS : i * ROWS + M] = current if degree < TAYLOR else sums[i]
        if degree < TAYLOR:
            picked[...] = jnp.dot(
                term[...].astype(BF16), picks_ref[...], preferred_element_type=F32
            )
    turned[:LANES] = term[...].T
    both = turned[pl.ds(pl.multiple_of(ka_pos * (2 * span), 2 * span), 2 * span), :]
    both = jnp.concatenate([both[:, i * ROWS : i * ROWS + M] for i in range(NOCC)], axis=1)
    both = jnp.concatenate([both[:span], both[span:]], axis=1)
    for k in range(k_local):
        out_ref[k] = orbitals_ref[k] + both[k * walkers : (k + 1) * walkers]


def call(kernel, out, scratch=(), scalars=0, operands=0, flops=None):
    spaces = [pltpu.SMEM] * scalars + [pltpu.VMEM] * operands
    cost = None
    if flops is not None:
        cost = pl.CostEstimate(flops=flops, bytes_accessed=0, transcendentals=0)
    return pl.pallas_call(
        kernel,
        out_shape=out,
        in_specs=[pl.BlockSpec(memory_space=space) for space in spaces],
        out_specs=jax.tree.map(lambda _: pl.BlockSpec(memory_space=pltpu.VMEM), out),
        scratch_shapes=list(scratch),
        cost_estimate=cost,
        compiler_params=pltpu.CompilerParams(vmem_limit_bytes=24 * 2**20),
    )


def direct(green, fields, orbitals, chol_half, chol_full, chol_count, kq_map):
    k_local, pair_width, chol_cols = chol_half.shape[1], chol_half.shape[3], chol_half.shape[4]
    ka_count, pb_count = lax.axis_size("ka"), lax.axis_size("pb")
    walkers = ka_count
    kpoints = green.shape[3]
    span = k_local * walkers
    shape = jax.ShapeDtypeStruct
    tiles = chol_cols // LANES
    own_green = green.reshape(kpoints, 2 * pair_width)
    greens = exchange(own_green, "ka", GREEN_ROUNDS)
    half = chol_half.reshape(k_local, 2, pair_width, chol_cols)
    full = jnp.transpose(
        chol_full.reshape(k_local, 2, M * M, tiles, LANES), (0, 2, 3, 1, 4)
    ).reshape(k_local, M * M * tiles * 2, LANES)
    own_fields = fields.reshape(walkers, chol_cols)
    own_orbitals = orbitals.reshape(k_local, walkers, 2 * pair_width)
    mask, picks = call(
        functools.partial(prepare_kernel, ka_count, pb_count, walkers),
        (shape((2 * walkers, chol_cols), F32), shape((LANES, 2 * LANES), BF16)),
        scalars=2,
        flops=10**9,
    )(kq_map, chol_count)
    bias, own = call(
        functools.partial(bias_kernel, ka_count, k_local),
        (
            shape((2 * walkers + span, chol_cols), F32),
            shape((k_local, 2 * walkers, pair_width), F32),
        ),
        [pltpu.VMEM((walkers, kpoints, 2 * pair_width), F32)],
        operands=len(greens) + 3,
    )(*greens, half, own_orbitals, mask)
    parts = exchange(bias, "ka", BIAS_ROUNDS)
    shares = call(
        functools.partial(exchange_kernel, k_local),
        shape((walkers, LANES), F32),
        operands=3,
    )(own, half, mask)
    width = -(-(M * M + 3) // LANES) * LANES
    blocks = call(
        functools.partial(operator_kernel, k_local),
        shape((ka_count * pb_count, 2 * span, width), BF16),
        [pltpu.VMEM((2 * M * M * tiles, LANES), F32), pltpu.VMEM((width, LANES), F32)],
        operands=len(parts) + 4,
    )(*parts, own_fields, mask, shares, full)
    group = operator_group(ka_count, pb_count)
    blocks = lax.all_to_all(
        blocks, ("pb", "ka"), 0, 0, axis_index_groups=[group], tiled=True
    )
    propagated, energy = call(
        functools.partial(taylor_kernel, pb_count, float(pb_count * chol_cols)),
        (shape((k_local, walkers, 2 * pair_width), F32), shape((1, 1), F32)),
        [
            pltpu.VMEM((width, LANES), F32),
            pltpu.VMEM((NOCC * ROWS, 2 * LANES), F32),
            pltpu.VMEM((LANES, LANES), F32),
        ],
        operands=len(parts) + 3,
    )(blocks, *parts, picks, own_orbitals)
    return (propagated[None], energy)


def on_device(green, fields, orbitals, chol_half, chol_full, chol_count, kq_map):
    ka_count, pb_count = lax.axis_size("ka"), lax.axis_size("pb")
    walkers = orbitals.shape[2]
    fits = 2 * pb_count * kq_map.shape[1] * walkers == LANES
    fits = fits and chol_half.shape[1] * walkers == 8 and chol_half.shape[4] == 2 * LANES
    fits = fits and ka_count == 4
    if fits and chol_half.shape[0] == 1 and walkers == ka_count:
        return direct(green, fields, orbitals, chol_half, chol_full, chol_count, kq_map)
    return with_collectives(green, fields, orbitals, chol_half, chol_full, chol_count, kq_map)


def solution(mesh):
    placed = (
        P("wa", ("grp", "ka"), "pb", None, None),
        P("wa", "pb", "grp", None),
        P("wa", "ka", "grp", None),
        P("pb", "ka", None, None, None),
        P("pb", "ka", None, None, None),
        P(),
        P(),
    )
    return jax.shard_map(
        on_device,
        mesh=mesh,
        in_specs=placed,
        out_specs=(P("wa", "ka", "grp", None), P("wa", ("grp", "ka"))),
        check_vma=False,
    )
```

```python
import functools

import jax
import jax.numpy as jnp
from jax import lax
from jax.experimental import pallas as pl
from jax.experimental.pallas import tpu as pltpu
from jax.sharding import PartitionSpec as P

M = 26
NOCC = 4
TAYLOR = 3
LANES = 128
ROWS = 32

GREEN_ROUNDS = (
    ((3, 0), (2, 1), (1, 3), (0, 2)),
    ((3, 1), (2, 0), (0, 3), (1, 2)),
    ((1, 0), (3, 2), (2, 3), (0, 1)),
)[::-1]
BIAS_ROUNDS = (
    ((0, 1), (1, 3), (2, 0), (3, 2)),
    ((0, 3), (3, 0), (1, 2), (2, 1)),
    ((0, 2), (1, 0), (2, 3), (3, 1)),
)[::-1]


BIAS_STEP = 0.5
PROP_STEP = 0.5

F32 = jnp.float32
BF16 = jnp.bfloat16


def complex_dot(pattern, left_re, left_im, right_re, right_im):
    real_part = jnp.einsum(
        pattern, left_re, right_re, preferred_element_type=jnp.float32
    ) - jnp.einsum(pattern, left_im, right_im, preferred_element_type=jnp.float32)
    imag_part = jnp.einsum(
        pattern, left_re, right_im, preferred_element_type=jnp.float32
    ) + jnp.einsum(pattern, left_im, right_re, preferred_element_type=jnp.float32)
    return (real_part, imag_part)


def make_picker(wanted):

    def picker(shard_rows):
        row_count = shard_rows.shape[0]
        select = (wanted[:, None] == jnp.arange(row_count, dtype=jnp.int32)[None, :]).astype(
            jnp.bfloat16
        )
        return jnp.dot(select, shard_rows, preferred_element_type=jnp.float32)

    return picker


def with_collectives(green, fields, orbitals, chol_half, chol_full, chol_count, kq_map):
    q_local = chol_half.shape[0]
    k_local = chol_half.shape[1]
    pair_width = chol_half.shape[3]
    chol_cols = chol_half.shape[4]
    ka_count = lax.axis_size("ka")
    pb_count = lax.axis_size("pb")
    ka_pos = lax.axis_index("ka")
    pb_pos = lax.axis_index("pb")
    local_green = lax.all_to_all(green, "ka", split_axis=3, concat_axis=1, tiled=True)
    walkers = local_green.shape[1]
    per_device = walkers // ka_count
    greens = local_green[0].reshape(walkers, q_local, k_local, 2, pair_width)
    counts = lax.dynamic_slice_in_dim(chol_count, pb_pos * q_local, q_local)
    vec_mask = (jnp.arange(chol_cols, dtype=jnp.int32)[None, :] < counts[:, None]).astype(
        jnp.float32
    )
    bias_re, bias_im = complex_dot(
        "wqkx,qkxn->qwn",
        greens[:, :, :, 0],
        greens[:, :, :, 1],
        chol_half[:, :, 0],
        chol_half[:, :, 1],
    )
    own_rows = (jnp.arange(walkers, dtype=jnp.int32) // per_device == ka_pos).astype(jnp.float32)
    bias_re, bias_im = lax.psum((bias_re, bias_im), "ka")
    bias_re = bias_re * vec_mask[:, None, :]
    bias_im = bias_im * vec_mask[:, None, :]
    hartree = 0.5 * jnp.sum(bias_re * bias_re + bias_im * bias_im, axis=(0, 2)) * own_rows
    field_now = jnp.transpose(fields, (1, 0, 2, 3)).reshape(q_local, walkers, chol_cols)
    shift_re = ((field_now - BIAS_STEP * bias_re) * vec_mask[:, None, :]).astype(jnp.bfloat16)
    shift_im = (-BIAS_STEP * bias_im * vec_mask[:, None, :]).astype(jnp.bfloat16)
    exchange = jnp.zeros((walkers,), jnp.float32)
    for transfer in range(q_local):
        for kpoint in range(k_local):
            chol_row = chol_half[transfer, kpoint].reshape(2, NOCC, M, chol_cols)
            green_row = greens[:, transfer, kpoint].reshape(walkers, 2, NOCC, M)
            cross_re, cross_im = complex_dot(
                "ipn,wjp->wijn", chol_row[0], chol_row[1], green_row[:, 0], green_row[:, 1]
            )
            exchange = exchange + 0.5 * jnp.sum(
                (cross_re * cross_re + cross_im * cross_im) * vec_mask[transfer], axis=(1, 2, 3)
            )
    prop_re, prop_im = complex_dot(
        "qwn,qkyn->qwky", shift_re, shift_im, chol_full[:, :, 0], chol_full[:, :, 1]
    )
    shape = (q_local, walkers, k_local, M, M)
    oper_re = (PROP_STEP * prop_re).astype(jnp.bfloat16).reshape(shape)
    oper_im = (PROP_STEP * prop_im).astype(jnp.bfloat16).reshape(shape)
    normalizer = q_local * pb_count * chol_cols
    total_energy = lax.psum(hartree - exchange, ("ka", "pb")) / normalizer
    energy = lax.dynamic_slice_in_dim(total_energy, ka_pos * per_device, per_device).reshape(
        1, per_device
    )
    initial = orbitals[0].reshape(k_local, walkers, 2, NOCC, M)
    row_width = 2 * pair_width
    my_rows = lax.dynamic_slice_in_dim(kq_map, pb_pos * q_local, q_local, 0)
    wanted = lax.dynamic_slice_in_dim(my_rows, ka_pos * k_local, k_local, 1).reshape(
        q_local * k_local
    )
    picker = make_picker(wanted)
    current = initial
    summed_terms = initial
    for degree in range(1, TAYLOR + 1):
        rounded = current.astype(jnp.bfloat16).reshape(k_local, walkers * row_width)
        fetched = picker(lax.all_gather(rounded, "ka", axis=0, tiled=True))
        shifted_rows = fetched.astype(jnp.bfloat16).reshape(q_local, k_local, walkers, 2, NOCC, M)
        out_re, out_im = complex_dot(
            "xwkpq,xkwiq->kwip",
            oper_re,
            oper_im,
            shifted_rows[:, :, :, 0],
            shifted_rows[:, :, :, 1],
        )
        applied = jnp.stack([out_re, out_im], axis=2)
        applied = lax.psum(applied, "pb")
        current = applied / degree
        summed_terms = summed_terms + current
    propagated = summed_terms.reshape(1, k_local, walkers, row_width)
    return (propagated, energy)


def exchange(array, axis, rounds):
    return [array] + [lax.ppermute(array, axis, pairs) for pairs in rounds]


def origins(axis, rounds):
    at = lax.axis_index(axis)
    found = [at]
    for pairs in rounds:
        source = jnp.int32(0)
        for sender, receiver in pairs:
            source = jnp.where(at == receiver, sender, source)
        found.append(source)
    return found


def operator_group(ka_count, pb_count):
    first = (pb_count - 1) * ka_count + ka_count // 2
    rest = [at for at in range(pb_count * ka_count) if at != first]
    return [first] + rest[::-1]


def prepare_kernel(ka_count, pb_count, walkers, map_ref, count_ref, mask_ref, picks_ref, own_ref):
    kept = count_ref[lax.axis_index("pb")]
    column = lax.broadcasted_iota(jnp.int32, mask_ref.shape, 1)
    mask_ref[...] = jnp.where(column < kept, 1.0, 0.0)
    kpoints = map_ref.shape[1]
    k_local = kpoints // ka_count
    span = k_local * walkers

    def place(k):
        return k // k_local * (2 * span) + lax.rem(k, k_local) * walkers

    lane = lax.broadcasted_iota(jnp.int32, (1, LANES), 1)
    lane_q = lane // (LANES // pb_count)
    lane_ka = lax.rem(lane, LANES // pb_count) // (2 * span)
    lane_part = lax.rem(lane, 2 * span) // span
    lane_k = lane_ka * k_local + lax.rem(lane, span) // walkers
    wanted = jnp.zeros((1, LANES), jnp.int32)
    for q in range(pb_count):
        for k in range(kpoints):
            wanted = jnp.where((lane_q == q) & (lane_k == k), place(map_ref[q, k]), wanted)
    wanted = wanted + lax.rem(lane, walkers)
    group = 2 * span
    own_q = lax.rem(lane, pb_count * group) // group
    own_k = lax.rem(lane, span) // walkers
    own = jnp.zeros((1, LANES), jnp.int32)
    first = lax.axis_index("ka") * k_local
    for q in range(pb_count):
        for k in range(k_local):
            own = jnp.where((own_q == q) & (own_k == k), place(map_ref[q, first + k]), own)
    own_ref[...] = jnp.broadcast_to(own + lax.rem(lane, walkers), own_ref.shape)
    row = lax.broadcasted_iota(jnp.int32, (LANES, LANES), 0)
    real = jnp.where(row == wanted, 1.0, 0.0)
    imag = jnp.where(row == wanted + span, jnp.where(lane_part == 0, 1.0, -1.0), 0.0)
    picks_ref[...] = jnp.concatenate([real, imag], axis=1).astype(BF16)


def bias_kernel(ka_count, k_local, *refs):
    *greens, chol_ref, orbitals_ref, mask_ref, bias_ref, own_ref, table = refs
    for source, green_ref in zip(origins("ka", GREEN_ROUNDS), greens):
        table[source] = green_ref[...].astype(F32)
    first = lax.axis_index("ka") * k_local
    width = chol_ref.shape[2]
    rows = 2 * ka_count
    total = jnp.zeros((rows, bias_ref.shape[1]), F32)
    for k in range(k_local):
        green = jnp.concatenate(
            [table[w, pl.ds(first + k, 1), :] for w in range(ka_count)], axis=0
        )
        real, imag = green[:, :width], green[:, width:]
        both = jnp.concatenate([real, imag], axis=0)
        turned = jnp.concatenate([-imag, real], axis=0)
        own_ref[k] = both
        total += jnp.dot(both.astype(BF16), chol_ref[k, 0], preferred_element_type=F32)
        total += jnp.dot(turned.astype(BF16), chol_ref[k, 1], preferred_element_type=F32)
    bias_ref[:rows] = total * mask_ref[...]
    window = jnp.concatenate([orbitals_ref[k] for k in range(k_local)], axis=0)
    count, width = window.shape
    bias_ref[rows : rows + count, :width] = window
    bias_ref[rows : rows + count, width:] = jnp.zeros((count, bias_ref.shape[1] - width), F32)


def exchange_kernel(
    k_local, pb_count, own_ref, chol_ref, mask_ref, lanes_ref, out_ref, fold_ref, picks_ref
):
    walkers, width, columns = own_ref.shape[1] // 2, own_ref.shape[2], chol_ref.shape[3]
    rows = 2 * walkers
    lane = lax.broadcasted_iota(jnp.int32, (rows, LANES), 1)
    total = jnp.zeros((rows, columns), F32)
    for k in range(k_local):
        both = jnp.concatenate([own_ref[k], jnp.zeros((rows, LANES - width), F32)], axis=1)
        turned = jnp.concatenate([-both[walkers:], both[:walkers]], axis=0)
        sides = []
        for side in (both, turned):
            rolled = {
                step: side if step == 0 else pltpu.roll(side, (step * M) % LANES, 1)
                for step in range(1 - NOCC, NOCC)
            }
            blocks = []
            for i in range(NOCC):
                inside = (lane >= i * M) & (lane < (i + 1) * M)
                for j in range(NOCC):
                    blocks.append(jnp.where(inside, rolled[i - j], 0.0))
            sides.append(jnp.concatenate(blocks, axis=0)[:, :width].astype(BF16))
        cross = jnp.dot(sides[0], chol_ref[k, 0], preferred_element_type=F32)
        cross += jnp.dot(sides[1], chol_ref[k, 1], preferred_element_type=F32)
        cross = cross * cross
        for block in range(NOCC * NOCC):
            total += cross[block * rows : (block + 1) * rows]
    total = total * mask_ref[:rows]
    total = total[:walkers] + total[walkers:]
    summed = 0.5 * jnp.sum(total, axis=1, keepdims=True)
    out_ref[...] = jnp.broadcast_to(summed, out_ref.shape)
    span = k_local * walkers
    group = 2 * span
    lane = lax.broadcasted_iota(jnp.int32, (1, LANES), 1)
    source = lax.rem(lane, pb_count * group) // group * (LANES // pb_count) + lax.rem(lane, group)
    source = source + lax.axis_index("ka") * group
    row = lax.broadcasted_iota(jnp.int32, (LANES, LANES), 0)
    fold_ref[...] = jnp.where(row == source, 1.0, 0.0).astype(BF16)
    wanted = lanes_ref[:1]
    sign = jnp.where(lax.rem(lane, group) < span, 1.0, -1.0)
    for i in range(NOCC):
        inside = lane // (LANES // NOCC) == i
        real = jnp.where(inside & (row == wanted), 1.0, 0.0)
        imag = jnp.where(inside & (row == wanted + span), sign, 0.0)
        both = jnp.concatenate([real, imag], axis=1)
        picks_ref[i * LANES : (i + 1) * LANES] = both.astype(BF16)


def operator_kernel(k_local, *refs):
    *parts, fields_ref, mask_ref, exchange_ref, chol_ref, out_ref, products, turned_ref = refs
    walkers, columns = fields_ref.shape
    bias = parts[0][: 2 * walkers]
    for part in parts[1:]:
        bias = bias + part[: 2 * walkers]
    pairs = M * M
    tiles = columns // LANES
    group = LANES // (2 * tiles)
    bias_re, bias_im = bias[:walkers], bias[walkers:]
    hartree = 0.5 * jnp.sum(bias_re * bias_re + bias_im * bias_im, axis=1, keepdims=True)
    own = lax.broadcasted_iota(jnp.int32, (walkers, 1), 0) == lax.axis_index("ka")
    energy = jnp.where(own, hartree, 0.0) - exchange_ref[:, :1]
    kept = mask_ref[:walkers]
    shift_re = (fields_ref[...] - BIAS_STEP * bias_re) * kept
    shift_im = -BIAS_STEP * bias_im * kept
    span = k_local * walkers
    weights = []
    for k in range(k_local):
        before, after = k * walkers, span - (k + 1) * walkers
        pieces = []
        for tile in range(tiles):
            at = slice(tile * LANES, (tile + 1) * LANES)
            for first, second in ((shift_re, shift_im), (-shift_im, shift_re)):
                for side in (first, second):
                    pieces += [(before, None), (walkers, side[:, at]), (after, None)]
                pieces.append((group - 2 * span, None))
        weights.append(
            jnp.concatenate(
                [jnp.zeros((n, LANES), F32) if p is None else p for n, p in pieces if n], axis=0
            ).astype(BF16)
        )
    products[...] = lax.dot_general(
        jnp.concatenate([chol_ref[k] for k in range(k_local)], axis=1),
        jnp.concatenate(weights, axis=1),
        (((1,), (1,)), ((), ())),
        preferred_element_type=F32,
    )
    lane = lax.broadcasted_iota(jnp.int32, (pairs, LANES), 1)
    merged = products[pl.ds(0, pairs, stride=2 * tiles), :]
    for at in range(1, 2 * tiles):
        row = products[pl.ds(at, pairs, stride=2 * tiles), :]
        merged = jnp.where(lane >= at * group, row, merged)
    turned_ref[:pairs] = merged
    copies, rows, width = out_ref.shape
    lane = lax.broadcasted_iota(jnp.int32, (rows, LANES), 1)
    for at in range(0, width, LANES):
        block = turned_ref[at : at + LANES].T
        block = PROP_STEP * sum(block[n * group : n * group + rows] for n in range(2 * tiles))
        if at + LANES > pairs:
            share = jnp.concatenate([energy, jnp.zeros((rows - walkers, 1), F32)], axis=0)
            block = jnp.where(lane + at < pairs, block, 0.0)
            for piece in range(3):
                head = share.astype(BF16).astype(F32)
                block = jnp.where(lane + at == pairs + piece, head, block)
                share = share - head
        for copy in range(copies):
            out_ref[copy, :, at : at + LANES] = block.astype(BF16)


def taylor_kernel(pb_count, normalizer, blocks_ref, *refs):
    *windows, picks_ref, fold_ref, own_picks_ref, orbitals_ref = refs[:-7]
    out_ref, energy_ref, turned, folded, picked, term, kept = refs[-7:]
    pairs = M * M
    pair = NOCC * M
    k_local, walkers, _ = out_ref.shape
    span = k_local * walkers
    ka_pos = lax.axis_index("ka")
    picks = picks_ref[...]
    term[...] = jnp.zeros_like(term)
    for source, window_ref in zip(origins("ka", BIAS_ROUNDS), windows):
        start = pl.multiple_of(source * (2 * span), 2 * span)
        window = window_ref[window_ref.shape[0] - span :]
        term[pl.ds(start, span), :pair] = window[:, :pair]
        term[pl.ds(start + span, span), :pair] = window[:, pair : 2 * pair]
    picked[...] = jnp.dot(term[...].T.astype(BF16), picks, preferred_element_type=F32)
    count, _, width = blocks_ref.shape
    group = operator_group(count // pb_count, pb_count)
    places = [group.index(n) for n in range(count)]
    turned[width:] = jnp.zeros((turned.shape[0] - width, LANES), F32)
    folded[width:] = jnp.zeros((folded.shape[0] - width, LANES), F32)
    for at in range(0, width, LANES):
        tile = jnp.concatenate([blocks_ref[n, :, at : at + LANES] for n in places], axis=0).T
        turned[at : at + LANES] = tile.astype(F32)
        folded[at : at + LANES] = jnp.dot(tile, fold_ref[...], preferred_element_type=F32)
    shares = turned[pairs : pairs + 3]
    lane = lax.broadcasted_iota(jnp.int32, shares.shape, 1)
    shares = jnp.where(lax.rem(lane, 2 * span) == ka_pos, shares, 0.0)
    shares = jnp.sum(jnp.sum(shares, axis=0, keepdims=True), axis=1, keepdims=True)
    energy_ref[...] = shares / normalizer
    lane = lax.broadcasted_iota(jnp.int32, (ROWS, LANES), 1)
    imaginary = lax.rem(lane, 2 * span) >= span

    def joined(straight, crossed):
        up, down = pltpu.roll(crossed, span, 1), pltpu.roll(crossed, LANES - span, 1)
        return straight + jnp.where(imaginary, up, down)

    sums = [None] * NOCC
    for degree in range(1, TAYLOR):
        stride = M if degree == 1 else ROWS
        straight = [jnp.zeros((ROWS, LANES), F32) for _ in range(NOCC)]
        crossed = [jnp.zeros((ROWS, LANES), F32) for _ in range(NOCC)]
        for c in range(M):
            column = turned[pl.ds(c, ROWS, stride=M), :]
            for i in range(NOCC):
                at = i * stride + c
                straight[i] += column * picked[at : at + 1, :LANES]
                crossed[i] += column * picked[at : at + 1, LANES:]
        currents = []
        for i in range(NOCC):
            applied = joined(straight[i], crossed[i])
            applied = applied + pltpu.roll(applied, LANES // pb_count, 1)
            currents.append(applied * (1.0 / degree))
            sums[i] = currents[i] if degree == 1 else sums[i] + currents[i]
        if degree < TAYLOR - 1:
            rows = jnp.concatenate(currents, axis=0).astype(BF16)
            picked[...] = jnp.dot(rows, picks, preferred_element_type=F32)
    wide = jnp.concatenate(currents, axis=1).astype(BF16)
    picked[:ROWS] = jnp.dot(wide, own_picks_ref[...], preferred_element_type=F32)
    kept[...] = jnp.concatenate(sums, axis=0).T
    sums = kept[pl.ds(pl.multiple_of(ka_pos * (2 * span), 2 * span), 2 * span), :]
    straight = [jnp.zeros((ROWS, LANES), F32) for _ in range(2)]
    crossed = [jnp.zeros((ROWS, LANES), F32) for _ in range(2)]
    for c in range(M):
        column = folded[pl.ds(c, ROWS, stride=M), :]
        straight[c % 2] += column * picked[c : c + 1, :LANES]
        crossed[c % 2] += column * picked[c : c + 1, LANES:]
    applied = joined(straight[0] + straight[1], crossed[0] + crossed[1])
    last = ((applied + pltpu.roll(applied, LANES - 2 * span, 1)) * (1.0 / TAYLOR)).T
    last = jnp.concatenate(
        [last[i * ROWS : i * ROWS + 2 * span] for i in range(NOCC)], axis=1
    )
    both = sums + last
    both = jnp.concatenate([both[:, i * ROWS : i * ROWS + M] for i in range(NOCC)], axis=1)
    both = jnp.concatenate([both[:span], both[span:]], axis=1)
    for k in range(k_local):
        out_ref[k] = orbitals_ref[k] + both[k * walkers : (k + 1) * walkers]


def call(kernel, out, scratch=(), scalars=0, operands=0, flops=None):
    spaces = [pltpu.SMEM] * scalars + [pltpu.VMEM] * operands
    cost = None
    if flops is not None:
        cost = pl.CostEstimate(flops=flops, bytes_accessed=0, transcendentals=0)
    return pl.pallas_call(
        kernel,
        out_shape=out,
        in_specs=[pl.BlockSpec(memory_space=space) for space in spaces],
        out_specs=jax.tree.map(lambda _: pl.BlockSpec(memory_space=pltpu.VMEM), out),
        scratch_shapes=list(scratch),
        cost_estimate=cost,
        compiler_params=pltpu.CompilerParams(vmem_limit_bytes=24 * 2**20),
    )


def direct(green, fields, orbitals, chol_half, chol_full, chol_count, kq_map):
    k_local, pair_width, chol_cols = chol_half.shape[1], chol_half.shape[3], chol_half.shape[4]
    ka_count, pb_count = lax.axis_size("ka"), lax.axis_size("pb")
    walkers = ka_count
    kpoints = green.shape[3]
    span = k_local * walkers
    shape = jax.ShapeDtypeStruct
    tiles = chol_cols // LANES
    own_green = green.reshape(kpoints, 2 * pair_width)
    greens = exchange(own_green, "ka", GREEN_ROUNDS)
    half = chol_half.reshape(k_local, 2, pair_width, chol_cols)
    full = jnp.transpose(
        chol_full.reshape(k_local, 2, M * M, tiles, LANES), (0, 2, 3, 1, 4)
    ).reshape(k_local, M * M * tiles * 2, LANES)
    own_fields = fields.reshape(walkers, chol_cols)
    own_orbitals = orbitals.reshape(k_local, walkers, 2 * pair_width)
    mask, picks, own_lanes = call(
        functools.partial(prepare_kernel, ka_count, pb_count, walkers),
        (
            shape((2 * walkers, chol_cols), F32),
            shape((LANES, 2 * LANES), BF16),
            shape((2 * walkers, LANES), jnp.int32),
        ),
        scalars=2,
        flops=10**9,
    )(kq_map, chol_count)
    bias, own = call(
        functools.partial(bias_kernel, ka_count, k_local),
        (
            shape((2 * walkers + span, chol_cols), F32),
            shape((k_local, 2 * walkers, pair_width), F32),
        ),
        [pltpu.VMEM((walkers, kpoints, 2 * pair_width), F32)],
        operands=len(greens) + 3,
    )(*greens, half, own_orbitals, mask)
    parts = exchange(bias, "ka", BIAS_ROUNDS)
    shares, fold, own_picks = call(
        functools.partial(exchange_kernel, k_local, pb_count),
        (
            shape((walkers, LANES), F32),
            shape((LANES, LANES), BF16),
            shape((NOCC * LANES, 2 * LANES), BF16),
        ),
        operands=4,
    )(own, half, mask, own_lanes)
    width = -(-(M * M + 3) // LANES) * LANES
    blocks = call(
        functools.partial(operator_kernel, k_local),
        shape((ka_count * pb_count, 2 * span, width), BF16),
        [pltpu.VMEM((2 * M * M * tiles, LANES), F32), pltpu.VMEM((width, LANES), F32)],
        operands=len(parts) + 4,
    )(*parts, own_fields, mask, shares, full)
    group = operator_group(ka_count, pb_count)
    blocks = lax.all_to_all(
        blocks, ("pb", "ka"), 0, 0, axis_index_groups=[group], tiled=True
    )
    propagated, energy = call(
        functools.partial(taylor_kernel, pb_count, float(pb_count * chol_cols)),
        (shape((k_local, walkers, 2 * pair_width), F32), shape((1, 1), F32)),
        [
            pltpu.VMEM((ROWS * M, LANES), F32),
            pltpu.VMEM((ROWS * M, LANES), F32),
            pltpu.VMEM((NOCC * ROWS, 2 * LANES), F32),
            pltpu.VMEM((LANES, LANES), F32),
            pltpu.VMEM((LANES, LANES), F32),
        ],
        operands=len(parts) + 5,
    )(blocks, *parts, picks, fold, own_picks, own_orbitals)
    return (propagated[None], energy)


def on_device(green, fields, orbitals, chol_half, chol_full, chol_count, kq_map):
    ka_count, pb_count = lax.axis_size("ka"), lax.axis_size("pb")
    walkers = orbitals.shape[2]
    fits = 2 * pb_count * kq_map.shape[1] * walkers == LANES
    fits = fits and chol_half.shape[1] * walkers == 8 and chol_half.shape[4] == 2 * LANES
    fits = fits and ka_count == 4 and pb_count == 2
    if fits and chol_half.shape[0] == 1 and walkers == ka_count:
        return direct(green, fields, orbitals, chol_half, chol_full, chol_count, kq_map)
    return with_collectives(green, fields, orbitals, chol_half, chol_full, chol_count, kq_map)


def solution(mesh):
    placed = (
        P("wa", ("grp", "ka"), "pb", None, None),
        P("wa", "pb", "grp", None),
        P("wa", "ka", "grp", None),
        P("pb", "ka", None, None, None),
        P("pb", "ka", None, None, None),
        P(),
        P(),
    )
    return jax.shard_map(
        on_device,
        mesh=mesh,
        in_specs=placed,
        out_specs=(P("wa", "ka", "grp", None), P("wa", ("grp", "ka"))),
        check_vma=False,
    )
```

```python
import functools

import jax
import jax.numpy as jnp
from jax import lax
from jax.experimental import pallas as pl
from jax.experimental.pallas import tpu as pltpu
from jax.sharding import PartitionSpec as P

M = 26
NOCC = 4
TAYLOR = 3
LANES = 128
ROWS = 32

GREEN_ROUNDS = (
    ((3, 0), (2, 1), (1, 3), (0, 2)),
    ((3, 1), (2, 0), (0, 3), (1, 2)),
    ((1, 0), (3, 2), (2, 3), (0, 1)),
)[::-1]
BIAS_ROUNDS = (
    ((0, 1), (1, 3), (2, 0), (3, 2)),
    ((0, 3), (3, 0), (1, 2), (2, 1)),
    ((0, 2), (1, 0), (2, 3), (3, 1)),
)[::-1]


BIAS_STEP = 0.5
PROP_STEP = 0.5

F32 = jnp.float32
BF16 = jnp.bfloat16


def complex_dot(pattern, left_re, left_im, right_re, right_im):
    real_part = jnp.einsum(
        pattern, left_re, right_re, preferred_element_type=jnp.float32
    ) - jnp.einsum(pattern, left_im, right_im, preferred_element_type=jnp.float32)
    imag_part = jnp.einsum(
        pattern, left_re, right_im, preferred_element_type=jnp.float32
    ) + jnp.einsum(pattern, left_im, right_re, preferred_element_type=jnp.float32)
    return (real_part, imag_part)


def make_picker(wanted):

    def picker(shard_rows):
        row_count = shard_rows.shape[0]
        select = (wanted[:, None] == jnp.arange(row_count, dtype=jnp.int32)[None, :]).astype(
            jnp.bfloat16
        )
        return jnp.dot(select, shard_rows, preferred_element_type=jnp.float32)

    return picker


def with_collectives(green, fields, orbitals, chol_half, chol_full, chol_count, kq_map):
    q_local = chol_half.shape[0]
    k_local = chol_half.shape[1]
    pair_width = chol_half.shape[3]
    chol_cols = chol_half.shape[4]
    ka_count = lax.axis_size("ka")
    pb_count = lax.axis_size("pb")
    ka_pos = lax.axis_index("ka")
    pb_pos = lax.axis_index("pb")
    local_green = lax.all_to_all(green, "ka", split_axis=3, concat_axis=1, tiled=True)
    walkers = local_green.shape[1]
    per_device = walkers // ka_count
    greens = local_green[0].reshape(walkers, q_local, k_local, 2, pair_width)
    counts = lax.dynamic_slice_in_dim(chol_count, pb_pos * q_local, q_local)
    vec_mask = (jnp.arange(chol_cols, dtype=jnp.int32)[None, :] < counts[:, None]).astype(
        jnp.float32
    )
    bias_re, bias_im = complex_dot(
        "wqkx,qkxn->qwn",
        greens[:, :, :, 0],
        greens[:, :, :, 1],
        chol_half[:, :, 0],
        chol_half[:, :, 1],
    )
    own_rows = (jnp.arange(walkers, dtype=jnp.int32) // per_device == ka_pos).astype(jnp.float32)
    bias_re, bias_im = lax.psum((bias_re, bias_im), "ka")
    bias_re = bias_re * vec_mask[:, None, :]
    bias_im = bias_im * vec_mask[:, None, :]
    hartree = 0.5 * jnp.sum(bias_re * bias_re + bias_im * bias_im, axis=(0, 2)) * own_rows
    field_now = jnp.transpose(fields, (1, 0, 2, 3)).reshape(q_local, walkers, chol_cols)
    shift_re = ((field_now - BIAS_STEP * bias_re) * vec_mask[:, None, :]).astype(jnp.bfloat16)
    shift_im = (-BIAS_STEP * bias_im * vec_mask[:, None, :]).astype(jnp.bfloat16)
    exchange = jnp.zeros((walkers,), jnp.float32)
    for transfer in range(q_local):
        for kpoint in range(k_local):
            chol_row = chol_half[transfer, kpoint].reshape(2, NOCC, M, chol_cols)
            green_row = greens[:, transfer, kpoint].reshape(walkers, 2, NOCC, M)
            cross_re, cross_im = complex_dot(
                "ipn,wjp->wijn", chol_row[0], chol_row[1], green_row[:, 0], green_row[:, 1]
            )
            exchange = exchange + 0.5 * jnp.sum(
                (cross_re * cross_re + cross_im * cross_im) * vec_mask[transfer], axis=(1, 2, 3)
            )
    prop_re, prop_im = complex_dot(
        "qwn,qkyn->qwky", shift_re, shift_im, chol_full[:, :, 0], chol_full[:, :, 1]
    )
    shape = (q_local, walkers, k_local, M, M)
    oper_re = (PROP_STEP * prop_re).astype(jnp.bfloat16).reshape(shape)
    oper_im = (PROP_STEP * prop_im).astype(jnp.bfloat16).reshape(shape)
    normalizer = q_local * pb_count * chol_cols
    total_energy = lax.psum(hartree - exchange, ("ka", "pb")) / normalizer
    energy = lax.dynamic_slice_in_dim(total_energy, ka_pos * per_device, per_device).reshape(
        1, per_device
    )
    initial = orbitals[0].reshape(k_local, walkers, 2, NOCC, M)
    row_width = 2 * pair_width
    my_rows = lax.dynamic_slice_in_dim(kq_map, pb_pos * q_local, q_local, 0)
    wanted = lax.dynamic_slice_in_dim(my_rows, ka_pos * k_local, k_local, 1).reshape(
        q_local * k_local
    )
    picker = make_picker(wanted)
    current = initial
    summed_terms = initial
    for degree in range(1, TAYLOR + 1):
        rounded = current.astype(jnp.bfloat16).reshape(k_local, walkers * row_width)
        fetched = picker(lax.all_gather(rounded, "ka", axis=0, tiled=True))
        shifted_rows = fetched.astype(jnp.bfloat16).reshape(q_local, k_local, walkers, 2, NOCC, M)
        out_re, out_im = complex_dot(
            "xwkpq,xkwiq->kwip",
            oper_re,
            oper_im,
            shifted_rows[:, :, :, 0],
            shifted_rows[:, :, :, 1],
        )
        applied = jnp.stack([out_re, out_im], axis=2)
        applied = lax.psum(applied, "pb")
        current = applied / degree
        summed_terms = summed_terms + current
    propagated = summed_terms.reshape(1, k_local, walkers, row_width)
    return (propagated, energy)


def exchange(array, axis, rounds):
    return [array] + [lax.ppermute(array, axis, pairs) for pairs in rounds]


def origins(axis, rounds):
    at = lax.axis_index(axis)
    found = [at]
    for pairs in rounds:
        source = jnp.int32(0)
        for sender, receiver in pairs:
            source = jnp.where(at == receiver, sender, source)
        found.append(source)
    return found


def operator_group(ka_count, pb_count):
    first = (pb_count - 1) * ka_count + ka_count // 2
    rest = [at for at in range(pb_count * ka_count) if at != first]
    return [first] + rest[::-1]


def prepare_kernel(ka_count, pb_count, walkers, map_ref, count_ref, mask_ref, picks_ref):
    kept = count_ref[lax.axis_index("pb")]
    column = lax.broadcasted_iota(jnp.int32, mask_ref.shape, 1)
    mask_ref[...] = jnp.where(column < kept, 1.0, 0.0)
    kpoints = map_ref.shape[1]
    k_local = kpoints // ka_count
    span = k_local * walkers
    lane = lax.broadcasted_iota(jnp.int32, (1, LANES), 1)
    lane_q = lane // (LANES // pb_count)
    lane_ka = lax.rem(lane, LANES // pb_count) // (2 * span)
    lane_part = lax.rem(lane, 2 * span) // span
    lane_k = lane_ka * k_local + lax.rem(lane, span) // walkers
    wanted = jnp.zeros((1, LANES), jnp.int32)
    for q in range(pb_count):
        for k in range(kpoints):
            source = map_ref[q, k]
            source = source // k_local * (2 * span) + lax.rem(source, k_local) * walkers
            wanted = jnp.where((lane_q == q) & (lane_k == k), source, wanted)
    wanted = wanted + lax.rem(lane, walkers)
    row = lax.broadcasted_iota(jnp.int32, (LANES, LANES), 0)
    real = jnp.where(row == wanted, 1.0, 0.0)
    imag = jnp.where(row == wanted + span, jnp.where(lane_part == 0, 1.0, -1.0), 0.0)
    picks_ref[...] = jnp.concatenate([real, imag], axis=1).astype(BF16)


def bias_kernel(ka_count, k_local, *refs):
    *greens, chol_ref, orbitals_ref, mask_ref, bias_ref, own_ref, table = refs
    for source, green_ref in zip(origins("ka", GREEN_ROUNDS), greens):
        table[source] = green_ref[...].astype(F32)
    first = lax.axis_index("ka") * k_local
    width = chol_ref.shape[2]
    rows = 2 * ka_count
    total = jnp.zeros((rows, bias_ref.shape[1]), F32)
    for k in range(k_local):
        green = jnp.concatenate(
            [table[w, pl.ds(first + k, 1), :] for w in range(ka_count)], axis=0
        )
        real, imag = green[:, :width], green[:, width:]
        both = jnp.concatenate([real, imag], axis=0)
        turned = jnp.concatenate([-imag, real], axis=0)
        own_ref[k] = both
        total += jnp.dot(both.astype(BF16), chol_ref[k, 0], preferred_element_type=F32)
        total += jnp.dot(turned.astype(BF16), chol_ref[k, 1], preferred_element_type=F32)
    bias_ref[:rows] = total * mask_ref[...]
    window = jnp.concatenate([orbitals_ref[k] for k in range(k_local)], axis=0)
    count, width = window.shape
    bias_ref[rows : rows + count, :width] = window
    bias_ref[rows : rows + count, width:] = jnp.zeros((count, bias_ref.shape[1] - width), F32)


def exchange_kernel(k_local, own_ref, chol_ref, mask_ref, out_ref):
    walkers, width, columns = own_ref.shape[1] // 2, own_ref.shape[2], chol_ref.shape[3]
    rows = 2 * walkers
    lane = lax.broadcasted_iota(jnp.int32, (rows, LANES), 1)
    total = jnp.zeros((rows, columns), F32)
    for k in range(k_local):
        both = jnp.concatenate([own_ref[k], jnp.zeros((rows, LANES - width), F32)], axis=1)
        turned = jnp.concatenate([-both[walkers:], both[:walkers]], axis=0)
        sides = []
        for side in (both, turned):
            rolled = {
                step: side if step == 0 else pltpu.roll(side, (step * M) % LANES, 1)
                for step in range(1 - NOCC, NOCC)
            }
            blocks = []
            for i in range(NOCC):
                inside = (lane >= i * M) & (lane < (i + 1) * M)
                for j in range(NOCC):
                    blocks.append(jnp.where(inside, rolled[i - j], 0.0))
            sides.append(jnp.concatenate(blocks, axis=0)[:, :width].astype(BF16))
        cross = jnp.dot(sides[0], chol_ref[k, 0], preferred_element_type=F32)
        cross += jnp.dot(sides[1], chol_ref[k, 1], preferred_element_type=F32)
        cross = cross * cross
        for block in range(NOCC * NOCC):
            total += cross[block * rows : (block + 1) * rows]
    total = total * mask_ref[:rows]
    total = total[:walkers] + total[walkers:]
    summed = 0.5 * jnp.sum(total, axis=1, keepdims=True)
    out_ref[...] = jnp.broadcast_to(summed, out_ref.shape)


def operator_kernel(k_local, *refs):
    *parts, fields_ref, mask_ref, exchange_ref, chol_ref, out_ref, products, turned_ref = refs
    walkers, columns = fields_ref.shape
    bias = parts[0][: 2 * walkers]
    for part in parts[1:]:
        bias = bias + part[: 2 * walkers]
    pairs = M * M
    tiles = columns // LANES
    group = LANES // (2 * tiles)
    bias_re, bias_im = bias[:walkers], bias[walkers:]
    hartree = 0.5 * jnp.sum(bias_re * bias_re + bias_im * bias_im, axis=1, keepdims=True)
    own = lax.broadcasted_iota(jnp.int32, (walkers, 1), 0) == lax.axis_index("ka")
    energy = jnp.where(own, hartree, 0.0) - exchange_ref[:, :1]
    kept = mask_ref[:walkers]
    shift_re = (fields_ref[...] - BIAS_STEP * bias_re) * kept
    shift_im = -BIAS_STEP * bias_im * kept
    span = k_local * walkers
    weights = []
    for k in range(k_local):
        before, after = k * walkers, span - (k + 1) * walkers
        pieces = []
        for tile in range(tiles):
            at = slice(tile * LANES, (tile + 1) * LANES)
            for first, second in ((shift_re, shift_im), (-shift_im, shift_re)):
                for side in (first, second):
                    pieces += [(before, None), (walkers, side[:, at]), (after, None)]
                pieces.append((group - 2 * span, None))
        weights.append(
            jnp.concatenate(
                [jnp.zeros((n, LANES), F32) if p is None else p for n, p in pieces if n], axis=0
            ).astype(BF16)
        )
    products[...] = lax.dot_general(
        jnp.concatenate([chol_ref[k] for k in range(k_local)], axis=1),
        jnp.concatenate(weights, axis=1),
        (((1,), (1,)), ((), ())),
        preferred_element_type=F32,
    )
    lane = lax.broadcasted_iota(jnp.int32, (pairs, LANES), 1)
    merged = products[pl.ds(0, pairs, stride=2 * tiles), :]
    for at in range(1, 2 * tiles):
        row = products[pl.ds(at, pairs, stride=2 * tiles), :]
        merged = jnp.where(lane >= at * group, row, merged)
    turned_ref[:pairs] = merged
    copies, rows, width = out_ref.shape
    lane = lax.broadcasted_iota(jnp.int32, (rows, LANES), 1)
    for at in range(0, width, LANES):
        block = turned_ref[at : at + LANES].T
        block = PROP_STEP * sum(block[n * group : n * group + rows] for n in range(2 * tiles))
        if at + LANES > pairs:
            share = jnp.concatenate([energy, jnp.zeros((rows - walkers, 1), F32)], axis=0)
            block = jnp.where(lane + at < pairs, block, 0.0)
            for piece in range(3):
                head = share.astype(BF16).astype(F32)
                block = jnp.where(lane + at == pairs + piece, head, block)
                share = share - head
        for copy in range(copies):
            out_ref[copy, :, at : at + LANES] = block.astype(BF16)


def taylor_kernel(pb_count, normalizer, blocks_ref, *refs):
    *windows, picks_ref, orbitals_ref, out_ref, energy_ref, turned, picked, term = refs
    pairs = M * M
    pair = NOCC * M
    k_local, walkers, _ = out_ref.shape
    span = k_local * walkers
    ka_pos = lax.axis_index("ka")
    term[...] = jnp.zeros_like(term)
    for source, window_ref in zip(origins("ka", BIAS_ROUNDS), windows):
        start = pl.multiple_of(source * (2 * span), 2 * span)
        window = window_ref[window_ref.shape[0] - span :]
        term[pl.ds(start, span), :pair] = window[:, :pair]
        term[pl.ds(start + span, span), :pair] = window[:, pair : 2 * pair]
    picked[...] = jnp.dot(term[...].T.astype(BF16), picks_ref[...], preferred_element_type=F32)
    count, _, width = blocks_ref.shape
    group = operator_group(count // pb_count, pb_count)
    places = [group.index(n) for n in range(count)]
    for at in range(0, width, LANES):
        tile = jnp.concatenate([blocks_ref[n, :, at : at + LANES] for n in places], axis=0)
        turned[at : at + LANES] = tile.T.astype(F32)
    shares = turned[pairs : pairs + 3]
    lane = lax.broadcasted_iota(jnp.int32, shares.shape, 1)
    shares = jnp.where(lax.rem(lane, 2 * span) == ka_pos, shares, 0.0)
    shares = jnp.sum(jnp.sum(shares, axis=0, keepdims=True), axis=1, keepdims=True)
    energy_ref[...] = shares / normalizer
    lane = lax.broadcasted_iota(jnp.int32, (M, LANES), 1)
    imaginary = lax.rem(lane, 2 * span) >= span
    sums = [jnp.zeros((M, LANES), F32) for _ in range(NOCC)]
    for degree in range(1, TAYLOR + 1):
        stride = M if degree == 1 else ROWS
        straight = [jnp.zeros((M, LANES), F32) for _ in range(NOCC)]
        crossed = [jnp.zeros((M, LANES), F32) for _ in range(NOCC)]
        for c in range(M):
            column = turned[pl.ds(c, M, stride=M), :]
            for i in range(NOCC):
                at = i * stride + c
                straight[i] += column * picked[at : at + 1, :LANES]
                crossed[i] += column * picked[at : at + 1, LANES:]
        for i in range(NOCC):
            other = jnp.where(
                imaginary, pltpu.roll(crossed[i], span, 1), pltpu.roll(crossed[i], LANES - span, 1)
            )
            applied = straight[i] + other
            applied = applied + pltpu.roll(applied, LANES // pb_count, 1)
            current = applied / degree
            sums[i] = sums[i] + current
            term[i * ROWS : i * ROWS + M] = current if degree < TAYLOR else sums[i]
        if degree < TAYLOR:
            picked[...] = jnp.dot(
                term[...].astype(BF16), picks_ref[...], preferred_element_type=F32
            )
    turned[:LANES] = term[...].T
    both = turned[pl.ds(pl.multiple_of(ka_pos * (2 * span), 2 * span), 2 * span), :]
    both = jnp.concatenate([both[:, i * ROWS : i * ROWS + M] for i in range(NOCC)], axis=1)
    both = jnp.concatenate([both[:span], both[span:]], axis=1)
    for k in range(k_local):
        out_ref[k] = orbitals_ref[k] + both[k * walkers : (k + 1) * walkers]


def call(kernel, out, scratch=(), scalars=0, operands=0, flops=None):
    spaces = [pltpu.SMEM] * scalars + [pltpu.VMEM] * operands
    cost = None
    if flops is not None:
        cost = pl.CostEstimate(flops=flops, bytes_accessed=0, transcendentals=0)
    return pl.pallas_call(
        kernel,
        out_shape=out,
        in_specs=[pl.BlockSpec(memory_space=space) for space in spaces],
        out_specs=jax.tree.map(lambda _: pl.BlockSpec(memory_space=pltpu.VMEM), out),
        scratch_shapes=list(scratch),
        cost_estimate=cost,
        compiler_params=pltpu.CompilerParams(vmem_limit_bytes=24 * 2**20),
    )


def direct(green, fields, orbitals, chol_half, chol_full, chol_count, kq_map):
    k_local, pair_width, chol_cols = chol_half.shape[1], chol_half.shape[3], chol_half.shape[4]
    ka_count, pb_count = lax.axis_size("ka"), lax.axis_size("pb")
    walkers = ka_count
    kpoints = green.shape[3]
    span = k_local * walkers
    shape = jax.ShapeDtypeStruct
    tiles = chol_cols // LANES
    own_green = green.reshape(kpoints, 2 * pair_width)
    greens = exchange(own_green, "ka", GREEN_ROUNDS)
    half = chol_half.reshape(k_local, 2, pair_width, chol_cols)
    full = jnp.transpose(
        chol_full.reshape(k_local, 2, M * M, tiles, LANES), (0, 2, 3, 1, 4)
    ).reshape(k_local, M * M * tiles * 2, LANES)
    own_fields = fields.reshape(walkers, chol_cols)
    own_orbitals = orbitals.reshape(k_local, walkers, 2 * pair_width)
    mask, picks = call(
        functools.partial(prepare_kernel, ka_count, pb_count, walkers),
        (shape((2 * walkers, chol_cols), F32), shape((LANES, 2 * LANES), BF16)),
        scalars=2,
        flops=10**9,
    )(kq_map, chol_count)
    bias, own = call(
        functools.partial(bias_kernel, ka_count, k_local),
        (
            shape((2 * walkers + span, chol_cols), F32),
            shape((k_local, 2 * walkers, pair_width), F32),
        ),
        [pltpu.VMEM((walkers, kpoints, 2 * pair_width), F32)],
        operands=len(greens) + 3,
    )(*greens, half, own_orbitals, mask)
    parts = exchange(bias, "ka", BIAS_ROUNDS)
    shares = call(
        functools.partial(exchange_kernel, k_local),
        shape((walkers, LANES), F32),
        operands=3,
    )(own, half, mask)
    width = -(-(M * M + 3) // LANES) * LANES
    blocks = call(
        functools.partial(operator_kernel, k_local),
        shape((1, 2 * span, width), BF16),
        [pltpu.VMEM((2 * M * M * tiles, LANES), F32), pltpu.VMEM((width, LANES), F32)],
        operands=len(parts) + 4,
    )(*parts, own_fields, mask, shares, full)
    group = operator_group(ka_count, pb_count)
    blocks = lax.all_gather(blocks, ("pb", "ka"), axis_index_groups=[group], tiled=True)
    propagated, energy = call(
        functools.partial(taylor_kernel, pb_count, float(pb_count * chol_cols)),
        (shape((k_local, walkers, 2 * pair_width), F32), shape((1, 1), F32)),
        [
            pltpu.VMEM((width, LANES), F32),
            pltpu.VMEM((NOCC * ROWS, 2 * LANES), F32),
            pltpu.VMEM((LANES, LANES), F32),
        ],
        operands=len(parts) + 3,
    )(blocks, *parts, picks, own_orbitals)
    return (propagated[None], energy)


def on_device(green, fields, orbitals, chol_half, chol_full, chol_count, kq_map):
    ka_count, pb_count = lax.axis_size("ka"), lax.axis_size("pb")
    walkers = orbitals.shape[2]
    fits = 2 * pb_count * kq_map.shape[1] * walkers == LANES
    fits = fits and chol_half.shape[1] * walkers == 8 and chol_half.shape[4] == 2 * LANES
    fits = fits and ka_count == 4
    if fits and chol_half.shape[0] == 1 and walkers == ka_count:
        return direct(green, fields, orbitals, chol_half, chol_full, chol_count, kq_map)
    return with_collectives(green, fields, orbitals, chol_half, chol_full, chol_count, kq_map)


def solution(mesh):
    placed = (
        P("wa", ("grp", "ka"), "pb", None, None),
        P("wa", "pb", "grp", None),
        P("wa", "ka", "grp", None),
        P("pb", "ka", None, None, None),
        P("pb", "ka", None, None, None),
        P(),
        P(),
    )
    return jax.shard_map(
        on_device,
        mesh=mesh,
        in_specs=placed,
        out_specs=(P("wa", "ka", "grp", None), P("wa", ("grp", "ka"))),
        check_vma=False,
    )
```

```python
import functools

import jax
import jax.numpy as jnp
from jax import lax
from jax.experimental import pallas as pl
from jax.experimental.pallas import tpu as pltpu
from jax.sharding import PartitionSpec as P

M = 26
NOCC = 4
TAYLOR = 3
LANES = 128
ROWS = 32

GREEN_ROUNDS = (
    ((3, 0), (2, 1), (1, 3), (0, 2)),
    ((3, 1), (2, 0), (0, 3), (1, 2)),
    ((1, 0), (3, 2), (2, 3), (0, 1)),
)[::-1]
BIAS_ROUNDS = (
    ((0, 1), (1, 3), (2, 0), (3, 2)),
    ((0, 3), (3, 0), (1, 2), (2, 1)),
    ((0, 2), (1, 0), (2, 3), (3, 1)),
)[::-1]


BIAS_STEP = 0.5
PROP_STEP = 0.5

F32 = jnp.float32
BF16 = jnp.bfloat16


def complex_dot(pattern, left_re, left_im, right_re, right_im):
    real_part = jnp.einsum(
        pattern, left_re, right_re, preferred_element_type=jnp.float32
    ) - jnp.einsum(pattern, left_im, right_im, preferred_element_type=jnp.float32)
    imag_part = jnp.einsum(
        pattern, left_re, right_im, preferred_element_type=jnp.float32
    ) + jnp.einsum(pattern, left_im, right_re, preferred_element_type=jnp.float32)
    return (real_part, imag_part)


def make_picker(wanted):

    def picker(shard_rows):
        row_count = shard_rows.shape[0]
        select = (wanted[:, None] == jnp.arange(row_count, dtype=jnp.int32)[None, :]).astype(
            jnp.bfloat16
        )
        return jnp.dot(select, shard_rows, preferred_element_type=jnp.float32)

    return picker


def with_collectives(green, fields, orbitals, chol_half, chol_full, chol_count, kq_map):
    q_local = chol_half.shape[0]
    k_local = chol_half.shape[1]
    pair_width = chol_half.shape[3]
    chol_cols = chol_half.shape[4]
    ka_count = lax.axis_size("ka")
    pb_count = lax.axis_size("pb")
    ka_pos = lax.axis_index("ka")
    pb_pos = lax.axis_index("pb")
    local_green = lax.all_to_all(green, "ka", split_axis=3, concat_axis=1, tiled=True)
    walkers = local_green.shape[1]
    per_device = walkers // ka_count
    greens = local_green[0].reshape(walkers, q_local, k_local, 2, pair_width)
    counts = lax.dynamic_slice_in_dim(chol_count, pb_pos * q_local, q_local)
    vec_mask = (jnp.arange(chol_cols, dtype=jnp.int32)[None, :] < counts[:, None]).astype(
        jnp.float32
    )
    bias_re, bias_im = complex_dot(
        "wqkx,qkxn->qwn",
        greens[:, :, :, 0],
        greens[:, :, :, 1],
        chol_half[:, :, 0],
        chol_half[:, :, 1],
    )
    own_rows = (jnp.arange(walkers, dtype=jnp.int32) // per_device == ka_pos).astype(jnp.float32)
    bias_re, bias_im = lax.psum((bias_re, bias_im), "ka")
    bias_re = bias_re * vec_mask[:, None, :]
    bias_im = bias_im * vec_mask[:, None, :]
    hartree = 0.5 * jnp.sum(bias_re * bias_re + bias_im * bias_im, axis=(0, 2)) * own_rows
    field_now = jnp.transpose(fields, (1, 0, 2, 3)).reshape(q_local, walkers, chol_cols)
    shift_re = ((field_now - BIAS_STEP * bias_re) * vec_mask[:, None, :]).astype(jnp.bfloat16)
    shift_im = (-BIAS_STEP * bias_im * vec_mask[:, None, :]).astype(jnp.bfloat16)
    exchange = jnp.zeros((walkers,), jnp.float32)
    for transfer in range(q_local):
        for kpoint in range(k_local):
            chol_row = chol_half[transfer, kpoint].reshape(2, NOCC, M, chol_cols)
            green_row = greens[:, transfer, kpoint].reshape(walkers, 2, NOCC, M)
            cross_re, cross_im = complex_dot(
                "ipn,wjp->wijn", chol_row[0], chol_row[1], green_row[:, 0], green_row[:, 1]
            )
            exchange = exchange + 0.5 * jnp.sum(
                (cross_re * cross_re + cross_im * cross_im) * vec_mask[transfer], axis=(1, 2, 3)
            )
    prop_re, prop_im = complex_dot(
        "qwn,qkyn->qwky", shift_re, shift_im, chol_full[:, :, 0], chol_full[:, :, 1]
    )
    shape = (q_local, walkers, k_local, M, M)
    oper_re = (PROP_STEP * prop_re).astype(jnp.bfloat16).reshape(shape)
    oper_im = (PROP_STEP * prop_im).astype(jnp.bfloat16).reshape(shape)
    normalizer = q_local * pb_count * chol_cols
    total_energy = lax.psum(hartree - exchange, ("ka", "pb")) / normalizer
    energy = lax.dynamic_slice_in_dim(total_energy, ka_pos * per_device, per_device).reshape(
        1, per_device
    )
    initial = orbitals[0].reshape(k_local, walkers, 2, NOCC, M)
    row_width = 2 * pair_width
    my_rows = lax.dynamic_slice_in_dim(kq_map, pb_pos * q_local, q_local, 0)
    wanted = lax.dynamic_slice_in_dim(my_rows, ka_pos * k_local, k_local, 1).reshape(
        q_local * k_local
    )
    picker = make_picker(wanted)
    current = initial
    summed_terms = initial
    for degree in range(1, TAYLOR + 1):
        rounded = current.astype(jnp.bfloat16).reshape(k_local, walkers * row_width)
        fetched = picker(lax.all_gather(rounded, "ka", axis=0, tiled=True))
        shifted_rows = fetched.astype(jnp.bfloat16).reshape(q_local, k_local, walkers, 2, NOCC, M)
        out_re, out_im = complex_dot(
            "xwkpq,xkwiq->kwip",
            oper_re,
            oper_im,
            shifted_rows[:, :, :, 0],
            shifted_rows[:, :, :, 1],
        )
        applied = jnp.stack([out_re, out_im], axis=2)
        applied = lax.psum(applied, "pb")
        current = applied / degree
        summed_terms = summed_terms + current
    propagated = summed_terms.reshape(1, k_local, walkers, row_width)
    return (propagated, energy)


def exchange(array, axis, rounds):
    return [array] + [lax.ppermute(array, axis, pairs) for pairs in rounds]


def origins(axis, rounds):
    at = lax.axis_index(axis)
    found = [at]
    for pairs in rounds:
        source = jnp.int32(0)
        for sender, receiver in pairs:
            source = jnp.where(at == receiver, sender, source)
        found.append(source)
    return found


def operator_group(ka_count, pb_count):
    first = (pb_count - 1) * ka_count + ka_count // 2
    rest = [at for at in range(pb_count * ka_count) if at != first]
    return [first] + rest[::-1]


def prepare_kernel(ka_count, pb_count, walkers, map_ref, count_ref, mask_ref, picks_ref):
    kept = count_ref[lax.axis_index("pb")]
    column = lax.broadcasted_iota(jnp.int32, mask_ref.shape, 1)
    mask_ref[...] = jnp.where(column < kept, 1.0, 0.0)
    kpoints = map_ref.shape[1]
    k_local = kpoints // ka_count
    span = k_local * walkers
    lane = lax.broadcasted_iota(jnp.int32, (1, LANES), 1)
    lane_q = lane // (LANES // pb_count)
    lane_ka = lax.rem(lane, LANES // pb_count) // (2 * span)
    lane_part = lax.rem(lane, 2 * span) // span
    lane_k = lane_ka * k_local + lax.rem(lane, span) // walkers
    wanted = jnp.zeros((1, LANES), jnp.int32)
    for q in range(pb_count):
        for k in range(kpoints):
            source = map_ref[q, k]
            source = source // k_local * (2 * span) + lax.rem(source, k_local) * walkers
            wanted = jnp.where((lane_q == q) & (lane_k == k), source, wanted)
    wanted = wanted + lax.rem(lane, walkers)
    row = lax.broadcasted_iota(jnp.int32, (LANES, LANES), 0)
    real = jnp.where(row == wanted, 1.0, 0.0)
    imag = jnp.where(row == wanted + span, jnp.where(lane_part == 0, 1.0, -1.0), 0.0)
    picks_ref[...] = jnp.concatenate([real, imag], axis=1).astype(BF16)


def bias_kernel(ka_count, k_local, *refs):
    *greens, chol_ref, orbitals_ref, mask_ref, bias_ref, own_ref, table = refs
    for source, green_ref in zip(origins("ka", GREEN_ROUNDS), greens):
        table[source] = green_ref[...].astype(F32)
    first = lax.axis_index("ka") * k_local
    width = chol_ref.shape[2]
    rows = 2 * ka_count
    total = jnp.zeros((rows, bias_ref.shape[1]), F32)
    for k in range(k_local):
        green = jnp.concatenate(
            [table[w, pl.ds(first + k, 1), :] for w in range(ka_count)], axis=0
        )
        real, imag = green[:, :width], green[:, width:]
        both = jnp.concatenate([real, imag], axis=0)
        turned = jnp.concatenate([-imag, real], axis=0)
        own_ref[k] = both
        total += jnp.dot(both.astype(BF16), chol_ref[k, 0], preferred_element_type=F32)
        total += jnp.dot(turned.astype(BF16), chol_ref[k, 1], preferred_element_type=F32)
    bias_ref[:rows] = total * mask_ref[...]
    window = jnp.concatenate([orbitals_ref[k] for k in range(k_local)], axis=0)
    count, width = window.shape
    bias_ref[rows : rows + count, :width] = window
    bias_ref[rows : rows + count, width:] = jnp.zeros((count, bias_ref.shape[1] - width), F32)


def exchange_kernel(k_local, own_ref, chol_ref, mask_ref, out_ref):
    walkers, width, columns = own_ref.shape[1] // 2, own_ref.shape[2], chol_ref.shape[3]
    rows = 2 * walkers
    lane = lax.broadcasted_iota(jnp.int32, (rows, LANES), 1)
    total = jnp.zeros((rows, columns), F32)
    for k in range(k_local):
        both = jnp.concatenate([own_ref[k], jnp.zeros((rows, LANES - width), F32)], axis=1)
        turned = jnp.concatenate([-both[walkers:], both[:walkers]], axis=0)
        sides = []
        for side in (both, turned):
            rolled = {
                step: side if step == 0 else pltpu.roll(side, (step * M) % LANES, 1)
                for step in range(1 - NOCC, NOCC)
            }
            blocks = []
            for i in range(NOCC):
                inside = (lane >= i * M) & (lane < (i + 1) * M)
                for j in range(NOCC):
                    blocks.append(jnp.where(inside, rolled[i - j], 0.0))
            sides.append(jnp.concatenate(blocks, axis=0)[:, :width].astype(BF16))
        cross = jnp.dot(sides[0], chol_ref[k, 0], preferred_element_type=F32)
        cross += jnp.dot(sides[1], chol_ref[k, 1], preferred_element_type=F32)
        cross = cross * cross
        for block in range(NOCC * NOCC):
            total += cross[block * rows : (block + 1) * rows]
    total = total * mask_ref[:rows]
    total = total[:walkers] + total[walkers:]
    summed = 0.5 * jnp.sum(total, axis=1, keepdims=True)
    out_ref[...] = jnp.broadcast_to(summed, out_ref.shape)


def operator_kernel(k_local, *refs):
    *parts, fields_ref, mask_ref, exchange_ref, chol_ref, out_ref, products, turned_ref = refs
    walkers, columns = fields_ref.shape
    bias = parts[0][: 2 * walkers]
    for part in parts[1:]:
        bias = bias + part[: 2 * walkers]
    pairs = M * M
    tiles = columns // LANES
    group = LANES // (2 * tiles)
    bias_re, bias_im = bias[:walkers], bias[walkers:]
    hartree = 0.5 * jnp.sum(bias_re * bias_re + bias_im * bias_im, axis=1, keepdims=True)
    own = lax.broadcasted_iota(jnp.int32, (walkers, 1), 0) == lax.axis_index("ka")
    energy = jnp.where(own, hartree, 0.0) - exchange_ref[:, :1]
    kept = mask_ref[:walkers]
    shift_re = (fields_ref[...] - BIAS_STEP * bias_re) * kept
    shift_im = -BIAS_STEP * bias_im * kept
    span = k_local * walkers
    weights = []
    for k in range(k_local):
        before, after = k * walkers, span - (k + 1) * walkers
        pieces = []
        for tile in range(tiles):
            at = slice(tile * LANES, (tile + 1) * LANES)
            for first, second in ((shift_re, shift_im), (-shift_im, shift_re)):
                for side in (first, second):
                    pieces += [(before, None), (walkers, side[:, at]), (after, None)]
                pieces.append((group - 2 * span, None))
        weights.append(
            jnp.concatenate(
                [jnp.zeros((n, LANES), F32) if p is None else p for n, p in pieces if n], axis=0
            ).astype(BF16)
        )
    products[...] = lax.dot_general(
        jnp.concatenate([chol_ref[k] for k in range(k_local)], axis=1),
        jnp.concatenate(weights, axis=1),
        (((1,), (1,)), ((), ())),
        preferred_element_type=F32,
    )
    lane = lax.broadcasted_iota(jnp.int32, (pairs, LANES), 1)
    merged = products[pl.ds(0, pairs, stride=2 * tiles), :]
    for at in range(1, 2 * tiles):
        row = products[pl.ds(at, pairs, stride=2 * tiles), :]
        merged = jnp.where(lane >= at * group, row, merged)
    turned_ref[:pairs] = merged
    copies, rows, width = out_ref.shape
    lane = lax.broadcasted_iota(jnp.int32, (rows, LANES), 1)
    for at in range(0, width, LANES):
        block = turned_ref[at : at + LANES].T
        block = PROP_STEP * sum(block[n * group : n * group + rows] for n in range(2 * tiles))
        if at + LANES > pairs:
            share = jnp.concatenate([energy, jnp.zeros((rows - walkers, 1), F32)], axis=0)
            block = jnp.where(lane + at < pairs, block, 0.0)
            for piece in range(3):
                head = share.astype(BF16).astype(F32)
                block = jnp.where(lane + at == pairs + piece, head, block)
                share = share - head
        for copy in range(copies):
            out_ref[copy, :, at : at + LANES] = block.astype(BF16)


def first_kernel(*refs):
    *windows, picks_ref, first_ref, term = refs
    pair = NOCC * M
    term[...] = jnp.zeros_like(term)
    for source, window_ref in zip(origins("ka", BIAS_ROUNDS), windows):
        span = window_ref.shape[0] // 2
        start = pl.multiple_of(source * (2 * span), 2 * span)
        window = window_ref[span:]
        term[pl.ds(start, span), :pair] = window[:, :pair]
        term[pl.ds(start + span, span), :pair] = window[:, pair : 2 * pair]
    first_ref[...] = jnp.dot(
        term[...].T.astype(BF16), picks_ref[...], preferred_element_type=F32
    )


def taylor_kernel(
    pb_count, normalizer, blocks_ref, first_ref, picks_ref, orbitals_ref, out_ref, energy_ref,
    turned, picked, term,
):
    pairs = M * M
    k_local, walkers, _ = out_ref.shape
    span = k_local * walkers
    ka_pos = lax.axis_index("ka")
    term[...] = jnp.zeros_like(term)
    count, _, width = blocks_ref.shape
    group = operator_group(count // pb_count, pb_count)
    places = [group.index(n) for n in range(count)]
    for at in range(0, width, LANES):
        tile = jnp.concatenate([blocks_ref[n, :, at : at + LANES] for n in places], axis=0)
        turned[at : at + LANES] = tile.T.astype(F32)
    shares = turned[pairs : pairs + 3]
    lane = lax.broadcasted_iota(jnp.int32, shares.shape, 1)
    shares = jnp.where(lax.rem(lane, 2 * span) == ka_pos, shares, 0.0)
    shares = jnp.sum(jnp.sum(shares, axis=0, keepdims=True), axis=1, keepdims=True)
    energy_ref[...] = shares / normalizer
    lane = lax.broadcasted_iota(jnp.int32, (M, LANES), 1)
    imaginary = lax.rem(lane, 2 * span) >= span
    sums = [jnp.zeros((M, LANES), F32) for _ in range(NOCC)]
    for degree in range(1, TAYLOR + 1):
        source, stride = (first_ref, M) if degree == 1 else (picked, ROWS)
        straight = [jnp.zeros((M, LANES), F32) for _ in range(NOCC)]
        crossed = [jnp.zeros((M, LANES), F32) for _ in range(NOCC)]
        for c in range(M):
            column = turned[pl.ds(c, M, stride=M), :]
            for i in range(NOCC):
                at = i * stride + c
                straight[i] += column * source[at : at + 1, :LANES]
                crossed[i] += column * source[at : at + 1, LANES:]
        for i in range(NOCC):
            other = jnp.where(
                imaginary, pltpu.roll(crossed[i], span, 1), pltpu.roll(crossed[i], LANES - span, 1)
            )
            applied = straight[i] + other
            applied = applied + pltpu.roll(applied, LANES // pb_count, 1)
            current = applied * (1.0 / degree)
            sums[i] = sums[i] + current
            term[i * ROWS : i * ROWS + M] = current if degree < TAYLOR else sums[i]
        if degree < TAYLOR:
            picked[...] = jnp.dot(
                term[...].astype(BF16), picks_ref[...], preferred_element_type=F32
            )
    turned[:LANES] = term[...].T
    both = turned[pl.ds(pl.multiple_of(ka_pos * (2 * span), 2 * span), 2 * span), :]
    both = jnp.concatenate([both[:, i * ROWS : i * ROWS + M] for i in range(NOCC)], axis=1)
    both = jnp.concatenate([both[:span], both[span:]], axis=1)
    for k in range(k_local):
        out_ref[k] = orbitals_ref[k] + both[k * walkers : (k + 1) * walkers]


def call(kernel, out, scratch=(), scalars=0, operands=0, flops=None):
    spaces = [pltpu.SMEM] * scalars + [pltpu.VMEM] * operands
    cost = None
    if flops is not None:
        cost = pl.CostEstimate(flops=flops, bytes_accessed=0, transcendentals=0)
    return pl.pallas_call(
        kernel,
        out_shape=out,
        in_specs=[pl.BlockSpec(memory_space=space) for space in spaces],
        out_specs=jax.tree.map(lambda _: pl.BlockSpec(memory_space=pltpu.VMEM), out),
        scratch_shapes=list(scratch),
        cost_estimate=cost,
        compiler_params=pltpu.CompilerParams(vmem_limit_bytes=24 * 2**20),
    )


def direct(green, fields, orbitals, chol_half, chol_full, chol_count, kq_map):
    k_local, pair_width, chol_cols = chol_half.shape[1], chol_half.shape[3], chol_half.shape[4]
    ka_count, pb_count = lax.axis_size("ka"), lax.axis_size("pb")
    walkers = ka_count
    kpoints = green.shape[3]
    span = k_local * walkers
    shape = jax.ShapeDtypeStruct
    tiles = chol_cols // LANES
    own_green = green.reshape(kpoints, 2 * pair_width)
    greens = exchange(own_green, "ka", GREEN_ROUNDS)
    half = chol_half.reshape(k_local, 2, pair_width, chol_cols)
    full = jnp.transpose(
        chol_full.reshape(k_local, 2, M * M, tiles, LANES), (0, 2, 3, 1, 4)
    ).reshape(k_local, M * M * tiles * 2, LANES)
    own_fields = fields.reshape(walkers, chol_cols)
    own_orbitals = orbitals.reshape(k_local, walkers, 2 * pair_width)
    mask, picks = call(
        functools.partial(prepare_kernel, ka_count, pb_count, walkers),
        (shape((2 * walkers, chol_cols), F32), shape((LANES, 2 * LANES), BF16)),
        scalars=2,
        flops=10**9,
    )(kq_map, chol_count)
    bias, own = call(
        functools.partial(bias_kernel, ka_count, k_local),
        (
            shape((2 * walkers + span, chol_cols), F32),
            shape((k_local, 2 * walkers, pair_width), F32),
        ),
        [pltpu.VMEM((walkers, kpoints, 2 * pair_width), F32)],
        operands=len(greens) + 3,
    )(*greens, half, own_orbitals, mask)
    parts = exchange(bias, "ka", BIAS_ROUNDS)
    shares = call(
        functools.partial(exchange_kernel, k_local),
        shape((walkers, LANES), F32),
        operands=3,
    )(own, half, mask)
    width = -(-(M * M + 3) // LANES) * LANES
    blocks = call(
        functools.partial(operator_kernel, k_local),
        shape((ka_count * pb_count, 2 * span, width), BF16),
        [pltpu.VMEM((2 * M * M * tiles, LANES), F32), pltpu.VMEM((width, LANES), F32)],
        operands=len(parts) + 4,
    )(*parts, own_fields, mask, shares, full)
    group = operator_group(ka_count, pb_count)
    blocks = lax.all_to_all(
        blocks, ("pb", "ka"), 0, 0, axis_index_groups=[group], tiled=True
    )
    first = call(
        first_kernel,
        shape((LANES, 2 * LANES), F32),
        [pltpu.VMEM((LANES, LANES), F32)],
        operands=len(parts) + 1,
    )(*parts, picks)
    propagated, energy = call(
        functools.partial(taylor_kernel, pb_count, float(pb_count * chol_cols)),
        (shape((k_local, walkers, 2 * pair_width), F32), shape((1, 1), F32)),
        [
            pltpu.VMEM((width, LANES), F32),
            pltpu.VMEM((NOCC * ROWS, 2 * LANES), F32),
            pltpu.VMEM((LANES, LANES), F32),
        ],
        operands=4,
    )(blocks, first, picks, own_orbitals)
    return (propagated[None], energy)


def on_device(green, fields, orbitals, chol_half, chol_full, chol_count, kq_map):
    ka_count, pb_count = lax.axis_size("ka"), lax.axis_size("pb")
    walkers = orbitals.shape[2]
    fits = 2 * pb_count * kq_map.shape[1] * walkers == LANES
    fits = fits and chol_half.shape[1] * walkers == 8 and chol_half.shape[4] == 2 * LANES
    fits = fits and ka_count == 4
    if fits and chol_half.shape[0] == 1 and walkers == ka_count:
        return direct(green, fields, orbitals, chol_half, chol_full, chol_count, kq_map)
    return with_collectives(green, fields, orbitals, chol_half, chol_full, chol_count, kq_map)


def solution(mesh):
    placed = (
        P("wa", ("grp", "ka"), "pb", None, None),
        P("wa", "pb", "grp", None),
        P("wa", "ka", "grp", None),
        P("pb", "ka", None, None, None),
        P("pb", "ka", None, None, None),
        P(),
        P(),
    )
    return jax.shard_map(
        on_device,
        mesh=mesh,
        in_specs=placed,
        out_specs=(P("wa", "ka", "grp", None), P("wa", ("grp", "ka"))),
        check_vma=False,
    )
```

```python
import functools

import jax
import jax.numpy as jnp
from jax import lax
from jax.experimental import pallas as pl
from jax.experimental.pallas import tpu as pltpu
from jax.sharding import PartitionSpec as P

M = 26
NOCC = 4
TAYLOR = 3
LANES = 128
ROWS = 32

GREEN_ROUNDS = (
    ((3, 0), (2, 1), (1, 3), (0, 2)),
    ((3, 1), (2, 0), (0, 3), (1, 2)),
    ((1, 0), (3, 2), (2, 3), (0, 1)),
)[::-1]
BIAS_ROUNDS = (
    ((0, 1), (1, 3), (2, 0), (3, 2)),
    ((0, 3), (3, 0), (1, 2), (2, 1)),
    ((0, 2), (1, 0), (2, 3), (3, 1)),
)[::-1]


BIAS_STEP = 0.5
PROP_STEP = 0.5

F32 = jnp.float32
BF16 = jnp.bfloat16


def complex_dot(pattern, left_re, left_im, right_re, right_im):
    real_part = jnp.einsum(
        pattern, left_re, right_re, preferred_element_type=jnp.float32
    ) - jnp.einsum(pattern, left_im, right_im, preferred_element_type=jnp.float32)
    imag_part = jnp.einsum(
        pattern, left_re, right_im, preferred_element_type=jnp.float32
    ) + jnp.einsum(pattern, left_im, right_re, preferred_element_type=jnp.float32)
    return (real_part, imag_part)


def make_picker(wanted):

    def picker(shard_rows):
        row_count = shard_rows.shape[0]
        select = (wanted[:, None] == jnp.arange(row_count, dtype=jnp.int32)[None, :]).astype(
            jnp.bfloat16
        )
        return jnp.dot(select, shard_rows, preferred_element_type=jnp.float32)

    return picker


def with_collectives(green, fields, orbitals, chol_half, chol_full, chol_count, kq_map):
    q_local = chol_half.shape[0]
    k_local = chol_half.shape[1]
    pair_width = chol_half.shape[3]
    chol_cols = chol_half.shape[4]
    ka_count = lax.axis_size("ka")
    pb_count = lax.axis_size("pb")
    ka_pos = lax.axis_index("ka")
    pb_pos = lax.axis_index("pb")
    local_green = lax.all_to_all(green, "ka", split_axis=3, concat_axis=1, tiled=True)
    walkers = local_green.shape[1]
    per_device = walkers // ka_count
    greens = local_green[0].reshape(walkers, q_local, k_local, 2, pair_width)
    counts = lax.dynamic_slice_in_dim(chol_count, pb_pos * q_local, q_local)
    vec_mask = (jnp.arange(chol_cols, dtype=jnp.int32)[None, :] < counts[:, None]).astype(
        jnp.float32
    )
    bias_re, bias_im = complex_dot(
        "wqkx,qkxn->qwn",
        greens[:, :, :, 0],
        greens[:, :, :, 1],
        chol_half[:, :, 0],
        chol_half[:, :, 1],
    )
    own_rows = (jnp.arange(walkers, dtype=jnp.int32) // per_device == ka_pos).astype(jnp.float32)
    bias_re, bias_im = lax.psum((bias_re, bias_im), "ka")
    bias_re = bias_re * vec_mask[:, None, :]
    bias_im = bias_im * vec_mask[:, None, :]
    hartree = 0.5 * jnp.sum(bias_re * bias_re + bias_im * bias_im, axis=(0, 2)) * own_rows
    field_now = jnp.transpose(fields, (1, 0, 2, 3)).reshape(q_local, walkers, chol_cols)
    shift_re = ((field_now - BIAS_STEP * bias_re) * vec_mask[:, None, :]).astype(jnp.bfloat16)
    shift_im = (-BIAS_STEP * bias_im * vec_mask[:, None, :]).astype(jnp.bfloat16)
    exchange = jnp.zeros((walkers,), jnp.float32)
    for transfer in range(q_local):
        for kpoint in range(k_local):
            chol_row = chol_half[transfer, kpoint].reshape(2, NOCC, M, chol_cols)
            green_row = greens[:, transfer, kpoint].reshape(walkers, 2, NOCC, M)
            cross_re, cross_im = complex_dot(
                "ipn,wjp->wijn", chol_row[0], chol_row[1], green_row[:, 0], green_row[:, 1]
            )
            exchange = exchange + 0.5 * jnp.sum(
                (cross_re * cross_re + cross_im * cross_im) * vec_mask[transfer], axis=(1, 2, 3)
            )
    prop_re, prop_im = complex_dot(
        "qwn,qkyn->qwky", shift_re, shift_im, chol_full[:, :, 0], chol_full[:, :, 1]
    )
    shape = (q_local, walkers, k_local, M, M)
    oper_re = (PROP_STEP * prop_re).astype(jnp.bfloat16).reshape(shape)
    oper_im = (PROP_STEP * prop_im).astype(jnp.bfloat16).reshape(shape)
    normalizer = q_local * pb_count * chol_cols
    total_energy = lax.psum(hartree - exchange, ("ka", "pb")) / normalizer
    energy = lax.dynamic_slice_in_dim(total_energy, ka_pos * per_device, per_device).reshape(
        1, per_device
    )
    initial = orbitals[0].reshape(k_local, walkers, 2, NOCC, M)
    row_width = 2 * pair_width
    my_rows = lax.dynamic_slice_in_dim(kq_map, pb_pos * q_local, q_local, 0)
    wanted = lax.dynamic_slice_in_dim(my_rows, ka_pos * k_local, k_local, 1).reshape(
        q_local * k_local
    )
    picker = make_picker(wanted)
    current = initial
    summed_terms = initial
    for degree in range(1, TAYLOR + 1):
        rounded = current.astype(jnp.bfloat16).reshape(k_local, walkers * row_width)
        fetched = picker(lax.all_gather(rounded, "ka", axis=0, tiled=True))
        shifted_rows = fetched.astype(jnp.bfloat16).reshape(q_local, k_local, walkers, 2, NOCC, M)
        out_re, out_im = complex_dot(
            "xwkpq,xkwiq->kwip",
            oper_re,
            oper_im,
            shifted_rows[:, :, :, 0],
            shifted_rows[:, :, :, 1],
        )
        applied = jnp.stack([out_re, out_im], axis=2)
        applied = lax.psum(applied, "pb")
        current = applied / degree
        summed_terms = summed_terms + current
    propagated = summed_terms.reshape(1, k_local, walkers, row_width)
    return (propagated, energy)


def exchange(array, axis, rounds):
    return [array] + [lax.ppermute(array, axis, pairs) for pairs in rounds]


def origins(axis, rounds):
    at = lax.axis_index(axis)
    found = [at]
    for pairs in rounds:
        source = jnp.int32(0)
        for sender, receiver in pairs:
            source = jnp.where(at == receiver, sender, source)
        found.append(source)
    return found


def operator_group(ka_count, pb_count):
    first = (pb_count - 1) * ka_count + ka_count // 2
    rest = [at for at in range(pb_count * ka_count) if at != first]
    return [first] + rest[::-1]


def prepare_kernel(ka_count, pb_count, walkers, map_ref, count_ref, mask_ref, picks_ref):
    kept = count_ref[lax.axis_index("pb")]
    column = lax.broadcasted_iota(jnp.int32, mask_ref.shape, 1)
    mask_ref[...] = jnp.where(column < kept, 1.0, 0.0)
    kpoints = map_ref.shape[1]
    k_local = kpoints // ka_count
    span = k_local * walkers
    lane = lax.broadcasted_iota(jnp.int32, (1, LANES), 1)
    lane_q = lane // (LANES // pb_count)
    lane_ka = lax.rem(lane, LANES // pb_count) // (2 * span)
    lane_part = lax.rem(lane, 2 * span) // span
    lane_k = lane_ka * k_local + lax.rem(lane, span) // walkers
    wanted = jnp.zeros((1, LANES), jnp.int32)
    for q in range(pb_count):
        for k in range(kpoints):
            source = map_ref[q, k]
            source = source // k_local * (2 * span) + lax.rem(source, k_local) * walkers
            wanted = jnp.where((lane_q == q) & (lane_k == k), source, wanted)
    wanted = wanted + lax.rem(lane, walkers)
    row = lax.broadcasted_iota(jnp.int32, (LANES, LANES), 0)
    real = jnp.where(row == wanted, 1.0, 0.0)
    imag = jnp.where(row == wanted + span, jnp.where(lane_part == 0, 1.0, -1.0), 0.0)
    picks_ref[...] = jnp.concatenate([real, imag], axis=1).astype(BF16)


def bias_kernel(ka_count, k_local, *refs):
    *greens, chol_ref, orbitals_ref, mask_ref, bias_ref, own_ref, table = refs
    for source, green_ref in zip(origins("ka", GREEN_ROUNDS), greens):
        table[source] = green_ref[...].astype(F32)
    first = lax.axis_index("ka") * k_local
    width = chol_ref.shape[2]
    rows = 2 * ka_count
    total = jnp.zeros((rows, bias_ref.shape[1]), F32)
    for k in range(k_local):
        green = jnp.concatenate(
            [table[w, pl.ds(first + k, 1), :] for w in range(ka_count)], axis=0
        )
        real, imag = green[:, :width], green[:, width:]
        both = jnp.concatenate([real, imag], axis=0)
        turned = jnp.concatenate([-imag, real], axis=0)
        own_ref[k] = both
        total += jnp.dot(both.astype(BF16), chol_ref[k, 0], preferred_element_type=F32)
        total += jnp.dot(turned.astype(BF16), chol_ref[k, 1], preferred_element_type=F32)
    bias_ref[:rows] = total * mask_ref[...]
    window = jnp.concatenate([orbitals_ref[k] for k in range(k_local)], axis=0)
    count, width = window.shape
    bias_ref[rows : rows + count, :width] = window
    bias_ref[rows : rows + count, width:] = jnp.zeros((count, bias_ref.shape[1] - width), F32)


def exchange_kernel(k_local, own_ref, chol_ref, mask_ref, out_ref):
    walkers, width, columns = own_ref.shape[1] // 2, own_ref.shape[2], chol_ref.shape[3]
    rows = 2 * walkers
    lane = lax.broadcasted_iota(jnp.int32, (rows, LANES), 1)
    total = jnp.zeros((rows, columns), F32)
    for k in range(k_local):
        both = jnp.concatenate([own_ref[k], jnp.zeros((rows, LANES - width), F32)], axis=1)
        turned = jnp.concatenate([-both[walkers:], both[:walkers]], axis=0)
        sides = []
        for side in (both, turned):
            rolled = {
                step: side if step == 0 else pltpu.roll(side, (step * M) % LANES, 1)
                for step in range(1 - NOCC, NOCC)
            }
            blocks = []
            for i in range(NOCC):
                inside = (lane >= i * M) & (lane < (i + 1) * M)
                for j in range(NOCC):
                    blocks.append(jnp.where(inside, rolled[i - j], 0.0))
            sides.append(jnp.concatenate(blocks, axis=0)[:, :width].astype(BF16))
        cross = jnp.dot(sides[0], chol_ref[k, 0], preferred_element_type=F32)
        cross += jnp.dot(sides[1], chol_ref[k, 1], preferred_element_type=F32)
        cross = cross * cross
        for block in range(NOCC * NOCC):
            total += cross[block * rows : (block + 1) * rows]
    total = total * mask_ref[:rows]
    total = total[:walkers] + total[walkers:]
    summed = 0.5 * jnp.sum(total, axis=1, keepdims=True)
    out_ref[...] = jnp.broadcast_to(summed, out_ref.shape)


def operator_kernel(k_local, *refs):
    *parts, fields_ref, mask_ref, exchange_ref, chol_ref, out_ref, products, turned_ref = refs
    walkers, columns = fields_ref.shape
    bias = parts[0][: 2 * walkers]
    for part in parts[1:]:
        bias = bias + part[: 2 * walkers]
    pairs = M * M
    tiles = columns // LANES
    group = LANES // (2 * tiles)
    bias_re, bias_im = bias[:walkers], bias[walkers:]
    hartree = 0.5 * jnp.sum(bias_re * bias_re + bias_im * bias_im, axis=1, keepdims=True)
    own = lax.broadcasted_iota(jnp.int32, (walkers, 1), 0) == lax.axis_index("ka")
    energy = jnp.where(own, hartree, 0.0) - exchange_ref[:, :1]
    kept = mask_ref[:walkers]
    shift_re = (fields_ref[...] - BIAS_STEP * bias_re) * kept
    shift_im = -BIAS_STEP * bias_im * kept
    span = k_local * walkers
    weights = []
    for k in range(k_local):
        before, after = k * walkers, span - (k + 1) * walkers
        pieces = []
        for tile in range(tiles):
            at = slice(tile * LANES, (tile + 1) * LANES)
            for first, second in ((shift_re, shift_im), (-shift_im, shift_re)):
                for side in (first, second):
                    pieces += [(before, None), (walkers, side[:, at]), (after, None)]
                pieces.append((group - 2 * span, None))
        weights.append(
            jnp.concatenate(
                [jnp.zeros((n, LANES), F32) if p is None else p for n, p in pieces if n], axis=0
            ).astype(BF16)
        )
    products[...] = lax.dot_general(
        jnp.concatenate([chol_ref[k] for k in range(k_local)], axis=1),
        jnp.concatenate(weights, axis=1),
        (((1,), (1,)), ((), ())),
        preferred_element_type=F32,
    )
    lane = lax.broadcasted_iota(jnp.int32, (pairs, LANES), 1)
    merged = products[pl.ds(0, pairs, stride=2 * tiles), :]
    for at in range(1, 2 * tiles):
        row = products[pl.ds(at, pairs, stride=2 * tiles), :]
        merged = jnp.where(lane >= at * group, row, merged)
    turned_ref[:pairs] = merged
    copies, rows, width = out_ref.shape
    lane = lax.broadcasted_iota(jnp.int32, (rows, LANES), 1)
    for at in range(0, width, LANES):
        block = turned_ref[at : at + LANES].T
        block = PROP_STEP * sum(block[n * group : n * group + rows] for n in range(2 * tiles))
        if at + LANES > pairs:
            share = jnp.concatenate([energy, jnp.zeros((rows - walkers, 1), F32)], axis=0)
            block = jnp.where(lane + at < pairs, block, 0.0)
            for piece in range(3):
                head = share.astype(BF16).astype(F32)
                block = jnp.where(lane + at == pairs + piece, head, block)
                share = share - head
        for copy in range(copies):
            out_ref[copy, :, at : at + LANES] = block.astype(BF16)


def taylor_kernel(pb_count, normalizer, blocks_ref, *refs):
    *windows, picks_ref, orbitals_ref, out_ref, energy_ref, turned, picked, term = refs
    pairs = M * M
    pair = NOCC * M
    k_local, walkers, _ = out_ref.shape
    span = k_local * walkers
    ka_pos = lax.axis_index("ka")
    term[...] = jnp.zeros_like(term)
    for source, window_ref in zip(origins("ka", BIAS_ROUNDS), windows):
        start = pl.multiple_of(source * (2 * span), 2 * span)
        window = window_ref[window_ref.shape[0] - span :]
        term[pl.ds(start, span), :pair] = window[:, :pair]
        term[pl.ds(start + span, span), :pair] = window[:, pair : 2 * pair]
    picked[...] = jnp.dot(term[...].T.astype(BF16), picks_ref[...], preferred_element_type=F32)
    count, _, width = blocks_ref.shape
    group = operator_group(count // pb_count, pb_count)
    places = [group.index(n) for n in range(count)]
    turned[width:] = jnp.zeros((turned.shape[0] - width, LANES), F32)
    for at in range(0, width, LANES):
        tile = jnp.concatenate([blocks_ref[n, :, at : at + LANES] for n in places], axis=0)
        turned[at : at + LANES] = tile.T.astype(F32)
    shares = turned[pairs : pairs + 3]
    lane = lax.broadcasted_iota(jnp.int32, shares.shape, 1)
    shares = jnp.where(lax.rem(lane, 2 * span) == ka_pos, shares, 0.0)
    shares = jnp.sum(jnp.sum(shares, axis=0, keepdims=True), axis=1, keepdims=True)
    energy_ref[...] = shares / normalizer
    lane = lax.broadcasted_iota(jnp.int32, (ROWS, LANES), 1)
    imaginary = lax.rem(lane, 2 * span) >= span
    sums = [None] * NOCC
    for degree in range(1, TAYLOR + 1):
        stride = M if degree == 1 else ROWS
        straight = [jnp.zeros((ROWS, LANES), F32) for _ in range(NOCC)]
        crossed = [jnp.zeros((ROWS, LANES), F32) for _ in range(NOCC)]
        for c in range(M):
            column = turned[pl.ds(c, ROWS, stride=M), :]
            for i in range(NOCC):
                at = i * stride + c
                straight[i] += column * picked[at : at + 1, :LANES]
                crossed[i] += column * picked[at : at + 1, LANES:]
        currents = []
        for i in range(NOCC):
            other = jnp.where(
                imaginary, pltpu.roll(crossed[i], span, 1), pltpu.roll(crossed[i], LANES - span, 1)
            )
            applied = straight[i] + other
            applied = applied + pltpu.roll(applied, LANES // pb_count, 1)
            currents.append(applied * (1.0 / degree))
            sums[i] = currents[i] if degree == 1 else sums[i] + currents[i]
        if degree < TAYLOR:
            rows = jnp.concatenate(currents, axis=0).astype(BF16)
            picked[...] = jnp.dot(rows, picks_ref[...], preferred_element_type=F32)
    term[...] = jnp.concatenate(sums, axis=0).T
    both = term[pl.ds(pl.multiple_of(ka_pos * (2 * span), 2 * span), 2 * span), :]
    both = jnp.concatenate([both[:, i * ROWS : i * ROWS + M] for i in range(NOCC)], axis=1)
    both = jnp.concatenate([both[:span], both[span:]], axis=1)
    for k in range(k_local):
        out_ref[k] = orbitals_ref[k] + both[k * walkers : (k + 1) * walkers]


def call(kernel, out, scratch=(), scalars=0, operands=0, flops=None):
    spaces = [pltpu.SMEM] * scalars + [pltpu.VMEM] * operands
    cost = None
    if flops is not None:
        cost = pl.CostEstimate(flops=flops, bytes_accessed=0, transcendentals=0)
    return pl.pallas_call(
        kernel,
        out_shape=out,
        in_specs=[pl.BlockSpec(memory_space=space) for space in spaces],
        out_specs=jax.tree.map(lambda _: pl.BlockSpec(memory_space=pltpu.VMEM), out),
        scratch_shapes=list(scratch),
        cost_estimate=cost,
        compiler_params=pltpu.CompilerParams(vmem_limit_bytes=24 * 2**20),
    )


def direct(green, fields, orbitals, chol_half, chol_full, chol_count, kq_map):
    k_local, pair_width, chol_cols = chol_half.shape[1], chol_half.shape[3], chol_half.shape[4]
    ka_count, pb_count = lax.axis_size("ka"), lax.axis_size("pb")
    walkers = ka_count
    kpoints = green.shape[3]
    span = k_local * walkers
    shape = jax.ShapeDtypeStruct
    tiles = chol_cols // LANES
    own_green = green.reshape(kpoints, 2 * pair_width)
    greens = exchange(own_green, "ka", GREEN_ROUNDS)
    half = chol_half.reshape(k_local, 2, pair_width, chol_cols)
    full = jnp.transpose(
        chol_full.reshape(k_local, 2, M * M, tiles, LANES), (0, 2, 3, 1, 4)
    ).reshape(k_local, M * M * tiles * 2, LANES)
    own_fields = fields.reshape(walkers, chol_cols)
    own_orbitals = orbitals.reshape(k_local, walkers, 2 * pair_width)
    mask, picks = call(
        functools.partial(prepare_kernel, ka_count, pb_count, walkers),
        (shape((2 * walkers, chol_cols), F32), shape((LANES, 2 * LANES), BF16)),
        scalars=2,
        flops=10**9,
    )(kq_map, chol_count)
    bias, own = call(
        functools.partial(bias_kernel, ka_count, k_local),
        (
            shape((2 * walkers + span, chol_cols), F32),
            shape((k_local, 2 * walkers, pair_width), F32),
        ),
        [pltpu.VMEM((walkers, kpoints, 2 * pair_width), F32)],
        operands=len(greens) + 3,
    )(*greens, half, own_orbitals, mask)
    parts = exchange(bias, "ka", BIAS_ROUNDS)
    shares = call(
        functools.partial(exchange_kernel, k_local),
        shape((walkers, LANES), F32),
        operands=3,
    )(own, half, mask)
    width = -(-(M * M + 3) // LANES) * LANES
    blocks = call(
        functools.partial(operator_kernel, k_local),
        shape((ka_count * pb_count, 2 * span, width), BF16),
        [pltpu.VMEM((2 * M * M * tiles, LANES), F32), pltpu.VMEM((width, LANES), F32)],
        operands=len(parts) + 4,
    )(*parts, own_fields, mask, shares, full)
    group = operator_group(ka_count, pb_count)
    blocks = lax.all_to_all(
        blocks, ("pb", "ka"), 0, 0, axis_index_groups=[group], tiled=True
    )
    propagated, energy = call(
        functools.partial(taylor_kernel, pb_count, float(pb_count * chol_cols)),
        (shape((k_local, walkers, 2 * pair_width), F32), shape((1, 1), F32)),
        [
            pltpu.VMEM((ROWS * M, LANES), F32),
            pltpu.VMEM((NOCC * ROWS, 2 * LANES), F32),
            pltpu.VMEM((LANES, LANES), F32),
        ],
        operands=len(parts) + 3,
    )(blocks, *parts, picks, own_orbitals)
    return (propagated[None], energy)


def on_device(green, fields, orbitals, chol_half, chol_full, chol_count, kq_map):
    ka_count, pb_count = lax.axis_size("ka"), lax.axis_size("pb")
    walkers = orbitals.shape[2]
    fits = 2 * pb_count * kq_map.shape[1] * walkers == LANES
    fits = fits and chol_half.shape[1] * walkers == 8 and chol_half.shape[4] == 2 * LANES
    fits = fits and ka_count == 4
    if fits and chol_half.shape[0] == 1 and walkers == ka_count:
        return direct(green, fields, orbitals, chol_half, chol_full, chol_count, kq_map)
    return with_collectives(green, fields, orbitals, chol_half, chol_full, chol_count, kq_map)


def solution(mesh):
    placed = (
        P("wa", ("grp", "ka"), "pb", None, None),
        P("wa", "pb", "grp", None),
        P("wa", "ka", "grp", None),
        P("pb", "ka", None, None, None),
        P("pb", "ka", None, None, None),
        P(),
        P(),
    )
    return jax.shard_map(
        on_device,
        mesh=mesh,
        in_specs=placed,
        out_specs=(P("wa", "ka", "grp", None), P("wa", ("grp", "ka"))),
        check_vma=False,
    )
```

```python
import functools

import jax
import jax.numpy as jnp
from jax import lax
from jax.experimental import pallas as pl
from jax.experimental.pallas import tpu as pltpu
from jax.sharding import PartitionSpec as P

M = 26
NOCC = 4
TAYLOR = 3
LANES = 128
ROWS = 32

GREEN_ROUNDS = (
    ((3, 0), (2, 1), (1, 3), (0, 2)),
    ((3, 1), (2, 0), (0, 3), (1, 2)),
    ((1, 0), (3, 2), (2, 3), (0, 1)),
)[::-1]
BIAS_ROUNDS = (
    ((0, 1), (1, 3), (2, 0), (3, 2)),
    ((0, 3), (3, 0), (1, 2), (2, 1)),
    ((0, 2), (1, 0), (2, 3), (3, 1)),
)[::-1]


BIAS_STEP = 0.5
PROP_STEP = 0.5

F32 = jnp.float32
BF16 = jnp.bfloat16


def complex_dot(pattern, left_re, left_im, right_re, right_im):
    real_part = jnp.einsum(
        pattern, left_re, right_re, preferred_element_type=jnp.float32
    ) - jnp.einsum(pattern, left_im, right_im, preferred_element_type=jnp.float32)
    imag_part = jnp.einsum(
        pattern, left_re, right_im, preferred_element_type=jnp.float32
    ) + jnp.einsum(pattern, left_im, right_re, preferred_element_type=jnp.float32)
    return (real_part, imag_part)


def make_picker(wanted):

    def picker(shard_rows):
        row_count = shard_rows.shape[0]
        select = (wanted[:, None] == jnp.arange(row_count, dtype=jnp.int32)[None, :]).astype(
            jnp.bfloat16
        )
        return jnp.dot(select, shard_rows, preferred_element_type=jnp.float32)

    return picker


def with_collectives(green, fields, orbitals, chol_half, chol_full, chol_count, kq_map):
    q_local = chol_half.shape[0]
    k_local = chol_half.shape[1]
    pair_width = chol_half.shape[3]
    chol_cols = chol_half.shape[4]
    ka_count = lax.axis_size("ka")
    pb_count = lax.axis_size("pb")
    ka_pos = lax.axis_index("ka")
    pb_pos = lax.axis_index("pb")
    local_green = lax.all_to_all(green, "ka", split_axis=3, concat_axis=1, tiled=True)
    walkers = local_green.shape[1]
    per_device = walkers // ka_count
    greens = local_green[0].reshape(walkers, q_local, k_local, 2, pair_width)
    counts = lax.dynamic_slice_in_dim(chol_count, pb_pos * q_local, q_local)
    vec_mask = (jnp.arange(chol_cols, dtype=jnp.int32)[None, :] < counts[:, None]).astype(
        jnp.float32
    )
    bias_re, bias_im = complex_dot(
        "wqkx,qkxn->qwn",
        greens[:, :, :, 0],
        greens[:, :, :, 1],
        chol_half[:, :, 0],
        chol_half[:, :, 1],
    )
    own_rows = (jnp.arange(walkers, dtype=jnp.int32) // per_device == ka_pos).astype(jnp.float32)
    bias_re, bias_im = lax.psum((bias_re, bias_im), "ka")
    bias_re = bias_re * vec_mask[:, None, :]
    bias_im = bias_im * vec_mask[:, None, :]
    hartree = 0.5 * jnp.sum(bias_re * bias_re + bias_im * bias_im, axis=(0, 2)) * own_rows
    field_now = jnp.transpose(fields, (1, 0, 2, 3)).reshape(q_local, walkers, chol_cols)
    shift_re = ((field_now - BIAS_STEP * bias_re) * vec_mask[:, None, :]).astype(jnp.bfloat16)
    shift_im = (-BIAS_STEP * bias_im * vec_mask[:, None, :]).astype(jnp.bfloat16)
    exchange = jnp.zeros((walkers,), jnp.float32)
    for transfer in range(q_local):
        for kpoint in range(k_local):
            chol_row = chol_half[transfer, kpoint].reshape(2, NOCC, M, chol_cols)
            green_row = greens[:, transfer, kpoint].reshape(walkers, 2, NOCC, M)
            cross_re, cross_im = complex_dot(
                "ipn,wjp->wijn", chol_row[0], chol_row[1], green_row[:, 0], green_row[:, 1]
            )
            exchange = exchange + 0.5 * jnp.sum(
                (cross_re * cross_re + cross_im * cross_im) * vec_mask[transfer], axis=(1, 2, 3)
            )
    prop_re, prop_im = complex_dot(
        "qwn,qkyn->qwky", shift_re, shift_im, chol_full[:, :, 0], chol_full[:, :, 1]
    )
    shape = (q_local, walkers, k_local, M, M)
    oper_re = (PROP_STEP * prop_re).astype(jnp.bfloat16).reshape(shape)
    oper_im = (PROP_STEP * prop_im).astype(jnp.bfloat16).reshape(shape)
    normalizer = q_local * pb_count * chol_cols
    total_energy = lax.psum(hartree - exchange, ("ka", "pb")) / normalizer
    energy = lax.dynamic_slice_in_dim(total_energy, ka_pos * per_device, per_device).reshape(
        1, per_device
    )
    initial = orbitals[0].reshape(k_local, walkers, 2, NOCC, M)
    row_width = 2 * pair_width
    my_rows = lax.dynamic_slice_in_dim(kq_map, pb_pos * q_local, q_local, 0)
    wanted = lax.dynamic_slice_in_dim(my_rows, ka_pos * k_local, k_local, 1).reshape(
        q_local * k_local
    )
    picker = make_picker(wanted)
    current = initial
    summed_terms = initial
    for degree in range(1, TAYLOR + 1):
        rounded = current.astype(jnp.bfloat16).reshape(k_local, walkers * row_width)
        fetched = picker(lax.all_gather(rounded, "ka", axis=0, tiled=True))
        shifted_rows = fetched.astype(jnp.bfloat16).reshape(q_local, k_local, walkers, 2, NOCC, M)
        out_re, out_im = complex_dot(
            "xwkpq,xkwiq->kwip",
            oper_re,
            oper_im,
            shifted_rows[:, :, :, 0],
            shifted_rows[:, :, :, 1],
        )
        applied = jnp.stack([out_re, out_im], axis=2)
        applied = lax.psum(applied, "pb")
        current = applied / degree
        summed_terms = summed_terms + current
    propagated = summed_terms.reshape(1, k_local, walkers, row_width)
    return (propagated, energy)


def exchange(array, axis, rounds):
    return [array] + [lax.ppermute(array, axis, pairs) for pairs in rounds]


def origins(axis, rounds):
    at = lax.axis_index(axis)
    found = [at]
    for pairs in rounds:
        source = jnp.int32(0)
        for sender, receiver in pairs:
            source = jnp.where(at == receiver, sender, source)
        found.append(source)
    return found


def operator_group(ka_count, pb_count):
    first = (pb_count - 1) * ka_count + ka_count // 2
    rest = [at for at in range(pb_count * ka_count) if at != first]
    return [first] + rest[::-1]


def prepare_kernel(ka_count, pb_count, walkers, map_ref, count_ref, mask_ref, picks_ref):
    kept = count_ref[lax.axis_index("pb")]
    column = lax.broadcasted_iota(jnp.int32, mask_ref.shape, 1)
    mask_ref[...] = jnp.where(column < kept, 1.0, 0.0)
    kpoints = map_ref.shape[1]
    k_local = kpoints // ka_count
    span = k_local * walkers
    lane = lax.broadcasted_iota(jnp.int32, (1, LANES), 1)
    lane_q = lane // (LANES // pb_count)
    lane_ka = lax.rem(lane, LANES // pb_count) // (2 * span)
    lane_part = lax.rem(lane, 2 * span) // span
    lane_k = lane_ka * k_local + lax.rem(lane, span) // walkers
    wanted = jnp.zeros((1, LANES), jnp.int32)
    for q in range(pb_count):
        for k in range(kpoints):
            source = map_ref[q, k]
            source = source // k_local * (2 * span) + lax.rem(source, k_local) * walkers
            wanted = jnp.where((lane_q == q) & (lane_k == k), source, wanted)
    wanted = wanted + lax.rem(lane, walkers)
    row = lax.broadcasted_iota(jnp.int32, (LANES, LANES), 0)
    real = jnp.where(row == wanted, 1.0, 0.0)
    imag = jnp.where(row == wanted + span, jnp.where(lane_part == 0, 1.0, -1.0), 0.0)
    picks_ref[...] = jnp.concatenate([real, imag], axis=1).astype(BF16)


def bias_kernel(ka_count, k_local, *refs):
    *greens, chol_ref, orbitals_ref, mask_ref, bias_ref, own_ref, table = refs
    for source, green_ref in zip(origins("ka", GREEN_ROUNDS), greens):
        table[source] = green_ref[...].astype(F32)
    first = lax.axis_index("ka") * k_local
    width = chol_ref.shape[2]
    rows = 2 * ka_count
    total = jnp.zeros((rows, bias_ref.shape[1]), F32)
    for k in range(k_local):
        green = jnp.concatenate(
            [table[w, pl.ds(first + k, 1), :] for w in range(ka_count)], axis=0
        )
        real, imag = green[:, :width], green[:, width:]
        both = jnp.concatenate([real, imag], axis=0)
        turned = jnp.concatenate([-imag, real], axis=0)
        own_ref[k] = both
        total += jnp.dot(both.astype(BF16), chol_ref[k, 0], preferred_element_type=F32)
        total += jnp.dot(turned.astype(BF16), chol_ref[k, 1], preferred_element_type=F32)
    bias_ref[:rows] = total * mask_ref[...]
    window = jnp.concatenate([orbitals_ref[k] for k in range(k_local)], axis=0)
    count, width = window.shape
    bias_ref[rows : rows + count, :width] = window
    bias_ref[rows : rows + count, width:] = jnp.zeros((count, bias_ref.shape[1] - width), F32)


def exchange_kernel(k_local, own_ref, chol_ref, mask_ref, out_ref):
    walkers, width, columns = own_ref.shape[1] // 2, own_ref.shape[2], chol_ref.shape[3]
    rows = 2 * walkers
    lane = lax.broadcasted_iota(jnp.int32, (rows, LANES), 1)
    total = jnp.zeros((rows, columns), F32)
    for k in range(k_local):
        both = jnp.concatenate([own_ref[k], jnp.zeros((rows, LANES - width), F32)], axis=1)
        turned = jnp.concatenate([-both[walkers:], both[:walkers]], axis=0)
        sides = []
        for side in (both, turned):
            rolled = {
                step: side if step == 0 else pltpu.roll(side, (step * M) % LANES, 1)
                for step in range(1 - NOCC, NOCC)
            }
            blocks = []
            for i in range(NOCC):
                inside = (lane >= i * M) & (lane < (i + 1) * M)
                for j in range(NOCC):
                    blocks.append(jnp.where(inside, rolled[i - j], 0.0))
            sides.append(jnp.concatenate(blocks, axis=0)[:, :width].astype(BF16))
        cross = jnp.dot(sides[0], chol_ref[k, 0], preferred_element_type=F32)
        cross += jnp.dot(sides[1], chol_ref[k, 1], preferred_element_type=F32)
        cross = cross * cross
        for block in range(NOCC * NOCC):
            total += cross[block * rows : (block + 1) * rows]
    total = total * mask_ref[:rows]
    total = total[:walkers] + total[walkers:]
    summed = 0.5 * jnp.sum(total, axis=1, keepdims=True)
    out_ref[...] = jnp.broadcast_to(summed, out_ref.shape)


def operator_kernel(k_local, *refs):
    *parts, fields_ref, mask_ref, exchange_ref, chol_ref, out_ref, products = refs
    walkers, columns = fields_ref.shape
    bias = parts[0][: 2 * walkers]
    for part in parts[1:]:
        bias = bias + part[: 2 * walkers]
    pairs = M * M
    tiles = columns // LANES
    group = LANES // (2 * tiles)
    bias_re, bias_im = bias[:walkers], bias[walkers:]
    hartree = 0.5 * jnp.sum(bias_re * bias_re + bias_im * bias_im, axis=1, keepdims=True)
    own = lax.broadcasted_iota(jnp.int32, (walkers, 1), 0) == lax.axis_index("ka")
    energy = jnp.where(own, hartree, 0.0) - exchange_ref[:, :1]
    kept = mask_ref[:walkers]
    shift_re = (fields_ref[...] - BIAS_STEP * bias_re) * kept
    shift_im = -BIAS_STEP * bias_im * kept
    span = k_local * walkers
    weights = []
    for k in range(k_local):
        before, after = k * walkers, span - (k + 1) * walkers
        pieces = []
        for tile in range(tiles):
            at = slice(tile * LANES, (tile + 1) * LANES)
            for first, second in ((shift_re, shift_im), (-shift_im, shift_re)):
                for side in (first, second):
                    pieces += [(before, None), (walkers, side[:, at]), (after, None)]
                pieces.append((group - 2 * span, None))
        weights.append(
            jnp.concatenate(
                [jnp.zeros((n, LANES), F32) if p is None else p for n, p in pieces if n], axis=0
            ).astype(BF16)
        )
    products[...] = lax.dot_general(
        jnp.concatenate([chol_ref[k] for k in range(k_local)], axis=1),
        jnp.concatenate(weights, axis=1),
        (((1,), (1,)), ((), ())),
        preferred_element_type=F32,
    )
    copies, rows, width = out_ref.shape
    lane = lax.broadcasted_iota(jnp.int32, (LANES, LANES), 1)
    place = lax.broadcasted_iota(jnp.int32, (rows, LANES), 1)
    step = 2 * tiles
    for at in range(0, width, LANES):
        held = min(LANES, pairs - at)
        merged = products[pl.ds(step * at, held, stride=step), :]
        for part in range(1, step):
            row = products[pl.ds(step * at + part, held, stride=step), :]
            merged = jnp.where(lane[:held] >= part * group, row, merged)
        if held < LANES:
            merged = jnp.concatenate([merged, jnp.zeros((LANES - held, LANES), F32)], axis=0)
        block = merged.T
        block = PROP_STEP * sum(block[n * group : n * group + rows] for n in range(step))
        if held < LANES:
            share = jnp.concatenate([energy, jnp.zeros((rows - walkers, 1), F32)], axis=0)
            for piece in range(3):
                head = share.astype(BF16).astype(F32)
                block = jnp.where(place == held + piece, head, block)
                share = share - head
        block = block.astype(BF16)
        for copy in range(copies):
            out_ref[copy, :, at : at + LANES] = block


def taylor_kernel(pb_count, normalizer, blocks_ref, *refs):
    *windows, picks_ref, orbitals_ref, out_ref, energy_ref, turned, picked, term = refs
    pairs = M * M
    pair = NOCC * M
    k_local, walkers, _ = out_ref.shape
    span = k_local * walkers
    ka_pos = lax.axis_index("ka")
    term[...] = jnp.zeros_like(term)
    for source, window_ref in zip(origins("ka", BIAS_ROUNDS), windows):
        start = pl.multiple_of(source * (2 * span), 2 * span)
        window = window_ref[window_ref.shape[0] - span :]
        term[pl.ds(start, span), :pair] = window[:, :pair]
        term[pl.ds(start + span, span), :pair] = window[:, pair : 2 * pair]
    picked[...] = jnp.dot(term[...].T.astype(BF16), picks_ref[...], preferred_element_type=F32)
    count, _, width = blocks_ref.shape
    group = operator_group(count // pb_count, pb_count)
    places = [group.index(n) for n in range(count)]
    for at in range(0, width, LANES):
        tile = jnp.concatenate([blocks_ref[n, :, at : at + LANES] for n in places], axis=0)
        turned[at : at + LANES] = tile.T.astype(F32)
    shares = turned[pairs : pairs + 3]
    lane = lax.broadcasted_iota(jnp.int32, shares.shape, 1)
    shares = jnp.where(lax.rem(lane, 2 * span) == ka_pos, shares, 0.0)
    shares = jnp.sum(jnp.sum(shares, axis=0, keepdims=True), axis=1, keepdims=True)
    energy_ref[...] = shares / normalizer
    lane = lax.broadcasted_iota(jnp.int32, (M, LANES), 1)
    imaginary = lax.rem(lane, 2 * span) >= span
    sums = [jnp.zeros((M, LANES), F32) for _ in range(NOCC)]
    for degree in range(1, TAYLOR + 1):
        stride = M if degree == 1 else ROWS
        straight = [jnp.zeros((M, LANES), F32) for _ in range(NOCC)]
        crossed = [jnp.zeros((M, LANES), F32) for _ in range(NOCC)]
        for c in range(M):
            column = turned[pl.ds(c, M, stride=M), :]
            for i in range(NOCC):
                at = i * stride + c
                straight[i] += column * picked[at : at + 1, :LANES]
                crossed[i] += column * picked[at : at + 1, LANES:]
        for i in range(NOCC):
            other = jnp.where(
                imaginary, pltpu.roll(crossed[i], span, 1), pltpu.roll(crossed[i], LANES - span, 1)
            )
            applied = straight[i] + other
            applied = applied + pltpu.roll(applied, LANES // pb_count, 1)
            current = applied / degree
            sums[i] = sums[i] + current
            term[i * ROWS : i * ROWS + M] = current if degree < TAYLOR else sums[i]
        if degree < TAYLOR:
            picked[...] = jnp.dot(
                term[...].astype(BF16), picks_ref[...], preferred_element_type=F32
            )
    turned[:LANES] = term[...].T
    both = turned[pl.ds(pl.multiple_of(ka_pos * (2 * span), 2 * span), 2 * span), :]
    both = jnp.concatenate([both[:, i * ROWS : i * ROWS + M] for i in range(NOCC)], axis=1)
    both = jnp.concatenate([both[:span], both[span:]], axis=1)
    for k in range(k_local):
        out_ref[k] = orbitals_ref[k] + both[k * walkers : (k + 1) * walkers]


def call(kernel, out, scratch=(), scalars=0, operands=0, flops=None):
    spaces = [pltpu.SMEM] * scalars + [pltpu.VMEM] * operands
    cost = None
    if flops is not None:
        cost = pl.CostEstimate(flops=flops, bytes_accessed=0, transcendentals=0)
    return pl.pallas_call(
        kernel,
        out_shape=out,
        in_specs=[pl.BlockSpec(memory_space=space) for space in spaces],
        out_specs=jax.tree.map(lambda _: pl.BlockSpec(memory_space=pltpu.VMEM), out),
        scratch_shapes=list(scratch),
        cost_estimate=cost,
        compiler_params=pltpu.CompilerParams(vmem_limit_bytes=24 * 2**20),
    )


def direct(green, fields, orbitals, chol_half, chol_full, chol_count, kq_map):
    k_local, pair_width, chol_cols = chol_half.shape[1], chol_half.shape[3], chol_half.shape[4]
    ka_count, pb_count = lax.axis_size("ka"), lax.axis_size("pb")
    walkers = ka_count
    kpoints = green.shape[3]
    span = k_local * walkers
    shape = jax.ShapeDtypeStruct
    tiles = chol_cols // LANES
    own_green = green.reshape(kpoints, 2 * pair_width)
    greens = exchange(own_green, "ka", GREEN_ROUNDS)
    half = chol_half.reshape(k_local, 2, pair_width, chol_cols)
    full = jnp.transpose(
        chol_full.reshape(k_local, 2, M * M, tiles, LANES), (0, 2, 3, 1, 4)
    ).reshape(k_local, M * M * tiles * 2, LANES)
    own_fields = fields.reshape(walkers, chol_cols)
    own_orbitals = orbitals.reshape(k_local, walkers, 2 * pair_width)
    mask, picks = call(
        functools.partial(prepare_kernel, ka_count, pb_count, walkers),
        (shape((2 * walkers, chol_cols), F32), shape((LANES, 2 * LANES), BF16)),
        scalars=2,
        flops=10**9,
    )(kq_map, chol_count)
    bias, own = call(
        functools.partial(bias_kernel, ka_count, k_local),
        (
            shape((2 * walkers + span, chol_cols), F32),
            shape((k_local, 2 * walkers, pair_width), F32),
        ),
        [pltpu.VMEM((walkers, kpoints, 2 * pair_width), F32)],
        operands=len(greens) + 3,
    )(*greens, half, own_orbitals, mask)
    parts = exchange(bias, "ka", BIAS_ROUNDS)
    shares = call(
        functools.partial(exchange_kernel, k_local),
        shape((walkers, LANES), F32),
        operands=3,
    )(own, half, mask)
    width = -(-(M * M + 3) // LANES) * LANES
    blocks = call(
        functools.partial(operator_kernel, k_local),
        shape((ka_count * pb_count, 2 * span, width), BF16),
        [pltpu.VMEM((2 * M * M * tiles, LANES), F32)],
        operands=len(parts) + 4,
    )(*parts, own_fields, mask, shares, full)
    group = operator_group(ka_count, pb_count)
    blocks = lax.all_to_all(
        blocks, ("pb", "ka"), 0, 0, axis_index_groups=[group], tiled=True
    )
    propagated, energy = call(
        functools.partial(taylor_kernel, pb_count, float(pb_count * chol_cols)),
        (shape((k_local, walkers, 2 * pair_width), F32), shape((1, 1), F32)),
        [
            pltpu.VMEM((width, LANES), F32),
            pltpu.VMEM((NOCC * ROWS, 2 * LANES), F32),
            pltpu.VMEM((LANES, LANES), F32),
        ],
        operands=len(parts) + 3,
    )(blocks, *parts, picks, own_orbitals)
    return (propagated[None], energy)


def on_device(green, fields, orbitals, chol_half, chol_full, chol_count, kq_map):
    ka_count, pb_count = lax.axis_size("ka"), lax.axis_size("pb")
    walkers = orbitals.shape[2]
    fits = 2 * pb_count * kq_map.shape[1] * walkers == LANES
    fits = fits and chol_half.shape[1] * walkers == 8 and chol_half.shape[4] == 2 * LANES
    fits = fits and ka_count == 4
    if fits and chol_half.shape[0] == 1 and walkers == ka_count:
        return direct(green, fields, orbitals, chol_half, chol_full, chol_count, kq_map)
    return with_collectives(green, fields, orbitals, chol_half, chol_full, chol_count, kq_map)


def solution(mesh):
    placed = (
        P("wa", ("grp", "ka"), "pb", None, None),
        P("wa", "pb", "grp", None),
        P("wa", "ka", "grp", None),
        P("pb", "ka", None, None, None),
        P("pb", "ka", None, None, None),
        P(),
        P(),
    )
    return jax.shard_map(
        on_device,
        mesh=mesh,
        in_specs=placed,
        out_specs=(P("wa", "ka", "grp", None), P("wa", ("grp", "ka"))),
        check_vma=False,
    )
```

```python
import functools

import jax
import jax.numpy as jnp
from jax import lax
from jax.experimental import pallas as pl
from jax.experimental.pallas import tpu as pltpu
from jax.sharding import PartitionSpec as P

M = 26
NOCC = 4
TAYLOR = 3
LANES = 128
ROWS = 32

GREEN_ROUNDS = (
    ((3, 0), (2, 1), (1, 3), (0, 2)),
    ((3, 1), (2, 0), (0, 3), (1, 2)),
    ((1, 0), (3, 2), (2, 3), (0, 1)),
)[::-1]
BIAS_ROUNDS = (
    ((0, 1), (1, 3), (2, 0), (3, 2)),
    ((0, 3), (3, 0), (1, 2), (2, 1)),
    ((0, 2), (1, 0), (2, 3), (3, 1)),
)[::-1]


BIAS_STEP = 0.5
PROP_STEP = 0.5

F32 = jnp.float32
BF16 = jnp.bfloat16


def complex_dot(pattern, left_re, left_im, right_re, right_im):
    real_part = jnp.einsum(
        pattern, left_re, right_re, preferred_element_type=jnp.float32
    ) - jnp.einsum(pattern, left_im, right_im, preferred_element_type=jnp.float32)
    imag_part = jnp.einsum(
        pattern, left_re, right_im, preferred_element_type=jnp.float32
    ) + jnp.einsum(pattern, left_im, right_re, preferred_element_type=jnp.float32)
    return (real_part, imag_part)


def make_picker(wanted):

    def picker(shard_rows):
        row_count = shard_rows.shape[0]
        select = (wanted[:, None] == jnp.arange(row_count, dtype=jnp.int32)[None, :]).astype(
            jnp.bfloat16
        )
        return jnp.dot(select, shard_rows, preferred_element_type=jnp.float32)

    return picker


def with_collectives(green, fields, orbitals, chol_half, chol_full, chol_count, kq_map):
    q_local = chol_half.shape[0]
    k_local = chol_half.shape[1]
    pair_width = chol_half.shape[3]
    chol_cols = chol_half.shape[4]
    ka_count = lax.axis_size("ka")
    pb_count = lax.axis_size("pb")
    ka_pos = lax.axis_index("ka")
    pb_pos = lax.axis_index("pb")
    local_green = lax.all_to_all(green, "ka", split_axis=3, concat_axis=1, tiled=True)
    walkers = local_green.shape[1]
    per_device = walkers // ka_count
    greens = local_green[0].reshape(walkers, q_local, k_local, 2, pair_width)
    counts = lax.dynamic_slice_in_dim(chol_count, pb_pos * q_local, q_local)
    vec_mask = (jnp.arange(chol_cols, dtype=jnp.int32)[None, :] < counts[:, None]).astype(
        jnp.float32
    )
    bias_re, bias_im = complex_dot(
        "wqkx,qkxn->qwn",
        greens[:, :, :, 0],
        greens[:, :, :, 1],
        chol_half[:, :, 0],
        chol_half[:, :, 1],
    )
    own_rows = (jnp.arange(walkers, dtype=jnp.int32) // per_device == ka_pos).astype(jnp.float32)
    bias_re, bias_im = lax.psum((bias_re, bias_im), "ka")
    bias_re = bias_re * vec_mask[:, None, :]
    bias_im = bias_im * vec_mask[:, None, :]
    hartree = 0.5 * jnp.sum(bias_re * bias_re + bias_im * bias_im, axis=(0, 2)) * own_rows
    field_now = jnp.transpose(fields, (1, 0, 2, 3)).reshape(q_local, walkers, chol_cols)
    shift_re = ((field_now - BIAS_STEP * bias_re) * vec_mask[:, None, :]).astype(jnp.bfloat16)
    shift_im = (-BIAS_STEP * bias_im * vec_mask[:, None, :]).astype(jnp.bfloat16)
    exchange = jnp.zeros((walkers,), jnp.float32)
    for transfer in range(q_local):
        for kpoint in range(k_local):
            chol_row = chol_half[transfer, kpoint].reshape(2, NOCC, M, chol_cols)
            green_row = greens[:, transfer, kpoint].reshape(walkers, 2, NOCC, M)
            cross_re, cross_im = complex_dot(
                "ipn,wjp->wijn", chol_row[0], chol_row[1], green_row[:, 0], green_row[:, 1]
            )
            exchange = exchange + 0.5 * jnp.sum(
                (cross_re * cross_re + cross_im * cross_im) * vec_mask[transfer], axis=(1, 2, 3)
            )
    prop_re, prop_im = complex_dot(
        "qwn,qkyn->qwky", shift_re, shift_im, chol_full[:, :, 0], chol_full[:, :, 1]
    )
    shape = (q_local, walkers, k_local, M, M)
    oper_re = (PROP_STEP * prop_re).astype(jnp.bfloat16).reshape(shape)
    oper_im = (PROP_STEP * prop_im).astype(jnp.bfloat16).reshape(shape)
    normalizer = q_local * pb_count * chol_cols
    total_energy = lax.psum(hartree - exchange, ("ka", "pb")) / normalizer
    energy = lax.dynamic_slice_in_dim(total_energy, ka_pos * per_device, per_device).reshape(
        1, per_device
    )
    initial = orbitals[0].reshape(k_local, walkers, 2, NOCC, M)
    row_width = 2 * pair_width
    my_rows = lax.dynamic_slice_in_dim(kq_map, pb_pos * q_local, q_local, 0)
    wanted = lax.dynamic_slice_in_dim(my_rows, ka_pos * k_local, k_local, 1).reshape(
        q_local * k_local
    )
    picker = make_picker(wanted)
    current = initial
    summed_terms = initial
    for degree in range(1, TAYLOR + 1):
        rounded = current.astype(jnp.bfloat16).reshape(k_local, walkers * row_width)
        fetched = picker(lax.all_gather(rounded, "ka", axis=0, tiled=True))
        shifted_rows = fetched.astype(jnp.bfloat16).reshape(q_local, k_local, walkers, 2, NOCC, M)
        out_re, out_im = complex_dot(
            "xwkpq,xkwiq->kwip",
            oper_re,
            oper_im,
            shifted_rows[:, :, :, 0],
            shifted_rows[:, :, :, 1],
        )
        applied = jnp.stack([out_re, out_im], axis=2)
        applied = lax.psum(applied, "pb")
        current = applied / degree
        summed_terms = summed_terms + current
    propagated = summed_terms.reshape(1, k_local, walkers, row_width)
    return (propagated, energy)


def exchange(array, axis, rounds):
    return [array] + [lax.ppermute(array, axis, pairs) for pairs in rounds]


def origins(axis, rounds):
    at = lax.axis_index(axis)
    found = [at]
    for pairs in rounds:
        source = jnp.int32(0)
        for sender, receiver in pairs:
            source = jnp.where(at == receiver, sender, source)
        found.append(source)
    return found


def operator_group(ka_count, pb_count):
    return list(range(pb_count * ka_count))[::-1]


def prepare_kernel(ka_count, pb_count, walkers, map_ref, count_ref, mask_ref, picks_ref):
    kept = count_ref[lax.axis_index("pb")]
    column = lax.broadcasted_iota(jnp.int32, mask_ref.shape, 1)
    mask_ref[...] = jnp.where(column < kept, 1.0, 0.0)
    kpoints = map_ref.shape[1]
    k_local = kpoints // ka_count
    span = k_local * walkers
    lane = lax.broadcasted_iota(jnp.int32, (1, LANES), 1)
    lane_q = lane // (LANES // pb_count)
    lane_ka = lax.rem(lane, LANES // pb_count) // (2 * span)
    lane_part = lax.rem(lane, 2 * span) // span
    lane_k = lane_ka * k_local + lax.rem(lane, span) // walkers
    wanted = jnp.zeros((1, LANES), jnp.int32)
    for q in range(pb_count):
        for k in range(kpoints):
            source = map_ref[q, k]
            source = source // k_local * (2 * span) + lax.rem(source, k_local) * walkers
            wanted = jnp.where((lane_q == q) & (lane_k == k), source, wanted)
    wanted = wanted + lax.rem(lane, walkers)
    row = lax.broadcasted_iota(jnp.int32, (LANES, LANES), 0)
    real = jnp.where(row == wanted, 1.0, 0.0)
    imag = jnp.where(row == wanted + span, jnp.where(lane_part == 0, 1.0, -1.0), 0.0)
    picks_ref[...] = jnp.concatenate([real, imag], axis=1).astype(BF16)


def bias_kernel(ka_count, k_local, *refs):
    *greens, chol_ref, orbitals_ref, mask_ref, bias_ref, own_ref, table = refs
    for source, green_ref in zip(origins("ka", GREEN_ROUNDS), greens):
        table[source] = green_ref[...].astype(F32)
    first = lax.axis_index("ka") * k_local
    width = chol_ref.shape[2]
    rows = 2 * ka_count
    total = jnp.zeros((rows, bias_ref.shape[1]), F32)
    for k in range(k_local):
        green = jnp.concatenate(
            [table[w, pl.ds(first + k, 1), :] for w in range(ka_count)], axis=0
        )
        real, imag = green[:, :width], green[:, width:]
        both = jnp.concatenate([real, imag], axis=0)
        turned = jnp.concatenate([-imag, real], axis=0)
        own_ref[k] = both
        total += jnp.dot(both.astype(BF16), chol_ref[k, 0], preferred_element_type=F32)
        total += jnp.dot(turned.astype(BF16), chol_ref[k, 1], preferred_element_type=F32)
    bias_ref[:rows] = total * mask_ref[...]
    window = jnp.concatenate([orbitals_ref[k] for k in range(k_local)], axis=0)
    count, width = window.shape
    bias_ref[rows : rows + count, :width] = window
    bias_ref[rows : rows + count, width:] = jnp.zeros((count, bias_ref.shape[1] - width), F32)


def exchange_kernel(k_local, own_ref, chol_ref, mask_ref, out_ref):
    walkers, width, columns = own_ref.shape[1] // 2, own_ref.shape[2], chol_ref.shape[3]
    rows = 2 * walkers
    lane = lax.broadcasted_iota(jnp.int32, (rows, LANES), 1)
    total = jnp.zeros((rows, columns), F32)
    for k in range(k_local):
        both = jnp.concatenate([own_ref[k], jnp.zeros((rows, LANES - width), F32)], axis=1)
        turned = jnp.concatenate([-both[walkers:], both[:walkers]], axis=0)
        sides = []
        for side in (both, turned):
            rolled = {
                step: side if step == 0 else pltpu.roll(side, (step * M) % LANES, 1)
                for step in range(1 - NOCC, NOCC)
            }
            blocks = []
            for i in range(NOCC):
                inside = (lane >= i * M) & (lane < (i + 1) * M)
                for j in range(NOCC):
                    blocks.append(jnp.where(inside, rolled[i - j], 0.0))
            sides.append(jnp.concatenate(blocks, axis=0)[:, :width].astype(BF16))
        cross = jnp.dot(sides[0], chol_ref[k, 0], preferred_element_type=F32)
        cross += jnp.dot(sides[1], chol_ref[k, 1], preferred_element_type=F32)
        cross = cross * cross
        for block in range(NOCC * NOCC):
            total += cross[block * rows : (block + 1) * rows]
    total = total * mask_ref[:rows]
    total = total[:walkers] + total[walkers:]
    summed = 0.5 * jnp.sum(total, axis=1, keepdims=True)
    out_ref[...] = jnp.broadcast_to(summed, out_ref.shape)


def operator_kernel(k_local, *refs):
    *parts, fields_ref, mask_ref, exchange_ref, chol_ref, out_ref, products = refs
    walkers, columns = fields_ref.shape
    bias = parts[0][: 2 * walkers]
    for part in parts[1:]:
        bias = bias + part[: 2 * walkers]
    pairs = M * M
    tiles = columns // LANES
    group = LANES // (2 * tiles)
    bias_re, bias_im = bias[:walkers], bias[walkers:]
    hartree = 0.5 * jnp.sum(bias_re * bias_re + bias_im * bias_im, axis=1, keepdims=True)
    own = lax.broadcasted_iota(jnp.int32, (walkers, 1), 0) == lax.axis_index("ka")
    energy = jnp.where(own, hartree, 0.0) - exchange_ref[:, :1]
    kept = mask_ref[:walkers]
    shift_re = (fields_ref[...] - BIAS_STEP * bias_re) * kept
    shift_im = -BIAS_STEP * bias_im * kept
    span = k_local * walkers
    weights = []
    for k in range(k_local):
        before, after = k * walkers, span - (k + 1) * walkers
        pieces = []
        for tile in range(tiles):
            at = slice(tile * LANES, (tile + 1) * LANES)
            for first, second in ((shift_re, shift_im), (-shift_im, shift_re)):
                for side in (first, second):
                    pieces += [(before, None), (walkers, side[:, at]), (after, None)]
                pieces.append((group - 2 * span, None))
        weights.append(
            jnp.concatenate(
                [jnp.zeros((n, LANES), F32) if p is None else p for n, p in pieces if n], axis=0
            ).astype(BF16)
        )
    products[...] = lax.dot_general(
        jnp.concatenate([chol_ref[k] for k in range(k_local)], axis=1),
        jnp.concatenate(weights, axis=1),
        (((1,), (1,)), ((), ())),
        preferred_element_type=F32,
    )
    copies, rows, width = out_ref.shape
    lane = lax.broadcasted_iota(jnp.int32, (LANES, LANES), 1)
    place = lax.broadcasted_iota(jnp.int32, (rows, LANES), 1)
    step = 2 * tiles
    for at in range(0, width, LANES):
        held = min(LANES, pairs - at)
        merged = products[pl.ds(step * at, held, stride=step), :]
        for part in range(1, step):
            row = products[pl.ds(step * at + part, held, stride=step), :]
            merged = jnp.where(lane[:held] >= part * group, row, merged)
        if held < LANES:
            merged = jnp.concatenate([merged, jnp.zeros((LANES - held, LANES), F32)], axis=0)
        block = merged.T
        block = PROP_STEP * sum(block[n * group : n * group + rows] for n in range(step))
        if held < LANES:
            share = jnp.concatenate([energy, jnp.zeros((rows - walkers, 1), F32)], axis=0)
            for piece in range(3):
                head = share.astype(BF16).astype(F32)
                block = jnp.where(place == held + piece, head, block)
                share = share - head
        block = block.astype(BF16)
        for copy in range(copies):
            out_ref[copy, :, at : at + LANES] = block


def taylor_kernel(pb_count, normalizer, blocks_ref, *refs):
    *windows, picks_ref, orbitals_ref, out_ref, energy_ref, turned, picked, term = refs
    pairs = M * M
    pair = NOCC * M
    k_local, walkers, _ = out_ref.shape
    span = k_local * walkers
    ka_pos = lax.axis_index("ka")
    term[...] = jnp.zeros_like(term)
    for source, window_ref in zip(origins("ka", BIAS_ROUNDS), windows):
        start = pl.multiple_of(source * (2 * span), 2 * span)
        window = window_ref[window_ref.shape[0] - span :]
        term[pl.ds(start, span), :pair] = window[:, :pair]
        term[pl.ds(start + span, span), :pair] = window[:, pair : 2 * pair]
    picked[...] = jnp.dot(term[...].T.astype(BF16), picks_ref[...], preferred_element_type=F32)
    count, _, width = blocks_ref.shape
    group = operator_group(count // pb_count, pb_count)
    places = [group.index(n) for n in range(count)]
    for at in range(0, width, LANES):
        tile = jnp.concatenate([blocks_ref[n, :, at : at + LANES] for n in places], axis=0)
        turned[at : at + LANES] = tile.T.astype(F32)
    shares = turned[pairs : pairs + 3]
    lane = lax.broadcasted_iota(jnp.int32, shares.shape, 1)
    shares = jnp.where(lax.rem(lane, 2 * span) == ka_pos, shares, 0.0)
    shares = jnp.sum(jnp.sum(shares, axis=0, keepdims=True), axis=1, keepdims=True)
    energy_ref[...] = shares / normalizer
    lane = lax.broadcasted_iota(jnp.int32, (M, LANES), 1)
    imaginary = lax.rem(lane, 2 * span) >= span
    sums = [jnp.zeros((M, LANES), F32) for _ in range(NOCC)]
    for degree in range(1, TAYLOR + 1):
        stride = M if degree == 1 else ROWS
        straight = [jnp.zeros((M, LANES), F32) for _ in range(NOCC)]
        crossed = [jnp.zeros((M, LANES), F32) for _ in range(NOCC)]
        for c in range(M):
            column = turned[pl.ds(c, M, stride=M), :]
            for i in range(NOCC):
                at = i * stride + c
                straight[i] += column * picked[at : at + 1, :LANES]
                crossed[i] += column * picked[at : at + 1, LANES:]
        for i in range(NOCC):
            other = jnp.where(
                imaginary, pltpu.roll(crossed[i], span, 1), pltpu.roll(crossed[i], LANES - span, 1)
            )
            applied = straight[i] + other
            applied = applied + pltpu.roll(applied, LANES // pb_count, 1)
            current = applied / degree
            sums[i] = sums[i] + current
            term[i * ROWS : i * ROWS + M] = current if degree < TAYLOR else sums[i]
        if degree < TAYLOR:
            picked[...] = jnp.dot(
                term[...].astype(BF16), picks_ref[...], preferred_element_type=F32
            )
    turned[:LANES] = term[...].T
    both = turned[pl.ds(pl.multiple_of(ka_pos * (2 * span), 2 * span), 2 * span), :]
    both = jnp.concatenate([both[:, i * ROWS : i * ROWS + M] for i in range(NOCC)], axis=1)
    both = jnp.concatenate([both[:span], both[span:]], axis=1)
    for k in range(k_local):
        out_ref[k] = orbitals_ref[k] + both[k * walkers : (k + 1) * walkers]


def call(kernel, out, scratch=(), scalars=0, operands=0, flops=None):
    spaces = [pltpu.SMEM] * scalars + [pltpu.VMEM] * operands
    cost = None
    if flops is not None:
        cost = pl.CostEstimate(flops=flops, bytes_accessed=0, transcendentals=0)
    return pl.pallas_call(
        kernel,
        out_shape=out,
        in_specs=[pl.BlockSpec(memory_space=space) for space in spaces],
        out_specs=jax.tree.map(lambda _: pl.BlockSpec(memory_space=pltpu.VMEM), out),
        scratch_shapes=list(scratch),
        cost_estimate=cost,
        compiler_params=pltpu.CompilerParams(vmem_limit_bytes=24 * 2**20),
    )


def direct(green, fields, orbitals, chol_half, chol_full, chol_count, kq_map):
    k_local, pair_width, chol_cols = chol_half.shape[1], chol_half.shape[3], chol_half.shape[4]
    ka_count, pb_count = lax.axis_size("ka"), lax.axis_size("pb")
    walkers = ka_count
    kpoints = green.shape[3]
    span = k_local * walkers
    shape = jax.ShapeDtypeStruct
    tiles = chol_cols // LANES
    own_green = green.reshape(kpoints, 2 * pair_width)
    greens = exchange(own_green, "ka", GREEN_ROUNDS)
    half = chol_half.reshape(k_local, 2, pair_width, chol_cols)
    full = jnp.transpose(
        chol_full.reshape(k_local, 2, M * M, tiles, LANES), (0, 2, 3, 1, 4)
    ).reshape(k_local, M * M * tiles * 2, LANES)
    own_fields = fields.reshape(walkers, chol_cols)
    own_orbitals = orbitals.reshape(k_local, walkers, 2 * pair_width)
    mask, picks = call(
        functools.partial(prepare_kernel, ka_count, pb_count, walkers),
        (shape((2 * walkers, chol_cols), F32), shape((LANES, 2 * LANES), BF16)),
        scalars=2,
        flops=10**9,
    )(kq_map, chol_count)
    bias, own = call(
        functools.partial(bias_kernel, ka_count, k_local),
        (
            shape((2 * walkers + span, chol_cols), F32),
            shape((k_local, 2 * walkers, pair_width), F32),
        ),
        [pltpu.VMEM((walkers, kpoints, 2 * pair_width), F32)],
        operands=len(greens) + 3,
    )(*greens, half, own_orbitals, mask)
    parts = exchange(bias, "ka", BIAS_ROUNDS)
    shares = call(
        functools.partial(exchange_kernel, k_local),
        shape((walkers, LANES), F32),
        operands=3,
    )(own, half, mask)
    width = -(-(M * M + 3) // LANES) * LANES
    blocks = call(
        functools.partial(operator_kernel, k_local),
        shape((ka_count * pb_count, 2 * span, width), BF16),
        [pltpu.VMEM((2 * M * M * tiles, LANES), F32)],
        operands=len(parts) + 4,
    )(*parts, own_fields, mask, shares, full)
    group = operator_group(ka_count, pb_count)
    blocks = lax.all_to_all(
        blocks, ("pb", "ka"), 0, 0, axis_index_groups=[group], tiled=True
    )
    propagated, energy = call(
        functools.partial(taylor_kernel, pb_count, float(pb_count * chol_cols)),
        (shape((k_local, walkers, 2 * pair_width), F32), shape((1, 1), F32)),
        [
            pltpu.VMEM((width, LANES), F32),
            pltpu.VMEM((NOCC * ROWS, 2 * LANES), F32),
            pltpu.VMEM((LANES, LANES), F32),
        ],
        operands=len(parts) + 3,
    )(blocks, *parts, picks, own_orbitals)
    return (propagated[None], energy)


def on_device(green, fields, orbitals, chol_half, chol_full, chol_count, kq_map):
    ka_count, pb_count = lax.axis_size("ka"), lax.axis_size("pb")
    walkers = orbitals.shape[2]
    fits = 2 * pb_count * kq_map.shape[1] * walkers == LANES
    fits = fits and chol_half.shape[1] * walkers == 8 and chol_half.shape[4] == 2 * LANES
    fits = fits and ka_count == 4
    if fits and chol_half.shape[0] == 1 and walkers == ka_count:
        return direct(green, fields, orbitals, chol_half, chol_full, chol_count, kq_map)
    return with_collectives(green, fields, orbitals, chol_half, chol_full, chol_count, kq_map)


def solution(mesh):
    placed = (
        P("wa", ("grp", "ka"), "pb", None, None),
        P("wa", "pb", "grp", None),
        P("wa", "ka", "grp", None),
        P("pb", "ka", None, None, None),
        P("pb", "ka", None, None, None),
        P(),
        P(),
    )
    return jax.shard_map(
        on_device,
        mesh=mesh,
        in_specs=placed,
        out_specs=(P("wa", "ka", "grp", None), P("wa", ("grp", "ka"))),
        check_vma=False,
    )
```

```python
import functools

import jax
import jax.numpy as jnp
from jax import lax
from jax.experimental import pallas as pl
from jax.experimental.pallas import tpu as pltpu
from jax.sharding import PartitionSpec as P

M = 26
NOCC = 4
TAYLOR = 3
LANES = 128
ROWS = 32

GREEN_ROUNDS = (
    ((3, 0), (2, 1), (1, 3), (0, 2)),
    ((3, 1), (2, 0), (0, 3), (1, 2)),
    ((1, 0), (3, 2), (2, 3), (0, 1)),
)[::-1]
BIAS_ROUNDS = (
    ((0, 1), (1, 3), (2, 0), (3, 2)),
    ((0, 3), (3, 0), (1, 2), (2, 1)),
    ((0, 2), (1, 0), (2, 3), (3, 1)),
)[::-1]


BIAS_STEP = 0.5
PROP_STEP = 0.5

F32 = jnp.float32
BF16 = jnp.bfloat16


def complex_dot(pattern, left_re, left_im, right_re, right_im):
    real_part = jnp.einsum(
        pattern, left_re, right_re, preferred_element_type=jnp.float32
    ) - jnp.einsum(pattern, left_im, right_im, preferred_element_type=jnp.float32)
    imag_part = jnp.einsum(
        pattern, left_re, right_im, preferred_element_type=jnp.float32
    ) + jnp.einsum(pattern, left_im, right_re, preferred_element_type=jnp.float32)
    return (real_part, imag_part)


def make_picker(wanted):

    def picker(shard_rows):
        row_count = shard_rows.shape[0]
        select = (wanted[:, None] == jnp.arange(row_count, dtype=jnp.int32)[None, :]).astype(
            jnp.bfloat16
        )
        return jnp.dot(select, shard_rows, preferred_element_type=jnp.float32)

    return picker


def with_collectives(green, fields, orbitals, chol_half, chol_full, chol_count, kq_map):
    q_local = chol_half.shape[0]
    k_local = chol_half.shape[1]
    pair_width = chol_half.shape[3]
    chol_cols = chol_half.shape[4]
    ka_count = lax.axis_size("ka")
    pb_count = lax.axis_size("pb")
    ka_pos = lax.axis_index("ka")
    pb_pos = lax.axis_index("pb")
    local_green = lax.all_to_all(green, "ka", split_axis=3, concat_axis=1, tiled=True)
    walkers = local_green.shape[1]
    per_device = walkers // ka_count
    greens = local_green[0].reshape(walkers, q_local, k_local, 2, pair_width)
    counts = lax.dynamic_slice_in_dim(chol_count, pb_pos * q_local, q_local)
    vec_mask = (jnp.arange(chol_cols, dtype=jnp.int32)[None, :] < counts[:, None]).astype(
        jnp.float32
    )
    bias_re, bias_im = complex_dot(
        "wqkx,qkxn->qwn",
        greens[:, :, :, 0],
        greens[:, :, :, 1],
        chol_half[:, :, 0],
        chol_half[:, :, 1],
    )
    own_rows = (jnp.arange(walkers, dtype=jnp.int32) // per_device == ka_pos).astype(jnp.float32)
    bias_re, bias_im = lax.psum((bias_re, bias_im), "ka")
    bias_re = bias_re * vec_mask[:, None, :]
    bias_im = bias_im * vec_mask[:, None, :]
    hartree = 0.5 * jnp.sum(bias_re * bias_re + bias_im * bias_im, axis=(0, 2)) * own_rows
    field_now = jnp.transpose(fields, (1, 0, 2, 3)).reshape(q_local, walkers, chol_cols)
    shift_re = ((field_now - BIAS_STEP * bias_re) * vec_mask[:, None, :]).astype(jnp.bfloat16)
    shift_im = (-BIAS_STEP * bias_im * vec_mask[:, None, :]).astype(jnp.bfloat16)
    exchange = jnp.zeros((walkers,), jnp.float32)
    for transfer in range(q_local):
        for kpoint in range(k_local):
            chol_row = chol_half[transfer, kpoint].reshape(2, NOCC, M, chol_cols)
            green_row = greens[:, transfer, kpoint].reshape(walkers, 2, NOCC, M)
            cross_re, cross_im = complex_dot(
                "ipn,wjp->wijn", chol_row[0], chol_row[1], green_row[:, 0], green_row[:, 1]
            )
            exchange = exchange + 0.5 * jnp.sum(
                (cross_re * cross_re + cross_im * cross_im) * vec_mask[transfer], axis=(1, 2, 3)
            )
    prop_re, prop_im = complex_dot(
        "qwn,qkyn->qwky", shift_re, shift_im, chol_full[:, :, 0], chol_full[:, :, 1]
    )
    shape = (q_local, walkers, k_local, M, M)
    oper_re = (PROP_STEP * prop_re).astype(jnp.bfloat16).reshape(shape)
    oper_im = (PROP_STEP * prop_im).astype(jnp.bfloat16).reshape(shape)
    normalizer = q_local * pb_count * chol_cols
    total_energy = lax.psum(hartree - exchange, ("ka", "pb")) / normalizer
    energy = lax.dynamic_slice_in_dim(total_energy, ka_pos * per_device, per_device).reshape(
        1, per_device
    )
    initial = orbitals[0].reshape(k_local, walkers, 2, NOCC, M)
    row_width = 2 * pair_width
    my_rows = lax.dynamic_slice_in_dim(kq_map, pb_pos * q_local, q_local, 0)
    wanted = lax.dynamic_slice_in_dim(my_rows, ka_pos * k_local, k_local, 1).reshape(
        q_local * k_local
    )
    picker = make_picker(wanted)
    current = initial
    summed_terms = initial
    for degree in range(1, TAYLOR + 1):
        rounded = current.astype(jnp.bfloat16).reshape(k_local, walkers * row_width)
        fetched = picker(lax.all_gather(rounded, "ka", axis=0, tiled=True))
        shifted_rows = fetched.astype(jnp.bfloat16).reshape(q_local, k_local, walkers, 2, NOCC, M)
        out_re, out_im = complex_dot(
            "xwkpq,xkwiq->kwip",
            oper_re,
            oper_im,
            shifted_rows[:, :, :, 0],
            shifted_rows[:, :, :, 1],
        )
        applied = jnp.stack([out_re, out_im], axis=2)
        applied = lax.psum(applied, "pb")
        current = applied / degree
        summed_terms = summed_terms + current
    propagated = summed_terms.reshape(1, k_local, walkers, row_width)
    return (propagated, energy)


def exchange(array, axis, rounds):
    return [array] + [lax.ppermute(array, axis, pairs) for pairs in rounds]


def origins(axis, rounds):
    at = lax.axis_index(axis)
    found = [at]
    for pairs in rounds:
        source = jnp.int32(0)
        for sender, receiver in pairs:
            source = jnp.where(at == receiver, sender, source)
        found.append(source)
    return found


def operator_group(ka_count, pb_count):
    first = (pb_count - 1) * ka_count + ka_count // 2
    rest = [at for at in range(pb_count * ka_count) if at != first]
    return [first] + rest[::-1]


def prepare_kernel(ka_count, pb_count, walkers, map_ref, count_ref, mask_ref, picks_ref):
    kept = count_ref[lax.axis_index("pb")]
    column = lax.broadcasted_iota(jnp.int32, mask_ref.shape, 1)
    mask_ref[...] = jnp.where(column < kept, 1.0, 0.0)
    kpoints = map_ref.shape[1]
    k_local = kpoints // ka_count
    span = k_local * walkers
    lane = lax.broadcasted_iota(jnp.int32, (1, LANES), 1)
    lane_q = lane // (LANES // pb_count)
    lane_ka = lax.rem(lane, LANES // pb_count) // (2 * span)
    lane_part = lax.rem(lane, 2 * span) // span
    lane_k = lane_ka * k_local + lax.rem(lane, span) // walkers
    wanted = jnp.zeros((1, LANES), jnp.int32)
    for q in range(pb_count):
        for k in range(kpoints):
            source = map_ref[q, k]
            source = source // k_local * (2 * span) + lax.rem(source, k_local) * walkers
            wanted = jnp.where((lane_q == q) & (lane_k == k), source, wanted)
    wanted = wanted + lax.rem(lane, walkers)
    row = lax.broadcasted_iota(jnp.int32, (LANES, LANES), 0)
    real = jnp.where(row == wanted, 1.0, 0.0)
    imag = jnp.where(row == wanted + span, jnp.where(lane_part == 0, 1.0, -1.0), 0.0)
    picks_ref[...] = jnp.concatenate([real, imag], axis=1).astype(BF16)


def bias_kernel(ka_count, k_local, *refs):
    *greens, chol_ref, orbitals_ref, mask_ref, bias_ref, own_ref, table = refs
    for source, green_ref in zip(origins("ka", GREEN_ROUNDS), greens):
        table[source] = green_ref[...].astype(F32)
    first = lax.axis_index("ka") * k_local
    width = chol_ref.shape[2]
    rows = 2 * ka_count
    total = jnp.zeros((rows, bias_ref.shape[1]), F32)
    for k in range(k_local):
        green = jnp.concatenate(
            [table[w, pl.ds(first + k, 1), :] for w in range(ka_count)], axis=0
        )
        real, imag = green[:, :width], green[:, width:]
        both = jnp.concatenate([real, imag], axis=0)
        turned = jnp.concatenate([-imag, real], axis=0)
        own_ref[k] = both
        total += jnp.dot(both.astype(BF16), chol_ref[k, 0], preferred_element_type=F32)
        total += jnp.dot(turned.astype(BF16), chol_ref[k, 1], preferred_element_type=F32)
    bias_ref[:rows] = total * mask_ref[...]
    window = jnp.concatenate([orbitals_ref[k] for k in range(k_local)], axis=0)
    count, width = window.shape
    bias_ref[rows : rows + count, :width] = window
    bias_ref[rows : rows + count, width:] = jnp.zeros((count, bias_ref.shape[1] - width), F32)


def exchange_kernel(k_local, own_ref, chol_ref, mask_ref, out_ref):
    walkers, width, columns = own_ref.shape[1] // 2, own_ref.shape[2], chol_ref.shape[3]
    rows = 2 * walkers
    lane = lax.broadcasted_iota(jnp.int32, (rows, LANES), 1)
    total = jnp.zeros((rows, columns), F32)
    for k in range(k_local):
        both = jnp.concatenate([own_ref[k], jnp.zeros((rows, LANES - width), F32)], axis=1)
        turned = jnp.concatenate([-both[walkers:], both[:walkers]], axis=0)
        sides = []
        for side in (both, turned):
            rolled = {
                step: side if step == 0 else pltpu.roll(side, (step * M) % LANES, 1)
                for step in range(1 - NOCC, NOCC)
            }
            blocks = []
            for i in range(NOCC):
                inside = (lane >= i * M) & (lane < (i + 1) * M)
                for j in range(NOCC):
                    blocks.append(jnp.where(inside, rolled[i - j], 0.0))
            sides.append(jnp.concatenate(blocks, axis=0)[:, :width].astype(BF16))
        cross = jnp.dot(sides[0], chol_ref[k, 0], preferred_element_type=F32)
        cross += jnp.dot(sides[1], chol_ref[k, 1], preferred_element_type=F32)
        cross = cross * cross
        for block in range(NOCC * NOCC):
            total += cross[block * rows : (block + 1) * rows]
    total = total * mask_ref[:rows]
    total = total[:walkers] + total[walkers:]
    summed = 0.5 * jnp.sum(total, axis=1, keepdims=True)
    out_ref[...] = jnp.broadcast_to(summed, out_ref.shape)


def operator_kernel(k_local, *refs):
    *parts, fields_ref, mask_ref, exchange_ref, chol_ref, out_ref, products = refs
    walkers, columns = fields_ref.shape
    bias = parts[0][: 2 * walkers]
    for part in parts[1:]:
        bias = bias + part[: 2 * walkers]
    pairs = M * M
    tiles = columns // LANES
    group = LANES // (2 * tiles)
    bias_re, bias_im = bias[:walkers], bias[walkers:]
    hartree = 0.5 * jnp.sum(bias_re * bias_re + bias_im * bias_im, axis=1, keepdims=True)
    own = lax.broadcasted_iota(jnp.int32, (walkers, 1), 0) == lax.axis_index("ka")
    energy = jnp.where(own, hartree, 0.0) - exchange_ref[:, :1]
    kept = mask_ref[:walkers]
    shift_re = (fields_ref[...] - BIAS_STEP * bias_re) * kept
    shift_im = -BIAS_STEP * bias_im * kept
    span = k_local * walkers
    weights = []
    for k in range(k_local):
        before, after = k * walkers, span - (k + 1) * walkers
        pieces = []
        for tile in range(tiles):
            at = slice(tile * LANES, (tile + 1) * LANES)
            for first, second in ((shift_re, shift_im), (-shift_im, shift_re)):
                for side in (first, second):
                    pieces += [(before, None), (walkers, side[:, at]), (after, None)]
                pieces.append((group - 2 * span, None))
        weights.append(
            jnp.concatenate(
                [jnp.zeros((n, LANES), F32) if p is None else p for n, p in pieces if n], axis=0
            ).astype(BF16)
        )
    products[...] = lax.dot_general(
        jnp.concatenate([chol_ref[k] for k in range(k_local)], axis=1),
        jnp.concatenate(weights, axis=1),
        (((1,), (1,)), ((), ())),
        preferred_element_type=F32,
    )
    copies, rows, width = out_ref.shape
    lane = lax.broadcasted_iota(jnp.int32, (LANES, LANES), 1)
    place = lax.broadcasted_iota(jnp.int32, (rows, LANES), 1)
    step = 2 * tiles
    for at in range(0, width, LANES):
        held = min(LANES, pairs - at)
        merged = products[pl.ds(step * at, held, stride=step), :]
        for part in range(1, step):
            row = products[pl.ds(step * at + part, held, stride=step), :]
            merged = jnp.where(lane[:held] >= part * group, row, merged)
        if held < LANES:
            merged = jnp.concatenate([merged, jnp.zeros((LANES - held, LANES), F32)], axis=0)
        block = merged.T
        block = PROP_STEP * sum(block[n * group : n * group + rows] for n in range(step))
        if held < LANES:
            share = jnp.concatenate([energy, jnp.zeros((rows - walkers, 1), F32)], axis=0)
            for piece in range(3):
                head = share.astype(BF16).astype(F32)
                block = jnp.where(place == held + piece, head, block)
                share = share - head
        block = block.astype(BF16)
        for copy in range(copies):
            out_ref[copy, :, at : at + LANES] = block


def taylor_kernel(pb_count, normalizer, blocks_ref, *refs):
    *windows, picks_ref, orbitals_ref, out_ref, energy_ref, turned, picked, term = refs
    pairs = M * M
    pair = NOCC * M
    k_local, walkers, _ = out_ref.shape
    span = k_local * walkers
    ka_pos = lax.axis_index("ka")
    term[...] = jnp.zeros_like(term)
    for source, window_ref in zip(origins("ka", BIAS_ROUNDS), windows):
        start = pl.multiple_of(source * (2 * span), 2 * span)
        window = window_ref[window_ref.shape[0] - span :]
        term[pl.ds(start, span), :pair] = window[:, :pair]
        term[pl.ds(start + span, span), :pair] = window[:, pair : 2 * pair]
    picked[...] = jnp.dot(term[...].T.astype(BF16), picks_ref[...], preferred_element_type=F32)
    count, _, width = blocks_ref.shape
    group = operator_group(count // pb_count, pb_count)
    places = [group.index(n) for n in range(count)]
    turned[width:] = jnp.zeros((turned.shape[0] - width, LANES), F32)
    for at in range(0, width, LANES):
        tile = jnp.concatenate([blocks_ref[n, :, at : at + LANES] for n in places], axis=0)
        turned[at : at + LANES] = tile.T.astype(F32)
    shares = turned[pairs : pairs + 3]
    lane = lax.broadcasted_iota(jnp.int32, shares.shape, 1)
    shares = jnp.where(lax.rem(lane, 2 * span) == ka_pos, shares, 0.0)
    shares = jnp.sum(jnp.sum(shares, axis=0, keepdims=True), axis=1, keepdims=True)
    energy_ref[...] = shares / normalizer
    lane = lax.broadcasted_iota(jnp.int32, (ROWS, LANES), 1)
    imaginary = lax.rem(lane, 2 * span) >= span
    sums = [None] * NOCC
    for degree in range(1, TAYLOR + 1):
        stride = M if degree == 1 else ROWS
        straight = [jnp.zeros((ROWS, LANES), F32) for _ in range(NOCC)]
        crossed = [jnp.zeros((ROWS, LANES), F32) for _ in range(NOCC)]
        for c in range(M):
            column = turned[pl.ds(c, ROWS, stride=M), :]
            for i in range(NOCC):
                at = i * stride + c
                straight[i] += column * picked[at : at + 1, :LANES]
                crossed[i] += column * picked[at : at + 1, LANES:]
        currents = []
        for i in range(NOCC):
            other = jnp.where(
                imaginary, pltpu.roll(crossed[i], span, 1), pltpu.roll(crossed[i], LANES - span, 1)
            )
            applied = straight[i] + other
            applied = applied + pltpu.roll(applied, LANES // pb_count, 1)
            currents.append(applied * (1.0 / degree))
            sums[i] = currents[i] if degree == 1 else sums[i] + currents[i]
        if degree < TAYLOR:
            rows = jnp.concatenate(currents, axis=0).astype(BF16)
            picked[...] = jnp.dot(rows, picks_ref[...], preferred_element_type=F32)
    term[...] = jnp.concatenate(sums, axis=0).T
    both = term[pl.ds(pl.multiple_of(ka_pos * (2 * span), 2 * span), 2 * span), :]
    both = jnp.concatenate([both[:, i * ROWS : i * ROWS + M] for i in range(NOCC)], axis=1)
    both = jnp.concatenate([both[:span], both[span:]], axis=1)
    for k in range(k_local):
        out_ref[k] = orbitals_ref[k] + both[k * walkers : (k + 1) * walkers]


def call(kernel, out, scratch=(), scalars=0, operands=0, flops=None):
    spaces = [pltpu.SMEM] * scalars + [pltpu.VMEM] * operands
    cost = None
    if flops is not None:
        cost = pl.CostEstimate(flops=flops, bytes_accessed=0, transcendentals=0)
    return pl.pallas_call(
        kernel,
        out_shape=out,
        in_specs=[pl.BlockSpec(memory_space=space) for space in spaces],
        out_specs=jax.tree.map(lambda _: pl.BlockSpec(memory_space=pltpu.VMEM), out),
        scratch_shapes=list(scratch),
        cost_estimate=cost,
        compiler_params=pltpu.CompilerParams(vmem_limit_bytes=24 * 2**20),
    )


def direct(green, fields, orbitals, chol_half, chol_full, chol_count, kq_map):
    k_local, pair_width, chol_cols = chol_half.shape[1], chol_half.shape[3], chol_half.shape[4]
    ka_count, pb_count = lax.axis_size("ka"), lax.axis_size("pb")
    walkers = ka_count
    kpoints = green.shape[3]
    span = k_local * walkers
    shape = jax.ShapeDtypeStruct
    tiles = chol_cols // LANES
    own_green = green.reshape(kpoints, 2 * pair_width)
    greens = exchange(own_green, "ka", GREEN_ROUNDS)
    half = chol_half.reshape(k_local, 2, pair_width, chol_cols)
    full = jnp.transpose(
        chol_full.reshape(k_local, 2, M * M, tiles, LANES), (0, 2, 3, 1, 4)
    ).reshape(k_local, M * M * tiles * 2, LANES)
    own_fields = fields.reshape(walkers, chol_cols)
    own_orbitals = orbitals.reshape(k_local, walkers, 2 * pair_width)
    mask, picks = call(
        functools.partial(prepare_kernel, ka_count, pb_count, walkers),
        (shape((2 * walkers, chol_cols), F32), shape((LANES, 2 * LANES), BF16)),
        scalars=2,
        flops=10**9,
    )(kq_map, chol_count)
    bias, own = call(
        functools.partial(bias_kernel, ka_count, k_local),
        (
            shape((2 * walkers + span, chol_cols), F32),
            shape((k_local, 2 * walkers, pair_width), F32),
        ),
        [pltpu.VMEM((walkers, kpoints, 2 * pair_width), F32)],
        operands=len(greens) + 3,
    )(*greens, half, own_orbitals, mask)
    parts = exchange(bias, "ka", BIAS_ROUNDS)
    shares = call(
        functools.partial(exchange_kernel, k_local),
        shape((walkers, LANES), F32),
        operands=3,
    )(own, half, mask)
    width = -(-(M * M + 3) // LANES) * LANES
    blocks = call(
        functools.partial(operator_kernel, k_local),
        shape((ka_count * pb_count, 2 * span, width), BF16),
        [pltpu.VMEM((2 * M * M * tiles, LANES), F32)],
        operands=len(parts) + 4,
    )(*parts, own_fields, mask, shares, full)
    group = operator_group(ka_count, pb_count)
    blocks = lax.all_to_all(
        blocks, ("pb", "ka"), 0, 0, axis_index_groups=[group], tiled=True
    )
    propagated, energy = call(
        functools.partial(taylor_kernel, pb_count, float(pb_count * chol_cols)),
        (shape((k_local, walkers, 2 * pair_width), F32), shape((1, 1), F32)),
        [
            pltpu.VMEM((ROWS * M, LANES), F32),
            pltpu.VMEM((NOCC * ROWS, 2 * LANES), F32),
            pltpu.VMEM((LANES, LANES), F32),
        ],
        operands=len(parts) + 3,
    )(blocks, *parts, picks, own_orbitals)
    return (propagated[None], energy)


def on_device(green, fields, orbitals, chol_half, chol_full, chol_count, kq_map):
    ka_count, pb_count = lax.axis_size("ka"), lax.axis_size("pb")
    walkers = orbitals.shape[2]
    fits = 2 * pb_count * kq_map.shape[1] * walkers == LANES
    fits = fits and chol_half.shape[1] * walkers == 8 and chol_half.shape[4] == 2 * LANES
    fits = fits and ka_count == 4
    if fits and chol_half.shape[0] == 1 and walkers == ka_count:
        return direct(green, fields, orbitals, chol_half, chol_full, chol_count, kq_map)
    return with_collectives(green, fields, orbitals, chol_half, chol_full, chol_count, kq_map)


def solution(mesh):
    placed = (
        P("wa", ("grp", "ka"), "pb", None, None),
        P("wa", "pb", "grp", None),
        P("wa", "ka", "grp", None),
        P("pb", "ka", None, None, None),
        P("pb", "ka", None, None, None),
        P(),
        P(),
    )
    return jax.shard_map(
        on_device,
        mesh=mesh,
        in_specs=placed,
        out_specs=(P("wa", "ka", "grp", None), P("wa", ("grp", "ka"))),
        check_vma=False,
    )
```
